128 devices in a mesh: seq: 32 (over z, y_hi, x), tensor: 4 (over y_lo, core).
Axes of the slice: x: 4, y: 4 (y_hi: 2, y_lo: 2; y = y_hi * 2 + y_lo), z: 4, core: 2. Of those that a mesh axis runs over, the one named last changes fastest.
Arguments:
- inputs: bfloat16 [8192, 768], P('seq'), may hold values from -6 to 6
- head_weights: bfloat16 [3, 768, 768], P(None, None, 'tensor'), may hold values from -0.3125 to 0.3125
- out_weight: bfloat16 [768, 768], P('tensor'), may hold values from -0.21875 to 0.21875
- up_weight: bfloat16 [768, 3072], P(None, 'tensor'), may hold values from -0.21875 to 0.21875
- down_weight: bfloat16 [3072, 768], P('tensor'), may hold values from -0.109375 to 0.109375
- in_gain: float32 [768], replicated, may hold values from 0.1 to 1.9
- in_shift: float32 [768], replicated, may hold values from -1.5 to 1.5
- mix_gain: float32 [768], P('tensor'), may hold values from 0.1 to 1.9
- mix_shift: float32 [768], P('tensor'), may hold values from -1.5 to 1.5
- mid_gain: float32 [768], replicated, may hold values from 0.1 to 1.9
- mid_shift: float32 [768], replicated, may hold values from -1.5 to 1.5
- inner_gain: float32 [3072], P('tensor'), may hold values from 0.1 to 1.9
- inner_shift: float32 [3072], P('tensor'), may hold values from -1.5 to 1.5
- valid_length: int32 [1], replicated, may hold values from 8064 to 8192
- cotangent: bfloat16 [8192, 768], P('seq'), may hold values from -6 to 6
Outputs:
- result: bfloat16 [8192, 768], P('seq')
- inputs_grad: bfloat16 [8192, 768], P('seq')
- head_weights_grad: float32 [3, 768, 768], P(None, None, 'tensor')
- out_weight_grad: float32 [768, 768], P('tensor')
- up_weight_grad: float32 [768, 3072], P(None, 'tensor')
- down_weight_grad: float32 [3072, 768], P('tensor')
- in_gain_grad: float32 [768], replicated
- in_shift_grad: float32 [768], replicated
- mix_gain_grad: float32 [768], P('tensor')
- mix_shift_grad: float32 [768], P('tensor')
- mid_gain_grad: float32 [768], replicated
- mid_shift_grad: float32 [768], replicated
- inner_gain_grad: float32 [3072], P('tensor')
- inner_shift_grad: float32 [3072], P('tensor')
The draws below stay inside these ranges and needn't reach their ends.
Inputs may be any that keep to these rules, and one draw needn't show every extreme that they name: Tokens at positions valid_length and above are padding.
All inputs are finite; a program needn't handle non-finite values.
Results may differ from the reference program's by a relative error of at most 0.03.
Values may be sent and summed in bfloat16 or wider, within the bound.
No kernel may reach another device: no remote copies, remote signals or barrier semaphores. Data moves between devices by JAX's collectives and lax.ppermute only.
A program may use at most 192 MiB of HBM per device.

```python
import jax
import jax.numpy as jnp
from jax import lax

D = 768
FF = 3072
HEADS = 12
HDIM = 64
TOK_DEV = 256
SEQLEN = 8192
SEG_A = 2048
SEG_B = 4096
SEG_C = 8192
SEG_D = 16384
SEG_E = 32768


def level_of(key, shape, cuts, least, top_value):
    loudness, own = 1.0, jax.random.fold_in(key, 6)
    for dim, shards_of in cuts:
        steps = jnp.exp(jax.random.uniform(jax.random.fold_in(own, dim), (shards_of,), jnp.float32, least / len(cuts), top_value / len(cuts)))
        loudness = loudness * jnp.repeat(steps, shape[dim] // shards_of).reshape([-1 if axis == dim else 1 for axis in range(len(shape))])
    return loudness


def noise(key, extent, scale, most, pieces=(), kind=jnp.bfloat16):
    level = level_of(key, extent, pieces, -0.22, 0.18) if pieces else 1.0
    result = jax.random.normal(key, extent, jnp.float32) * scale * level
    return jnp.minimum(jnp.maximum(result, -most), most).astype(kind)


def setup_inputs(seed: int = 0) -> dict:
    arg_keys = jax.random.split(jax.random.key(seed), 16)
    return {
        "inputs": noise(arg_keys[0], (SEQLEN, D), 1.0, 6.0, ((0, 32),)),
        "head_weights": noise(arg_keys[1], (3, D, D), (D // 2) ** -0.5, 0.3125, ((2, 4),)),
        "out_weight": noise(arg_keys[2], (D, D), D ** -0.5, 0.21875, ((0, 4),)),
        "up_weight": noise(arg_keys[3], (D, FF), D ** -0.5, 0.21875, ((1, 4),)),
        "down_weight": noise(arg_keys[4], (FF, D), FF ** -0.5, 0.109375, ((0, 4),)),
        "in_gain": jnp.clip(1.0 + 0.18 * jax.random.normal(arg_keys[5], (D,), jnp.float32), 0.1, 1.9),
        "in_shift": noise(arg_keys[6], (D,), 0.3, 1.5, (), jnp.float32),
        "mix_gain": jnp.clip(1.0 + 0.18 * jax.random.normal(arg_keys[7], (D,), jnp.float32), 0.1, 1.9),
        "mix_shift": noise(arg_keys[8], (D,), 0.3, 1.5, ((0, 4),), jnp.float32),
        "mid_gain": jnp.clip(1.0 + 0.18 * jax.random.normal(arg_keys[9], (D,), jnp.float32), 0.1, 1.9),
        "mid_shift": noise(arg_keys[10], (D,), 0.3, 1.5, (), jnp.float32),
        "inner_gain": jnp.clip(1.0 + 0.18 * jax.random.normal(arg_keys[11], (FF,), jnp.float32), 0.1, 1.9),
        "inner_shift": noise(arg_keys[12], (FF,), 0.3, 1.5, ((0, 4),), jnp.float32),
        "valid_length": jax.random.randint(arg_keys[13], (1,), SEQLEN - TOK_DEV // 2, SEQLEN + 1).astype(jnp.int32),
        "cotangent": noise(arg_keys[14], (SEQLEN, D), 1.0, 6.0, ((0, 32),)),
    }


EPSILON = 1e-05
DILATIONS = (1, 2, 4, 6, 12)
EXACT = lax.Precision.HIGHEST

@jax.custom_vjp
def low(v):
    return lax.optimization_barrier(v.astype(jnp.bfloat16)).astype(jnp.float32)

@jax.custom_vjp
def low_back(v):
    return v

def low_keep(v):
    return (low(v), None)

def low_pass(kept, grad):
    return (grad,)

def back_keep(v):
    return (v, None)

def back_low(kept, grad):
    return (low(grad),)
low.defvjp(low_keep, low_pass)
low_back.defvjp(back_keep, back_low)

def rounded(values):
    return low(low_back(values))

def layer_norm(values, norm_gain, norm_shift):
    row_mean = lax.optimization_barrier(jnp.mean(values, axis=-1, keepdims=True))
    spread = lax.optimization_barrier(jnp.mean(values * values, axis=-1, keepdims=True)) - row_mean * row_mean
    return (values - row_mean) * lax.rsqrt(spread + EPSILON) * norm_gain + norm_shift

def pattern_weights(row_pos, col_pos, head_index, valid_count):
    segment_sizes = (SEG_A, SEG_B, SEG_C, SEG_D, SEG_E)
    weight_sum = jnp.zeros((row_pos.shape[0], col_pos.shape[0]), jnp.float32)
    for segment, dilation in zip(segment_sizes, DILATIONS):
        offset = head_index % dilation
        matches = row_pos[:, None] // segment == col_pos[None, :] // segment
        matches = matches & (row_pos[:, None] % dilation == offset) & (col_pos[None, :] % dilation == offset)
        weight_sum = weight_sum + matches.astype(jnp.float32)
    allowed = (col_pos[None, :] <= row_pos[:, None]) & (col_pos[None, :] < valid_count)
    return jnp.where(allowed, weight_sum, 0.0)

def head_block(queries, key_block, value_block, multiple):
    scores = low_back(jnp.dot(queries, key_block.T, precision=EXACT) * HDIM ** (-0.5))
    present = multiple > 0
    highest = lax.optimization_barrier(jnp.max(jnp.where(present, scores, -1e+30), axis=1, keepdims=True))
    weighted = multiple * jnp.exp(jnp.where(present, scores - highest, -10000.0))
    shares = weighted / lax.optimization_barrier(jnp.sum(weighted, axis=1, keepdims=True))
    return low_back(jnp.dot(low(shares), value_block, precision=EXACT))

def attend(queries, key_rows, value_rows, valid_count):
    block_rows = min(SEQLEN, 1024)
    block_count = SEQLEN // block_rows
    col_pos = jnp.arange(SEQLEN, dtype=jnp.int32)

    @jax.checkpoint
    def one_block(block_index):
        head_index = (block_index // block_count).astype(jnp.int32)
        row_start = (block_index % block_count * block_rows).astype(jnp.int32)
        zero_index = jnp.zeros((), jnp.int32)
        query_block = lax.dynamic_slice(queries, (row_start, head_index * HDIM), (block_rows, HDIM))
        key_block = lax.dynamic_slice(key_rows, (zero_index, head_index * HDIM), (SEQLEN, HDIM))
        value_block = lax.dynamic_slice(value_rows, (zero_index, head_index * HDIM), (SEQLEN, HDIM))
        row_pos = row_start + jnp.arange(block_rows, dtype=jnp.int32)
        multiple = pattern_weights(row_pos, col_pos, head_index, valid_count)
        return head_block(query_block, key_block, value_block, multiple)
    blocks_out = lax.map(one_block, jnp.arange(HEADS * block_count, dtype=jnp.int32))
    blocks_out = blocks_out.reshape(HEADS, block_count, block_rows, HDIM)
    return blocks_out.transpose(1, 2, 0, 3).reshape(SEQLEN, HEADS * HDIM)

def reference(inputs, head_weights, out_weight, up_weight, down_weight, in_gain, in_shift, mix_gain, mix_shift, mid_gain, mid_shift, inner_gain, inner_shift, valid_length, cotangent):
    valid_count = valid_length[0]
    row_valid = (jnp.arange(SEQLEN, dtype=jnp.int32) < valid_count)[:, None]

    def forward(source, heads_w, out_w, up_w, down_w, gain_in, shift_in, gain_mix, shift_mix, gain_mid, shift_mid, gain_inner, shift_inner):
        normed = low(layer_norm(source, gain_in, shift_in))
        projected = rounded(jnp.einsum('td,cde->cte', normed, heads_w, precision=EXACT))
        mixed = attend(projected[0], projected[1], projected[2], valid_count)
        mix_normed = low(layer_norm(mixed, gain_mix, shift_mix))
        hidden = source + low_back(jnp.dot(mix_normed, out_w, precision=EXACT))
        mid_normed = low(layer_norm(hidden, gain_mid, shift_mid))
        pre_act = low_back(jnp.dot(mid_normed, up_w, precision=EXACT))
        active = jax.nn.gelu(pre_act, approximate=True)
        inner_normed = low(layer_norm(active, gain_inner, shift_inner))
        output = hidden + low_back(jnp.dot(inner_normed, down_w, precision=EXACT))
        return jnp.where(row_valid, output, 0.0)
    floats = (inputs.astype(jnp.float32), head_weights.astype(jnp.float32), out_weight.astype(jnp.float32), up_weight.astype(jnp.float32), down_weight.astype(jnp.float32), in_gain.astype(jnp.float32), in_shift.astype(jnp.float32), mix_gain.astype(jnp.float32), mix_shift.astype(jnp.float32), mid_gain.astype(jnp.float32), mid_shift.astype(jnp.float32), inner_gain.astype(jnp.float32), inner_shift.astype(jnp.float32))
    output, pullback = jax.vjp(forward, *floats)
    gradients = pullback(cotangent.astype(jnp.float32))
    return (output.astype(jnp.bfloat16), gradients[0].astype(jnp.bfloat16), gradients[1], gradients[2], gradients[3], gradients[4], gradients[5], gradients[6], gradients[7], gradients[8], gradients[9], gradients[10], gradients[11], gradients[12])
```

```python
import functools

import jax
import jax.numpy as jnp
import numpy as np
from jax import lax
from jax.experimental import pallas as pl
from jax.experimental.pallas import tpu as pltpu
from jax.sharding import Mesh
from jax.sharding import PartitionSpec as P


HDIM = 64
HEADS_HERE = 3
TOK = 256
PLANE = 8
SLOTS = 128
EPSILON = 1e-05
NONE = -1e30
NEAR = (1, 2, 4, 6, 12)
MID = (2, 4, 6, 12)
FAR = (4, 6, 12)
F32 = jnp.float32
BF16 = jnp.bfloat16
SEQ = ("z", "yh", "x")
TENSOR = ("yl", "c")
FLIP = [(0, 1), (1, 0)]


def dot(a, b, dims=((1,), (0,))):
    return lax.dot_general(a, b, (dims, ((), ())), preferred_element_type=F32)


def split3(v):
    hi = v.astype(BF16).astype(F32)
    mid = (v - hi).astype(BF16).astype(F32)
    return hi, mid, (v - hi - mid).astype(BF16).astype(F32)


def mid_offsets(head):
    slot = lax.broadcasted_iota(jnp.int32, (1, SLOTS), 1)
    return 2 * slot + lax.rem(head, 2)


def far_offsets(head, base):
    slot = lax.broadcasted_iota(jnp.int32, (1, SLOTS), 1)
    which = lax.rem(slot, 4)
    kind = jnp.where(which == 0, 0, 2 * which + 2)
    first = lax.div(base + 12 - head, 12) - 1
    return 12 * (first + lax.div(slot, 4)) + kind + head - base, kind


def one_hot_rows(offsets):
    rows = lax.broadcasted_iota(jnp.int32, (TOK, SLOTS), 0)
    return (rows == offsets).astype(F32).astype(BF16)


def count_table(kind, usable, dilations):
    row = lax.broadcasted_iota(jnp.int32, (16, kind.shape[1]), 0)
    count = jnp.zeros(row.shape, F32)
    for step in dilations:
        count += jnp.where((lax.rem(row, step) == 0) & (lax.rem(kind, step) == 0), 1.0, 0.0)
    live = (count > 0) & usable
    log_count = jnp.log(jnp.maximum(count, 1.0))
    hi = log_count.astype(BF16).astype(F32)
    return jnp.where(live, hi, NONE), jnp.where(live, log_count - hi, 0.0)


def query_rows(head, base, plane, q, qa, qb, qc, lo):
    own_kind = lax.rem(base - head + 12 + lax.broadcasted_iota(jnp.int32, (1, TOK), 1), 12)
    mid_at = mid_offsets(head)
    block = lax.rem(base, 2048)
    parts = [
        (q, own_kind, own_kind >= 0, NEAR),
        (qa, lax.rem(base + 2048 + mid_at - head + 12, 12), (mid_at >= 0) & (lax.rem(plane, 2) == 0), MID),
    ]
    for visitor, origin in ((qb, plane + 2), (qc, 3 - plane)):
        at, kind = far_offsets(head, origin * 2048 + block)
        parts.append((visitor, kind, (at >= 0) & (at < TOK) & (plane < 2), FAR))
    columns = []
    for ref, kind, usable, dilations in parts:
        hi, low = count_table(kind, usable, dilations)
        scaled = ref[lo : lo + HDIM, :].astype(F32) * 0.125
        columns.append(jnp.concatenate([scaled, hi, low, jnp.zeros((32, scaled.shape[1]), F32)], 0))
    return columns


def key_columns(head, key_base, kv, lo):
    kind = lax.rem(key_base - head + 12 + lax.broadcasted_iota(jnp.int32, (16, TOK), 1), 12)
    hot = (kind == lax.broadcasted_iota(jnp.int32, (16, TOK), 0)).astype(F32).astype(BF16)
    return jnp.concatenate([kv[lo : lo + HDIM, :], hot, hot, jnp.ones((32, TOK), BF16)], 0)


def value_columns(kv, lo):
    return jnp.concatenate([kv[192 + lo : 192 + lo + HDIM, :], jnp.ones((HDIM, TOK), BF16)], 0)


def diagonal_mask(base, valid):
    rows = lax.broadcasted_iota(jnp.int32, (TOK, TOK), 0)
    cols = lax.broadcasted_iota(jnp.int32, (TOK, TOK), 1)
    return (cols <= rows) & (cols + base < valid)


def forward_kernel(sc, q, qa, qb, qc, *refs):
    kvs = refs[:PLANE]
    o_near, st_near, pay_a, pay_b, pay_c, loc = refs[PLANE : PLANE + 6]
    left, s_near, s_far, m_near, m_far, acc_near, acc_far = refs[PLANE + 6 :]
    head0, base, place, plane, valid = (sc[i] for i in range(5))
    lane = lax.broadcasted_iota(jnp.int32, (1, 128), 1)
    st_near[...] = jnp.zeros((TOK, 128), F32)
    loc[...] = jnp.zeros((384, 128), F32)
    extra = [jnp.where(lane[:, :64] == 9, 1.0, jnp.zeros((SLOTS, 64), F32)) for _ in range(3)]
    for h in range(HEADS_HERE):
        lo = h * HDIM
        head = head0 + h
        columns = query_rows(head, base, plane, q, qa, qb, qc, lo)
        at = 0
        for part in columns:
            left[at : at + part.shape[1], :] = part.T.astype(BF16)
            at += part.shape[1]
        m_near[...] = jnp.full((TOK, 128), NONE * 2, F32)
        m_far[...] = jnp.full((384, 128), NONE * 2, F32)
        acc_near[...] = jnp.zeros((TOK, 128), F32)
        acc_far[...] = jnp.zeros((384, 128), F32)
        for k in range(PLANE):
            block = lax.rem(place - k + PLANE, PLANE)
            right = key_columns(head, plane * 2048 + block * TOK, kvs[k], lo)

            @pl.when(k <= place)
            def _():
                s = dot(left[0:TOK, :], right)
                if k == 0:
                    s = jnp.where(diagonal_mask(base, valid), s, NONE)
                s_near[k] = s
                m_near[...] = jnp.maximum(m_near[...], jnp.maximum(s[:, :128], s[:, 128:]))

            @pl.when(plane < 3)
            def _():
                s = dot(left[TOK:, :], right)
                s_far[k] = s
                m_far[...] = jnp.maximum(m_far[...], jnp.maximum(s[:, :128], s[:, 128:]))

        top_near = jnp.max(m_near[...], 1, keepdims=True)
        top_far = jnp.max(m_far[...], 1, keepdims=True)
        for k in range(PLANE):
            values = value_columns(kvs[k], lo)

            @pl.when(k <= place)
            def _():
                w = jnp.exp(s_near[k] - top_near).astype(BF16)
                acc_near[...] += dot(w, values, ((1,), (1,)))

            @pl.when(plane < 3)
            def _():
                w = jnp.exp(s_far[k] - top_far).astype(BF16)
                acc_far[...] += dot(w, values, ((1,), (1,)))

        total = acc_near[:, 64:65]
        o_near[:, lo : lo + HDIM] = acc_near[:, :64] / total
        st_near[...] = jnp.where(lane == h, top_near + jnp.log(total), st_near[...])
        total = jnp.maximum(acc_far[:, 64:65], 1e-30)
        out = (acc_far[:, :64] / total).astype(BF16)
        lse = jnp.maximum(top_far + jnp.log(total), NONE)
        loc[...] = jnp.where(lane == h, lse, loc[...])
        terms = split3(lse)
        for i, pay in enumerate((pay_a, pay_b, pay_c)):
            rows = slice(i * SLOTS, (i + 1) * SLOTS)
            pay[:, lo : lo + HDIM] = out[rows, :]
            for j, term in enumerate(terms):
                extra[i] = jnp.where(lane[:, :64] == 3 * h + j, term[rows, :], extra[i])
    for i, pay in enumerate((pay_a, pay_b, pay_c)):
        pay[:, 192:256] = extra[i].astype(BF16)


def combine_kernel(sc, o_near, st_near, ra, rb, rc, o_all, mixed, st_all):
    head0, base = sc[0], sc[1]
    lane = lax.broadcasted_iota(jnp.int32, (1, 128), 1)
    st = jnp.zeros((TOK, 128), F32)
    for h in range(HEADS_HERE):
        lo = h * HDIM
        head = head0 + h
        pick_mid = one_hot_rows(mid_offsets(head))
        pick_far = one_hot_rows(far_offsets(head, base)[0])
        own = st_near[:, h : h + 1]
        outs, logs = [o_near[:, lo : lo + HDIM]], [own]
        for pay, pick in ((ra, pick_mid), (rb, pick_far), (rc, pick_far)):
            wide = dot(pick, pay[...])
            log = wide[:, 192 + 3 * h : 193 + 3 * h] + wide[:, 193 + 3 * h : 194 + 3 * h] + wide[:, 194 + 3 * h : 195 + 3 * h]
            outs.append(wide[:, lo : lo + HDIM])
            logs.append(jnp.where(wide[:, 201:202] > 0.5, log, NONE))
        top = functools.reduce(jnp.maximum, logs)
        weights = [jnp.exp(v - top) for v in logs]
        total = sum(weights)
        mixed_h = sum(w * o for w, o in zip(weights, outs)) / total
        o_all[:, lo : lo + HDIM] = mixed_h
        mixed[:, lo : lo + HDIM] = mixed_h.astype(BF16)
        st = jnp.where(lane == h, top + jnp.log(total), st)
        for i in range(3):
            st = jnp.where(lane == 3 + 3 * i + h, weights[i + 1] / total, st)
    st_all[...] = st


def prepare_kernel(sc, grad, o_all, st_all, st_near, pay_a, pay_b, pay_c):
    head0, base = sc[0], sc[1]
    lane = lax.broadcasted_iota(jnp.int32, (1, 128), 1)
    st = jnp.zeros((TOK, 128), F32)
    pays = [jnp.zeros((SLOTS, 256), F32) for _ in range(3)]
    wide_lane = lax.broadcasted_iota(jnp.int32, (1, 256), 1)
    full = grad[...].astype(F32)
    product = full * o_all[...]
    full = jnp.concatenate([full, jnp.zeros((TOK, 64), F32)], 1)
    for h in range(HEADS_HERE):
        lo = h * HDIM
        head = head0 + h
        centre = jnp.sum(product[:, lo : lo + HDIM], 1, keepdims=True)
        st = jnp.where(lane == h, st_all[:, h : h + 1], st)
        st = jnp.where(lane == 3 + h, centre, st)
        pick_mid = one_hot_rows(mid_offsets(head))
        pick_far = one_hot_rows(far_offsets(head, base)[0])
        mine = jnp.where((wide_lane >= lo) & (wide_lane < lo + HDIM), full, 0.0)
        for i, pick in enumerate((pick_mid, pick_far, pick_far)):
            share = st_all[:, 3 + 3 * i + h : 4 + 3 * i + h]
            wide = mine * share
            for j, term in enumerate(split3(centre * share)):
                wide = jnp.where(wide_lane == 192 + 3 * h + j, term, wide)
            pays[i] += dot(pick, wide.astype(BF16), ((0,), (0,)))
    st_near[...] = st
    for pay, value in zip((pay_a, pay_b, pay_c), pays):
        pay[...] = value.astype(BF16)


def backward_kernel(sc, q, qa, qb, qc, grad, st_near, pay_a, pay_b, pay_c, loc, *refs):
    kvs = refs[:PLANE]
    dq_near, dq_a, dq_b, dq_c = refs[PLANE : PLANE + 4]
    dkvs = refs[PLANE + 4 : 2 * PLANE + 4]
    left, grad_left, turned, acc_q, acc_kv = refs[2 * PLANE + 4 :]
    head0, base, place, plane, valid = (sc[i] for i in range(5))
    lane = lax.broadcasted_iota(jnp.int32, (1, 128), 1)
    for pay in (dq_a, dq_b, dq_c):
        pay[...] = jnp.zeros((SLOTS, 256), BF16)
    for h in range(HEADS_HERE):
        lo = h * HDIM
        head = head0 + h
        columns = query_rows(head, base, plane, q, qa, qb, qc, lo)
        logs = [st_near[:, h : h + 1]] + [loc[i * SLOTS : (i + 1) * SLOTS, h : h + 1] for i in range(3)]
        grads = [grad[:, lo : lo + HDIM].astype(F32)] + [v[:, lo : lo + HDIM].astype(F32) for v in (pay_a, pay_b, pay_c)]
        centres = [st_near[:, 3 + h : 4 + h]]
        for v in (pay_a, pay_b, pay_c):
            e = v[:, 192:256].astype(F32)
            centres.append(e[:, 3 * h : 3 * h + 1] + e[:, 3 * h + 1 : 3 * h + 2] + e[:, 3 * h + 2 : 3 * h + 3])
        at = 0
        for part, log, g, centre in zip(columns, logs, grads, centres):
            n = part.shape[1]
            rows = slice(at, at + n)
            natural = part.T
            for j, term in enumerate(split3(jnp.where(log > NONE * 0.1, -log, 0.0))):
                natural = jnp.where(lane == 96 + j, term, natural)
            left[rows, :] = natural.astype(BF16)
            natural = jnp.concatenate([g, jnp.zeros((n, 64), F32)], 1)
            for j, term in enumerate(split3(-centre)):
                natural = jnp.where(lane == 64 + j, term, natural)
            grad_left[rows, :] = natural.astype(BF16)
            turned[0:64, rows] = part[0:64, :].astype(BF16)
            turned[64:128, rows] = natural.T[0:64, :].astype(BF16)
            at += n
        acc_q[...] = jnp.zeros((640, HDIM), F32)
        for k in range(PLANE):
            block = lax.rem(place - k + PLANE, PLANE)
            right = key_columns(head, plane * 2048 + block * TOK, kvs[k], lo)
            values = value_columns(kvs[k], lo)
            acc_kv[...] = jnp.zeros((128, TOK), F32)

            def part(rows, masked):
                s = dot(left[rows, :], right)
                if masked:
                    s = jnp.where(diagonal_mask(base, valid), s, NONE)
                w = jnp.exp(s)
                ds = (w * dot(grad_left[rows, :], values)).astype(BF16)
                acc_q[rows, :] += dot(ds, kvs[k][lo : lo + HDIM, :], ((1,), (1,)))
                acc_kv[0:64, :] += dot(turned[0:64, rows], ds)
                acc_kv[64:128, :] += dot(turned[64:128, rows], w.astype(BF16))

            @pl.when(k <= place)
            def _():
                part(slice(0, TOK), k == 0)

            @pl.when(plane < 3)
            def _():
                part(slice(TOK, 640), False)

            dkvs[k][lo : lo + HDIM, :] = acc_kv[0:64, :].astype(BF16)
            dkvs[k][192 + lo : 192 + lo + HDIM, :] = acc_kv[64:128, :].astype(BF16)
        dq_near[:, lo : lo + HDIM] = acc_q[0:TOK, :] * 0.125
        for i, pay in enumerate((dq_a, dq_b, dq_c)):
            pay[:, lo : lo + HDIM] = (acc_q[TOK + i * SLOTS : TOK + (i + 1) * SLOTS, :] * 0.125).astype(BF16)


def collect_kernel(sc, dq_near, ra, rb, rc, dq):
    head0, base = sc[0], sc[1]
    for h in range(HEADS_HERE):
        lo = h * HDIM
        head = head0 + h
        pick_mid = one_hot_rows(mid_offsets(head))
        pick_far = one_hot_rows(far_offsets(head, base)[0])
        far = (rb[...].astype(F32) + rc[...].astype(F32)).astype(BF16)
        wide = dot(pick_mid, ra[...]) + dot(pick_far, far)
        dq[:, lo : lo + HDIM] = (dq_near[:, lo : lo + HDIM] + wide[:, lo : lo + HDIM]).astype(BF16)


def call(kernel, out_shapes, scratch=()):
    def run(sc, *args):
        return pl.pallas_call(
            kernel,
            out_shape=[jax.ShapeDtypeStruct(s, d) for s, d in out_shapes],
            in_specs=[pl.BlockSpec(memory_space=pltpu.SMEM)] + [pl.BlockSpec(memory_space=pltpu.VMEM)] * len(args),
            out_specs=[pl.BlockSpec(memory_space=pltpu.VMEM)] * len(out_shapes),
            scratch_shapes=list(scratch),
            compiler_params=pltpu.CompilerParams(vmem_limit_bytes=48 * 1024 * 1024),
        )(sc, *args)

    return run


def norm_rows(v, gain, shift):
    mean = jnp.sum(v, 1, keepdims=True) / v.shape[1]
    spread = jnp.sum(v * v, 1, keepdims=True) / v.shape[1] - mean * mean
    scale = lax.rsqrt(spread + EPSILON)
    unit = (v - mean) * scale
    return unit * gain + shift, unit, scale


def norm_rows_back(grad, unit, scale, gain):
    q = grad * gain
    n = grad.shape[1]
    return scale * (q - jnp.sum(q, 1, keepdims=True) / n - unit * jnp.sum(q * unit, 1, keepdims=True) / n)


PAIR_A = [(0, 1), (1, 0), (2, 3), (3, 2)]
PAIR_B = [(0, 3), (3, 0), (1, 2), (2, 1)]
ORDERS = (
    ("xa", "xb", "za", "zb", "y"),
    ("xb", "xa", "zb", "za", "y"),
    ("za", "zb", "xa", "xb", "y"),
    ("zb", "za", "xb", "xa", "y"),
)


def halving_steps():
    x, z, y = lax.axis_index("x"), lax.axis_index("z"), lax.axis_index("yh")

    def side_a(i):
        return jnp.where((i == 0) | (i == 3), 0, 1)

    def side_b(i):
        return jnp.where(i < 2, 0, 1)

    return {
        "xa": ("x", PAIR_A, side_a(x)),
        "xb": ("x", PAIR_B, side_b(x)),
        "za": ("z", PAIR_A, side_a(z)),
        "zb": ("z", PAIR_B, side_b(z)),
        "y": ("yh", FLIP, y),
    }


def sum_over_seq(v):
    steps = halving_steps()
    parts = jnp.split(v, 4)
    for i in range(5):
        for j in range(4):
            axis, perm, side = steps[ORDERS[j][i]]
            n = parts[j].shape[0] // 2
            keep = lax.dynamic_slice_in_dim(parts[j], side * n, n, 0)
            send = lax.dynamic_slice_in_dim(parts[j], (1 - side) * n, n, 0)
            parts[j] = keep + lax.ppermute(send, axis, perm)
    for i in range(4, -1, -1):
        for j in range(4):
            axis, perm, side = steps[ORDERS[j][i]]
            other = lax.ppermute(parts[j], axis, perm)
            parts[j] = jnp.where(
                side == 0, jnp.concatenate([parts[j], other]), jnp.concatenate([other, parts[j]])
            )
    return jnp.concatenate(parts)


def sum_over_tensor(v):
    core = lax.axis_index("c")
    n = v.shape[0] // 2
    keep = lax.dynamic_slice_in_dim(v, core * n, n, 0)
    send = lax.dynamic_slice_in_dim(v, (1 - core) * n, n, 0)
    half = keep + lax.ppermute(send, "c", FLIP)
    half = half + lax.ppermute(half, "yl", FLIP)
    other = lax.ppermute(half, "c", FLIP)
    return jnp.where(core == 0, jnp.concatenate([half, other]), jnp.concatenate([other, half]))


def sum_small_over_tensor(v):
    v = v + lax.ppermute(v, "c", FLIP)
    return v + lax.ppermute(v, "yl", FLIP)


def gather_over_tensor(v):
    across = lax.ppermute(v, "yl", FLIP)
    beside = lax.ppermute(v, "c", FLIP)
    both = lax.ppermute(across, "c", FLIP)
    core, low = lax.axis_index("c"), lax.axis_index("yl")
    here = [jnp.where(core == 0, v, beside), jnp.where(core == 0, beside, v)]
    there = [jnp.where(core == 0, across, both), jnp.where(core == 0, both, across)]
    return [jnp.where(low == 0, a, b) for a, b in zip(here + there, there + here)]


MID_GO = [(1, 0), (3, 2)]
B_GO = [(2, 0), (3, 1)]
C_GO = [(3, 0), (2, 1)]


def back(perm):
    return [(b, a) for a, b in perm]


def smooth(v):
    return jax.nn.gelu(v, approximate=True)


def per_device(
    inputs,
    head_weights,
    out_weight,
    up_weight,
    down_weight,
    in_gain,
    in_shift,
    mix_gain,
    mix_shift,
    mid_gain,
    mid_shift,
    inner_gain,
    inner_shift,
    valid_length,
    cotangent,
):
    z, yh, x = (lax.axis_index(a) for a in SEQ)
    place = yh * 4 + x
    tensor = lax.axis_index("yl") * 2 + lax.axis_index("c")
    head0 = tensor * HEADS_HERE
    base = (z * PLANE + place) * TOK
    valid = valid_length[0]
    sc = jnp.stack([head0, base, place, z, valid]).astype(jnp.int32)
    row_valid = (base + jnp.arange(TOK, dtype=jnp.int32) < valid)[:, None]

    vectors = jnp.stack(split3(mix_gain) + split3(mix_shift)).astype(BF16)
    packed = jnp.concatenate([out_weight.T, vectors, jnp.zeros((10, 192), BF16)], 0)
    packed = lax.all_gather(packed, TENSOR, axis=0)
    out_full = packed[:, :768].transpose(1, 0, 2).reshape(768, 768)
    gain_full = jnp.sum(packed[:, 768:771].astype(F32), 1).reshape(768)
    shift_full = jnp.sum(packed[:, 771:774].astype(F32), 1).reshape(768)

    source = inputs.astype(F32)
    normed, in_unit, in_scale = norm_rows(source, in_gain, in_shift)
    normed_low = normed.astype(BF16)
    projected = jnp.einsum("td,cde->cet", normed_low, head_weights, preferred_element_type=F32).astype(BF16)
    queries = projected[0]
    pairs = projected[1:].reshape(384, TOK)

    kvs = [pairs] + [
        lax.ppermute(pairs, ("yh", "x"), [(i, (i + k) % PLANE) for i in range(PLANE)]) for k in range(1, PLANE)
    ]
    pick_mid = jnp.stack([one_hot_rows(mid_offsets(head0 + h)) for h in range(HEADS_HERE)])
    pick_far = jnp.stack([one_hot_rows(far_offsets(head0 + h, base)[0]) for h in range(HEADS_HERE)])
    by_head = queries.reshape(HEADS_HERE, HDIM, TOK)
    q_mid = jnp.einsum("het,htj->hej", by_head, pick_mid, preferred_element_type=F32).astype(BF16).reshape(192, SLOTS)
    q_far = jnp.einsum("het,htj->hej", by_head, pick_far, preferred_element_type=F32).astype(BF16).reshape(192, SLOTS)
    qa = lax.ppermute(q_mid, "z", MID_GO)
    qb = lax.ppermute(q_far, "z", B_GO)
    qc = lax.ppermute(q_far, "z", C_GO)

    o_near, st_near, pay_a, pay_b, pay_c, loc = call(
        forward_kernel,
        [((TOK, 192), F32), ((TOK, 128), F32)] + [((SLOTS, 256), BF16)] * 3 + [((384, 128), F32)],
        [
            pltpu.VMEM((640, 128), BF16),
            pltpu.VMEM((PLANE, TOK, TOK), F32),
            pltpu.VMEM((PLANE, 384, TOK), F32),
            pltpu.VMEM((TOK, 128), F32),
            pltpu.VMEM((384, 128), F32),
            pltpu.VMEM((TOK, 128), F32),
            pltpu.VMEM((384, 128), F32),
        ],
    )(sc, queries, qa, qb, qc, *kvs)
    ra = lax.ppermute(pay_a, "z", back(MID_GO))
    rb = lax.ppermute(pay_b, "z", back(B_GO))
    rc = lax.ppermute(pay_c, "z", back(C_GO))
    o_all, mixed, st_all = call(
        combine_kernel, [((TOK, 192), F32), ((TOK, 192), BF16), ((TOK, 128), F32)]
    )(sc, o_near, st_near, ra, rb, rc)

    attended = jnp.concatenate(gather_over_tensor(mixed), 1).astype(F32)
    mix_normed, mix_unit, mix_scale = norm_rows(attended, gain_full, shift_full)
    mix_low = mix_normed.astype(BF16)
    branch = jnp.einsum("te,de->td", mix_low, out_full, preferred_element_type=F32)
    hidden = source + branch
    mid_normed, mid_unit, mid_scale = norm_rows(hidden, mid_gain, mid_shift)
    mid_low = mid_normed.astype(BF16)
    pre_act = jnp.dot(mid_low, up_weight, preferred_element_type=F32)
    active = smooth(pre_act)

    upstream = jnp.where(row_valid, cotangent.astype(F32), 0.0)
    feed_grad = upstream.astype(BF16)
    inner_grad = jnp.einsum("td,fd->tf", feed_grad, down_weight, preferred_element_type=F32)
    inner_scaled = inner_grad * inner_gain
    sums = sum_small_over_tensor(
        jnp.stack(
            [
                jnp.sum(active, 1),
                jnp.sum(active * active, 1),
                jnp.sum(inner_scaled, 1),
                jnp.sum(inner_scaled * active, 1),
            ]
        )
    )
    width = 3072
    inner_mean = (sums[0] / width)[:, None]
    inner_scale = lax.rsqrt((sums[1] / width)[:, None] - inner_mean * inner_mean + EPSILON)
    inner_unit = (active - inner_mean) * inner_scale
    inner_low = (inner_unit * inner_gain + inner_shift).astype(BF16)
    first_back = sums[2][:, None]
    second_back = inner_scale * (sums[3][:, None] - inner_mean * first_back)
    active_grad = inner_scale * (inner_scaled - first_back / width - inner_unit * second_back / width)
    pre_grad = jax.vjp(smooth, pre_act)[1](active_grad)[0].astype(BF16)
    mid_part = jnp.einsum("tf,df->td", pre_grad, up_weight, preferred_element_type=F32).astype(BF16)
    mid_grad = sum_over_tensor(mid_part).astype(F32)

    feed_part = jnp.dot(inner_low, down_weight, preferred_element_type=F32).astype(BF16)
    feed_out = sum_over_tensor(feed_part).astype(F32)
    result = jnp.where(row_valid, hidden + feed_out, 0.0).astype(BF16)
    inner_gain_grad = jnp.sum(inner_grad * inner_unit, 0)
    inner_shift_grad = jnp.sum(inner_grad, 0)
    down_grad = jnp.einsum("tf,td->fd", inner_low, feed_grad, preferred_element_type=F32)
    up_grad = jnp.einsum("td,tf->df", mid_low, pre_grad, preferred_element_type=F32)

    mid_gain_grad = jnp.sum(mid_grad * mid_unit, 0)
    mid_shift_grad = jnp.sum(mid_grad, 0)
    hidden_grad = upstream + norm_rows_back(mid_grad, mid_unit, mid_scale, mid_gain)
    branch_grad = hidden_grad.astype(BF16)
    mix_grad = jnp.einsum("td,de->te", branch_grad, out_full, preferred_element_type=F32)
    attended_grad = norm_rows_back(mix_grad, mix_unit, mix_scale, gain_full)
    mine = tensor * 192

    def own_columns(v):
        return lax.dynamic_slice_in_dim(v, mine, 192, 1)

    attended_grad = own_columns(attended_grad).astype(BF16)
    mix_grad_own = own_columns(mix_grad)
    mix_gain_grad = jnp.sum(mix_grad_own * own_columns(mix_unit), 0)
    mix_shift_grad = jnp.sum(mix_grad_own, 0)
    out_grad = jnp.einsum("te,td->ed", own_columns(mix_low), branch_grad, preferred_element_type=F32)

    st_near, pay_a, pay_b, pay_c = call(
        prepare_kernel, [((TOK, 128), F32)] + [((SLOTS, 256), BF16)] * 3
    )(sc, attended_grad, o_all, st_all)
    ga = lax.ppermute(pay_a, "z", MID_GO)
    gb = lax.ppermute(pay_b, "z", B_GO)
    gc = lax.ppermute(pay_c, "z", C_GO)

    ff_grads = jnp.concatenate([down_grad.astype(BF16), up_grad.astype(BF16), out_grad.astype(BF16), jnp.zeros((320, 768), BF16)], 0)
    ff_grads = sum_over_seq(ff_grads)

    out = call(
        backward_kernel,
        [((TOK, 192), F32)] + [((SLOTS, 256), BF16)] * 3 + [((384, TOK), BF16)] * PLANE,
        [
            pltpu.VMEM((640, 128), BF16),
            pltpu.VMEM((640, 128), BF16),
            pltpu.VMEM((128, 640), BF16),
            pltpu.VMEM((640, HDIM), F32),
            pltpu.VMEM((128, TOK), F32),
        ],
    )(sc, queries, qa, qb, qc, attended_grad, st_near, ga, gb, gc, loc, *kvs)
    dq_near, pay_a, pay_b, pay_c = out[:4]
    ra = lax.ppermute(pay_a, "z", back(MID_GO))
    rb = lax.ppermute(pay_b, "z", back(B_GO))
    rc = lax.ppermute(pay_c, "z", back(C_GO))
    dkv = out[4].astype(F32)
    for k in range(1, PLANE):
        dkv += lax.ppermute(
            out[4 + k], ("yh", "x"), [(i, (i - k) % PLANE) for i in range(PLANE)]
        ).astype(F32)
    dkv = dkv.astype(BF16).reshape(2, 192, TOK)
    (dq,) = call(collect_kernel, [((TOK, 192), BF16)])(sc, dq_near, ra, rb, rc)

    head_grad = jnp.stack(
        [
            jnp.einsum("td,te->de", normed_low, dq, preferred_element_type=F32),
            jnp.einsum("td,et->de", normed_low, dkv[0], preferred_element_type=F32),
            jnp.einsum("td,et->de", normed_low, dkv[1], preferred_element_type=F32),
        ]
    ).astype(BF16)
    normed_part = (
        jnp.einsum("te,de->td", dq, head_weights[0], preferred_element_type=F32)
        + jnp.einsum("et,de->td", dkv[0], head_weights[1], preferred_element_type=F32)
        + jnp.einsum("et,de->td", dkv[1], head_weights[2], preferred_element_type=F32)
    )
    normed_grad = sum_over_tensor(normed_part.astype(BF16)).astype(F32)
    inputs_grad = (hidden_grad + norm_rows_back(normed_grad, in_unit, in_scale, in_gain)).astype(BF16)
    in_sums = sum_small_over_tensor(jnp.stack([jnp.sum(normed_part * in_unit, 0), jnp.sum(normed_part, 0)]))

    pad = jnp.zeros((576,), F32)
    small = jnp.concatenate(
        [
            in_sums.reshape(-1),
            mid_gain_grad,
            mid_shift_grad,
            inner_gain_grad,
            inner_shift_grad,
            mix_gain_grad,
            mix_shift_grad,
            pad,
            pad,
        ]
    ).astype(BF16)
    small = jnp.concatenate([small, jnp.zeros((320 * 256 - small.shape[0],), BF16)])
    last = jnp.concatenate([head_grad.reshape(1728, 256), small.reshape(320, 256)], 0)
    last = sum_over_seq(last).astype(F32)
    head_grad = last[:1728].reshape(3, 768, 192)
    small = last[1728:].reshape(-1)
    ff_grads = ff_grads.astype(F32)
    vec = [small[i * 768 : (i + 1) * 768] for i in range(6)]
    return (
        result,
        inputs_grad,
        head_grad,
        ff_grads[1536:1728],
        ff_grads[768:1536],
        ff_grads[:768],
        vec[0],
        vec[1],
        small[4608:4800],
        small[4800:4992],
        vec[2],
        vec[3],
        vec[4],
        vec[5],
    )


def solution(mesh):
    fine = Mesh(np.asarray(mesh.devices).reshape(4, 2, 4, 2, 2), SEQ + TENSOR)
    in_specs = (
        P(SEQ, None),
        P(None, None, TENSOR),
        P(TENSOR, None),
        P(None, TENSOR),
        P(TENSOR, None),
        P(),
        P(),
        P(TENSOR),
        P(TENSOR),
        P(),
        P(),
        P(TENSOR),
        P(TENSOR),
        P(),
        P(SEQ, None),
    )
    out_specs = (
        P(SEQ, None),
        P(SEQ, None),
        P(None, None, TENSOR),
        P(TENSOR, None),
        P(None, TENSOR),
        P(TENSOR, None),
        P(),
        P(),
        P(TENSOR),
        P(TENSOR),
        P(),
        P(),
        P(TENSOR),
        P(TENSOR),
    )
    return jax.shard_map(per_device, mesh=fine, in_specs=in_specs, out_specs=out_specs, check_vma=False)
```

```python
import functools

import jax
import jax.numpy as jnp
import numpy as np
from jax import lax
from jax.experimental import pallas as pl
from jax.experimental.pallas import tpu as pltpu
from jax.sharding import Mesh
from jax.sharding import PartitionSpec as P


HDIM = 64
HEADS_HERE = 3
TOK = 256
PLANE = 8
SLOTS = 128
KEYS = PLANE * SLOTS
PARTS = 32
ROW = 24
EPSILON = 1e-05
NONE = -1e30
NEAR = (1, 2, 4, 6, 12)
MID = (2, 4, 6, 12)
FAR = (4, 6, 12)
F32 = jnp.float32
BF16 = jnp.bfloat16
SEQ = ("z", "yh", "x")
TENSOR = ("yl", "c")
FLIP = [(0, 1), (1, 0)]
NN = ((1,), (0,))
NT = ((1,), (1,))
TN = ((0,), (0,))


def dot(a, b, dims=NN):
    return lax.dot_general(a, b, (dims, ((), ())), preferred_element_type=F32)


def split3(v):
    hi = v.astype(BF16).astype(F32)
    mid = (v - hi).astype(BF16).astype(F32)
    return hi, mid, v - hi - mid


def mid_offsets(head):
    slot = lax.broadcasted_iota(jnp.int32, (1, SLOTS), 1)
    return 2 * slot + lax.rem(head, 2)


def far_offsets(head, base):
    slot = lax.broadcasted_iota(jnp.int32, (1, SLOTS), 1)
    which = lax.rem(slot, 4)
    kind = jnp.where(which == 0, 0, 2 * which + 2)
    first = lax.div(base + 12 - head, 12) - 1
    return 12 * (first + lax.div(slot, 4)) + kind + head - base, kind


def one_hot_rows(offsets):
    rows = lax.broadcasted_iota(jnp.int32, (TOK, SLOTS), 0)
    return (rows == offsets).astype(F32).astype(BF16)


def picks(head, base):
    return one_hot_rows(mid_offsets(head)), one_hot_rows(far_offsets(head, base)[0])


def count_table(kind, usable, dilations):
    row = lax.broadcasted_iota(jnp.int32, (16, kind.shape[1]), 0)
    count = jnp.zeros(row.shape, F32)
    for step in dilations:
        count += jnp.where((lax.rem(row, step) == 0) & (lax.rem(kind, step) == 0), 1.0, 0.0)
    live = (count > 0) & usable & (row < 12)
    log_count = jnp.log(jnp.maximum(count, 1.0))
    hi = log_count.astype(BF16).astype(F32)
    return jnp.where(live, hi, NONE), jnp.where(live, log_count - hi, 0.0)


def query_rows(head, base, plane, q, visitors, lo):
    own_kind = lax.rem(base - head + 12 + lax.broadcasted_iota(jnp.int32, (1, TOK), 1), 12)
    mid_at = mid_offsets(head)
    block = lax.rem(base, 2048)
    parts = [
        (q, own_kind, own_kind >= 0, NEAR),
        (visitors[0], lax.rem(base + 2048 + mid_at - head + 12, 12), mid_at >= 0, MID),
    ]
    for visitor, origin in ((visitors[1], plane + 2), (visitors[2], 3 - plane)):
        at, kind = far_offsets(head, origin * 2048 + block)
        parts.append((visitor, kind, (at >= 0) & (at < TOK), FAR))
    columns = []
    for ref, kind, usable, dilations in parts:
        hi, low = count_table(kind, usable, dilations)
        columns.append(jnp.concatenate([ref[lo : lo + HDIM, :].astype(F32) * 0.125, hi, low], 0))
    return columns


def one_hot_kind(kind):
    return (kind == lax.broadcasted_iota(jnp.int32, (16, kind.shape[1]), 0)).astype(F32).astype(BF16)


def ones(rows, columns):
    return jnp.ones((rows, columns), BF16)


def diagonal_mask(base, valid):
    rows = lax.broadcasted_iota(jnp.int32, (TOK, TOK), 0)
    cols = lax.broadcasted_iota(jnp.int32, (TOK, TOK), 1)
    return (cols <= rows) & (cols + base < valid)


def norm_rows(v, gain, shift):
    mean = jnp.sum(v, 1, keepdims=True) / v.shape[1]
    spread = jnp.sum(v * v, 1, keepdims=True) / v.shape[1] - mean * mean
    scale = lax.rsqrt(spread + EPSILON)
    unit = (v - mean) * scale
    return unit * gain + shift, unit, scale


def norm_rows_back(grad, unit, scale, gain):
    q = grad * gain
    n = grad.shape[1]
    return scale * (q - jnp.sum(q, 1, keepdims=True) / n - unit * (jnp.sum(q * unit, 1, keepdims=True) / n))


def project_kernel(sc, inputs, weights, gain, shift, normed, q, pairs, q_mid, q_far):
    head0, base = sc[0], sc[1]
    v = norm_rows(inputs[...].astype(F32), gain[...], shift[...])[0].astype(BF16)
    normed[...] = v
    q[...] = dot(weights[0], v, NT).astype(BF16)
    pairs[0:192, :] = dot(weights[1], v, NT).astype(BF16)
    pairs[192:384, :] = dot(weights[2], v, NT).astype(BF16)
    for h in range(HEADS_HERE):
        rows = slice(h * HDIM, (h + 1) * HDIM)
        pick_mid, pick_far = picks(head0 + h, base)
        q_mid[rows, :] = dot(q[rows, :], pick_mid).astype(BF16)
        q_far[rows, :] = dot(q[rows, :], pick_far).astype(BF16)


def forward_kernel(sc, q, qa, qb, qc, *refs):
    kvs = refs[:PLANE]
    o_near, st_near, pay_a, pay_b, pay_c, loc, right, right_a, right_f, value_a, value_f = refs[PLANE : PLANE + 11]
    rows_near, rows_far, left_near, left_a, left_f, m_near, m_a, m_f, acc_near, acc_a, acc_f = refs[PLANE + 11 :]
    head0, base, place, plane, valid = (sc[i] for i in range(5))
    heads = range(HEADS_HERE)
    mid_here, far_here = lax.rem(plane, 2) == 0, plane < 2
    for h in heads:
        lo = h * HDIM
        head = head0 + h
        parts = query_rows(head, base, plane, q, (qa, qb, qc), lo)
        rows_near[h] = jnp.concatenate([parts[0], jnp.zeros((32, TOK), F32)], 0)
        rows_far[h] = jnp.concatenate([jnp.concatenate(parts[1:], 1), jnp.zeros((32, 384), F32)], 0)
        left_near[h] = rows_near[h].T.astype(BF16)
        turned = rows_far[h].T.astype(BF16)
        left_a[h] = turned[0:SLOTS]
        left_f[h] = turned[SLOTS:]
        mid_at = mid_offsets(head)
        for k in range(PLANE):
            start = plane * 2048 + lax.rem(place - k + PLANE, PLANE) * TOK
            kind = lax.rem(start - head + 12 + lax.broadcasted_iota(jnp.int32, (1, TOK), 1), 12)
            hot = one_hot_kind(kind)
            right[h, k] = jnp.concatenate([kvs[k][lo : lo + HDIM, :], hot, hot, ones(32, TOK)], 0)
            far_at, far_kind = far_offsets(head, start)
            far_kind = jnp.where((far_at >= 0) & (far_at < TOK), far_kind, 12)
            both = jnp.concatenate([kvs[k][lo : lo + HDIM, :], kvs[k][192 + lo : 192 + lo + HDIM, :]], 0)
            at = slice(k * SLOTS, (k + 1) * SLOTS)
            mid_kind = lax.rem(start + mid_at - head + 12, 12)
            for pick, kinds, r, v in (
                (one_hot_rows(mid_at), mid_kind, right_a, value_a),
                (one_hot_rows(far_at), far_kind, right_f, value_f),
            ):
                small = dot(both, pick).astype(BF16)
                hot = one_hot_kind(kinds)
                r[h, :, at] = jnp.concatenate([small[0:HDIM], hot, hot, ones(32, SLOTS)], 0)
                v[h, :, at] = jnp.concatenate([small[HDIM:], ones(16, SLOTS)], 0)
    m_near[...] = jnp.full(m_near.shape, 2 * NONE, F32)
    for k in range(PLANE):

        @pl.when(k <= place)
        def _():
            for h in heads:
                s = dot(left_near[h], right[h, k])
                if k == 0:
                    s = jnp.where(diagonal_mask(base, valid), s, NONE)
                m_near[h] = jnp.maximum(m_near[h], jnp.maximum(s[:, :128], s[:, 128:]))

    def widest(s):
        return functools.reduce(jnp.maximum, [s[:, i * 128 : (i + 1) * 128] for i in range(s.shape[1] // 128)])

    @pl.when(mid_here)
    def _():
        for h in heads:
            m_a[h] = widest(dot(left_a[h], right_a[h]))

    @pl.when(far_here)
    def _():
        for h in heads:
            m_f[h] = widest(dot(left_f[h], right_f[h]))

    def finish(m, rows, left):
        top = jnp.max(m.T, 0, keepdims=True)
        minus = jnp.concatenate(list(split3(-top)) + [jnp.zeros((29, top.shape[1]), F32)], 0)
        left[...] = jnp.concatenate([rows, minus], 0).T.astype(BF16)
        return top

    def weigh(s):
        return jnp.exp(s).astype(BF16)

    tops = []
    for h in heads:
        tops.append(finish(m_near[h], rows_near[h, 0:96, :], left_near.at[h]))
    acc_near[...] = jnp.zeros(acc_near.shape, F32)
    for k in range(PLANE):

        @pl.when(k <= place)
        def _():
            for h in heads:
                lo = h * HDIM
                s = dot(left_near[h], right[h, k])
                if k == 0:
                    s = jnp.where(diagonal_mask(base, valid), s, NONE)
                values = jnp.concatenate([kvs[k][192 + lo : 192 + lo + HDIM, :], ones(16, TOK)], 0)
                acc_near[h] += dot(values, weigh(s), NT)

    st_near[...] = jnp.zeros(st_near.shape, F32)
    for h in heads:
        total = acc_near[h, 64:65, :]
        o_near[h * HDIM : (h + 1) * HDIM, :] = acc_near[h, 0:64, :] / total
        st_near[h : h + 1, :] = tops[h] + jnp.log(total)

    loc[...] = jnp.zeros(loc.shape, F32)

    def far_part(h, m, left, rights, values, at, pays):
        n = SLOTS * len(pays)
        top = finish(m, rows_far[h, 0:96, at : at + n], left)
        acc = dot(values, weigh(dot(left[...], rights)), NT)
        total = acc[64:65, :]
        log = jnp.maximum(top + jnp.log(total), NONE)
        loc[h : h + 1, at : at + n] = log
        out = acc[0:64, :] / total
        for i, pay in enumerate(pays):
            pay[h * HDIM : (h + 1) * HDIM, :] = out[:, i * SLOTS : (i + 1) * SLOTS].astype(BF16)
            for j, term in enumerate(split3(log[:, i * SLOTS : (i + 1) * SLOTS])):
                extra[i][3 * h + j] = term

    row = lax.broadcasted_iota(jnp.int32, (16, SLOTS), 0)

    def stack(terms):
        out = jnp.where(row == 9, 1.0, 0.0)
        for i, term in terms.items():
            out = jnp.where(row == i, term, out)
        return out.astype(BF16)

    extra = [{}]

    @pl.when(mid_here)
    def _():
        for h in heads:
            far_part(h, m_a[h], left_a.at[h], right_a[h], value_a[h], 0, (pay_a,))
        pay_a[192:208, :] = stack(extra[0])

    extra = [{}, {}]

    @pl.when(far_here)
    def _():
        for h in heads:
            far_part(h, m_f[h], left_f.at[h], right_f[h], value_f[h], SLOTS, (pay_b, pay_c))
        pay_b[192:208, :] = stack(extra[0])
        pay_c[192:208, :] = stack(extra[1])


def combine_kernel(sc, o_near, st_near, ra, rb, rc, o_all, mixed, st_all):
    head0, base = sc[0], sc[1]
    st_all[...] = jnp.zeros(st_all.shape, F32)
    for h in range(HEADS_HERE):
        rows = slice(h * HDIM, (h + 1) * HDIM)
        pick_mid, pick_far = picks(head0 + h, base)
        outs, logs = [o_near[rows, :]], [st_near[h : h + 1, :]]
        for pay, pick in ((ra, pick_mid), (rb, pick_far), (rc, pick_far)):
            wide = dot(jnp.concatenate([pay[rows, :], pay[192:208, :]], 0), pick, NT)
            log = wide[64 + 3 * h : 65 + 3 * h] + wide[65 + 3 * h : 66 + 3 * h] + wide[66 + 3 * h : 67 + 3 * h]
            outs.append(wide[0:64])
            logs.append(jnp.where(wide[73:74] > 0.5, log, NONE))
        top = functools.reduce(jnp.maximum, logs)
        weights = [jnp.exp(v - top) for v in logs]
        total = sum(weights)
        mixed_h = sum((w / total) * o for w, o in zip(weights, outs))
        o_all[rows, :] = mixed_h
        mixed[rows, :] = mixed_h.astype(BF16)
        st_all[h : h + 1, :] = top + jnp.log(total)
        for i in range(3):
            st_all[3 + 3 * i + h : 4 + 3 * i + h, :] = weights[i + 1] / total


def mix_norm(pieces):
    first = sum(jnp.sum(pieces[i].astype(F32), 0, keepdims=True) for i in range(4)) / 768
    second = sum(jnp.sum(jnp.square(pieces[i].astype(F32)), 0, keepdims=True) for i in range(4)) / 768
    return first, lax.rsqrt(second - first * first + EPSILON)


def column(packed, i, at):
    c = packed[i, :, 768 + at : 771 + at].astype(F32)
    return c[:, 0:1] + c[:, 1:2] + c[:, 2:3]


def gelu_parts(v):
    a, b = 0.7978845608028654, 0.044715
    square = v * v
    t = jnp.tanh(a * v * (1.0 + b * square))
    active = 0.5 * v * (1.0 + t)
    slope = 0.5 * (1.0 + t) + 0.5 * v * (1.0 - t * t) * (a * (1.0 + 3.0 * b * square))
    return active, slope


def middle_kernel(
    sc, inputs, own, beside, across, both, packed, up, down, gain, shift, inner_gain, cotangent,
    pieces, hidden, mid_low, pre, inner_grad, sums,
):
    tensor, base, valid = sc[5], sc[1], sc[4]
    for i, ref in enumerate((own, beside, across, both)):
        pieces[jnp.bitwise_xor(tensor, i)] = ref[...]
    mean, scale = mix_norm(pieces)
    total = inputs[...].astype(F32)
    branch = None
    for i in range(4):
        low = ((pieces[i].astype(F32) - mean) * scale * column(packed, i, 0) + column(packed, i, 3)).astype(BF16)
        term = dot(low, packed[i, :, 0:768], TN)
        branch = term if branch is None else branch + term
    total = total + branch
    hidden[...] = total
    low = norm_rows(total, gain[...], shift[...])[0].astype(BF16)
    mid_low[...] = low
    pre[...] = dot(low, up[...])
    active = gelu_parts(pre[...])[0]
    row = base + lax.broadcasted_iota(jnp.int32, (TOK, 1), 0)
    feed = jnp.where(row < valid, cotangent[...].astype(F32), 0.0).astype(BF16)
    grad = dot(feed, down[...], NT)
    inner_grad[...] = grad
    scaled = grad * inner_gain[...]
    lane = lax.broadcasted_iota(jnp.int32, (1, 128), 1)
    st = jnp.zeros((TOK, 128), F32)
    for i, v in enumerate((active, active * active, scaled, scaled * active)):
        st = jnp.where(lane == i, jnp.sum(v, 1, keepdims=True), st)
    sums[...] = st.T[0:8]


def inner_kernel(sums, pre, inner_grad, up, gain, shift, inner_low, pre_grad, mid_part, vectors):
    st = jnp.concatenate([sums[...], jnp.zeros((120, TOK), F32)], 0).T
    width = 3072
    mean = st[:, 0:1] / width
    scale = lax.rsqrt(st[:, 1:2] / width - mean * mean + EPSILON)
    first = st[:, 2:3]
    second = scale * (st[:, 3:4] - mean * first)
    active, slope = gelu_parts(pre[...])
    unit = (active - mean) * scale
    inner_low[...] = (unit * gain[...] + shift[...]).astype(BF16)
    grad = inner_grad[...]
    vectors[...] = jnp.zeros(vectors.shape, F32)
    vectors[0:1, :] = jnp.sum(grad * unit, 0, keepdims=True)
    vectors[1:2, :] = jnp.sum(grad, 0, keepdims=True)
    back = scale * (grad * gain[...] - first / width - unit * (second / width))
    low = (back * slope).astype(BF16)
    pre_grad[...] = low
    mid_part[...] = dot(low, up[...], NT).astype(BF16)


def outer_kernel(
    sc, mid_grad, hidden, cotangent, gain, shift, pieces, packed, o_all, st_all,
    hidden_grad, grad_mixed, st_near, pay_a, pay_b, pay_c, out_grad, vectors, columns, scratch,
):
    head0, base, valid, tensor = sc[0], sc[1], sc[4], sc[5]
    row = base + lax.broadcasted_iota(jnp.int32, (TOK, 1), 0)
    upstream = jnp.where(row < valid, cotangent[...].astype(F32), 0.0)
    _, unit, scale = norm_rows(hidden[...], gain[...], shift[...])
    grad = mid_grad[...].astype(F32)
    vectors[...] = jnp.zeros(vectors.shape, F32)
    vectors[0:1, :] = jnp.sum(grad * unit, 0, keepdims=True)
    vectors[1:2, :] = jnp.sum(grad, 0, keepdims=True)
    total = upstream + norm_rows_back(grad, unit, scale, gain[...])
    hidden_grad[...] = total
    branch = total.astype(BF16)

    mean, scale = mix_norm(pieces)
    first, second = jnp.zeros((1, TOK), F32), jnp.zeros((1, TOK), F32)
    for i in range(4):
        grad = dot(packed[i, :, 0:768], branch, NT)
        scratch[i] = grad
        q = grad * column(packed, i, 0)
        first += jnp.sum(q, 0, keepdims=True)
        second += jnp.sum(q * (pieces[i].astype(F32) - mean), 0, keepdims=True)
    second = second * scale
    unit = (pieces[tensor].astype(F32) - mean) * scale
    grad = scratch[tensor]
    gain_own, shift_own = column(packed, tensor, 0), column(packed, tensor, 3)
    low = (unit * gain_own + shift_own).astype(BF16)
    out_grad[...] = dot(low, branch).astype(BF16)
    lane = lax.broadcasted_iota(jnp.int32, (1, 128), 1)
    columns[...] = jnp.where(
        lane == 0, jnp.sum(grad * unit, 1, keepdims=True), jnp.where(lane == 1, jnp.sum(grad, 1, keepdims=True), 0.0)
    )
    back = scale * (grad * gain_own - first / 768 - unit * (second / 768))
    back = back.astype(BF16).astype(F32)
    grad_mixed[...] = back.astype(BF16)
    st_near[...] = jnp.zeros(st_near.shape, F32)
    tails = [[], [], []]
    for h in range(HEADS_HERE):
        rows = slice(h * HDIM, (h + 1) * HDIM)
        mine = back[rows]
        centre = jnp.sum(mine * o_all[rows, :], 0, keepdims=True)
        st_near[h : h + 1, :] = st_all[h : h + 1, :]
        st_near[3 + h : 4 + h, :] = centre
        pick_mid, pick_far = picks(head0 + h, base)
        for i, (pay, pick) in enumerate(((pay_a, pick_mid), (pay_b, pick_far), (pay_c, pick_far))):
            share = st_all[3 + 3 * i + h : 4 + 3 * i + h, :]
            terms = list(split3(centre * share)) + [jnp.zeros((13, TOK), F32)]
            wide = jnp.concatenate([mine * share] + terms, 0).astype(BF16)
            small = dot(wide, pick)
            pay[rows, :] = small[0:64].astype(BF16)
            tails[i].append(small[64:67])
    for pay, tail in zip((pay_a, pay_b, pay_c), tails):
        pay[192:208, :] = jnp.concatenate(tail + [jnp.zeros((7, SLOTS), F32)], 0).astype(BF16)


def backward_kernel(sc, q, qa, qb, qc, grad, st, ga, gb, gc, loc, right, right_a, right_f, value_a, value_f, *refs):
    kvs = refs[:PLANE]
    dq_near, dq_a, dq_b, dq_c, dkv = refs[PLANE : PLANE + 5]
    rows_q, rows_g, left, grad_left, small_a, small_f, acc_q, acc_kv = refs[PLANE + 5 :]
    head0, base, place, plane, valid = (sc[i] for i in range(5))
    heads = range(HEADS_HERE)
    mid_here, far_here = lax.rem(plane, 2) == 0, plane < 2
    for h in heads:
        lo = h * HDIM
        parts = query_rows(head0 + h, base, plane, q, (qa, qb, qc), lo)
        minus = jnp.concatenate([st[h : h + 1, :], loc[h : h + 1, :]], 1)
        minus = split3(jnp.where(minus > NONE * 0.1, -minus, 0.0))
        rows = jnp.concatenate(
            [jnp.concatenate(parts, 1)] + list(minus) + [jnp.zeros((29, 640), F32)], 0
        )
        rows_q[h] = rows.astype(BF16)
        left[h] = rows.T.astype(BF16)
        columns, centres = [grad[lo : lo + HDIM, :].astype(F32)], [st[3 + h : 4 + h, :]]
        for pay in (ga, gb, gc):
            columns.append(pay[lo : lo + HDIM, :].astype(F32))
            tail = pay[192:208, :].astype(F32)
            centres.append(tail[3 * h : 3 * h + 1] + tail[3 * h + 1 : 3 * h + 2] + tail[3 * h + 2 : 3 * h + 3])
        minus = split3(-jnp.concatenate(centres, 1))
        rows = jnp.concatenate(
            [jnp.concatenate(columns, 1)] + list(minus) + [jnp.zeros((13, 640), F32)], 0
        )
        rows_g[h] = rows.astype(BF16)
        grad_left[h] = rows.T.astype(BF16)

    @pl.when(plane < 3)
    def _():
        small_a[...] = jnp.zeros(small_a.shape, BF16)
        small_f[...] = jnp.zeros(small_f.shape, BF16)

    def part(h, at, rights, values, diagonal=False):
        s = dot(left[h, at, :], rights)
        if diagonal:
            s = jnp.where(diagonal_mask(base, valid), s, NONE)
        w = jnp.exp(s)
        ds = (w * dot(grad_left[h, at, :], values)).astype(BF16)
        dq = dot(rights[0:64], ds, NT)
        dk = dot(rows_q[h, 0:64, at], ds)
        dv = dot(rows_g[h, 0:64, at], w.astype(BF16))
        return dq, jnp.concatenate([dk, dv], 0)

    @pl.when(mid_here)
    def _():
        for h in heads:
            dq, small = part(h, slice(TOK, TOK + SLOTS), right_a[h], value_a[h])
            dq_a[h * HDIM : (h + 1) * HDIM, :] = (dq * 0.125).astype(BF16)
            small_a[h] = small.astype(BF16)

    @pl.when(far_here)
    def _():
        for h in heads:
            dq, small = part(h, slice(TOK + SLOTS, 640), right_f[h], value_f[h])
            dq = (dq * 0.125).astype(BF16)
            dq_b[h * HDIM : (h + 1) * HDIM, :] = dq[:, :SLOTS]
            dq_c[h * HDIM : (h + 1) * HDIM, :] = dq[:, SLOTS:]
            small_f[h] = small.astype(BF16)

    acc_q[...] = jnp.zeros(acc_q.shape, F32)
    for k in range(PLANE):
        block = lax.rem(place - k + PLANE, PLANE)
        at = slice(k * SLOTS, (k + 1) * SLOTS)

        @pl.when(plane < 3)
        def _():
            for h in heads:
                pick = jnp.concatenate(picks(head0 + h, plane * 2048 + block * TOK), 1)
                acc_kv[h] = dot(jnp.concatenate([small_a[h, :, at], small_f[h, :, at]], 1), pick, NT)

        @pl.when(plane == 3)
        def _():
            acc_kv[...] = jnp.zeros(acc_kv.shape, F32)

        @pl.when(k <= place)
        def _():
            for h in heads:
                lo = h * HDIM
                values = jnp.concatenate([kvs[k][192 + lo : 192 + lo + HDIM, :], ones(16, TOK)], 0)
                dq, both = part(h, slice(0, TOK), right[h, k], values, k == 0)
                acc_q[h] += dq
                acc_kv[h] += both

        for h in heads:
            lo = h * HDIM
            dkv[block, lo : lo + HDIM, :] = acc_kv[h, 0:64, :].astype(BF16)
            dkv[block, 192 + lo : 192 + lo + HDIM, :] = acc_kv[h, 64:128, :].astype(BF16)
    for h in heads:
        dq_near[h * HDIM : (h + 1) * HDIM, :] = acc_q[h] * 0.125


def weights_kernel(sc, normed, weights, dq_near, ra, rb, rc, dkv, out_grad, small, sums, part, grads):
    head0, base = sc[0], sc[1]
    for h in range(HEADS_HERE):
        rows = slice(h * HDIM, (h + 1) * HDIM)
        pick_mid, pick_far = picks(head0 + h, base)
        dq = dq_near[rows, :] + dot(ra[rows, :], pick_mid, NT) + dot(rb[rows, :], pick_far, NT) + dot(rc[rows, :], pick_far, NT)
        grads[rows, :] = dq.astype(BF16)
    total = dkv[0].astype(F32)
    for k in range(1, PLANE):
        total += dkv[k].astype(F32)
    grads[192:576, :] = total.astype(BF16)
    sums[0:576, 0:768] = dot(grads[...], normed[...]).astype(BF16)
    sums[576:768, 0:768] = out_grad[...]
    sums[:, 768:896] = small[...]
    back = dot(grads[0:192, :], weights[0], TN)
    back += dot(grads[192:384, :], weights[1], TN)
    back += dot(grads[384:576, :], weights[2], TN)
    part[...] = back.astype(BF16)


def reduce_kernel(inputs, hidden_grad, gain, shift, own, beside, across, both, got, inputs_grad, spread):
    _, unit, scale = norm_rows(inputs[...].astype(F32), gain[...], shift[...])
    grad = (own[...].astype(F32) + beside[...].astype(F32)) + (across[...].astype(F32) + both[...].astype(F32))
    inputs_grad[...] = (hidden_grad[...] + norm_rows_back(grad, unit, scale, gain[...])).astype(BF16)
    total = got[0].astype(F32)
    for i in range(1, PARTS):
        total += got[i].astype(F32)
    spread[0] = total.astype(BF16)
    first, second = jnp.sum(grad * unit, 0, keepdims=True), jnp.sum(grad, 0, keepdims=True)
    for i in range(6):
        at = slice(i * 128, (i + 1) * 128)
        spread[0, 8 + i : 9 + i, 768:896] = first[:, at].astype(BF16)
        spread[0, 16 + i : 17 + i, 768:896] = second[:, at].astype(BF16)
    for i in range(1, PARTS):
        spread[i] = spread[0]


def call(kernel, out_shapes, scratch=(), scalars=True, limit=48):
    def run(*args):
        specs = [pl.BlockSpec(memory_space=pltpu.VMEM)] * len(args)
        if scalars:
            specs[0] = pl.BlockSpec(memory_space=pltpu.SMEM)
        return pl.pallas_call(
            kernel,
            out_shape=[jax.ShapeDtypeStruct(s, d) for s, d in out_shapes],
            in_specs=specs,
            out_specs=[pl.BlockSpec(memory_space=pltpu.VMEM)] * len(out_shapes),
            scratch_shapes=list(scratch),
            compiler_params=pltpu.CompilerParams(vmem_limit_bytes=limit * 1024 * 1024),
        )(*args)

    return run


def sum_over_tensor(v):
    core = lax.axis_index("c")
    n = v.shape[0] // 2
    keep = lax.dynamic_slice_in_dim(v, core * n, n, 0)
    send = lax.dynamic_slice_in_dim(v, (1 - core) * n, n, 0)
    half = keep + lax.ppermute(send, "c", FLIP)
    half = half + lax.ppermute(half, "yl", FLIP)
    other = lax.ppermute(half, "c", FLIP)
    return jnp.where(core == 0, jnp.concatenate([half, other]), jnp.concatenate([other, half]))


def sum_small_over_tensor(v):
    v = v + lax.ppermute(v, "c", FLIP)
    return v + lax.ppermute(v, "yl", FLIP)


def others_over_tensor(v):
    across = lax.ppermute(v, "yl", FLIP)
    beside = lax.ppermute(v, "c", FLIP)
    return beside, across, lax.ppermute(across, "c", FLIP)


def sum_over_seq(v):
    for axis in ("x", "z", "yh"):
        v = lax.psum_scatter(v, axis, scatter_dimension=0, tiled=True)
    for axis in ("yh", "z", "x"):
        v = lax.all_gather(v, axis, axis=0, tiled=True)
    return v


MID_GO = [(1, 0), (3, 2)]
B_GO = [(2, 0), (3, 1)]
C_GO = [(3, 0), (2, 1)]


def back(perm):
    return [(b, a) for a, b in perm]


def visit(a, b, c, turn=lambda perm: perm):
    return tuple(lax.ppermute(v, "z", turn(perm)) for v, perm in ((a, MID_GO), (b, B_GO), (c, C_GO)))


def per_device(
    inputs,
    head_weights,
    out_weight,
    up_weight,
    down_weight,
    in_gain,
    in_shift,
    mix_gain,
    mix_shift,
    mid_gain,
    mid_shift,
    inner_gain,
    inner_shift,
    valid_length,
    cotangent,
):
    z, yh, x = (lax.axis_index(a) for a in SEQ)
    place = yh * 4 + x
    tensor = lax.axis_index("yl") * 2 + lax.axis_index("c")
    base = (z * PLANE + place) * TOK
    valid = valid_length[0]
    sc = jnp.stack([tensor * HEADS_HERE, base, place, z, valid, tensor]).astype(jnp.int32)
    row_valid = (base + jnp.arange(TOK, dtype=jnp.int32) < valid)[:, None]
    in_gain, in_shift, mid_gain, mid_shift, inner_gain, inner_shift = (
        v.reshape(1, 768) for v in (in_gain, in_shift, mid_gain, mid_shift, inner_gain, inner_shift)
    )

    vectors = jnp.stack(split3(mix_gain) + split3(mix_shift), 1).astype(BF16)
    packed = jnp.concatenate([out_weight, vectors, jnp.zeros((192, 122), BF16)], 1)
    packed = lax.all_gather(packed, TENSOR, axis=0)

    weights = head_weights.transpose(0, 2, 1)
    normed, q, pairs, q_mid, q_far = call(
        project_kernel,
        [((TOK, 768), BF16), ((192, TOK), BF16), ((384, TOK), BF16), ((192, SLOTS), BF16), ((192, SLOTS), BF16)],
    )(sc, inputs, weights, in_gain, in_shift)

    kvs = [pairs] + [
        lax.ppermute(pairs, ("yh", "x"), [(i, (i + k) % PLANE) for i in range(PLANE)]) for k in range(1, PLANE)
    ]
    visitors = visit(q_mid, q_far, q_far)
    n = HEADS_HERE
    o_near, st_near, pay_a, pay_b, pay_c, loc, *keys = call(
        forward_kernel,
        [((192, TOK), F32), ((8, TOK), F32)]
        + [((208, SLOTS), BF16)] * 3
        + [((8, 384), F32), ((n, PLANE, 128, TOK), BF16)]
        + [((n, 128, KEYS), BF16)] * 2
        + [((n, 80, KEYS), BF16)] * 2,
        [
            pltpu.VMEM((n, 128, TOK), F32),
            pltpu.VMEM((n, 128, 384), F32),
            pltpu.VMEM((n, TOK, 128), BF16),
            pltpu.VMEM((n, 128, 128), BF16),
            pltpu.VMEM((n, 256, 128), BF16),
            pltpu.VMEM((n, TOK, 128), F32),
            pltpu.VMEM((n, 128, 128), F32),
            pltpu.VMEM((n, 256, 128), F32),
            pltpu.VMEM((n, 80, TOK), F32),
            pltpu.VMEM((n, 80, 128), F32),
            pltpu.VMEM((n, 80, 256), F32),
        ],
    )(sc, q, *visitors, *kvs)
    returned = visit(pay_a, pay_b, pay_c, back)
    o_all, mixed, st_all = call(
        combine_kernel, [((192, TOK), F32), ((192, TOK), BF16), ((16, TOK), F32)]
    )(sc, o_near, st_near, *returned)

    pieces, hidden, mid_low, pre, inner_grad, sums = call(
        middle_kernel,
        [
            ((4, 192, TOK), BF16),
            ((TOK, 768), F32),
            ((TOK, 768), BF16),
            ((TOK, 768), F32),
            ((TOK, 768), F32),
            ((8, TOK), F32),
        ],
    )(sc, inputs, mixed, *others_over_tensor(mixed), packed, up_weight, down_weight, mid_gain, mid_shift, inner_gain, cotangent)
    sums = sum_small_over_tensor(sums)
    inner_low, pre_grad, mid_part, inner_vectors = call(
        inner_kernel,
        [((TOK, 768), BF16), ((TOK, 768), BF16), ((TOK, 768), BF16), ((8, 768), F32)],
        scalars=False,
    )(sums, pre, inner_grad, up_weight, inner_gain, inner_shift)
    mid_grad = sum_over_tensor(mid_part)

    feed_grad = jnp.where(row_valid, cotangent, jnp.zeros((), BF16))
    down_grad = jnp.einsum("tf,td->fd", inner_low, feed_grad, preferred_element_type=F32)
    up_grad = jnp.einsum("td,tf->df", mid_low, pre_grad, preferred_element_type=F32)
    feed_grads = sum_over_seq(jnp.concatenate([down_grad.astype(BF16), up_grad.astype(BF16)], 0)).astype(F32)
    feed_part = jnp.dot(inner_low, down_weight, preferred_element_type=F32).astype(BF16)

    hidden_grad, grad_mixed, st_near, pay_a, pay_b, pay_c, out_grad, mid_vectors, mix_columns = call(
        outer_kernel,
        [((TOK, 768), F32), ((192, TOK), BF16), ((8, TOK), F32)]
        + [((208, SLOTS), BF16)] * 3
        + [((192, 768), BF16), ((8, 768), F32), ((192, 128), F32)],
        [pltpu.VMEM((4, 192, TOK), F32)],
    )(sc, mid_grad, hidden, cotangent, mid_gain, mid_shift, pieces, packed, o_all, st_all)
    grads = visit(pay_a, pay_b, pay_c)

    feed_part, _ = lax.optimization_barrier((feed_part, mid_grad))
    feed_out = sum_over_tensor(feed_part).astype(F32)
    result = jnp.where(row_valid, hidden + feed_out, 0.0).astype(BF16)

    dq_near, dq_a, dq_b, dq_c, dkv = call(
        backward_kernel,
        [((192, TOK), F32)] + [((192, SLOTS), BF16)] * 3 + [((PLANE, 384, TOK), BF16)],
        [
            pltpu.VMEM((n, 128, 640), BF16),
            pltpu.VMEM((n, 80, 640), BF16),
            pltpu.VMEM((n, 640, 128), BF16),
            pltpu.VMEM((n, 640, 80), BF16),
            pltpu.VMEM((n, 128, KEYS), BF16),
            pltpu.VMEM((n, 128, KEYS), BF16),
            pltpu.VMEM((n, HDIM, TOK), F32),
            pltpu.VMEM((n, 128, TOK), F32),
        ],
    )(sc, q, *visitors, grad_mixed, st_near, *grads, loc, *keys, *kvs)
    dqs = visit(dq_a, dq_b, dq_c, back)
    dkv = lax.all_to_all(dkv, ("yh", "x"), 0, 0, tiled=True)

    small = jnp.concatenate(
        [mid_vectors[0], mid_vectors[1], inner_vectors[0], inner_vectors[1], mix_columns[:, 0], mix_columns[:, 1]]
    ).astype(BF16)
    small = jnp.pad(small.reshape(PARTS, 1, 108), ((0, 0), (0, ROW - 1), (0, 20))).reshape(PARTS * ROW, 128)
    sums, part = call(
        weights_kernel,
        [((PARTS * ROW, 896), BF16), ((TOK, 768), BF16)],
        [pltpu.VMEM((576, TOK), BF16)],
    )(sc, normed, weights, dq_near, *dqs, dkv, out_grad, small)
    parts = (
        lax.ppermute(part, "c", FLIP),
        lax.ppermute(part, "yl", FLIP),
        lax.ppermute(part, TENSOR, [(0, 3), (1, 2), (2, 1), (3, 0)]),
    )
    got = lax.all_to_all(sums.reshape(PARTS, ROW, 896), SEQ, 0, 0, tiled=True)
    inputs_grad, spread = call(
        reduce_kernel, [((TOK, 768), BF16), ((PARTS, ROW, 896), BF16)], scalars=False
    )(inputs, hidden_grad, in_gain, in_shift, part, *parts, got)
    last = lax.all_to_all(spread, SEQ, 0, 0, tiled=True)
    grads = last[:, :, :768].reshape(768, 768).astype(F32)
    small = last[:, 0, 768:876].reshape(-1).astype(F32)
    in_sums = jnp.sum(last[:, 8:, 768:896].astype(F32), 0)
    return (
        result,
        inputs_grad,
        grads[:576].reshape(3, 192, 768).transpose(0, 2, 1),
        grads[576:],
        feed_grads[768:],
        feed_grads[:768],
        in_sums[0:6].reshape(-1),
        in_sums[8:14].reshape(-1),
        small[3072:3264],
        small[3264:3456],
        small[0:768],
        small[768:1536],
        small[1536:2304],
        small[2304:3072],
    )


def solution(mesh):
    fine = Mesh(np.asarray(mesh.devices).reshape(4, 2, 4, 2, 2), SEQ + TENSOR)
    in_specs = (
        P(SEQ, None),
        P(None, None, TENSOR),
        P(TENSOR, None),
        P(None, TENSOR),
        P(TENSOR, None),
        P(),
        P(),
        P(TENSOR),
        P(TENSOR),
        P(),
        P(),
        P(TENSOR),
        P(TENSOR),
        P(),
        P(SEQ, None),
    )
    out_specs = (
        P(SEQ, None),
        P(SEQ, None),
        P(None, None, TENSOR),
        P(TENSOR, None),
        P(None, TENSOR),
        P(TENSOR, None),
        P(),
        P(),
        P(TENSOR),
        P(TENSOR),
        P(),
        P(),
        P(TENSOR),
        P(TENSOR),
    )
    return jax.shard_map(per_device, mesh=fine, in_specs=in_specs, out_specs=out_specs, check_vma=False)
```

```python
import functools

import jax
import jax.numpy as jnp
import numpy as np
from jax import lax
from jax.experimental import pallas as pl
from jax.experimental.pallas import tpu as pltpu
from jax.sharding import Mesh
from jax.sharding import PartitionSpec as P


HDIM = 64
HEADS_HERE = 3
TOK = 256
PLANE = 8
SLOTS = 128
KEYS = PLANE * SLOTS
PARTS = 32
ROW = 24
EPSILON = 1e-05
NONE = -1e30
NEAR = (1, 2, 4, 6, 12)
MID = (2, 4, 6, 12)
FAR = (4, 6, 12)
F32 = jnp.float32
BF16 = jnp.bfloat16
SEQ = ("z", "yh", "x")
TENSOR = ("yl", "c")
FLIP = [(0, 1), (1, 0)]
NN = ((1,), (0,))
NT = ((1,), (1,))
TN = ((0,), (0,))


def dot(a, b, dims=NN):
    return lax.dot_general(a, b, (dims, ((), ())), preferred_element_type=F32)


def split3(v):
    hi = v.astype(BF16).astype(F32)
    mid = (v - hi).astype(BF16).astype(F32)
    return hi, mid, v - hi - mid


def mid_offsets(head):
    slot = lax.broadcasted_iota(jnp.int32, (1, SLOTS), 1)
    return 2 * slot + lax.rem(head, 2)


def far_offsets(head, base):
    slot = lax.broadcasted_iota(jnp.int32, (1, SLOTS), 1)
    which = lax.rem(slot, 4)
    kind = jnp.where(which == 0, 0, 2 * which + 2)
    first = lax.div(base + 12 - head, 12) - 1
    return 12 * (first + lax.div(slot, 4)) + kind + head - base, kind


def one_hot_rows(offsets):
    rows = lax.broadcasted_iota(jnp.int32, (TOK, SLOTS), 0)
    return (rows == offsets).astype(F32).astype(BF16)


def picks(head, base):
    return one_hot_rows(mid_offsets(head)), one_hot_rows(far_offsets(head, base)[0])


def count_table(kind, usable, dilations):
    row = lax.broadcasted_iota(jnp.int32, (16, kind.shape[1]), 0)
    count = jnp.zeros(row.shape, F32)
    for step in dilations:
        count += jnp.where((lax.rem(row, step) == 0) & (lax.rem(kind, step) == 0), 1.0, 0.0)
    live = (count > 0) & usable & (row < 12)
    log_count = jnp.log(jnp.maximum(count, 1.0))
    hi = log_count.astype(BF16).astype(F32)
    return jnp.where(live, hi, NONE), jnp.where(live, log_count - hi, 0.0)


def score_columns(ref, lo, kind, usable, dilations):
    hi, low = count_table(kind, usable, dilations)
    return jnp.concatenate([ref[lo : lo + HDIM, :].astype(F32) * 0.125, hi, low], 0)


def own_columns(head, base, q, lo):
    kind = lax.rem(base - head + 12 + lax.broadcasted_iota(jnp.int32, (1, TOK), 1), 12)
    return score_columns(q, lo, kind, kind >= 0, NEAR)


def query_columns(head, base, plane, visitors, lo):
    if len(visitors) == 1:
        at = mid_offsets(head)
        return score_columns(visitors[0], lo, lax.rem(base + 2048 + at - head + 12, 12), at >= 0, MID)
    parts = []
    for visitor, origin in zip(visitors, (plane + 2, 3 - plane)):
        at, kind = far_offsets(head, origin * 2048 + lax.rem(base, 2048))
        parts.append(score_columns(visitor, lo, kind, (at >= 0) & (at < TOK), FAR))
    return jnp.concatenate(parts, 1)


def one_hot_kind(kind):
    return (kind == lax.broadcasted_iota(jnp.int32, (16, kind.shape[1]), 0)).astype(F32).astype(BF16)


def ones(rows, columns):
    return jnp.ones((rows, columns), BF16)


def diagonal_mask(base, valid):
    rows = lax.broadcasted_iota(jnp.int32, (TOK, TOK), 0)
    cols = lax.broadcasted_iota(jnp.int32, (TOK, TOK), 1)
    return (cols <= rows) & (cols + base < valid)


def norm_rows(v, gain, shift):
    mean = jnp.sum(v, 1, keepdims=True) / v.shape[1]
    spread = jnp.sum(v * v, 1, keepdims=True) / v.shape[1] - mean * mean
    scale = lax.rsqrt(spread + EPSILON)
    unit = (v - mean) * scale
    return unit * gain + shift, unit, scale


def norm_rows_back(grad, unit, scale, gain):
    q = grad * gain
    n = grad.shape[1]
    return scale * (q - jnp.sum(q, 1, keepdims=True) / n - unit * (jnp.sum(q * unit, 1, keepdims=True) / n))


def project_kernel(inputs, weights, gain, shift, normed, q, pairs):
    v = norm_rows(inputs[...].astype(F32), gain[...], shift[...])[0].astype(BF16)
    normed[...] = v
    q[...] = dot(weights[0], v, NT).astype(BF16)
    pairs[0:192, :] = dot(weights[1], v, NT).astype(BF16)
    pairs[192:384, :] = dot(weights[2], v, NT).astype(BF16)


def select_kernel(sc, q, out_weight, mix_gain, mix_shift, q_mid, q_far, packed):
    head0, base = sc[0], sc[1]
    for h in range(HEADS_HERE):
        rows = slice(h * HDIM, (h + 1) * HDIM)
        pick_mid, pick_far = picks(head0 + h, base)
        q_mid[rows, :] = dot(q[rows, :], pick_mid).astype(BF16)
        q_far[rows, :] = dot(q[rows, :], pick_far).astype(BF16)
    packed[0:192, :] = out_weight[...]
    terms = list(split3(mix_gain[...])) + list(split3(mix_shift[...])) + [jnp.zeros((10, 192), F32)]
    packed[192:208, 0:192] = jnp.concatenate(terms, 0).astype(BF16)


def weigh(s):
    return jnp.exp(s).astype(BF16)


def widest(s):
    return functools.reduce(jnp.maximum, [s[:, i * 128 : (i + 1) * 128] for i in range(s.shape[1] // 128)])


def shifted(m, rows):
    top = jnp.max(m.T, 0, keepdims=True)
    minus = jnp.concatenate(list(split3(-top)) + [jnp.zeros((29, top.shape[1]), F32)], 0)
    return top, jnp.concatenate([rows, minus], 0).T.astype(BF16)


def forward_far_kernel(sc, qa, qb, qc, *refs):
    kvs = refs[:PLANE]
    pay_a, pay_b, pay_c, loc, right_a, right_f, value_a, value_f = refs[PLANE:]
    head0, base, place, plane = (sc[i] for i in range(4))
    heads = range(HEADS_HERE)
    row = lax.broadcasted_iota(jnp.int32, (16, SLOTS), 0)
    loc[...] = jnp.zeros(loc.shape, F32)

    def gather(pick_of, kind_of, rights, values):
        for h in heads:
            lo = h * HDIM
            for k in range(PLANE):
                start = plane * 2048 + lax.rem(place - k + PLANE, PLANE) * TOK
                both = jnp.concatenate([kvs[k][lo : lo + HDIM, :], kvs[k][192 + lo : 192 + lo + HDIM, :]], 0)
                at = slice(k * SLOTS, (k + 1) * SLOTS)
                small = dot(both, pick_of(head0 + h, start)).astype(BF16)
                hot = one_hot_kind(kind_of(head0 + h, start))
                rights[h, :, at] = jnp.concatenate([small[0:HDIM], hot, hot, ones(32, SLOTS)], 0)
                values[h, :, at] = jnp.concatenate([small[HDIM:], ones(16, SLOTS)], 0)

    def attend(queries, rights, values, first, pays):
        extra = [jnp.where(row == 9, 1.0, 0.0) for _ in pays]
        rows = [query_columns(head0 + h, base, plane, queries, h * HDIM) for h in heads]
        zeros = jnp.zeros((32, SLOTS * len(pays)), F32)
        marks = [widest(dot(jnp.concatenate([rows[h], zeros], 0).T.astype(BF16), rights[h])) for h in heads]
        lefts = [shifted(marks[h], rows[h]) for h in heads]
        accs = [dot(values[h], weigh(dot(lefts[h][1], rights[h])), NT) for h in heads]
        for h in heads:
            total = accs[h][64:65, :]
            log = jnp.maximum(lefts[h][0] + jnp.log(total), NONE)
            out = accs[h][0:64, :] / total
            for i, pay in enumerate(pays):
                at = slice(i * SLOTS, (i + 1) * SLOTS)
                loc[h : h + 1, first + i * SLOTS : first + (i + 1) * SLOTS] = log[:, at]
                pay[h * HDIM : (h + 1) * HDIM, :] = out[:, at].astype(BF16)
                for j, term in enumerate(split3(log[:, at])):
                    extra[i] = jnp.where(row == 3 * h + j, term, extra[i])
        for e, pay in zip(extra, pays):
            pay[192:208, :] = e.astype(BF16)

    def far_kind(head, start):
        at, kind = far_offsets(head, start)
        return jnp.where((at >= 0) & (at < TOK), kind, 12)

    @pl.when(lax.rem(plane, 2) == 0)
    def _():
        gather(
            lambda head, start: one_hot_rows(mid_offsets(head)),
            lambda head, start: lax.rem(start + mid_offsets(head) - head + 12, 12),
            right_a,
            value_a,
        )
        attend((qa,), right_a, value_a, 0, (pay_a,))

    @pl.when(plane < 2)
    def _():
        gather(lambda head, start: one_hot_rows(far_offsets(head, start)[0]), far_kind, right_f, value_f)
        attend((qb, qc), right_f, value_f, SLOTS, (pay_b, pay_c))


def forward_near_kernel(sc, q, *refs):
    kvs = refs[:PLANE]
    o_near, st_near, right, rows, left, marks, acc = refs[PLANE:]
    head0, base, place, plane, valid = (sc[i] for i in range(5))
    heads = range(HEADS_HERE)
    for h in heads:
        lo = h * HDIM
        head = head0 + h
        rows[h] = own_columns(head, base, q, lo)
        left[h] = jnp.concatenate([rows[h], jnp.zeros((32, TOK), F32)], 0).T.astype(BF16)
    marks[...] = jnp.full(marks.shape, 2 * NONE, F32)
    for k in range(PLANE):

        @pl.when(k <= place)
        def _():
            start = base - k * TOK
            for h in heads:
                lo = h * HDIM
                kind = lax.rem(start - (head0 + h) + 12 + lax.broadcasted_iota(jnp.int32, (1, TOK), 1), 12)
                hot = one_hot_kind(kind)
                right[h, k] = jnp.concatenate([kvs[k][lo : lo + HDIM, :], hot, hot, ones(32, TOK)], 0)
                s = dot(left[h], right[h, k])
                if k == 0:
                    s = jnp.where(diagonal_mask(base, valid), s, NONE)
                marks[h] = jnp.maximum(marks[h], widest(s))

    tops = []
    for h in heads:
        top, turned = shifted(marks[h], rows[h])
        tops.append(top)
        left[h] = turned
    acc[...] = jnp.zeros(acc.shape, F32)
    for k in range(PLANE):

        @pl.when(k <= place)
        def _():
            for h in heads:
                lo = h * HDIM
                s = dot(left[h], right[h, k])
                if k == 0:
                    s = jnp.where(diagonal_mask(base, valid), s, NONE)
                values = jnp.concatenate([kvs[k][192 + lo : 192 + lo + HDIM, :], ones(16, TOK)], 0)
                acc[h] += dot(values, weigh(s), NT)

    st_near[...] = jnp.zeros(st_near.shape, F32)
    for h in heads:
        total = acc[h, 64:65, :]
        o_near[h * HDIM : (h + 1) * HDIM, :] = acc[h, 0:64, :] / total
        st_near[h : h + 1, :] = tops[h] + jnp.log(total)


def combine_kernel(sc, o_near, st_near, ra, rb, rc, o_all, mixed, st_all):
    head0, base = sc[0], sc[1]
    st_all[...] = jnp.zeros(st_all.shape, F32)
    for h in range(HEADS_HERE):
        rows = slice(h * HDIM, (h + 1) * HDIM)
        pick_mid, pick_far = picks(head0 + h, base)
        outs, logs = [o_near[rows, :]], [st_near[h : h + 1, :]]
        for pay, pick in ((ra, pick_mid), (rb, pick_far), (rc, pick_far)):
            wide = dot(jnp.concatenate([pay[rows, :], pay[192:208, :]], 0), pick, NT)
            log = wide[64 + 3 * h : 65 + 3 * h] + wide[65 + 3 * h : 66 + 3 * h] + wide[66 + 3 * h : 67 + 3 * h]
            outs.append(wide[0:64])
            logs.append(jnp.where(wide[73:74] > 0.5, log, NONE))
        top = functools.reduce(jnp.maximum, logs)
        weights = [jnp.exp(v - top) for v in logs]
        total = sum(weights)
        mixed_h = sum((w / total) * o for w, o in zip(weights, outs))
        o_all[rows, :] = mixed_h
        mixed[rows, :] = mixed_h.astype(BF16)
        st_all[h : h + 1, :] = top + jnp.log(total)
        for i in range(3):
            st_all[3 + 3 * i + h : 4 + 3 * i + h, :] = weights[i + 1] / total


def mix_norm(pieces):
    first = sum(jnp.sum(pieces[i].astype(F32), 0, keepdims=True) for i in range(4)) / 768
    second = sum(jnp.sum(jnp.square(pieces[i].astype(F32)), 0, keepdims=True) for i in range(4)) / 768
    return first, lax.rsqrt(second - first * first + EPSILON)


def mix_parameters(packed, i):
    tail = jnp.concatenate([packed[i, 192:208, 0:256].astype(F32), jnp.zeros((112, 256), F32)], 0).T[0:192]
    return tail[:, 0:1] + tail[:, 1:2] + tail[:, 2:3], tail[:, 3:4] + tail[:, 4:5] + tail[:, 5:6]


def gelu_parts(v):
    a, b = 0.7978845608028654, 0.044715
    square = v * v
    t = jnp.tanh(a * v * (1.0 + b * square))
    active = 0.5 * v * (1.0 + t)
    slope = 0.5 * (1.0 + t) + 0.5 * v * (1.0 - t * t) * (a * (1.0 + 3.0 * b * square))
    return active, slope


def middle_kernel(
    sc, inputs, own, beside, across, both, packed_own, packed_beside, packed_across, packed_both,
    up, down, gain, shift, inner_gain, cotangent,
    pieces, packed, hidden, mid_low, pre, inner_grad, feed_grad, sums,
):
    tensor, base, valid = sc[5], sc[1], sc[4]
    for i, ref in enumerate((own, beside, across, both)):
        pieces[jnp.bitwise_xor(tensor, i)] = ref[...]
    for i, ref in enumerate((packed_own, packed_beside, packed_across, packed_both)):
        packed[jnp.bitwise_xor(tensor, i)] = ref[...]
    mean, scale = mix_norm(pieces)
    total = inputs[...].astype(F32)
    branch = None
    for i in range(4):
        mix_gain, mix_shift = mix_parameters(packed, i)
        low = ((pieces[i].astype(F32) - mean) * scale * mix_gain + mix_shift).astype(BF16)
        term = dot(low, packed[i, 0:192, :], TN)
        branch = term if branch is None else branch + term
    total = total + branch
    hidden[...] = total
    low = norm_rows(total, gain[...], shift[...])[0].astype(BF16)
    mid_low[...] = low
    pre[...] = dot(low, up[...])
    active = gelu_parts(pre[...])[0]
    row = base + lax.broadcasted_iota(jnp.int32, (TOK, 1), 0)
    feed = jnp.where(row < valid, cotangent[...].astype(F32), 0.0).astype(BF16)
    feed_grad[...] = feed
    grad = dot(feed, down[...], NT)
    inner_grad[...] = grad
    scaled = grad * inner_gain[...]
    lane = lax.broadcasted_iota(jnp.int32, (1, 128), 1)
    st = jnp.zeros((TOK, 128), F32)
    for i, v in enumerate((active, active * active, scaled, scaled * active)):
        st = jnp.where(lane == i, jnp.sum(v, 1, keepdims=True), st)
    sums[...] = st.T[0:8]


def halves(core, v, keep, send):
    for c in range(2):

        @pl.when(core == c)
        def _():
            keep[...] = v[c * 128 : (c + 1) * 128].astype(BF16)
            send[...] = v[(1 - c) * 128 : (2 - c) * 128].astype(BF16)


def whole(core, own, other):
    own, other = own[...].astype(F32), other[...].astype(F32)
    return jnp.concatenate([jnp.where(core == 0, own, other), jnp.where(core == 0, other, own)], 0)


def inner_kernel(sc, sums, pre, inner_grad, up, gain, shift, inner_low, pre_grad, keep, send, vectors):
    st = jnp.concatenate([sums[...], jnp.zeros((120, TOK), F32)], 0).T
    width = 3072
    mean = st[:, 0:1] / width
    scale = lax.rsqrt(st[:, 1:2] / width - mean * mean + EPSILON)
    first = st[:, 2:3]
    second = scale * (st[:, 3:4] - mean * first)
    active, slope = gelu_parts(pre[...])
    unit = (active - mean) * scale
    inner_low[...] = (unit * gain[...] + shift[...]).astype(BF16)
    grad = inner_grad[...]
    vectors[...] = jnp.zeros(vectors.shape, F32)
    vectors[0:1, :] = jnp.sum(grad * unit, 0, keepdims=True)
    vectors[1:2, :] = jnp.sum(grad, 0, keepdims=True)
    back = scale * (grad * gain[...] - first / width - unit * (second / width))
    low = (back * slope).astype(BF16)
    pre_grad[...] = low
    halves(sc[6], dot(low, up[...], NT), keep, send)


def outer_kernel(
    sc, mid_own, mid_other, hidden, cotangent, gain, shift, pieces, packed, o_all, st_all,
    hidden_grad, grad_mixed, st_near, pay_a, pay_b, pay_c, out_grad, vectors, scratch,
):
    head0, base, valid, tensor = sc[0], sc[1], sc[4], sc[5]
    row = base + lax.broadcasted_iota(jnp.int32, (TOK, 1), 0)
    upstream = jnp.where(row < valid, cotangent[...].astype(F32), 0.0)
    _, unit, scale = norm_rows(hidden[...], gain[...], shift[...])
    grad = whole(sc[6], mid_own, mid_other)
    vectors[...] = jnp.zeros(vectors.shape, F32)
    vectors[0:1, :] = jnp.sum(grad * unit, 0, keepdims=True)
    vectors[1:2, :] = jnp.sum(grad, 0, keepdims=True)
    total = upstream + norm_rows_back(grad, unit, scale, gain[...])
    hidden_grad[...] = total
    branch = total.astype(BF16)

    mean, scale = mix_norm(pieces)
    first, second = jnp.zeros((1, TOK), F32), jnp.zeros((1, TOK), F32)
    for i in range(4):
        grad = dot(packed[i, 0:192, :], branch, NT)
        scratch[i] = grad
        q = grad * mix_parameters(packed, i)[0]
        first += jnp.sum(q, 0, keepdims=True)
        second += jnp.sum(q * (pieces[i].astype(F32) - mean), 0, keepdims=True)
    second = second * scale
    unit = (pieces[tensor].astype(F32) - mean) * scale
    grad = scratch[tensor]
    gain_own, shift_own = mix_parameters(packed, tensor)
    low = (unit * gain_own + shift_own).astype(BF16)
    out_grad[0:24] = dot(low, branch).reshape(24, 8, 768).astype(BF16)
    out_grad[24:32] = jnp.zeros((8, 8, 768), BF16)
    lane = lax.broadcasted_iota(jnp.int32, (1, 128), 1)
    columns = jnp.where(
        lane == 0, jnp.sum(grad * unit, 1, keepdims=True), jnp.where(lane == 1, jnp.sum(grad, 1, keepdims=True), 0.0)
    )
    vectors[2:4, 0:192] = columns.T[0:2]
    back = scale * (grad * gain_own - first / 768 - unit * (second / 768))
    back = back.astype(BF16).astype(F32)
    grad_mixed[...] = back.astype(BF16)
    st_near[...] = jnp.zeros(st_near.shape, F32)
    tails = [[], [], []]
    for h in range(HEADS_HERE):
        rows = slice(h * HDIM, (h + 1) * HDIM)
        mine = back[rows]
        centre = jnp.sum(mine * o_all[rows, :], 0, keepdims=True)
        st_near[h : h + 1, :] = st_all[h : h + 1, :]
        st_near[3 + h : 4 + h, :] = centre
        pick_mid, pick_far = picks(head0 + h, base)
        for i, (pay, pick) in enumerate(((pay_a, pick_mid), (pay_b, pick_far), (pay_c, pick_far))):
            share = st_all[3 + 3 * i + h : 4 + 3 * i + h, :]
            terms = list(split3(centre * share)) + [jnp.zeros((13, TOK), F32)]
            wide = jnp.concatenate([mine * share] + terms, 0).astype(BF16)
            small = dot(wide, pick)
            pay[rows, :] = small[0:64].astype(BF16)
            tails[i].append(small[64:67])
    for pay, tail in zip((pay_a, pay_b, pay_c), tails):
        pay[192:208, :] = jnp.concatenate(tail + [jnp.zeros((7, SLOTS), F32)], 0).astype(BF16)


def gradients(left, grad_left, rows_q, rows_g, rights, values, mask=None):
    s = dot(left, rights)
    if mask is not None:
        s = jnp.where(mask, s, NONE)
    w = jnp.exp(s)
    ds = (w * dot(grad_left, values)).astype(BF16)
    dq = dot(rights[0:64], ds, NT)
    return dq, jnp.concatenate([dot(rows_q, ds), dot(rows_g, w.astype(BF16))], 0)


def with_logs(rows, logs):
    minus = split3(jnp.where(logs > NONE * 0.1, -logs, 0.0))
    return jnp.concatenate([rows] + list(minus) + [jnp.zeros((29, logs.shape[1]), F32)], 0)


def with_centres(rows, centres):
    return jnp.concatenate([rows] + list(split3(-centres)) + [jnp.zeros((13, centres.shape[1]), F32)], 0)


def backward_near_kernel(sc, q, grad, st, right, *refs):
    kvs = refs[:PLANE]
    dq_near, dkv, rows_q, rows_g, left, grad_left, acc_q = refs[PLANE:]
    head0, base, place, plane, valid = (sc[i] for i in range(5))
    heads = range(HEADS_HERE)
    for h in heads:
        lo = h * HDIM
        rows = with_logs(own_columns(head0 + h, base, q, lo), st[h : h + 1, :])
        rows_q[h] = rows[0:64].astype(BF16)
        left[h] = rows.T.astype(BF16)
        rows = with_centres(grad[lo : lo + HDIM, :].astype(F32), st[3 + h : 4 + h, :])
        rows_g[h] = rows[0:64].astype(BF16)
        grad_left[h] = rows.T.astype(BF16)
    acc_q[...] = jnp.zeros(acc_q.shape, F32)
    for k in range(PLANE):
        block = lax.rem(place - k + PLANE, PLANE)

        @pl.when(k > place)
        def _():
            dkv[block] = jnp.zeros((384, TOK), BF16)

        @pl.when(k <= place)
        def _():
            mask = diagonal_mask(base, valid) if k == 0 else None
            for h in heads:
                lo = h * HDIM
                values = jnp.concatenate([kvs[k][192 + lo : 192 + lo + HDIM, :], ones(16, TOK)], 0)
                dq, both = gradients(left[h], grad_left[h], rows_q[h], rows_g[h], right[h, k], values, mask)
                acc_q[h] += dq
                dkv[block, lo : lo + HDIM, :] = both[0:64].astype(BF16)
                dkv[block, 192 + lo : 192 + lo + HDIM, :] = both[64:128].astype(BF16)

    for h in heads:
        dq_near[h * HDIM : (h + 1) * HDIM, :] = acc_q[h] * 0.125


def backward_far_kernel(sc, dkv_near, qa, qb, qc, ga, gb, gc, loc, right_a, right_f, value_a, value_f, *refs):
    dq_a, dq_b, dq_c, dkv, small_a, small_f = refs
    head0, base, place, plane = (sc[i] for i in range(4))
    heads = range(HEADS_HERE)

    def part(queries, pays, first, rights, values, dqs, small):
        n = SLOTS * len(pays)
        for h in heads:
            lo = h * HDIM
            rows = query_columns(head0 + h, base, plane, queries, lo)
            rows = with_logs(rows, loc[h : h + 1, first : first + n])
            columns, centres = [], []
            for pay in pays:
                columns.append(pay[lo : lo + HDIM, :].astype(F32))
                tail = pay[192:208, :].astype(F32)
                centres.append(tail[3 * h : 3 * h + 1] + tail[3 * h + 1 : 3 * h + 2] + tail[3 * h + 2 : 3 * h + 3])
            grads = with_centres(jnp.concatenate(columns, 1), jnp.concatenate(centres, 1))
            dq, both = gradients(
                rows.T.astype(BF16),
                grads.T.astype(BF16),
                rows[0:64].astype(BF16),
                grads[0:64].astype(BF16),
                rights[h],
                values[h],
            )
            dq = (dq * 0.125).astype(BF16)
            for i, out in enumerate(dqs):
                out[lo : lo + HDIM, :] = dq[:, i * SLOTS : (i + 1) * SLOTS]
            small[h] = both.astype(BF16)

    @pl.when((plane == 1) | (plane == 2))
    def _():
        small_a[...] = jnp.zeros(small_a.shape, BF16)
        small_f[...] = jnp.zeros(small_f.shape, BF16)

    @pl.when(lax.rem(plane, 2) == 0)
    def _():
        part((qa,), (ga,), 0, right_a, value_a, (dq_a,), small_a)

    @pl.when(plane < 2)
    def _():
        part((qb, qc), (gb, gc), SLOTS, right_f, value_f, (dq_b, dq_c), small_f)

    @pl.when(plane == 3)
    def _():
        dkv[...] = dkv_near[...]

    @pl.when(plane < 3)
    def _():
        for k in range(PLANE):
            block = lax.rem(place - k + PLANE, PLANE)
            at = slice(k * SLOTS, (k + 1) * SLOTS)
            for h in heads:
                lo = h * HDIM
                pick = jnp.concatenate(picks(head0 + h, plane * 2048 + block * TOK), 1)
                wide = dot(jnp.concatenate([small_a[h, :, at], small_f[h, :, at]], 1), pick, NT)
                for i, at_row in ((0, lo), (64, 192 + lo)):
                    near = dkv_near[block, at_row : at_row + HDIM, :].astype(F32)
                    dkv[block, at_row : at_row + HDIM, :] = (near + wide[i : i + 64]).astype(BF16)


def weights_kernel(sc, normed, weights, dq_near, ra, rb, rc, dkv, sums, keep, send, grads):
    head0, base = sc[0], sc[1]
    for h in range(HEADS_HERE):
        rows = slice(h * HDIM, (h + 1) * HDIM)
        pick_mid, pick_far = picks(head0 + h, base)
        dq = dq_near[rows, :] + dot(ra[rows, :], pick_mid, NT) + dot(rb[rows, :], pick_far, NT) + dot(rc[rows, :], pick_far, NT)
        grads[rows, :] = dq.astype(BF16)
    total = dkv[0].astype(F32)
    for k in range(1, PLANE):
        total += dkv[k].astype(F32)
    grads[192:576, :] = total.astype(BF16)
    full = dot(grads[...], normed[...]).T.reshape(PARTS, ROW, 576)
    sums[:, :, 0:576] = full.astype(BF16)
    sums[:, :, 576:640] = jnp.zeros((PARTS, ROW, 64), BF16)
    back = dot(grads[0:192, :], weights[0], TN)
    back += dot(grads[192:384, :], weights[1], TN)
    back += dot(grads[384:576, :], weights[2], TN)
    halves(sc[6], back, keep, send)


def reduce_kernel(sc, inputs, hidden_grad, gain, shift, own, other, got, inputs_grad, spread):
    _, unit, scale = norm_rows(inputs[...].astype(F32), gain[...], shift[...])
    grad = whole(sc[6], own, other)
    inputs_grad[...] = (hidden_grad[...] + norm_rows_back(grad, unit, scale, gain[...])).astype(BF16)
    total = got[0].astype(F32)
    for i in range(1, PARTS):
        total += got[i].astype(F32)
    spread[0, :, 0:576] = total[:, 0:576].astype(BF16)
    first, second = jnp.sum(grad * unit, 0, keepdims=True), jnp.sum(grad, 0, keepdims=True)
    rows = [v[:, i * 64 : (i + 1) * 64] for v in (first, second) for i in range(12)]
    spread[0, :, 576:640] = jnp.concatenate(rows, 0).astype(BF16)
    for i in range(1, PARTS):
        spread[i] = spread[0]


PAIR_A = [(0, 1), (1, 0), (2, 3), (3, 2)]
PAIR_B = [(0, 3), (3, 0), (1, 2), (2, 1)]
STEPS = {"xa": ("x", PAIR_A, 0), "xb": ("x", PAIR_B, 1), "za": ("z", PAIR_A, 2), "zb": ("z", PAIR_B, 3), "y": ("yh", FLIP, 4)}
FIRST = ("xa", "xb", "za", "zb")
SECOND = ("xb", "xa", "zb", "za")
THIRD = ("za", "xa")
FOURTH = ("zb", "xb")


def side_of(sides, name):
    return sides[STEPS[name][2]]


def travel(v, name):
    axis, perm, _ = STEPS[name]
    return lax.ppermute(v, axis, perm)


def cut_sides():
    x, z, y = lax.axis_index("x"), lax.axis_index("z"), lax.axis_index("yh")
    a = [jnp.where((i == 0) | (i == 3), 0, 1) for i in (x, z)]
    b = [jnp.where(i < 2, 0, 1) for i in (x, z)]
    return jnp.stack([a[0], b[0], a[1], b[1], y]).astype(jnp.int32)


def part_of(ref, side, n):
    return ref[pl.ds(side * n, n)].astype(F32)


def products_kernel(sc, inner_low, feed_grad, mid_low, pre_grad, down, full_d, full_u, feed_keep, feed_send):
    full_d[...] = dot(inner_low[...], feed_grad[...], TN).reshape(PARTS, ROW, 768).astype(BF16)
    full_u[...] = dot(mid_low[...], pre_grad[...], TN).reshape(PARTS, ROW, 768).astype(BF16)
    halves(sc[6], dot(inner_low[...], down[...]), feed_keep, feed_send)


def first_kernel(sides, full_d, full_u, out_grad, mid_vectors, inner_vectors, *refs):
    keeps, sends, extra = refs[0:4], refs[4:8], refs[8]
    extra[...] = jnp.zeros(extra.shape, BF16)
    extra[0] = jnp.concatenate([mid_vectors[0:4], inner_vectors[0:2], jnp.zeros((2, 768), F32)], 0).astype(BF16)
    for j in range(4):
        side = side_of(sides, FIRST[j])
        columns = slice((j % 2) * 384, (j % 2 + 1) * 384)
        full, rest = ((full_d, out_grad), (full_u, extra))[j // 2]
        for ref, s in ((keeps[j], side), (sends[j], 1 - side)):
            ref[:, 0:24, :] = full[pl.ds(s * 16, 16), :, columns]
            ref[:, 24:32, :] = rest[pl.ds(s * 16, 16), :, columns]


def second_kernel(sides, *refs):
    keeps, gots, new_keeps, new_sends = refs[0:4], refs[4:8], refs[8:12], refs[12:16]
    for j in range(4):
        side = side_of(sides, SECOND[j])
        new_keeps[j][...] = (part_of(keeps[j], side, 8) + part_of(gots[j], side, 8)).astype(BF16)
        new_sends[j][...] = (part_of(keeps[j], 1 - side, 8) + part_of(gots[j], 1 - side, 8)).astype(BF16)


def third_kernel(sides, *refs):
    keeps, gots, new_keeps, new_sends = refs[0:4], refs[4:8], refs[8:10], refs[10:12]
    for j in range(4):
        i, columns = j // 2, slice((j % 2) * 384, (j % 2 + 1) * 384)
        side = side_of(sides, THIRD[i])
        new_keeps[i][:, :, columns] = (part_of(keeps[j], side, 4) + part_of(gots[j], side, 4)).astype(BF16)
        new_sends[i][:, :, columns] = (part_of(keeps[j], 1 - side, 4) + part_of(gots[j], 1 - side, 4)).astype(BF16)


def fourth_kernel(sides, *refs):
    keeps, gots, new_keeps, new_sends = refs[0:2], refs[2:4], refs[4:6], refs[6:8]
    for i in range(2):
        side = side_of(sides, FOURTH[i])
        new_keeps[i][...] = (part_of(keeps[i], side, 2) + part_of(gots[i], side, 2)).astype(BF16)
        new_sends[i][...] = (part_of(keeps[i], 1 - side, 2) + part_of(gots[i], 1 - side, 2)).astype(BF16)


def fifth_kernel(sides, *refs):
    keeps, gots, new_keep, new_send = refs[0:2], refs[2:4], refs[4], refs[5]
    side = side_of(sides, "y")
    for i in range(2):
        new_keep[i] = (keeps[i][side].astype(F32) + gots[i][side].astype(F32)).astype(BF16)
        new_send[i] = (keeps[i][1 - side].astype(F32) + gots[i][1 - side].astype(F32)).astype(BF16)


def join_y_kernel(sides, own, other, *outs):
    side = side_of(sides, "y")
    for i in range(2):
        outs[i][side] = own[i]
        outs[i][1 - side] = other[i]


def join_pairs_kernel(names, sides, *refs):
    n = len(names)
    owns, others, outs = refs[0:n], refs[n : 2 * n], refs[2 * n : 3 * n]
    for i, name in enumerate(names):
        size = owns[i].shape[0]
        side = side_of(sides, name)
        outs[i][pl.ds(side * size, size)] = owns[i][...]
        outs[i][pl.ds((1 - side) * size, size)] = others[i][...]


def join_streams_kernel(sides, own_d, own_u, other_d, other_u, *outs):
    for j in range(4):
        own, other = ((own_d, other_d), (own_u, other_u))[j // 2]
        side = side_of(sides, THIRD[j // 2])
        columns = slice((j % 2) * 384, (j % 2 + 1) * 384)
        outs[j][pl.ds(side * 4, 4)] = own[:, :, columns]
        outs[j][pl.ds((1 - side) * 4, 4)] = other[:, :, columns]


def join_all_kernel(sides, *refs):
    owns, others = refs[0:4], refs[4:8]
    down, up, out, vectors, rest_d, rest_u = refs[8:]
    for j in range(4):
        side = side_of(sides, FIRST[j])
        columns = slice((j % 2) * 384, (j % 2 + 1) * 384)
        full, rest = ((down, rest_d), (up, rest_u))[j // 2]
        for ref, s in ((owns[j], side), (others[j], 1 - side)):
            full[pl.ds(s * 16, 16), :, columns] = ref[:, 0:24, :].astype(F32)
            rest[pl.ds(s * 16, 16), :, columns] = ref[:, 24:32, :].astype(F32)
    out[...] = rest_d[0:24]
    vectors[...] = rest_u[0]


def final_kernel(got, head_grad, in_sums):
    head_grad[...] = got[:, :, 0:576].astype(F32).reshape(768, 576).T
    in_sums[...] = jnp.sum(got[:, :, 576:640].astype(F32), 0)


def add_kernel(a, b, out):
    out[...] = (a[...].astype(F32) + b[...].astype(F32)).astype(out.dtype)


TIMES = {
    "project_kernel": 1.2,
    "forward_far_kernel": 4.3,
    "forward_near_kernel": 7.0,
    "combine_kernel": 1.0,
    "middle_kernel": 3.4,
    "inner_kernel": 2.0,
    "outer_kernel": 2.3,
    "products_kernel": 3.0,
    "backward_near_kernel": 8.0,
    "backward_far_kernel": 5.8,
    "weights_kernel": 2.0,
    "reduce_kernel": 2.0,
    "join_all_kernel": 3.0,
}


def call(kernel, out_shapes, scratch=(), scalars=1, limit=8):
    def run(*args, after=()):
        n, extra = len(args), len(after)
        name = getattr(kernel, "func", kernel).__name__
        specs = [pl.BlockSpec(memory_space=pltpu.VMEM)] * n + [pl.BlockSpec(memory_space=pl.ANY)] * extra
        for i in range(scalars):
            specs[i] = pl.BlockSpec(memory_space=pltpu.SMEM)

        def body(*refs):
            kernel(*refs[:n], *refs[n + extra :])

        return pl.pallas_call(
            body,
            out_shape=[jax.ShapeDtypeStruct(s, d) for s, d in out_shapes],
            in_specs=specs,
            out_specs=[pl.BlockSpec(memory_space=pltpu.VMEM)] * len(out_shapes),
            scratch_shapes=list(scratch),
            compiler_params=pltpu.CompilerParams(vmem_limit_bytes=limit * 1024 * 1024),
            name=name,
            cost_estimate=pl.CostEstimate(
                flops=int(TIMES.get(name, 0.6) * 1e9), bytes_accessed=0, transcendentals=0
            ),
        )(*args, *after)

    return run


def add(a, b, after=()):
    (out,) = call(add_kernel, [(a.shape, a.dtype)], scalars=0)(a, b, after=after)
    return out


def others_over_tensor(v):
    across = lax.ppermute(v, "yl", FLIP)
    beside = lax.ppermute(v, "c", FLIP)
    return beside, across, lax.ppermute(across, "c", FLIP)


MID_GO = [(1, 0), (3, 2)]
B_GO = [(2, 0), (3, 1)]
C_GO = [(3, 0), (2, 1)]


def back(perm):
    return [(b, a) for a, b in perm]


def visit(a, b, c, turn=lambda perm: perm):
    return tuple(lax.ppermute(v, "z", turn(perm)) for v, perm in ((a, MID_GO), (b, B_GO), (c, C_GO)))


def per_device(
    inputs,
    head_weights,
    out_weight,
    up_weight,
    down_weight,
    in_gain,
    in_shift,
    mix_gain,
    mix_shift,
    mid_gain,
    mid_shift,
    inner_gain,
    inner_shift,
    valid_length,
    cotangent,
):
    z, yh, x = (lax.axis_index(a) for a in SEQ)
    place = yh * 4 + x
    tensor = lax.axis_index("yl") * 2 + lax.axis_index("c")
    base = (z * PLANE + place) * TOK
    valid = valid_length[0]
    core = lax.axis_index("c")
    sc = jnp.stack([tensor * HEADS_HERE, base, place, z, valid, tensor, core]).astype(jnp.int32)
    sides = cut_sides()
    row_valid = (base + jnp.arange(TOK, dtype=jnp.int32) < valid)[:, None]
    in_gain, in_shift, mid_gain, mid_shift, inner_gain, inner_shift = (
        v.reshape(1, 768) for v in (in_gain, in_shift, mid_gain, mid_shift, inner_gain, inner_shift)
    )
    mix_gain, mix_shift = mix_gain.reshape(1, 192), mix_shift.reshape(1, 192)
    n = HEADS_HERE
    half = ((128, 768), BF16)

    weights = head_weights.transpose(0, 2, 1)
    normed, q, pairs = call(
        project_kernel, [((TOK, 768), BF16), ((192, TOK), BF16), ((384, TOK), BF16)], scalars=0
    )(inputs, weights, in_gain, in_shift)
    kvs = [pairs] + [
        lax.ppermute(pairs, ("yh", "x"), [(i, (i + k) % PLANE) for i in range(PLANE)]) for k in range(1, PLANE)
    ]
    q_mid, q_far, packed = call(
        select_kernel, [((192, SLOTS), BF16), ((192, SLOTS), BF16), ((208, 768), BF16)]
    )(sc, q, out_weight, mix_gain, mix_shift, after=(kvs[4],))
    visitors = visit(q_mid, q_far, q_far)
    pay_a, pay_b, pay_c, loc, *far_keys = call(
        forward_far_kernel,
        [((208, SLOTS), BF16)] * 3
        + [((8, 384), F32)]
        + [((n, 128, KEYS), BF16)] * 2
        + [((n, 80, KEYS), BF16)] * 2,
        limit=16,
    )(sc, *visitors, *kvs)
    returned = visit(pay_a, pay_b, pay_c, back)
    packed, _ = lax.optimization_barrier((packed, pay_a))
    packed_others = (
        lax.ppermute(packed, "c", FLIP),
        lax.ppermute(packed, "yl", FLIP),
        lax.ppermute(packed, TENSOR, [(0, 3), (1, 2), (2, 1), (3, 0)]),
    )
    o_near, st_near, right = call(
        forward_near_kernel,
        [((192, TOK), F32), ((8, TOK), F32), ((n, PLANE, 128, TOK), BF16)],
        [
            pltpu.VMEM((n, 96, TOK), F32),
            pltpu.VMEM((n, TOK, 128), BF16),
            pltpu.VMEM((n, TOK, 128), F32),
            pltpu.VMEM((n, 80, TOK), F32),
        ],
    )(sc, q, *kvs)
    o_all, mixed, st_all = call(
        combine_kernel, [((192, TOK), F32), ((192, TOK), BF16), ((16, TOK), F32)]
    )(sc, o_near, st_near, *returned)

    pieces, packed, hidden, mid_low, pre, inner_grad, feed_grad, sums = call(
        middle_kernel,
        [
            ((4, 192, TOK), BF16),
            ((4, 208, 768), BF16),
            ((TOK, 768), F32),
            ((TOK, 768), BF16),
            ((TOK, 768), F32),
            ((TOK, 768), F32),
            ((TOK, 768), BF16),
            ((8, TOK), F32),
        ],
        limit=12,
    )(
        sc, inputs, mixed, *others_over_tensor(mixed), packed, *packed_others, up_weight, down_weight,
        mid_gain, mid_shift, inner_gain, cotangent,
    )
    sums = sums + lax.ppermute(sums, "c", FLIP)
    sums = sums + lax.ppermute(sums, "yl", FLIP)
    inner_low, pre_grad, keep, send, inner_vectors = call(
        inner_kernel,
        [((TOK, 768), BF16), ((TOK, 768), BF16), half, half, ((8, 768), F32)],
    )(sc, sums, pre, inner_grad, up_weight, inner_gain, inner_shift)
    mid_half = add(keep, lax.ppermute(send, "c", FLIP))

    full_d, full_u, feed_keep, feed_send = call(
        products_kernel, [((PARTS, ROW, 768), BF16)] * 2 + [half, half], limit=12
    )(sc, inner_low, feed_grad, mid_low, pre_grad, down_weight, after=(mid_half,))
    mid_half = add(mid_half, lax.ppermute(mid_half, "yl", FLIP), after=(full_d,))
    mid_other = lax.ppermute(mid_half, "c", FLIP)
    hidden_grad, grad_mixed, st_near, pay_a, pay_b, pay_c, out_grad, mid_vectors = call(
        outer_kernel,
        [((TOK, 768), F32), ((192, TOK), BF16), ((8, TOK), F32)]
        + [((208, SLOTS), BF16)] * 3
        + [((PARTS, 8, 768), BF16), ((8, 768), F32)],
        [pltpu.VMEM((4, 192, TOK), F32)],
        limit=12,
    )(sc, mid_half, mid_other, hidden, cotangent, mid_gain, mid_shift, pieces, packed, o_all, st_all)
    grads = visit(pay_a, pay_b, pay_c)

    out = call(first_kernel, [((16, 32, 384), BF16)] * 8, [pltpu.VMEM((PARTS, 8, 768), BF16)])(
        sides, full_d, full_u, out_grad, mid_vectors, inner_vectors
    )
    keeps, sends = out[0:4], out[4:8]
    gots = [travel(v, name) for v, name in zip(sends, FIRST)]
    feed_half = add(feed_keep, lax.ppermute(feed_send, "c", FLIP), after=(pay_a,))
    feed_got = lax.ppermute(feed_half, "yl", FLIP)

    dq_near, dkv = call(
        backward_near_kernel,
        [((192, TOK), F32), ((PLANE, 384, TOK), BF16)],
        [
            pltpu.VMEM((n, 64, TOK), BF16),
            pltpu.VMEM((n, 64, TOK), BF16),
            pltpu.VMEM((n, TOK, 128), BF16),
            pltpu.VMEM((n, TOK, 80), BF16),
            pltpu.VMEM((n, HDIM, TOK), F32),
        ],
    )(sc, q, grad_mixed, st_near, right, *kvs, after=(feed_half, keeps[0]))
    out = call(second_kernel, [((8, 32, 384), BF16)] * 8)(sides, *keeps, *gots, after=(dq_near,))
    keeps, sends = out[0:4], out[4:8]
    gots = [travel(v, name) for v, name in zip(sends, SECOND)]
    feed_half = add(feed_half, feed_got, after=(dq_near,))
    feed_other = lax.ppermute(feed_half, "c", FLIP)

    dq_a, dq_b, dq_c, dkv = call(
        backward_far_kernel,
        [((192, SLOTS), BF16)] * 3 + [((PLANE, 384, TOK), BF16)],
        [pltpu.VMEM((n, 128, KEYS), BF16), pltpu.VMEM((n, 128, KEYS), BF16)],
        limit=16,
    )(sc, dkv, *visitors, *grads, loc, *far_keys, after=(keeps[0], feed_half))
    dkv = lax.all_to_all(dkv, ("yh", "x"), 0, 0, tiled=True)
    dqs = visit(dq_a, dq_b, dq_c, back)

    out = call(third_kernel, [((4, 32, 768), BF16)] * 4)(sides, *keeps, *gots, after=(dq_a,))
    keeps, sends = out[0:2], out[2:4]
    gots = [travel(v, name) for v, name in zip(sends, THIRD)]
    out = call(fourth_kernel, [((2, 32, 768), BF16)] * 4)(sides, *keeps, *gots)
    keeps, sends = out[0:2], out[2:4]
    gots = [travel(v, name) for v, name in zip(sends, FOURTH)]
    keep, fifth_send = call(fifth_kernel, [((2, 32, 768), BF16)] * 2)(sides, *keeps, *gots)
    have = add(keep, travel(fifth_send, "y"))
    have = call(join_y_kernel, [((2, 32, 768), BF16)] * 2)(sides, have, travel(have, "y"))
    have = call(functools.partial(join_pairs_kernel, FOURTH), [((4, 32, 768), BF16)] * 2)(
        sides, *have, *[travel(v, name) for v, name in zip(have, FOURTH)]
    )
    up_again = have[0]
    have = call(join_streams_kernel, [((8, 32, 384), BF16)] * 4)(
        sides, *have, *[travel(v, name) for v, name in zip(have, THIRD)]
    )
    have = call(functools.partial(join_pairs_kernel, SECOND), [((16, 32, 384), BF16)] * 4)(
        sides, *have, *[travel(v, name) for v, name in zip(have, SECOND)]
    )
    down_grad, up_grad, out_grad, vectors = call(
        join_all_kernel,
        [((PARTS, ROW, 768), F32)] * 2 + [((24, 8, 768), F32), ((8, 768), F32)],
        [pltpu.VMEM((PARTS, 8, 768), F32)] * 2,
        limit=12,
    )(
        sides, *have, *[travel(v, name) for v, name in zip(have, FIRST)]
    )

    sums, keep, send = call(
        weights_kernel,
        [((PARTS, ROW, 640), BF16), half, half],
        [pltpu.VMEM((576, TOK), BF16)],
        limit=12,
    )(sc, normed, weights, dq_near, *dqs, dkv, after=(fifth_send,))
    got = lax.all_to_all(sums, SEQ, 0, 0, tiled=True)
    in_half = add(keep, lax.ppermute(send, "c", FLIP))
    in_half = add(in_half, lax.ppermute(in_half, "yl", FLIP))
    in_other = lax.ppermute(in_half, "c", FLIP)
    inputs_grad, spread = call(reduce_kernel, [((TOK, 768), BF16), ((PARTS, ROW, 640), BF16)])(
        sc, inputs, hidden_grad, in_gain, in_shift, in_half, in_other, got, after=(up_again,)
    )
    last = lax.all_to_all(spread, SEQ, 0, 0, tiled=True)

    feed_out = jnp.where(
        core == 0, jnp.concatenate([feed_half, feed_other]), jnp.concatenate([feed_other, feed_half])
    ).astype(F32)
    result = jnp.where(row_valid, hidden + feed_out, 0.0).astype(BF16)
    head_grad, in_sums = call(final_kernel, [((576, 768), F32), ((ROW, 64), F32)], scalars=0)(last)
    return (
        result,
        inputs_grad,
        head_grad.reshape(3, 192, 768).transpose(0, 2, 1),
        out_grad.reshape(192, 768),
        up_grad.reshape(768, 768),
        down_grad.reshape(768, 768),
        in_sums[0:12].reshape(-1),
        in_sums[12:24].reshape(-1),
        vectors[2, 0:192],
        vectors[3, 0:192],
        vectors[0],
        vectors[1],
        vectors[4],
        vectors[5],
    )


def solution(mesh):
    fine = Mesh(np.asarray(mesh.devices).reshape(4, 2, 4, 2, 2), SEQ + TENSOR)
    in_specs = (
        P(SEQ, None),
        P(None, None, TENSOR),
        P(TENSOR, None),
        P(None, TENSOR),
        P(TENSOR, None),
        P(),
        P(),
        P(TENSOR),
        P(TENSOR),
        P(),
        P(),
        P(TENSOR),
        P(TENSOR),
        P(),
        P(SEQ, None),
    )
    out_specs = (
        P(SEQ, None),
        P(SEQ, None),
        P(None, None, TENSOR),
        P(TENSOR, None),
        P(None, TENSOR),
        P(TENSOR, None),
        P(),
        P(),
        P(TENSOR),
        P(TENSOR),
        P(),
        P(),
        P(TENSOR),
        P(TENSOR),
    )
    return jax.shard_map(per_device, mesh=fine, in_specs=in_specs, out_specs=out_specs, check_vma=False)
```

```python
import functools
import itertools

import jax
import jax.numpy as jnp
import numpy as np
from jax import lax
from jax.experimental import pallas as pl
from jax.experimental.pallas import tpu as pltpu
from jax.sharding import Mesh
from jax.sharding import PartitionSpec as P


HDIM = 64
HEADS_HERE = 3
TOK = 256
PLANE = 8
SLOTS = 128
KEYS = PLANE * SLOTS
PARTS = 32
ROW = 24
EPSILON = 1e-05
NONE = -1e30
NEAR = (1, 2, 4, 6, 12)
MID = (2, 4, 6, 12)
FAR = (4, 6, 12)
F32 = jnp.float32
BF16 = jnp.bfloat16
SEQ = ("z", "yh", "x")
TENSOR = ("yl", "c")
FLIP = [(0, 1), (1, 0)]
NN = ((1,), (0,))
NT = ((1,), (1,))
TN = ((0,), (0,))


class Here:
    def __init__(self):
        self.plane, y, self.x = (lax.axis_index(a) for a in SEQ)
        low, self.core = (lax.axis_index(a) for a in TENSOR)
        self.y = y
        self.place = y * 4 + self.x
        self.tensor = low * 2 + self.core
        self.head0 = self.tensor * HEADS_HERE
        self.base = (self.plane * PLANE + self.place) * TOK


def dot(a, b, dims=NN):
    return lax.dot_general(a, b, (dims, ((), ())), preferred_element_type=F32)


def split3(v):
    hi = v.astype(BF16).astype(F32)
    mid = (v - hi).astype(BF16).astype(F32)
    return hi, mid, v - hi - mid


def mid_offsets(head):
    slot = lax.broadcasted_iota(jnp.int32, (1, SLOTS), 1)
    return 2 * slot + lax.rem(head, 2)


def far_offsets(head, base):
    slot = lax.broadcasted_iota(jnp.int32, (1, SLOTS), 1)
    which = lax.rem(slot, 4)
    kind = jnp.where(which == 0, 0, 2 * which + 2)
    first = lax.div(base + 12 - head, 12) - 1
    return 12 * (first + lax.div(slot, 4)) + kind + head - base, kind


def one_hot_rows(offsets):
    rows = lax.broadcasted_iota(jnp.int32, (TOK, SLOTS), 0)
    return (rows == offsets).astype(F32).astype(BF16)


def picks(head, base):
    return one_hot_rows(mid_offsets(head)), one_hot_rows(far_offsets(head, base)[0])


def count_table(kind, usable, dilations):
    row = lax.broadcasted_iota(jnp.int32, (16, kind.shape[1]), 0)
    count = jnp.zeros(row.shape, F32)
    for step in dilations:
        count += jnp.where((lax.rem(row, step) == 0) & (lax.rem(kind, step) == 0), 1.0, 0.0)
    live = (count > 0) & usable & (row < 12)
    log_count = jnp.log(jnp.maximum(count, 1.0))
    hi = log_count.astype(BF16).astype(F32)
    return jnp.where(live, hi, NONE), jnp.where(live, log_count - hi, 0.0)


def score_columns(ref, lo, kind, usable, dilations):
    hi, low = count_table(kind, usable, dilations)
    return jnp.concatenate([ref[lo : lo + HDIM, :].astype(F32) * 0.125, hi, low], 0)


def own_columns(head, base, q, lo):
    kind = lax.rem(base - head + 12 + lax.broadcasted_iota(jnp.int32, (1, TOK), 1), 12)
    return score_columns(q, lo, kind, kind >= 0, NEAR)


def query_columns(head, base, plane, visitors, lo):
    if len(visitors) == 1:
        at = mid_offsets(head)
        return score_columns(visitors[0], lo, lax.rem(base + 2048 + at - head + 12, 12), at >= 0, MID)
    parts = []
    for visitor, origin in zip(visitors, (plane + 2, 3 - plane)):
        at, kind = far_offsets(head, origin * 2048 + lax.rem(base, 2048))
        parts.append(score_columns(visitor, lo, kind, (at >= 0) & (at < TOK), FAR))
    return jnp.concatenate(parts, 1)


def one_hot_kind(kind):
    return (kind == lax.broadcasted_iota(jnp.int32, (16, kind.shape[1]), 0)).astype(F32).astype(BF16)


def ones(rows, columns):
    return jnp.ones((rows, columns), BF16)


def diagonal_mask(base, valid):
    rows = lax.broadcasted_iota(jnp.int32, (TOK, TOK), 0)
    cols = lax.broadcasted_iota(jnp.int32, (TOK, TOK), 1)
    return (cols <= rows) & (cols + base < valid)


def norm_rows(v, gain, shift):
    mean = jnp.sum(v, 1, keepdims=True) / v.shape[1]
    spread = jnp.sum(v * v, 1, keepdims=True) / v.shape[1] - mean * mean
    scale = lax.rsqrt(spread + EPSILON)
    unit = (v - mean) * scale
    return unit * gain + shift, unit, scale


def norm_rows_back(grad, unit, scale, gain):
    q = grad * gain
    n = grad.shape[1]
    return scale * (q - jnp.sum(q, 1, keepdims=True) / n - unit * (jnp.sum(q * unit, 1, keepdims=True) / n))


def project_kernel(inputs, weights, gain, shift, q, spread):
    v = norm_rows(inputs[...].astype(F32), gain[...], shift[...])[0].astype(BF16)
    spread[0, 0:192, :] = dot(weights[1], v, NT).astype(BF16)
    spread[0, 192:384, :] = dot(weights[2], v, NT).astype(BF16)
    for i in range(1, PLANE):
        spread[i] = spread[0]
    q[...] = dot(weights[0], v, NT).astype(BF16)


def select_kernel(q, out_weight, mix_gain, mix_shift, q_mid, q_far, packed):
    here = Here()
    head0, base = here.head0, here.base
    for h in range(HEADS_HERE):
        rows = slice(h * HDIM, (h + 1) * HDIM)
        pick_mid, pick_far = picks(head0 + h, base)
        q_mid[rows, :] = dot(q[rows, :], pick_mid).astype(BF16)
        q_far[rows, :] = dot(q[rows, :], pick_far).astype(BF16)
    packed[0:192, :] = out_weight[...]
    terms = list(split3(mix_gain[...])) + list(split3(mix_shift[...])) + [jnp.zeros((10, 192), F32)]
    packed[192:208, 0:192] = jnp.concatenate(terms, 0).astype(BF16)


def weigh(s):
    return jnp.exp(s).astype(BF16)


def widest(s):
    return functools.reduce(jnp.maximum, [s[:, i * 128 : (i + 1) * 128] for i in range(s.shape[1] // 128)])


def shifted(m, rows):
    top = jnp.max(m.T, 0, keepdims=True)
    minus = jnp.concatenate(list(split3(-top)) + [jnp.zeros((29, top.shape[1]), F32)], 0)
    return top, jnp.concatenate([rows, minus], 0).T.astype(BF16)


def near_keys(kvs, block, lo, head, base):
    kind = lax.rem(base - head + 12 + lax.broadcasted_iota(jnp.int32, (1, TOK), 1), 12)
    hot = one_hot_kind(kind)
    return jnp.concatenate([kvs[block, lo : lo + HDIM, :], hot, hot, ones(32, TOK)], 0)


def near_values(kvs, block, lo):
    return jnp.concatenate([kvs[block, 192 + lo : 192 + lo + HDIM, :], ones(16, TOK)], 0)


def gather_keys(kvs, head0, plane, far, rights, values):
    for h in range(HEADS_HERE):
        lo, head = h * HDIM, head0 + h
        for k in range(PLANE):
            start = plane * 2048 + k * TOK
            if far:
                offsets, kind = far_offsets(head, start)
                kind = jnp.where((offsets >= 0) & (offsets < TOK), kind, 12)
            else:
                offsets = mid_offsets(head)
                kind = lax.rem(start + offsets - head + 12, 12)
            both = jnp.concatenate([kvs[k, lo : lo + HDIM, :], kvs[k, 192 + lo : 192 + lo + HDIM, :]], 0)
            at = slice(k * SLOTS, (k + 1) * SLOTS)
            small = dot(both, one_hot_rows(offsets)).astype(BF16)
            hot = one_hot_kind(kind)
            rights[h, :, at] = jnp.concatenate([small[0:HDIM], hot, hot, ones(32, SLOTS)], 0)
            values[h, :, at] = jnp.concatenate([small[HDIM:], ones(16, SLOTS)], 0)


def forward_far_kernel(qa, qb, qc, kvs, pay_a, pay_b, pay_c, loc, right_a, right_f, value_a, value_f):
    here = Here()
    head0, base, plane = here.head0, here.base, here.plane
    heads = range(HEADS_HERE)
    row = lax.broadcasted_iota(jnp.int32, (16, SLOTS), 0)
    loc[...] = jnp.zeros(loc.shape, F32)
    wait_for(qa, qb, qc)

    def attend(queries, rights, values, first, pays):
        extra = [jnp.where(row == 9, 1.0, 0.0) for _ in pays]
        rows = [query_columns(head0 + h, base, plane, queries, h * HDIM) for h in heads]
        zeros = jnp.zeros((32, SLOTS * len(pays)), F32)
        marks = [widest(dot(jnp.concatenate([rows[h], zeros], 0).T.astype(BF16), rights[h])) for h in heads]
        lefts = [shifted(marks[h], rows[h]) for h in heads]
        accs = [dot(values[h], weigh(dot(lefts[h][1], rights[h])), NT) for h in heads]
        for h in heads:
            total = accs[h][64:65, :]
            log = jnp.maximum(lefts[h][0] + jnp.log(total), NONE)
            out = accs[h][0:64, :] / total
            for i, pay in enumerate(pays):
                at = slice(i * SLOTS, (i + 1) * SLOTS)
                loc[h : h + 1, first + i * SLOTS : first + (i + 1) * SLOTS] = log[:, at]
                pay[h * HDIM : (h + 1) * HDIM, :] = out[:, at].astype(BF16)
                for j, term in enumerate(split3(log[:, at])):
                    extra[i] = jnp.where(row == 3 * h + j, term, extra[i])
        for e, pay in zip(extra, pays):
            pay[192:208, :] = e.astype(BF16)

    @pl.when(lax.rem(plane, 2) == 0)
    def _():
        gather_keys(kvs, head0, plane, False, right_a, value_a)
        attend((qa,), right_a, value_a, 0, (pay_a,))

    @pl.when(plane < 2)
    def _():
        gather_keys(kvs, head0, plane, True, right_f, value_f)
        attend((qb, qc), right_f, value_f, SLOTS, (pay_b, pay_c))


def forward_near_kernel(length, q, kvs, o_near, st_near, right, rows, left, marks, acc):
    here, valid = Here(), length[0]
    head0, base, place = here.head0, here.base, here.place
    heads = range(HEADS_HERE)
    for h in heads:
        lo = h * HDIM
        head = head0 + h
        rows[h] = own_columns(head, base, q, lo)
        left[h] = jnp.concatenate([rows[h], jnp.zeros((32, TOK), F32)], 0).T.astype(BF16)
    marks[...] = jnp.full(marks.shape, 2 * NONE, F32)
    wait_for(kvs)
    for k in range(PLANE):

        @pl.when(k <= place)
        def _():
            for h in heads:
                right[h, k] = near_keys(kvs, place - k, h * HDIM, head0 + h, base - k * TOK)
                s = dot(left[h], right[h, k])
                if k == 0:
                    s = jnp.where(diagonal_mask(base, valid), s, NONE)
                marks[h] = jnp.maximum(marks[h], widest(s))

    tops = []
    for h in heads:
        top, turned = shifted(marks[h], rows[h])
        tops.append(top)
        left[h] = turned
    acc[...] = jnp.zeros(acc.shape, F32)
    for k in range(PLANE):

        @pl.when(k <= place)
        def _():
            for h in heads:
                lo = h * HDIM
                s = dot(left[h], right[h, k])
                if k == 0:
                    s = jnp.where(diagonal_mask(base, valid), s, NONE)
                acc[h] += dot(near_values(kvs, place - k, lo), weigh(s), NT)

    st_near[...] = jnp.zeros(st_near.shape, F32)
    for h in heads:
        total = acc[h, 64:65, :]
        o_near[h * HDIM : (h + 1) * HDIM, :] = acc[h, 0:64, :] / total
        st_near[h : h + 1, :] = tops[h] + jnp.log(total)


def combine_kernel(o_near, st_near, ra, rb, rc, mixed, st_all):
    here = Here()
    head0, base = here.head0, here.base
    st_all[...] = jnp.zeros(st_all.shape, F32)
    for h in range(HEADS_HERE):
        rows = slice(h * HDIM, (h + 1) * HDIM)
        pick_mid, pick_far = picks(head0 + h, base)
        outs, logs = [o_near[rows, :]], [st_near[h : h + 1, :]]
        for pay, pick in ((ra, pick_mid), (rb, pick_far), (rc, pick_far)):
            wide = dot(jnp.concatenate([pay[rows, :], pay[192:208, :]], 0), pick, NT)
            log = wide[64 + 3 * h : 65 + 3 * h] + wide[65 + 3 * h : 66 + 3 * h] + wide[66 + 3 * h : 67 + 3 * h]
            outs.append(wide[0:64])
            logs.append(jnp.where(wide[73:74] > 0.5, log, NONE))
        top = functools.reduce(jnp.maximum, logs)
        weights = [jnp.exp(v - top) for v in logs]
        total = sum(weights)
        mixed[rows, :] = sum((w / total) * o for w, o in zip(weights, outs)).astype(BF16)
        st_all[h : h + 1, :] = top + jnp.log(total)
        for i in range(3):
            st_all[3 + 3 * i + h : 4 + 3 * i + h, :] = weights[i + 1] / total


def mix_norm(pieces):
    first = sum(jnp.sum(pieces[i].astype(F32), 0, keepdims=True) for i in range(4)) / 768
    second = sum(jnp.sum(jnp.square(pieces[i].astype(F32)), 0, keepdims=True) for i in range(4)) / 768
    return first, lax.rsqrt(second - first * first + EPSILON)


def mix_parameters(packed, i):
    tail = jnp.concatenate([packed[i, 192:208, 0:256].astype(F32), jnp.zeros((112, 256), F32)], 0).T[0:192]
    return tail[:, 0:1] + tail[:, 1:2] + tail[:, 2:3], tail[:, 3:4] + tail[:, 4:5] + tail[:, 5:6]


def gelu_parts(v):
    a, b = 0.7978845608028654, 0.044715
    square = v * v
    t = jnp.tanh(a * v * (1.0 + b * square))
    active = 0.5 * v * (1.0 + t)
    slope = 0.5 * (1.0 + t) + 0.5 * v * (1.0 - t * t) * (a * (1.0 + 3.0 * b * square))
    return active, slope


def half_blocks(core, v):
    half = jnp.where(core == 0, v[0:128], v[128:256])
    return jnp.concatenate([half[:, i * 256 : (i + 1) * 256] for i in range(3)], 0).astype(BF16)


def feed_kernel(length, down, cotangent, feed_blocks, inner_grad):
    here = Here()
    row = here.base + lax.broadcasted_iota(jnp.int32, (TOK, 1), 0)
    feed = jnp.where(row < length[0], cotangent[...].astype(F32), 0.0)
    feed_blocks[...] = half_blocks(here.core, feed)
    grad = dot(feed.astype(BF16), down[...], NT)
    inner_grad[...] = grad


def middle_kernel(
    inputs, pieces, packed, up, gain, shift, inner_gain, inner_grad, st_all,
    hidden, pieces_kept, st_kept, mid_blocks, pre, sums,
):
    st_kept[...] = st_all[...]
    st_kept.flush()
    pieces.wait()
    pieces_kept[...] = pieces[...]
    pieces_kept.flush()
    mean, scale = mix_norm(pieces)
    total = inputs[...].astype(F32)
    branch = None
    for i in range(4):
        mix_gain, mix_shift = mix_parameters(packed, i)
        low = ((pieces[i].astype(F32) - mean) * scale * mix_gain + mix_shift).astype(BF16)
        term = dot(low, packed[i, 0:192, :], TN)
        branch = term if branch is None else branch + term
    total = total + branch
    hidden[...] = total
    hidden.flush()
    low = norm_rows(total, gain[...], shift[...])[0]
    mid_blocks[...] = half_blocks(Here().core, low)
    pre[...] = dot(low.astype(BF16), up[...])
    active = gelu_parts(pre[...])[0]
    lane = lax.broadcasted_iota(jnp.int32, (1, 128), 1)
    st = jnp.zeros((TOK, 128), F32)
    scaled = inner_grad[...] * inner_gain[...]
    for i, v in enumerate((active, active * active, scaled, scaled * active)):
        st = jnp.where(lane == i, jnp.sum(v, 1, keepdims=True), st)
    sums[...] = st.T[0:8]


def halves(core, v, keep, send):
    for c in range(2):

        @pl.when(core == c)
        def _():
            keep[...] = v[c * 128 : (c + 1) * 128].astype(BF16)
            send[...] = v[(1 - c) * 128 : (2 - c) * 128].astype(BF16)


def whole(core, own, other):
    own, other = own[...].astype(F32), other[...].astype(F32)
    return jnp.concatenate([jnp.where(core == 0, own, other), jnp.where(core == 0, other, own)], 0)


def inner_kernel(sums, pre, inner_grad, up, gain, shift, inner_low, pre_grad, keep, send, vectors):
    st = jnp.concatenate([sums[...], jnp.zeros((120, TOK), F32)], 0).T
    width = 3072
    mean = st[:, 0:1] / width
    scale = lax.rsqrt(st[:, 1:2] / width - mean * mean + EPSILON)
    first = st[:, 2:3]
    second = scale * (st[:, 3:4] - mean * first)
    active, slope = gelu_parts(pre[...])
    unit = (active - mean) * scale
    inner_low[...] = (unit * gain[...] + shift[...]).astype(BF16)
    grad = inner_grad[...]
    vectors[...] = jnp.zeros(vectors.shape, F32)
    vectors[0:1, :] = jnp.sum(grad * unit, 0, keepdims=True)
    vectors[1:2, :] = jnp.sum(grad, 0, keepdims=True)
    back = scale * (grad * gain[...] - first / width - unit * (second / width))
    low = (back * slope).astype(BF16)
    pre_grad[...] = low
    halves(Here().core, dot(low, up[...], NT), keep, send)


def outer_kernel(
    length, mid_own, mid_other, hidden, cotangent, gain, shift, pieces, packed, st_all,
    inner_vectors, hidden_grad, grad_mixed, st_near, pay_a, pay_b, pay_c, out_grad, all_vectors, scratch,
):
    here, valid = Here(), length[0]
    head0, base, tensor = here.head0, here.base, here.tensor
    row = base + lax.broadcasted_iota(jnp.int32, (TOK, 1), 0)
    upstream = jnp.where(row < valid, cotangent[...].astype(F32), 0.0)
    _, unit, scale = norm_rows(hidden[...], gain[...], shift[...])
    grad = whole(here.core, mid_own, mid_other)
    vectors = [jnp.sum(grad * unit, 0, keepdims=True), jnp.sum(grad, 0, keepdims=True)]
    total = upstream + norm_rows_back(grad, unit, scale, gain[...])
    hidden_grad[...] = total
    hidden_grad.flush()
    branch = total.astype(BF16)

    mean, scale = mix_norm(pieces)
    first, second = jnp.zeros((1, TOK), F32), jnp.zeros((1, TOK), F32)
    for i in range(4):
        grad = dot(packed[i, 0:192, :], branch, NT)
        scratch[i] = grad
        q = grad * mix_parameters(packed, i)[0]
        first += jnp.sum(q, 0, keepdims=True)
        second += jnp.sum(q * (pieces[i].astype(F32) - mean), 0, keepdims=True)
    second = second * scale
    output = pieces[tensor].astype(F32)
    unit = (output - mean) * scale
    grad = scratch[tensor]
    gain_own, shift_own = mix_parameters(packed, tensor)
    low = (unit * gain_own + shift_own).astype(BF16)
    lane = lax.broadcasted_iota(jnp.int32, (1, 128), 1)
    columns = jnp.where(
        lane == 0, jnp.sum(grad * unit, 1, keepdims=True), jnp.where(lane == 1, jnp.sum(grad, 1, keepdims=True), 0.0)
    )
    vectors += [inner_vectors[0:2], jnp.concatenate([columns.T[0:2], jnp.zeros((2, 576), F32)], 1)]
    all_vectors[...] = jnp.concatenate(vectors + [jnp.zeros((2, 768), F32)], 0)
    out_grad[...] = dot(low, branch).astype(BF16)
    out_grad.flush()
    all_vectors.flush()
    back = scale * (grad * gain_own - first / 768 - unit * (second / 768))
    back = back.astype(BF16).astype(F32)
    grad_mixed[...] = back.astype(BF16)
    st_near[...] = jnp.zeros(st_near.shape, F32)
    tails = [[], [], []]
    for h in range(HEADS_HERE):
        rows = slice(h * HDIM, (h + 1) * HDIM)
        mine = back[rows]
        centre = jnp.sum(mine * output[rows], 0, keepdims=True)
        st_near[h : h + 1, :] = st_all[h : h + 1, :]
        st_near[3 + h : 4 + h, :] = centre
        pick_mid, pick_far = picks(head0 + h, base)
        for i, (pay, pick) in enumerate(((pay_a, pick_mid), (pay_b, pick_far), (pay_c, pick_far))):
            share = st_all[3 + 3 * i + h : 4 + 3 * i + h, :]
            terms = list(split3(centre * share)) + [jnp.zeros((13, TOK), F32)]
            wide = jnp.concatenate([mine * share] + terms, 0).astype(BF16)
            small = dot(wide, pick)
            pay[rows, :] = small[0:64].astype(BF16)
            tails[i].append(small[64:67])
    for pay, tail in zip((pay_a, pay_b, pay_c), tails):
        pay[192:208, :] = jnp.concatenate(tail + [jnp.zeros((7, SLOTS), F32)], 0).astype(BF16)


def gradients(left, grad_left, rows_q, rows_g, rights, values, mask=None):
    s = dot(left, rights)
    if mask is not None:
        s = jnp.where(mask, s, NONE)
    w = jnp.exp(s)
    ds = (w * dot(grad_left, values)).astype(BF16)
    dq = dot(rights[0:64], ds, NT)
    return dq, jnp.concatenate([dot(rows_q, ds), dot(rows_g, w.astype(BF16))], 0)


def with_logs(rows, logs):
    minus = split3(jnp.where(logs > NONE * 0.1, -logs, 0.0))
    return jnp.concatenate([rows] + list(minus) + [jnp.zeros((29, logs.shape[1]), F32)], 0)


def with_centres(rows, centres):
    return jnp.concatenate([rows] + list(split3(-centres)) + [jnp.zeros((13, centres.shape[1]), F32)], 0)


def backward_near_kernel(length, q, grad, st, kvs, dq_near, dkv, rows_q, rows_g, left, grad_left, acc_q):
    here, valid = Here(), length[0]
    head0, base, place = here.head0, here.base, here.place
    heads = range(HEADS_HERE)
    for h in heads:
        lo = h * HDIM
        rows = with_logs(own_columns(head0 + h, base, q, lo), st[h : h + 1, :])
        rows_q[h] = rows[0:64].astype(BF16)
        left[h] = rows.T.astype(BF16)
        rows = with_centres(grad[lo : lo + HDIM, :].astype(F32), st[3 + h : 4 + h, :])
        rows_g[h] = rows[0:64].astype(BF16)
        grad_left[h] = rows.T.astype(BF16)
    acc_q[...] = jnp.zeros(acc_q.shape, F32)
    for k in range(PLANE):
        block = lax.rem(place - k + PLANE, PLANE)

        @pl.when(k > place)
        def _():
            dkv[block] = jnp.zeros((384, TOK), BF16)

        @pl.when(k <= place)
        def _():
            mask = diagonal_mask(base, valid) if k == 0 else None
            for h in heads:
                lo = h * HDIM
                keys = near_keys(kvs, place - k, lo, head0 + h, base - k * TOK)
                values = near_values(kvs, place - k, lo)
                dq, both = gradients(left[h], grad_left[h], rows_q[h], rows_g[h], keys, values, mask)
                acc_q[h] += dq
                dkv[block, lo : lo + HDIM, :] = both[0:64].astype(BF16)
                dkv[block, 192 + lo : 192 + lo + HDIM, :] = both[64:128].astype(BF16)

    for h in heads:
        dq_near[h * HDIM : (h + 1) * HDIM, :] = acc_q[h] * 0.125


def backward_far_kernel(dkv_near, qa, qb, qc, ga, gb, gc, loc, kvs, *refs):
    dq_a, dq_b, dq_c, dkv, small_a, small_f, right_a, right_f, value_a, value_f = refs
    here = Here()
    head0, base, plane = here.head0, here.base, here.plane
    heads = range(HEADS_HERE)
    wait_for(qa, qb, qc, loc)

    def part(queries, pays, first, rights, values, dqs, small):
        n = SLOTS * len(pays)
        for h in heads:
            lo = h * HDIM
            rows = query_columns(head0 + h, base, plane, queries, lo)
            rows = with_logs(rows, loc[h : h + 1, first : first + n])
            columns, centres = [], []
            for pay in pays:
                columns.append(pay[lo : lo + HDIM, :].astype(F32))
                tail = pay[192:208, :].astype(F32)
                centres.append(tail[3 * h : 3 * h + 1] + tail[3 * h + 1 : 3 * h + 2] + tail[3 * h + 2 : 3 * h + 3])
            grads = with_centres(jnp.concatenate(columns, 1), jnp.concatenate(centres, 1))
            dq, both = gradients(
                rows.T.astype(BF16),
                grads.T.astype(BF16),
                rows[0:64].astype(BF16),
                grads[0:64].astype(BF16),
                rights[h],
                values[h],
            )
            dq = (dq * 0.125).astype(BF16)
            for i, out in enumerate(dqs):
                out[lo : lo + HDIM, :] = dq[:, i * SLOTS : (i + 1) * SLOTS]
            small[h] = both.astype(BF16)

    @pl.when((plane == 1) | (plane == 2))
    def _():
        small_a[...] = jnp.zeros(small_a.shape, BF16)
        small_f[...] = jnp.zeros(small_f.shape, BF16)

    @pl.when(lax.rem(plane, 2) == 0)
    def _():
        gather_keys(kvs, head0, plane, False, right_a, value_a)
        part((qa,), (ga,), 0, right_a, value_a, (dq_a,), small_a)

    @pl.when(plane < 2)
    def _():
        gather_keys(kvs, head0, plane, True, right_f, value_f)
        part((qb, qc), (gb, gc), SLOTS, right_f, value_f, (dq_b, dq_c), small_f)

    wait_for(dkv_near)

    @pl.when(plane == 3)
    def _():
        dkv[...] = dkv_near[...]

    @pl.when(plane < 3)
    def _():
        for block in range(PLANE):
            at = slice(block * SLOTS, (block + 1) * SLOTS)
            for h in heads:
                lo = h * HDIM
                pick = jnp.concatenate(picks(head0 + h, plane * 2048 + block * TOK), 1)
                wide = dot(jnp.concatenate([small_a[h, :, at], small_f[h, :, at]], 1), pick, NT)
                for i, at_row in ((0, lo), (64, 192 + lo)):
                    near = dkv_near[block, at_row : at_row + HDIM, :].astype(F32)
                    dkv[block, at_row : at_row + HDIM, :] = (near + wide[i : i + 64]).astype(BF16)


def part_kernel(inputs, gain, shift, weights, dq_near, ra, rb, rc, dkv, grads, keep, send, in_sums):
    here = Here()
    head0, base = here.head0, here.base
    total = dkv[0].astype(F32)
    for k in range(1, PLANE):
        total += dkv[k].astype(F32)
    grads[192:576, :] = total.astype(BF16)
    for h in range(HEADS_HERE):
        rows = slice(h * HDIM, (h + 1) * HDIM)
        pick_mid, pick_far = picks(head0 + h, base)
        dq = dq_near[rows, :] + dot(ra[rows, :], pick_mid, NT) + dot(rb[rows, :], pick_far, NT) + dot(rc[rows, :], pick_far, NT)
        grads[rows, :] = dq.astype(BF16)
    back = dot(grads[0:192, :], weights[0], TN)
    back += dot(grads[192:384, :], weights[1], TN)
    back += dot(grads[384:576, :], weights[2], TN)
    halves(here.core, back, keep, send)
    unit = norm_rows(inputs[...].astype(F32), gain[...], shift[...])[1]
    sums = [jnp.sum(back * unit, 0, keepdims=True), jnp.sum(back, 0, keepdims=True), jnp.zeros((6, 768), F32)]
    in_sums[...] = jnp.concatenate(sums, 0)


def weights_kernel(grads, inputs, gain, shift, out_grad, vectors, sums):
    normed = norm_rows(inputs[...].astype(F32), gain[...], shift[...])[0].astype(BF16)
    full = jnp.concatenate([dot(grads[...], normed), out_grad[...].astype(F32)], 0).T
    sums[:, :, 0:768] = full.reshape(PARTS, ROW, 768).astype(BF16)
    sums[:, :, 768:896] = jnp.zeros((PARTS, ROW, 128), BF16)
    mixed = jnp.concatenate([vectors[4:5, 0:192], vectors[5:6, 0:192], jnp.zeros((1, 384), F32)], 1)
    for i, v in enumerate((vectors[0:1], vectors[1:2], vectors[2:3], vectors[3:4], mixed)):
        rows = [v[:, j * 128 : (j + 1) * 128] for j in range(6)] + [jnp.zeros((2, 128), F32)]
        sums[i, 0:8, 768:896] = jnp.concatenate(rows, 0).astype(BF16)


def reduce_kernel(got, in_sums, down, up, down_out, up_out):
    total = got[0].astype(F32)
    for i in range(1, PARTS):
        total += got[i].astype(F32)
    rows = [[in_sums[j : j + 1, i * 128 : (i + 1) * 128] for i in range(6)] + [jnp.zeros((2, 128), F32)] for j in (0, 1)]
    down_out[:, 0:768] = down[...]
    down_out[:, 768:1152] = total[:, 0:384].astype(BF16)
    up_out[:, 0:768] = up[...]
    up_out[:, 768:1152] = total[:, 384:768].astype(BF16)
    up_out[:, 1152:1280] = jnp.concatenate([total[0:8, 768:896], *rows[0], *rows[1]], 0).astype(BF16)


def input_grad_kernel(inputs, hidden_grad, gain, shift, own, other, inputs_grad):
    _, unit, scale = norm_rows(inputs[...].astype(F32), gain[...], shift[...])
    grad = whole(Here().core, own, other)
    inputs_grad[...] = (hidden_grad[...] + norm_rows_back(grad, unit, scale, gain[...])).astype(BF16)


CHUNK = 48
PAIR_A = [(0, 1), (1, 0), (2, 3), (3, 2)]
PAIR_B = [(0, 3), (3, 0), (1, 2), (2, 1)]
STEPS = {"xa": ("x", PAIR_A), "xb": ("x", PAIR_B), "za": ("z", PAIR_A), "zb": ("z", PAIR_B)}


def travel(v, name):
    axis, perm = STEPS[name]
    return lax.ppermute(v, axis, perm)


def slices_kernel(inner_low, pre_grad, mid_blocks, feed_blocks, down, slices, feed_keep, feed_send):
    for first, ref in ((0, inner_low), (192, pre_grad)):
        turned = ref[...].astype(F32).T.astype(BF16)
        for i in range(4):
            slices[i, first : first + 192, :] = turned[i * 192 : (i + 1) * 192]
    for i in range(4):
        slices[i, 384:768, :] = mid_blocks[...]
        slices[i, 768:1152, :] = feed_blocks[...]
    slices.flush()
    halves(Here().core, dot(inner_low[...], down[...]), feed_keep, feed_send)


def products_kernel(slices, others, keep, send, full, *operands):
    here = Here()
    products = []
    for (first, second), rows, columns in zip(((0, 768), (192, 384)), operands[0:2], operands[2:4]):
        for i in range(4):
            columns[:, i * TOK : (i + 1) * TOK] = slices[i, first : first + 192, :]
            for b in range(3):
                block = slice(b * 256, (b + 1) * 256)
                own = pl.multiple_of(i * TOK + here.core * 128, 128)
                other = pl.multiple_of(i * TOK + 128 - here.core * 128, 128)
                rows[pl.ds(own, 128), block] = slices[i, second + b * 128 : second + (b + 1) * 128, :]
                rows[pl.ds(other, 128), block] = others[i, second - 384 + b * 128 : second - 256 + b * 128, :]
        products.append(dot(columns[...], rows[...]))
    down, up = products
    full[:, :, 0:24, :] = down.reshape(4, 2, 24, 768).astype(BF16)
    full[:, :, 24:48, :] = up.reshape(4, 2, 24, 768).astype(BF16)
    high = lax.div(here.plane, 2)
    keep[...] = full[pl.ds(2 * high, 2)]
    send[...] = full[pl.ds(2 - 2 * high, 2)]


def halve_kernel(axis, keep, got, new_keep, new_send):
    i = lax.rem(Here().plane, 2) if axis == "z" else Here().y
    new_keep[...] = (keep[i].astype(F32) + got[i].astype(F32)).astype(BF16)
    new_send[...] = (keep[1 - i].astype(F32) + got[1 - i].astype(F32)).astype(BF16)


def chunk_sum_kernel(keep, got, down, up):
    total = keep[...].astype(F32) + got[...].astype(F32)
    down[...] = total[0:24].astype(BF16)
    up[...] = total[24:48].astype(BF16)


def join_y_kernel(down, up, other_down, other_up, down_out, up_out):
    y = Here().y
    for own, other, out in ((down, other_down, down_out), (up, other_up, up_out)):
        out[y] = own[...]
        out[1 - y] = other[...]


def join_pair(i, name, own, other, out):
    high = lax.div(i, 2)
    if name == "b1":
        out[high] = own[...]
        out[1 - high] = other[...]
    elif name == "a1":
        low = lax.rem(i, 2)
        out[low] = own[...]
        out[1 - low] = other[...]
    elif name == "a2":
        first = jnp.where(high == 0, i, 3 - i)
        out[first] = own[0]
        out[3 - first] = own[1]
        out[1 - first] = other[0]
        out[2 + first] = other[1]
    else:
        out[pl.ds(2 * high, 2)] = own[...]
        out[pl.ds(2 - 2 * high, 2)] = other[...]


def join_kernel(steps, *refs):
    here, n = Here(), len(steps)
    for i, step in enumerate(steps):
        join_pair(here.x if step[0] == "x" else here.plane, step[1:], refs[i], refs[n + i], refs[2 * n + i])


def split_kernel(down, up, *outs):
    for j in range(4):
        full = (down, up)[j // 2]
        half = (full.shape[3] - 768) // 2
        outs[j][:, :, :, 0:384] = full[:, :, :, (j % 2) * 384 : (j % 2 + 1) * 384]
        outs[j][:, :, :, 384 : 384 + half] = full[:, :, :, 768 + (j % 2) * half : 768 + (j % 2 + 1) * half]


def unpack_kernel(*refs):
    streams, (down, up, head_grad, out_grad, vectors, up_turned, tail) = refs[0:4], refs[4:]
    for j in range(2):
        columns = slice(j * 384, (j + 1) * 384)
        for x, z, y in itertools.product(range(4), range(4), range(2)):
            i, k = x * 8 + z * 2 + y, z * 8 + y * 4 + x
            d, u = streams[j][x, z, y].astype(F32), streams[2 + j][z, x, y].astype(F32)
            down[i, :, columns] = d[:, 0:384]
            up_turned[i, :, columns] = u[:, 0:384]
            tail[k, :, j * 192 : (j + 1) * 192] = d[:, 384:576]
            tail[k, :, 384 + j * 256 : 640 + j * 256] = u[:, 384:640]
    up[...] = up_turned[...].reshape(768, 768).T
    full = tail[:, :, 0:768].reshape(768, 768).T
    head_grad[...] = full[0:576]
    out_grad[...] = full[576:768]
    rows = [tail[i, 0:6, 768:896] for i in range(5)]
    rows += [jnp.sum(tail[:, i : i + 6, 768:896], 0) for i in (8, 16)]
    rows = [jnp.concatenate([v[i : i + 1] for i in range(6)], 1) for v in rows]
    vectors[...] = jnp.concatenate([*rows, jnp.zeros((1, 768), F32)], 0)


def add_kernel(a, b, out):
    out[...] = (a[...].astype(F32) + b[...].astype(F32)).astype(out.dtype)


TIMES = {
    "project_kernel": 1.2,
    "forward_far_kernel": 4.3,
    "forward_near_kernel": 7.0,
    "combine_kernel": 1.0,
    "feed_kernel": 1.5,
    "middle_kernel": 3.4,
    "inner_kernel": 2.0,
    "outer_kernel": 2.3,
    "products_kernel": 3.0,
    "backward_near_kernel": 8.0,
    "backward_far_kernel": 5.8,
    "part_kernel": 2.0,
    "weights_kernel": 2.0,
    "reduce_kernel": 2.0,
    "unpack_kernel": 0.1,
    "join_kernel": 0.1,
}


class Fetched:
    def __init__(self, copies, ref):
        self.copies, self.ref, self.shape = copies, ref, ref.shape

    def wait(self):
        for copy in self.copies:
            copy.wait()
        self.copies = ()

    def __getitem__(self, index):
        self.wait()
        return self.ref[index]


class Stored:
    def __init__(self, copy, ref):
        self.copy, self.ref, self.shape, self.started = copy, ref, ref.shape, False

    def flush(self):
        if not self.started:
            self.copy.start()
        self.started = True

    def __getitem__(self, index):
        return self.ref[index]

    def __setitem__(self, index, value):
        self.ref[index] = value


def wait_for(*operands):
    for operand in operands:
        if isinstance(operand, Fetched):
            operand.wait()


def call(kernel, out_shapes, scratch=(), scalars=0, limit=8, fetch=(), stacks=(), store=()):
    def run(*args, after=(), behind=()):
        after = (*after, *[pltpu.with_memory_space_constraint(v, pltpu.HBM) for v in behind])
        n, extra, outs = len(args), len(after), len(out_shapes)
        name = getattr(kernel, "func", kernel).__name__
        vmem, hbm = pl.BlockSpec(memory_space=pltpu.VMEM), pl.BlockSpec(memory_space=pltpu.HBM)
        specs = [vmem] * n + [pl.BlockSpec(memory_space=pl.ANY)] * (extra - len(behind)) + [hbm] * len(behind)
        out_specs = [hbm if i in store else vmem for i in range(outs)]
        for i in range(scalars):
            specs[i] = pl.BlockSpec(memory_space=pltpu.SMEM)
        buffers, sizes = [], {}
        for i in sorted((*fetch, *stacks)):
            sizes[i] = 4 if i in stacks else 1
            for j in range(sizes[i]):
                specs[i + j] = hbm
            shape = args[i].shape
            shape = (4, *shape) if i in stacks else (1, *shape) if len(shape) == 1 else shape
            buffers.append(pltpu.VMEM(shape, args[i].dtype))
        for i in store:
            buffers.append(pltpu.VMEM(*out_shapes[i]))
        total = sum(sizes.values()) + len(store)
        if total:
            buffers.append(pltpu.SemaphoreType.DMA((total,)))

        def body(*refs):
            results = list(refs[n + extra : n + extra + outs])
            own = refs[n + extra + outs : n + extra + outs + len(scratch)]
            landing = refs[n + extra + outs + len(scratch) :]
            operands, pending, i, slot = [], [], 0, 0
            while i < n:
                if i not in sizes:
                    operands.append(refs[i])
                    i += 1
                    continue
                ref, copies = landing[len(pending)], []
                for j in range(sizes[i]):
                    place = ref
                    if i in stacks:
                        place = ref.at[jnp.bitwise_xor(Here().tensor, j)]
                    elif len(args[i].shape) == 1:
                        place = ref.at[0]
                    copies.append(pltpu.make_async_copy(refs[i + j], place, landing[-1].at[slot]))
                    copies[-1].start()
                    slot += 1
                pending.append(Fetched(copies, ref))
                operands.append(pending[-1])
                i += sizes[i]
            for k, i in enumerate(store):
                ref = landing[len(pending) + k]
                copy = pltpu.make_async_copy(ref, results[i], landing[-1].at[slot])
                results[i] = Stored(copy, ref)
                slot += 1
            kernel(*operands, *results, *own)
            for operand in pending:
                operand.wait()
            for i in store:
                results[i].flush()
            for i in store:
                results[i].copy.wait()

        args = list(args)
        for i, size in sizes.items():
            for j in range(i, i + size):
                args[j] = pltpu.with_memory_space_constraint(args[j], pltpu.HBM)
        return pl.pallas_call(
            body,
            out_shape=[(pltpu.HBM if i in store else jax.ShapeDtypeStruct)(*shape) for i, shape in enumerate(out_shapes)],
            in_specs=specs,
            out_specs=out_specs,
            scratch_shapes=[*scratch, *buffers],
            compiler_params=pltpu.CompilerParams(vmem_limit_bytes=limit * 1024 * 1024),
            name=name,
            cost_estimate=pl.CostEstimate(
                flops=int(TIMES.get(name, 0.6) * 1e9), bytes_accessed=0, transcendentals=0
            ),
        )(*args, *after)

    return run


def add(a, b, after=()):
    (out,) = call(add_kernel, [(a.shape, a.dtype)])(a, b, after=after)
    return out


def others_over_tensor(v):
    across = lax.ppermute(v, "yl", FLIP)
    beside = lax.ppermute(v, "c", FLIP)
    return beside, across, lax.ppermute(across, "c", FLIP)


MID_GO = [(1, 0), (3, 2)]
B_GO = [(2, 0), (3, 1)]
C_GO = [(3, 0), (2, 1)]


def back(perm):
    return [(b, a) for a, b in perm]


def visit(a, b, c, turn=lambda perm: perm):
    return tuple(lax.ppermute(v, "z", turn(perm)) for v, perm in ((a, MID_GO), (b, B_GO), (c, C_GO)))


def per_device(
    inputs,
    head_weights,
    out_weight,
    up_weight,
    down_weight,
    in_gain,
    in_shift,
    mix_gain,
    mix_shift,
    mid_gain,
    mid_shift,
    inner_gain,
    inner_shift,
    valid_length,
    cotangent,
):
    here = Here()
    core = here.core
    row_valid = (here.base + jnp.arange(TOK, dtype=jnp.int32) < valid_length[0])[:, None]
    n = HEADS_HERE
    half = ((128, 768), BF16)

    weights = head_weights.transpose(0, 2, 1)
    q, spread = call(
        project_kernel, [((192, TOK), BF16), ((PLANE, 384, TOK), BF16)], fetch=(0, 1, 2, 3), limit=12
    )(inputs, weights, in_gain, in_shift)
    kvs = lax.all_to_all(spread, ("yh", "x"), 0, 0, tiled=True)
    q_mid, q_far, packed = call(
        select_kernel,
        [((192, SLOTS), BF16), ((192, SLOTS), BF16), ((208, 768), BF16)],
        fetch=(1, 2, 3),
        store=(2,),
    )(q, out_weight, mix_gain, mix_shift)
    visitors = visit(q_mid, q_far, q_far)
    feed_blocks, inner_grad = call(
        feed_kernel,
        [((384, 256), BF16), ((TOK, 768), F32)],
        scalars=1,
        fetch=(1, 2),
        store=(0, 1),
        limit=12,
    )(valid_length, down_weight, cotangent, after=(q_mid,))
    pay_a, pay_b, pay_c, loc = call(
        forward_far_kernel,
        [((208, SLOTS), BF16)] * 3 + [((8, 384), F32)],
        [
            *[pltpu.VMEM((n, 128, KEYS), BF16)] * 2,
            *[pltpu.VMEM((n, 80, KEYS), BF16)] * 2,
        ],
        limit=16,
        fetch=(0, 1, 2),
        store=(3,),
    )(*visitors, kvs, behind=(inner_grad,))
    returned = visit(pay_a, pay_b, pay_c, back)
    packed, _ = lax.optimization_barrier((packed, pay_a))
    packed_beside, packed_across = lax.ppermute(packed, "c", FLIP), lax.ppermute(packed, "yl", FLIP)
    o_near, st_near = call(
        forward_near_kernel,
        [((192, TOK), F32), ((8, TOK), F32)],
        [
            pltpu.VMEM((n, PLANE, 128, TOK), BF16),
            pltpu.VMEM((n, 96, TOK), F32),
            pltpu.VMEM((n, TOK, 128), BF16),
            pltpu.VMEM((n, TOK, 128), F32),
            pltpu.VMEM((n, 80, TOK), F32),
        ],
        scalars=1,
    )(valid_length, q, kvs)
    mixed, st_all = call(
        combine_kernel, [((192, TOK), BF16), ((16, TOK), F32)], fetch=(2, 3, 4)
    )(o_near, st_near, *returned)
    pieces = (mixed, *others_over_tensor(mixed))
    relay, _ = lax.optimization_barrier((packed_across, o_near))
    packed = (packed, packed_beside, packed_across, lax.ppermute(relay, "c", FLIP))
    hidden, pieces, st_all, mid_blocks, pre, sums = call(
        middle_kernel,
        [
            ((TOK, 768), F32),
            ((4, 192, TOK), BF16),
            ((16, TOK), F32),
            ((384, 256), BF16),
            ((TOK, 768), F32),
            ((8, TOK), F32),
        ],
        limit=20,
        fetch=(0, 9, 10, 11, 12, 13),
        stacks=(1, 5),
        store=(0, 1, 2),
    )(inputs, *pieces, *packed, up_weight, mid_gain, mid_shift, inner_gain, inner_grad, st_all)
    sums = sums + lax.ppermute(sums, "c", FLIP)
    sums = sums + lax.ppermute(sums, "yl", FLIP)
    inner_low, pre_grad, keep, send, inner_vectors = call(
        inner_kernel,
        [((TOK, 768), BF16), ((TOK, 768), BF16), half, half, ((8, 768), F32)],
        fetch=(2, 3, 4, 5),
        limit=12,
    )(sums, pre, inner_grad, up_weight, inner_gain, inner_shift)
    mid_half = add(keep, lax.ppermute(send, "c", FLIP))

    slices, feed_keep, feed_send = call(
        slices_kernel, [((4, 1152, TOK), BF16), half, half], fetch=(3, 4), store=(0,), limit=16
    )(inner_low, pre_grad, mid_blocks, feed_blocks, down_weight, after=(mid_half,))
    slices = lax.all_to_all(slices, "x", 0, 0, tiled=True)
    mid_half = add(mid_half, lax.ppermute(mid_half, "yl", FLIP), after=(feed_keep,))
    mid_other = lax.ppermute(mid_half, "c", FLIP)
    hidden_grad, grad_mixed, st_near, pay_a, pay_b, pay_c, out_grad, vectors = call(
        outer_kernel,
        [((TOK, 768), F32), ((192, TOK), BF16), ((8, TOK), F32)]
        + [((208, SLOTS), BF16)] * 3
        + [((192, 768), BF16), ((8, 768), F32)],
        [pltpu.VMEM((4, 192, TOK), F32)],
        limit=20,
        scalars=1,
        fetch=(3, 4, 5, 6, 7, 12),
        stacks=(8,),
        store=(0, 6, 7),
    )(valid_length, mid_half, mid_other, hidden, cotangent, mid_gain, mid_shift, pieces, *packed, st_all, inner_vectors)
    grads = visit(pay_a, pay_b, pay_c)

    dq_near, dkv = call(
        backward_near_kernel,
        [((192, TOK), F32), ((PLANE, 384, TOK), BF16)],
        [
            pltpu.VMEM((n, 64, TOK), BF16),
            pltpu.VMEM((n, 64, TOK), BF16),
            pltpu.VMEM((n, TOK, 128), BF16),
            pltpu.VMEM((n, TOK, 80), BF16),
            pltpu.VMEM((n, HDIM, TOK), F32),
        ],
        scalars=1,
        limit=12,
        store=(0, 1),
    )(valid_length, q, grad_mixed, st_near, kvs)
    dq_a, dq_b, dq_c, dkv = call(
        backward_far_kernel,
        [((192, SLOTS), BF16)] * 3 + [((PLANE, 384, TOK), BF16)],
        [
            pltpu.VMEM((n, 128, KEYS), BF16),
            pltpu.VMEM((n, 128, KEYS), BF16),
            *[pltpu.VMEM((n, 128, KEYS), BF16)] * 2,
            *[pltpu.VMEM((n, 80, KEYS), BF16)] * 2,
        ],
        limit=20,
        fetch=(0, 1, 2, 3, 7),
        store=(3,),
    )(dkv, *visitors, *grads, loc, kvs)
    dkv = lax.all_to_all(dkv, ("yh", "x"), 0, 0, tiled=True)
    dqs = visit(dq_a, dq_b, dq_c, back)

    feed_half = add(feed_keep, lax.ppermute(feed_send, "c", FLIP), after=(dq_a,))
    slices, _ = lax.optimization_barrier((slices, dq_a))
    others = lax.ppermute(slices[:, 384:1152], "c", FLIP)
    keep, send = call(
        products_kernel,
        [((2, 2, CHUNK, 768), BF16)] * 2,
        [
            pltpu.VMEM((4, 2, CHUNK, 768), BF16),
            *[pltpu.VMEM((4 * TOK, 768), BF16)] * 2,
            *[pltpu.VMEM((192, 4 * TOK), BF16)] * 2,
        ],
        limit=16,
    )(slices, others, after=(dq_a, feed_half))
    keep, send = call(functools.partial(halve_kernel, "z"), [((2, CHUNK, 768), BF16)] * 2)(keep, travel(send, "zb"))
    keep, send = call(functools.partial(halve_kernel, "y"), [((CHUNK, 768), BF16)] * 2)(keep, travel(send, "za"))
    sum_keep, sum_send = keep, send
    feed_half = add(feed_half, lax.ppermute(feed_half, "yl", FLIP))
    feed_other = lax.ppermute(feed_half, "c", FLIP)
    gradients_t, keep, send, in_sums = call(
        part_kernel,
        [((576, TOK), BF16), half, half, ((8, 768), F32)],
        limit=12,
        fetch=(0, 1, 2, 3, 4, 5, 6, 7),
    )(inputs, in_gain, in_shift, weights, dq_near, *dqs, dkv, after=(sum_keep, feed_half))
    (sums,) = call(weights_kernel, [((PARTS, ROW, 896), BF16)], limit=16, fetch=(1, 2, 3, 4, 5), store=(0,))(
        gradients_t, inputs, in_gain, in_shift, out_grad, vectors
    )
    got = lax.all_to_all(sums, SEQ, 0, 0, tiled=True)
    in_sums = in_sums + lax.ppermute(in_sums, "c", FLIP)
    in_sums = in_sums + lax.ppermute(in_sums, "yl", FLIP)
    have = call(chunk_sum_kernel, [((24, 768), BF16)] * 2)(
        sum_keep, lax.ppermute(sum_send, "yh", FLIP)
    )
    have = call(reduce_kernel, [((24, 1152), BF16), ((24, 1280), BF16)])(got, in_sums, *have)
    in_half = add(keep, lax.ppermute(send, "c", FLIP))
    have = call(join_y_kernel, [((2, 24, 1152), BF16), ((2, 24, 1280), BF16)])(
        *have, *[lax.ppermute(v, "yh", FLIP) for v in have], after=(in_half,)
    )
    in_half = add(in_half, lax.ppermute(in_half, "yl", FLIP))
    have = call(
        functools.partial(join_kernel, ("zb1", "xb1")), [((2, 2, 24, 1152), BF16), ((2, 2, 24, 1280), BF16)]
    )(*have, *[travel(v, name) for v, name in zip(have, ("zb", "xb"))], after=(in_half,))
    (inputs_grad,) = call(input_grad_kernel, [((TOK, 768), BF16)], fetch=(0, 1, 2, 3), limit=12)(
        inputs, hidden_grad, in_gain, in_shift, in_half, lax.ppermute(in_half, "c", FLIP)
    )
    have = call(
        functools.partial(join_kernel, ("za2", "xa2")), [((4, 2, 24, 1152), BF16), ((4, 2, 24, 1280), BF16)]
    )(*have, *[travel(v, name) for v, name in zip(have, ("za", "xa"))])
    widths = (576, 576, 640, 640)
    have = call(split_kernel, [((4, 2, 24, w), BF16) for w in widths])(*have)
    have = call(
        functools.partial(join_kernel, ("xb1", "xa1", "zb1", "za1")), [((2, 4, 2, 24, w), BF16) for w in widths]
    )(*have, *[travel(v, name) for v, name in zip(have, ("xb", "xa", "zb", "za"))], after=(inputs_grad,))
    have = call(
        functools.partial(join_kernel, ("xa2", "xb2", "za2", "zb2")),
        [((4, 4, 2, 24, w), BF16) for w in widths],
        limit=12,
    )(*have, *[travel(v, name) for v, name in zip(have, ("xa", "xb", "za", "zb"))])
    down_grad, up_grad, head_grad, out_grad, vectors = call(
        unpack_kernel,
        [
            ((PARTS, ROW, 768), F32),
            ((768, 768), F32),
            ((576, 768), F32),
            ((192, 768), F32),
            ((8, 768), F32),
        ],
        [pltpu.VMEM((PARTS, ROW, 768), F32), pltpu.VMEM((PARTS, ROW, 896), F32)],
        limit=24,
    )(*have)
    feed_out = jnp.where(
        core == 0, jnp.concatenate([feed_half, feed_other]), jnp.concatenate([feed_other, feed_half])
    ).astype(F32)
    result = jnp.where(row_valid, hidden + feed_out, 0.0).astype(BF16)
    return (
        result,
        inputs_grad,
        head_grad.reshape(3, 192, 768).transpose(0, 2, 1),
        out_grad,
        up_grad,
        down_grad.reshape(768, 768),
        vectors[5],
        vectors[6],
        vectors[4, 0:192],
        vectors[4, 192:384],
        vectors[0],
        vectors[1],
        vectors[2],
        vectors[3],
    )


def solution(mesh):
    fine = Mesh(np.asarray(mesh.devices).reshape(4, 2, 4, 2, 2), SEQ + TENSOR)
    in_specs = (
        P(SEQ, None),
        P(None, None, TENSOR),
        P(TENSOR, None),
        P(None, TENSOR),
        P(TENSOR, None),
        P(),
        P(),
        P(TENSOR),
        P(TENSOR),
        P(),
        P(),
        P(TENSOR),
        P(TENSOR),
        P(),
        P(SEQ, None),
    )
    out_specs = (
        P(SEQ, None),
        P(SEQ, None),
        P(None, None, TENSOR),
        P(TENSOR, None),
        P(None, TENSOR),
        P(TENSOR, None),
        P(),
        P(),
        P(TENSOR),
        P(TENSOR),
        P(),
        P(),
        P(TENSOR),
        P(TENSOR),
    )
    return jax.shard_map(per_device, mesh=fine, in_specs=in_specs, out_specs=out_specs, check_vma=False)
```

```python
import functools
import itertools

import jax
import jax.numpy as jnp
import numpy as np
from jax import lax
from jax.experimental import pallas as pl
from jax.experimental.pallas import tpu as pltpu
from jax.sharding import Mesh
from jax.sharding import PartitionSpec as P


HDIM = 64
HEADS_HERE = 3
TOK = 256
PLANE = 8
SLOTS = 128
KEYS = PLANE * SLOTS
PARTS = 32
ROW = 24
EPSILON = 1e-05
NONE = -1e30
NEAR = (1, 2, 4, 6, 12)
MID = (2, 4, 6, 12)
FAR = (4, 6, 12)
F32 = jnp.float32
BF16 = jnp.bfloat16
SEQ = ("z", "yh", "x")
TENSOR = ("yl", "c")
FLIP = [(0, 1), (1, 0)]
NN = ((1,), (0,))
NT = ((1,), (1,))
TN = ((0,), (0,))


class Here:
    def __init__(self):
        self.plane, y, self.x = (lax.axis_index(a) for a in SEQ)
        low, self.core = (lax.axis_index(a) for a in TENSOR)
        self.y = y
        self.place = y * 4 + self.x
        self.tensor = low * 2 + self.core
        self.head0 = self.tensor * HEADS_HERE
        self.base = (self.plane * PLANE + self.place) * TOK


def dot(a, b, dims=NN):
    return lax.dot_general(a, b, (dims, ((), ())), preferred_element_type=F32)


def split3(v):
    hi = v.astype(BF16).astype(F32)
    mid = (v - hi).astype(BF16).astype(F32)
    return hi, mid, v - hi - mid


def mid_offsets(head):
    slot = lax.broadcasted_iota(jnp.int32, (1, SLOTS), 1)
    return 2 * slot + lax.rem(head, 2)


def far_offsets(head, base):
    slot = lax.broadcasted_iota(jnp.int32, (1, SLOTS), 1)
    which = lax.rem(slot, 4)
    kind = jnp.where(which == 0, 0, 2 * which + 2)
    first = lax.div(base + 12 - head, 12) - 1
    return 12 * (first + lax.div(slot, 4)) + kind + head - base, kind


def one_hot_rows(offsets):
    rows = lax.broadcasted_iota(jnp.int32, (TOK, SLOTS), 0)
    return (rows == offsets).astype(F32).astype(BF16)


def picks(head, base):
    return one_hot_rows(mid_offsets(head)), one_hot_rows(far_offsets(head, base)[0])


def count_table(kind, usable, dilations):
    row = lax.broadcasted_iota(jnp.int32, (16, kind.shape[1]), 0)
    count = jnp.zeros(row.shape, F32)
    for step in dilations:
        count += jnp.where((lax.rem(row, step) == 0) & (lax.rem(kind, step) == 0), 1.0, 0.0)
    live = (count > 0) & usable & (row < 12)
    log_count = jnp.log(jnp.maximum(count, 1.0))
    hi = log_count.astype(BF16).astype(F32)
    return jnp.where(live, hi, NONE), jnp.where(live, log_count - hi, 0.0)


def score_columns(ref, lo, kind, usable, dilations):
    hi, low = count_table(kind, usable, dilations)
    return jnp.concatenate([ref[lo : lo + HDIM, :].astype(F32) * 0.125, hi, low], 0)


def own_columns(head, base, q, lo):
    kind = lax.rem(base - head + 12 + lax.broadcasted_iota(jnp.int32, (1, TOK), 1), 12)
    return score_columns(q, lo, kind, kind >= 0, NEAR)


def query_columns(head, base, plane, visitors, lo):
    if len(visitors) == 1:
        at = mid_offsets(head)
        return score_columns(visitors[0], lo, lax.rem(base + 2048 + at - head + 12, 12), at >= 0, MID)
    parts = []
    for visitor, origin in zip(visitors, (plane + 2, 3 - plane)):
        at, kind = far_offsets(head, origin * 2048 + lax.rem(base, 2048))
        parts.append(score_columns(visitor, lo, kind, (at >= 0) & (at < TOK), FAR))
    return jnp.concatenate(parts, 1)


def one_hot_kind(kind):
    return (kind == lax.broadcasted_iota(jnp.int32, (16, kind.shape[1]), 0)).astype(F32).astype(BF16)


def ones(rows, columns):
    return jnp.ones((rows, columns), BF16)


def diagonal_mask(base, valid):
    rows = lax.broadcasted_iota(jnp.int32, (TOK, TOK), 0)
    cols = lax.broadcasted_iota(jnp.int32, (TOK, TOK), 1)
    return (cols <= rows) & (cols + base < valid)


def norm_rows(v, gain, shift):
    mean = jnp.sum(v, 1, keepdims=True) / v.shape[1]
    spread = jnp.sum(v * v, 1, keepdims=True) / v.shape[1] - mean * mean
    scale = lax.rsqrt(spread + EPSILON)
    unit = (v - mean) * scale
    return unit * gain + shift, unit, scale


def norm_rows_back(grad, unit, scale, gain):
    q = grad * gain
    n = grad.shape[1]
    return scale * (q - jnp.sum(q, 1, keepdims=True) / n - unit * (jnp.sum(q * unit, 1, keepdims=True) / n))


def project_kernel(inputs, weights, gain, shift, q, spread):
    v = norm_rows(inputs[...].astype(F32), gain[...], shift[...])[0].astype(BF16)
    spread[0, 0:192, :] = dot(weights[1], v, NT).astype(BF16)
    spread[0, 192:384, :] = dot(weights[2], v, NT).astype(BF16)
    for i in range(1, PLANE):
        spread[i] = spread[0]
    q[...] = dot(weights[0], v, NT).astype(BF16)


def select_kernel(q, out_weight, mix_gain, mix_shift, q_mid, q_far, packed):
    here = Here()
    head0, base = here.head0, here.base
    for h in range(HEADS_HERE):
        rows = slice(h * HDIM, (h + 1) * HDIM)
        pick_mid, pick_far = picks(head0 + h, base)
        q_mid[rows, :] = dot(q[rows, :], pick_mid).astype(BF16)
        q_far[rows, :] = dot(q[rows, :], pick_far).astype(BF16)
    packed[0:192, :] = out_weight[...]
    terms = list(split3(mix_gain[...])) + list(split3(mix_shift[...])) + [jnp.zeros((10, 192), F32)]
    packed[192:208, 0:192] = jnp.concatenate(terms, 0).astype(BF16)


def weigh(s):
    return jnp.exp(s).astype(BF16)


def widest(s):
    return functools.reduce(jnp.maximum, [s[:, i * 128 : (i + 1) * 128] for i in range(s.shape[1] // 128)])


def shifted(m, rows):
    top = jnp.max(m.T, 0, keepdims=True)
    minus = jnp.concatenate(list(split3(-top)) + [jnp.zeros((29, top.shape[1]), F32)], 0)
    return top, jnp.concatenate([rows, minus], 0).T.astype(BF16)


def near_keys(kvs, block, lo, head, base):
    kind = lax.rem(base - head + 12 + lax.broadcasted_iota(jnp.int32, (1, TOK), 1), 12)
    hot = one_hot_kind(kind)
    return jnp.concatenate([kvs[block, lo : lo + HDIM, :], hot, hot, ones(32, TOK)], 0)


def near_values(kvs, block, lo):
    return jnp.concatenate([kvs[block, 192 + lo : 192 + lo + HDIM, :], ones(16, TOK)], 0)


def gather_keys(kvs, head0, plane, far, rights, values):
    for h in range(HEADS_HERE):
        lo, head = h * HDIM, head0 + h
        for k in range(PLANE):
            start = plane * 2048 + k * TOK
            if far:
                offsets, kind = far_offsets(head, start)
                kind = jnp.where((offsets >= 0) & (offsets < TOK), kind, 12)
            else:
                offsets = mid_offsets(head)
                kind = lax.rem(start + offsets - head + 12, 12)
            both = jnp.concatenate([kvs[k, lo : lo + HDIM, :], kvs[k, 192 + lo : 192 + lo + HDIM, :]], 0)
            at = slice(k * SLOTS, (k + 1) * SLOTS)
            small = dot(both, one_hot_rows(offsets)).astype(BF16)
            hot = one_hot_kind(kind)
            rights[h, :, at] = jnp.concatenate([small[0:HDIM], hot, hot, ones(32, SLOTS)], 0)
            values[h, :, at] = jnp.concatenate([small[HDIM:], ones(16, SLOTS)], 0)


def forward_far_kernel(qa, qb, qc, kvs, pay_a, pay_b, pay_c, loc, right_a, right_f, value_a, value_f):
    here = Here()
    head0, base, plane = here.head0, here.base, here.plane
    heads = range(HEADS_HERE)
    row = lax.broadcasted_iota(jnp.int32, (16, SLOTS), 0)
    loc[...] = jnp.zeros(loc.shape, F32)

    def attend(queries, rights, values, first, pays):
        extra = [jnp.where(row == 9, 1.0, 0.0) for _ in pays]
        rows = [query_columns(head0 + h, base, plane, queries, h * HDIM) for h in heads]
        zeros = jnp.zeros((32, SLOTS * len(pays)), F32)
        marks = [widest(dot(jnp.concatenate([rows[h], zeros], 0).T.astype(BF16), rights[h])) for h in heads]
        lefts = [shifted(marks[h], rows[h]) for h in heads]
        accs = [dot(values[h], weigh(dot(lefts[h][1], rights[h])), NT) for h in heads]
        for h in heads:
            total = accs[h][64:65, :]
            log = jnp.maximum(lefts[h][0] + jnp.log(total), NONE)
            out = accs[h][0:64, :] / total
            for i, pay in enumerate(pays):
                at = slice(i * SLOTS, (i + 1) * SLOTS)
                loc[h : h + 1, first + i * SLOTS : first + (i + 1) * SLOTS] = log[:, at]
                pay[h * HDIM : (h + 1) * HDIM, :] = out[:, at].astype(BF16)
                for j, term in enumerate(split3(log[:, at])):
                    extra[i] = jnp.where(row == 3 * h + j, term, extra[i])
        for e, pay in zip(extra, pays):
            pay[192:208, :] = e.astype(BF16)

    @pl.when(lax.rem(plane, 2) == 0)
    def _():
        gather_keys(kvs, head0, plane, False, right_a, value_a)
        attend((qa,), right_a, value_a, 0, (pay_a,))

    @pl.when(plane < 2)
    def _():
        gather_keys(kvs, head0, plane, True, right_f, value_f)
        attend((qb, qc), right_f, value_f, SLOTS, (pay_b, pay_c))


def forward_near_kernel(length, q, kvs, o_near, st_near, right, rows, left, marks, acc):
    here, valid = Here(), length[0]
    head0, base, place = here.head0, here.base, here.place
    heads = range(HEADS_HERE)
    for h in heads:
        lo = h * HDIM
        head = head0 + h
        rows[h] = own_columns(head, base, q, lo)
        left[h] = jnp.concatenate([rows[h], jnp.zeros((32, TOK), F32)], 0).T.astype(BF16)
    marks[...] = jnp.full(marks.shape, 2 * NONE, F32)
    wait_for(kvs)
    for k in range(PLANE):

        @pl.when(k <= place)
        def _():
            for h in heads:
                right[h, k] = near_keys(kvs, place - k, h * HDIM, head0 + h, base - k * TOK)
                s = dot(left[h], right[h, k])
                if k == 0:
                    s = jnp.where(diagonal_mask(base, valid), s, NONE)
                marks[h] = jnp.maximum(marks[h], widest(s))

    tops = []
    for h in heads:
        top, turned = shifted(marks[h], rows[h])
        tops.append(top)
        left[h] = turned
    acc[...] = jnp.zeros(acc.shape, F32)
    for k in range(PLANE):

        @pl.when(k <= place)
        def _():
            for h in heads:
                lo = h * HDIM
                s = dot(left[h], right[h, k])
                if k == 0:
                    s = jnp.where(diagonal_mask(base, valid), s, NONE)
                acc[h] += dot(near_values(kvs, place - k, lo), weigh(s), NT)

    st_near[...] = jnp.zeros(st_near.shape, F32)
    for h in heads:
        total = acc[h, 64:65, :]
        o_near[h * HDIM : (h + 1) * HDIM, :] = acc[h, 0:64, :] / total
        st_near[h : h + 1, :] = tops[h] + jnp.log(total)


def combine_kernel(o_near, st_near, ra, rb, rc, mixed, st_all):
    here = Here()
    head0, base = here.head0, here.base
    st_all[...] = jnp.zeros(st_all.shape, F32)
    for h in range(HEADS_HERE):
        rows = slice(h * HDIM, (h + 1) * HDIM)
        pick_mid, pick_far = picks(head0 + h, base)
        outs, logs = [o_near[rows, :]], [st_near[h : h + 1, :]]
        for pay, pick in ((ra, pick_mid), (rb, pick_far), (rc, pick_far)):
            wide = dot(jnp.concatenate([pay[rows, :], pay[192:208, :]], 0), pick, NT)
            log = wide[64 + 3 * h : 65 + 3 * h] + wide[65 + 3 * h : 66 + 3 * h] + wide[66 + 3 * h : 67 + 3 * h]
            outs.append(wide[0:64])
            logs.append(jnp.where(wide[73:74] > 0.5, log, NONE))
        top = functools.reduce(jnp.maximum, logs)
        weights = [jnp.exp(v - top) for v in logs]
        total = sum(weights)
        mixed[rows, :] = sum((w / total) * o for w, o in zip(weights, outs)).astype(BF16)
        st_all[h : h + 1, :] = top + jnp.log(total)
        for i in range(3):
            st_all[3 + 3 * i + h : 4 + 3 * i + h, :] = weights[i + 1] / total


def mix_norm(pieces):
    first = sum(jnp.sum(pieces[i].astype(F32), 0, keepdims=True) for i in range(4)) / 768
    second = sum(jnp.sum(jnp.square(pieces[i].astype(F32)), 0, keepdims=True) for i in range(4)) / 768
    return first, lax.rsqrt(second - first * first + EPSILON)


def mix_parameters(packed, i):
    tail = jnp.concatenate([packed[i, 192:208, 0:256].astype(F32), jnp.zeros((112, 256), F32)], 0).T[0:192]
    return tail[:, 0:1] + tail[:, 1:2] + tail[:, 2:3], tail[:, 3:4] + tail[:, 4:5] + tail[:, 5:6]


def gelu_parts(v):
    a, b = 0.7978845608028654, 0.044715
    square = v * v
    t = jnp.tanh(a * v * (1.0 + b * square))
    active = 0.5 * v * (1.0 + t)
    slope = 0.5 * (1.0 + t) + 0.5 * v * (1.0 - t * t) * (a * (1.0 + 3.0 * b * square))
    return active, slope


def half_blocks(core, v):
    half = jnp.where(core == 0, v[0:128], v[128:256])
    return jnp.concatenate([half[:, i * 256 : (i + 1) * 256] for i in range(3)], 0).astype(BF16)


def feed_kernel(length, down, cotangent, feed_blocks, inner_grad):
    here = Here()
    row = here.base + lax.broadcasted_iota(jnp.int32, (TOK, 1), 0)
    feed = jnp.where(row < length[0], cotangent[...].astype(F32), 0.0)
    feed_blocks[...] = half_blocks(here.core, feed)
    grad = dot(feed.astype(BF16), down[...], NT)
    inner_grad[...] = grad


def middle_kernel(
    inputs, pieces, packed, up, gain, shift, inner_gain, inner_grad, st_all,
    hidden, pieces_kept, st_kept, mid_blocks, pre, sums,
):
    st_kept[...] = st_all[...]
    st_kept.flush()
    pieces.wait()
    pieces_kept[...] = pieces[...]
    pieces_kept.flush()
    mean, scale = mix_norm(pieces)
    total = inputs[...].astype(F32)
    branch = None
    for i in range(4):
        mix_gain, mix_shift = mix_parameters(packed, i)
        low = ((pieces[i].astype(F32) - mean) * scale * mix_gain + mix_shift).astype(BF16)
        term = dot(low, packed[i, 0:192, :], TN)
        branch = term if branch is None else branch + term
    total = total + branch
    hidden[...] = total
    hidden.flush()
    low = norm_rows(total, gain[...], shift[...])[0]
    mid_blocks[...] = half_blocks(Here().core, low)
    pre[...] = dot(low.astype(BF16), up[...])
    active = gelu_parts(pre[...])[0]
    lane = lax.broadcasted_iota(jnp.int32, (1, 128), 1)
    st = jnp.zeros((TOK, 128), F32)
    scaled = inner_grad[...] * inner_gain[...]
    for i, v in enumerate((active, active * active, scaled, scaled * active)):
        st = jnp.where(lane == i, jnp.sum(v, 1, keepdims=True), st)
    sums[...] = st.T[0:8]


def halves(core, v, keep, send):
    for c in range(2):

        @pl.when(core == c)
        def _():
            keep[...] = v[c * 128 : (c + 1) * 128].astype(BF16)
            send[...] = v[(1 - c) * 128 : (2 - c) * 128].astype(BF16)


def whole(core, own, other):
    return jnp.concatenate([jnp.where(core == 0, own, other), jnp.where(core == 0, other, own)], 0)


def inner_kernel(sums, pre, inner_grad, up, gain, shift, inner_low, pre_grad, keep, send, vectors):
    st = jnp.concatenate([sums[...], jnp.zeros((120, TOK), F32)], 0).T
    width = 3072
    mean = st[:, 0:1] / width
    scale = lax.rsqrt(st[:, 1:2] / width - mean * mean + EPSILON)
    first = st[:, 2:3]
    second = scale * (st[:, 3:4] - mean * first)
    active, slope = gelu_parts(pre[...])
    unit = (active - mean) * scale
    inner_low[...] = (unit * gain[...] + shift[...]).astype(BF16)
    grad = inner_grad[...]
    vectors[...] = jnp.zeros(vectors.shape, F32)
    vectors[0:1, :] = jnp.sum(grad * unit, 0, keepdims=True)
    vectors[1:2, :] = jnp.sum(grad, 0, keepdims=True)
    back = scale * (grad * gain[...] - first / width - unit * (second / width))
    low = (back * slope).astype(BF16)
    pre_grad[...] = low
    halves(Here().core, dot(low, up[...], NT), keep, send)


def outer_kernel(
    length, mid_own, mid_got, other_own, other_got, hidden, cotangent, gain, shift, pieces, packed, st_all,
    inner_vectors, hidden_grad, grad_mixed, st_near, pay_a, pay_b, pay_c, out_grad, all_vectors, scratch,
):
    here, valid = Here(), length[0]
    head0, base, tensor = here.head0, here.base, here.tensor
    row = base + lax.broadcasted_iota(jnp.int32, (TOK, 1), 0)
    upstream = jnp.where(row < valid, cotangent[...].astype(F32), 0.0)
    _, unit, scale = norm_rows(hidden[...], gain[...], shift[...])
    own = mid_own[...].astype(F32) + mid_got[...].astype(F32)
    grad = whole(here.core, own, other_own[...].astype(F32) + other_got[...].astype(F32))
    vectors = [jnp.sum(grad * unit, 0, keepdims=True), jnp.sum(grad, 0, keepdims=True)]
    total = upstream + norm_rows_back(grad, unit, scale, gain[...])
    hidden_grad[...] = total
    hidden_grad.flush()
    branch = total.astype(BF16)

    mean, scale = mix_norm(pieces)
    first, second = jnp.zeros((1, TOK), F32), jnp.zeros((1, TOK), F32)
    for i in range(4):
        grad = dot(packed[i, 0:192, :], branch, NT)
        scratch[i] = grad
        q = grad * mix_parameters(packed, i)[0]
        first += jnp.sum(q, 0, keepdims=True)
        second += jnp.sum(q * (pieces[i].astype(F32) - mean), 0, keepdims=True)
    second = second * scale
    output = pieces[tensor].astype(F32)
    unit = (output - mean) * scale
    grad = scratch[tensor]
    gain_own, shift_own = mix_parameters(packed, tensor)
    low = (unit * gain_own + shift_own).astype(BF16)
    lane = lax.broadcasted_iota(jnp.int32, (1, 128), 1)
    columns = jnp.where(
        lane == 0, jnp.sum(grad * unit, 1, keepdims=True), jnp.where(lane == 1, jnp.sum(grad, 1, keepdims=True), 0.0)
    )
    vectors += [inner_vectors[0:2], jnp.concatenate([columns.T[0:2], jnp.zeros((2, 576), F32)], 1)]
    all_vectors[...] = jnp.concatenate(vectors + [jnp.zeros((2, 768), F32)], 0)
    out_grad[...] = dot(low, branch).astype(BF16)
    out_grad.flush()
    all_vectors.flush()
    back = scale * (grad * gain_own - first / 768 - unit * (second / 768))
    back = back.astype(BF16).astype(F32)
    grad_mixed[...] = back.astype(BF16)
    st_near[...] = jnp.zeros(st_near.shape, F32)
    tails = [[], [], []]
    for h in range(HEADS_HERE):
        rows = slice(h * HDIM, (h + 1) * HDIM)
        mine = back[rows]
        centre = jnp.sum(mine * output[rows], 0, keepdims=True)
        st_near[h : h + 1, :] = st_all[h : h + 1, :]
        st_near[3 + h : 4 + h, :] = centre
        pick_mid, pick_far = picks(head0 + h, base)
        for i, (pay, pick) in enumerate(((pay_a, pick_mid), (pay_b, pick_far), (pay_c, pick_far))):
            share = st_all[3 + 3 * i + h : 4 + 3 * i + h, :]
            terms = list(split3(centre * share)) + [jnp.zeros((13, TOK), F32)]
            wide = jnp.concatenate([mine * share] + terms, 0).astype(BF16)
            small = dot(wide, pick)
            pay[rows, :] = small[0:64].astype(BF16)
            tails[i].append(small[64:67])
    for pay, tail in zip((pay_a, pay_b, pay_c), tails):
        pay[192:208, :] = jnp.concatenate(tail + [jnp.zeros((7, SLOTS), F32)], 0).astype(BF16)


def gradients(left, grad_left, rows_q, rows_g, rights, values, mask=None):
    s = dot(left, rights)
    if mask is not None:
        s = jnp.where(mask, s, NONE)
    w = jnp.exp(s)
    ds = (w * dot(grad_left, values)).astype(BF16)
    dq = dot(rights[0:64], ds, NT)
    return dq, jnp.concatenate([dot(rows_q, ds), dot(rows_g, w.astype(BF16))], 0)


def with_logs(rows, logs):
    minus = split3(jnp.where(logs > NONE * 0.1, -logs, 0.0))
    return jnp.concatenate([rows] + list(minus) + [jnp.zeros((29, logs.shape[1]), F32)], 0)


def with_centres(rows, centres):
    return jnp.concatenate([rows] + list(split3(-centres)) + [jnp.zeros((13, centres.shape[1]), F32)], 0)


def backward_near_kernel(length, q, grad, st, kvs, dq_near, dkv, rows_q, rows_g, left, grad_left, acc_q):
    here, valid = Here(), length[0]
    head0, base, place = here.head0, here.base, here.place
    heads = range(HEADS_HERE)
    for h in heads:
        lo = h * HDIM
        rows = with_logs(own_columns(head0 + h, base, q, lo), st[h : h + 1, :])
        rows_q[h] = rows[0:64].astype(BF16)
        left[h] = rows.T.astype(BF16)
        rows = with_centres(grad[lo : lo + HDIM, :].astype(F32), st[3 + h : 4 + h, :])
        rows_g[h] = rows[0:64].astype(BF16)
        grad_left[h] = rows.T.astype(BF16)
    acc_q[...] = jnp.zeros(acc_q.shape, F32)
    for k in range(PLANE):
        block = lax.rem(place - k + PLANE, PLANE)

        @pl.when(k > place)
        def _():
            dkv[block] = jnp.zeros((384, TOK), BF16)

        @pl.when(k <= place)
        def _():
            mask = diagonal_mask(base, valid) if k == 0 else None
            for h in heads:
                lo = h * HDIM
                keys = near_keys(kvs, place - k, lo, head0 + h, base - k * TOK)
                values = near_values(kvs, place - k, lo)
                dq, both = gradients(left[h], grad_left[h], rows_q[h], rows_g[h], keys, values, mask)
                acc_q[h] += dq
                dkv[block, lo : lo + HDIM, :] = both[0:64].astype(BF16)
                dkv[block, 192 + lo : 192 + lo + HDIM, :] = both[64:128].astype(BF16)

        dkv.flush_part(block)

    for h in heads:
        dq_near[h * HDIM : (h + 1) * HDIM, :] = acc_q[h] * 0.125


def backward_far_kernel(dkv_near, qa, qb, qc, ga, gb, gc, loc, kvs, *refs):
    dq_a, dq_b, dq_c, dkv, small_a, small_f, right_a, right_f, value_a, value_f = refs
    here = Here()
    head0, base, plane = here.head0, here.base, here.plane
    heads = range(HEADS_HERE)
    wait_for(qa, qb, qc, loc)

    def part(queries, pays, first, rights, values, dqs, small):
        n = SLOTS * len(pays)
        for h in heads:
            lo = h * HDIM
            rows = query_columns(head0 + h, base, plane, queries, lo)
            rows = with_logs(rows, loc[h : h + 1, first : first + n])
            columns, centres = [], []
            for pay in pays:
                columns.append(pay[lo : lo + HDIM, :].astype(F32))
                tail = pay[192:208, :].astype(F32)
                centres.append(tail[3 * h : 3 * h + 1] + tail[3 * h + 1 : 3 * h + 2] + tail[3 * h + 2 : 3 * h + 3])
            grads = with_centres(jnp.concatenate(columns, 1), jnp.concatenate(centres, 1))
            dq, both = gradients(
                rows.T.astype(BF16),
                grads.T.astype(BF16),
                rows[0:64].astype(BF16),
                grads[0:64].astype(BF16),
                rights[h],
                values[h],
            )
            dq = (dq * 0.125).astype(BF16)
            for i, out in enumerate(dqs):
                out[lo : lo + HDIM, :] = dq[:, i * SLOTS : (i + 1) * SLOTS]
            small[h] = both.astype(BF16)

    @pl.when((plane == 1) | (plane == 2))
    def _():
        small_a[...] = jnp.zeros(small_a.shape, BF16)
        small_f[...] = jnp.zeros(small_f.shape, BF16)

    @pl.when(lax.rem(plane, 2) == 0)
    def _():
        gather_keys(kvs, head0, plane, False, right_a, value_a)
        part((qa,), (ga,), 0, right_a, value_a, (dq_a,), small_a)

    @pl.when(plane < 2)
    def _():
        gather_keys(kvs, head0, plane, True, right_f, value_f)
        part((qb, qc), (gb, gc), SLOTS, right_f, value_f, (dq_b, dq_c), small_f)

    wait_for(dkv_near)

    @pl.when(plane == 3)
    def _():
        dkv[...] = dkv_near[...]
        for block in range(PLANE):
            dkv.flush_part(block)

    @pl.when(plane < 3)
    def _():
        for block in range(PLANE):
            at = slice(block * SLOTS, (block + 1) * SLOTS)
            for h in heads:
                lo = h * HDIM
                pick = jnp.concatenate(picks(head0 + h, plane * 2048 + block * TOK), 1)
                wide = dot(jnp.concatenate([small_a[h, :, at], small_f[h, :, at]], 1), pick, NT)
                for i, at_row in ((0, lo), (64, 192 + lo)):
                    near = dkv_near[block, at_row : at_row + HDIM, :].astype(F32)
                    dkv[block, at_row : at_row + HDIM, :] = (near + wide[i : i + 64]).astype(BF16)
            dkv.flush_part(block)


def weights_kernel(
    inputs, gain, shift, weights, dq_near, ra, rb, rc, dkv, out_grad, vectors, sums, keep, send, in_sums, grads
):
    here = Here()
    head0, base = here.head0, here.base
    normed, unit, _ = norm_rows(inputs[...].astype(F32), gain[...], shift[...])
    for h in range(HEADS_HERE):
        rows = slice(h * HDIM, (h + 1) * HDIM)
        pick_mid, pick_far = picks(head0 + h, base)
        dq = dq_near[rows, :] + dot(ra[rows, :], pick_mid, NT) + dot(rb[rows, :], pick_far, NT) + dot(rc[rows, :], pick_far, NT)
        grads[rows, :] = dq.astype(BF16)
    total = dkv[0].astype(F32)
    for k in range(1, PLANE):
        total += dkv[k].astype(F32)
    grads[192:576, :] = total.astype(BF16)
    sums[0:24, :, 0:768] = dot(grads[...], normed.astype(BF16)).reshape(24, ROW, 768).astype(BF16)
    sums[24:32, :, 0:768] = out_grad[...].astype(F32).reshape(8, ROW, 768).astype(BF16)
    sums[:, :, 768:896] = jnp.zeros((PARTS, ROW, 128), BF16)
    mixed = jnp.concatenate([vectors[4:5, 0:192], vectors[5:6, 0:192], jnp.zeros((1, 384), F32)], 1)
    for i, v in enumerate((vectors[0:1], vectors[1:2], vectors[2:3], vectors[3:4], mixed)):
        rows = [v[:, j * 128 : (j + 1) * 128] for j in range(6)] + [jnp.zeros((2, 128), F32)]
        sums[i, 0:8, 768:896] = jnp.concatenate(rows, 0).astype(BF16)
    sums.flush()
    back = dot(grads[0:192, :], weights[0], TN)
    back += dot(grads[192:384, :], weights[1], TN)
    back += dot(grads[384:576, :], weights[2], TN)
    halves(here.core, back, keep, send)
    rows = [jnp.sum(back * unit, 0, keepdims=True), jnp.sum(back, 0, keepdims=True), jnp.zeros((6, 768), F32)]
    in_sums[...] = jnp.concatenate(rows, 0)


def reduce_kernel(got, in_sums, down, up, out):
    total = got[0].astype(F32)
    for i in range(1, PARTS):
        total += got[i].astype(F32)
    rows = [[in_sums[j : j + 1, i * 128 : (i + 1) * 128] for i in range(6)] + [jnp.zeros((2, 128), F32)] for j in (0, 1)]
    out[:, 0:768] = down[...]
    out[:, 768:1152] = total[:, 0:384].astype(BF16)
    out[:, 1152:1920] = up[...]
    out[:, 1920:2304] = total[:, 384:768].astype(BF16)
    out[:, 2304:2432] = jnp.concatenate([total[0:8, 768:896], *rows[0], *rows[1]], 0).astype(BF16)


def input_grad_kernel(inputs, hidden_grad, gain, shift, own, other, inputs_grad):
    _, unit, scale = norm_rows(inputs[...].astype(F32), gain[...], shift[...])
    grad = whole(Here().core, own[...].astype(F32), other[...].astype(F32))
    inputs_grad[...] = (hidden_grad[...] + norm_rows_back(grad, unit, scale, gain[...])).astype(BF16)


CHUNK = 48
PAIR_A = [(0, 1), (1, 0), (2, 3), (3, 2)]
PAIR_B = [(0, 3), (3, 0), (1, 2), (2, 1)]
STEPS = {"xa": ("x", PAIR_A), "xb": ("x", PAIR_B), "za": ("z", PAIR_A), "zb": ("z", PAIR_B)}


def travel(v, name):
    axis, perm = STEPS[name]
    return lax.ppermute(v, axis, perm)


def slices_kernel(inner_low, pre_grad, mid_blocks, feed_blocks, down, slices, feed_keep, feed_send):
    for first, ref in ((0, inner_low), (192, pre_grad)):
        turned = ref[...].astype(F32).T.astype(BF16)
        for i in range(4):
            slices[i, first : first + 192, :] = turned[i * 192 : (i + 1) * 192]
    for i in range(4):
        slices[i, 384:768, :] = mid_blocks[...]
        slices[i, 768:1152, :] = feed_blocks[...]
    slices.flush()
    halves(Here().core, dot(inner_low[...], down[...]), feed_keep, feed_send)


def products_kernel(slices, others, keep, send, full, *operands):
    here = Here()
    products = []
    for (first, second), rows, columns in zip(((0, 768), (192, 384)), operands[0:2], operands[2:4]):
        for i in range(4):
            columns[:, i * TOK : (i + 1) * TOK] = slices[i, first : first + 192, :]
            for b in range(3):
                block = slice(b * 256, (b + 1) * 256)
                own = pl.multiple_of(i * TOK + here.core * 128, 128)
                other = pl.multiple_of(i * TOK + 128 - here.core * 128, 128)
                rows[pl.ds(own, 128), block] = slices[i, second + b * 128 : second + (b + 1) * 128, :]
                rows[pl.ds(other, 128), block] = others[i, second + b * 128 : second + (b + 1) * 128, :]
        products.append(dot(columns[...], rows[...]))
    down, up = products
    full[:, :, 0:24, :] = down.reshape(4, 2, 24, 768).astype(BF16)
    full[:, :, 24:48, :] = up.reshape(4, 2, 24, 768).astype(BF16)
    high = lax.div(here.plane, 2)
    keep[...] = full[pl.ds(2 * high, 2)]
    send[...] = full[pl.ds(2 - 2 * high, 2)]


def halve_kernel(axis, keep, got, new_keep, new_send):
    i = lax.rem(Here().plane, 2) if axis == "z" else Here().y
    new_keep[...] = (keep[i].astype(F32) + got[i].astype(F32)).astype(BF16)
    new_send[...] = (keep[1 - i].astype(F32) + got[1 - i].astype(F32)).astype(BF16)


def chunk_sum_kernel(keep, got, down, up):
    total = keep[...].astype(F32) + got[...].astype(F32)
    down[...] = total[0:24].astype(BF16)
    up[...] = total[24:48].astype(BF16)


def join_y_kernel(own, other, down, up):
    y = Here().y
    for at, part in ((y, own), (1 - y, other)):
        down[at] = part[:, 0:1152]
        up[at] = part[:, 1152:2432]


def join_pair(i, name, own, other, out):
    high = lax.div(i, 2)
    if name == "b1":
        out[high] = own[...]
        out[1 - high] = other[...]
    elif name == "a1":
        low = lax.rem(i, 2)
        out[low] = own[...]
        out[1 - low] = other[...]
    elif name == "a2":
        first = jnp.where(high == 0, i, 3 - i)
        out[first] = own[0]
        out[3 - first] = own[1]
        out[1 - first] = other[0]
        out[2 + first] = other[1]
    else:
        out[pl.ds(2 * high, 2)] = own[...]
        out[pl.ds(2 - 2 * high, 2)] = other[...]


def join_kernel(steps, *refs):
    here, n = Here(), len(steps)
    for i, step in enumerate(steps):
        join_pair(here.x if step[0] == "x" else here.plane, step[1:], refs[i], refs[n + i], refs[2 * n + i])


WIDTHS = (512, 640, 640, 640)


def split_kernel(down, up, *outs):
    for j in range(4):
        first, width = ((0, 128), (128, 256), (0, 256), (256, 256))[j]
        full = (down, up)[j // 2]
        outs[j][:, :, :, 0:384] = full[:, :, :, (j % 2) * 384 : (j % 2 + 1) * 384]
        outs[j][:, :, :, 384 : 384 + width] = full[:, :, :, 768 + first : 768 + first + width]


def unpack_kernel(*refs):
    owns, others = refs[0:4], refs[4:8]
    down, up, head_grad, out_grad, *vectors, up_turned, tail = refs[8:]
    here = Here()
    places = []
    for i, step in ((here.x, "a"), (here.x, "b"), (here.plane, "a"), (here.plane, "b")):
        high = lax.div(i, 2)
        if step == "a":
            first = jnp.where(high == 0, i, 3 - i)
            places.append(((first, 3 - first), (1 - first, 2 + first)))
        else:
            places.append(((2 * high, 2 * high + 1), (2 - 2 * high, 3 - 2 * high)))

    for d, u, y, e in itertools.product(range(2), range(4), range(2), range(2)):
        for pair, side in ((0, owns), (1, others)):
            z, x = places[2 + d][pair][e], u
            value = side[2 + d][e, x, y].astype(F32)
            up_turned[x * 8 + z * 2 + y, :, d * 384 : (d + 1) * 384] = value[:, 0:384]
            tail[z * 8 + y * 4 + x, :, 384 + d * 256 : 640 + d * 256] = value[:, 384:640]
    up[...] = up_turned[...].reshape(768, 768).T
    up.flush()
    for d, u, y, e in itertools.product(range(2), range(4), range(2), range(2)):
        for pair, side in ((0, owns), (1, others)):
            x, z = places[d][pair][e], u
            value = side[d][e, z, y].astype(F32)
            down[x * 8 + z * 2 + y, :, d * 384 : (d + 1) * 384] = value[:, 0:384]
            tail[z * 8 + y * 4 + x, :, d * 128 : 128 + d * 256] = value[:, 384:]
    down.flush()
    head_grad[...] = tail[0:24, :, 0:768]
    head_grad.flush()
    out_grad[...] = tail[24:32, :, 0:768]
    out_grad.flush()
    rows = [tail[i, 0:6, 768:896] for i in range(5)] + [jnp.sum(tail[:, i : i + 6, 768:896], 0) for i in (8, 16)]
    rows = [jnp.concatenate([v[i : i + 1] for i in range(6)], 1) for v in rows]
    rows[4:5] = [rows[4][:, 0:192], rows[4][:, 192:384]]
    for ref, row in zip(vectors, rows):
        ref[...] = row.reshape(ref.shape)


def add_kernel(a, b, out):
    out[...] = (a[...].astype(F32) + b[...].astype(F32)).astype(out.dtype)


TIMES = {
    "project_kernel": 1.2,
    "forward_far_kernel": 4.3,
    "forward_near_kernel": 7.0,
    "combine_kernel": 1.0,
    "feed_kernel": 1.5,
    "middle_kernel": 3.4,
    "inner_kernel": 2.0,
    "outer_kernel": 4.0,
    "slices_kernel": 3.0,
    "products_kernel": 3.0,
    "backward_near_kernel": 9.0,
    "backward_far_kernel": 7.0,
    "weights_kernel": 4.0,
    "reduce_kernel": 2.0,
    "unpack_kernel": 0.1,
    "join_kernel": 0.1,
}


class Fetched:
    def __init__(self, copies, ref):
        self.copies, self.ref, self.shape = copies, ref, ref.shape

    def wait(self):
        for copy in self.copies:
            copy.wait()
        self.copies = ()

    def __getitem__(self, index):
        self.wait()
        return self.ref[index]


class Stored:
    def __init__(self, copy, ref):
        self.copy, self.ref, self.shape, self.started = copy, ref, ref.shape, False
        self.parts = None

    def flush(self):
        if not self.started:
            self.copy.start()
        self.started = True

    def flush_part(self, i):
        self.started = True
        self.parts(i).start()

    def finish(self):
        self.flush()
        self.copy.wait()

    def __getitem__(self, index):
        return self.ref[index]

    def __setitem__(self, index, value):
        self.ref[index] = value


def part_copy(ref, target, semaphore, i):
    return pltpu.make_async_copy(ref.at[i], target.at[i], semaphore)


def wait_for(*operands):
    for operand in operands:
        if isinstance(operand, Fetched):
            operand.wait()


def call(kernel, out_shapes, scratch=(), scalars=0, limit=8, fetch=(), stacks=(), store=(), free=()):
    def run(*args, after=(), behind=()):
        after = (*after, *[pltpu.with_memory_space_constraint(v, pltpu.HBM) for v in behind])
        n, extra, outs = len(args), len(after), len(out_shapes)
        name = getattr(kernel, "func", kernel).__name__
        vmem, hbm = pl.BlockSpec(memory_space=pltpu.VMEM), pl.BlockSpec(memory_space=pltpu.HBM)
        specs = [vmem] * n + [pl.BlockSpec(memory_space=pl.ANY)] * (extra - len(behind)) + [hbm] * len(behind)
        out_specs = [hbm if i in store else vmem for i in range(outs)]
        for i in range(scalars):
            specs[i] = pl.BlockSpec(memory_space=pltpu.SMEM)
        buffers, sizes = [], {}
        for i in sorted((*fetch, *stacks)):
            sizes[i] = 4 if i in stacks else 1
            for j in range(sizes[i]):
                specs[i + j] = pl.BlockSpec(memory_space=pl.ANY) if i in free else hbm
            shape = args[i].shape
            shape = (4, *shape) if i in stacks else (1, *shape) if len(shape) == 1 else shape
            buffers.append(pltpu.VMEM(shape, args[i].dtype))
        for i in store:
            buffers.append(pltpu.VMEM(*out_shapes[i]))
        total = sum(sizes.values()) + len(store)
        if total:
            buffers.append(pltpu.SemaphoreType.DMA((total,)))

        def body(*refs):
            results = list(refs[n + extra : n + extra + outs])
            own = refs[n + extra + outs : n + extra + outs + len(scratch)]
            landing = refs[n + extra + outs + len(scratch) :]
            operands, pending, i, slot = [], [], 0, 0
            while i < n:
                if i not in sizes:
                    operands.append(refs[i])
                    i += 1
                    continue
                ref, copies = landing[len(pending)], []
                for j in range(sizes[i]):
                    place = ref
                    if i in stacks:
                        place = ref.at[jnp.bitwise_xor(Here().tensor, j)]
                    elif len(args[i].shape) == 1:
                        place = ref.at[0]
                    copies.append(pltpu.make_async_copy(refs[i + j], place, landing[-1].at[slot]))
                    copies[-1].start()
                    slot += 1
                pending.append(Fetched(copies, ref))
                operands.append(pending[-1])
                i += sizes[i]
            for k, i in enumerate(store):
                ref = landing[len(pending) + k]
                copy_target = results[i]
                copy = pltpu.make_async_copy(ref, copy_target, landing[-1].at[slot])
                results[i] = Stored(copy, ref)
                results[i].parts = functools.partial(part_copy, ref, copy_target, landing[-1].at[slot])
                slot += 1
            kernel(*operands, *results, *own)
            for operand in pending:
                operand.wait()
            for i in store:
                results[i].flush()
            for i in store:
                results[i].finish()

        args = list(args)
        for i, size in sizes.items():
            for j in range(i, i + size if i not in free else i):
                args[j] = pltpu.with_memory_space_constraint(args[j], pltpu.HBM)
        return pl.pallas_call(
            body,
            out_shape=[(pltpu.HBM if i in store else jax.ShapeDtypeStruct)(*shape) for i, shape in enumerate(out_shapes)],
            in_specs=specs,
            out_specs=out_specs,
            scratch_shapes=[*scratch, *buffers],
            compiler_params=pltpu.CompilerParams(vmem_limit_bytes=limit * 1024 * 1024),
            name=name,
            cost_estimate=pl.CostEstimate(
                flops=int(TIMES.get(name, 0.6) * 1e9), bytes_accessed=0, transcendentals=0
            ),
        )(*args, *after)

    return run


def add(a, b, after=()):
    (out,) = call(add_kernel, [(a.shape, a.dtype)])(a, b, after=after)
    return out


def others_over_tensor(v):
    across = lax.ppermute(v, "yl", FLIP)
    beside = lax.ppermute(v, "c", FLIP)
    return beside, across, lax.ppermute(across, "c", FLIP)


MID_GO = [(1, 0), (3, 2)]
B_GO = [(2, 0), (3, 1)]
C_GO = [(3, 0), (2, 1)]


def back(perm):
    return [(b, a) for a, b in perm]


def visit(a, b, c, turn=lambda perm: perm):
    return tuple(lax.ppermute(v, "z", turn(perm)) for v, perm in ((a, MID_GO), (b, B_GO), (c, C_GO)))


def per_device(
    inputs,
    head_weights,
    out_weight,
    up_weight,
    down_weight,
    in_gain,
    in_shift,
    mix_gain,
    mix_shift,
    mid_gain,
    mid_shift,
    inner_gain,
    inner_shift,
    valid_length,
    cotangent,
):
    here = Here()
    core = here.core
    row_valid = (here.base + jnp.arange(TOK, dtype=jnp.int32) < valid_length[0])[:, None]
    n = HEADS_HERE
    half = ((128, 768), BF16)

    weights = head_weights.transpose(0, 2, 1)
    q, spread = call(
        project_kernel, [((192, TOK), BF16), ((PLANE, 384, TOK), BF16)], fetch=(0, 1, 2, 3), limit=12
    )(inputs, weights, in_gain, in_shift)
    kvs = lax.all_to_all(spread, ("yh", "x"), 0, 0, tiled=True)
    q_mid, q_far, packed = call(
        select_kernel,
        [((192, SLOTS), BF16), ((192, SLOTS), BF16), ((208, 768), BF16)],
        fetch=(1, 2, 3),
        store=(2,),
    )(q, out_weight, mix_gain, mix_shift)
    visitors = visit(q_mid, q_far, q_far)
    feed_blocks, inner_grad = call(
        feed_kernel,
        [((384, 256), BF16), ((TOK, 768), F32)],
        scalars=1,
        fetch=(1, 2),
        store=(0, 1),
        limit=12,
    )(valid_length, down_weight, cotangent, after=(q_mid,))
    pay_a, pay_b, pay_c, loc = call(
        forward_far_kernel,
        [((208, SLOTS), BF16)] * 3 + [((8, 384), F32)],
        [
            *[pltpu.VMEM((n, 128, KEYS), BF16)] * 2,
            *[pltpu.VMEM((n, 80, KEYS), BF16)] * 2,
        ],
        limit=16,
        store=(3,),
    )(*visitors, kvs, behind=(inner_grad,))
    returned = visit(pay_a, pay_b, pay_c, back)
    packed, _ = lax.optimization_barrier((packed, pay_a))
    packed_beside, packed_across = lax.ppermute(packed, "c", FLIP), lax.ppermute(packed, "yl", FLIP)
    o_near, st_near = call(
        forward_near_kernel,
        [((192, TOK), F32), ((8, TOK), F32)],
        [
            pltpu.VMEM((n, PLANE, 128, TOK), BF16),
            pltpu.VMEM((n, 96, TOK), F32),
            pltpu.VMEM((n, TOK, 128), BF16),
            pltpu.VMEM((n, TOK, 128), F32),
            pltpu.VMEM((n, 80, TOK), F32),
        ],
        scalars=1,
    )(valid_length, q, kvs)
    mixed, st_all = call(combine_kernel, [((192, TOK), BF16), ((16, TOK), F32)])(o_near, st_near, *returned)
    pieces = (mixed, *others_over_tensor(mixed))
    relay, _ = lax.optimization_barrier((packed_across, o_near))
    packed = (packed, packed_beside, packed_across, lax.ppermute(relay, "c", FLIP))
    hidden, pieces, st_all, mid_blocks, pre, sums = call(
        middle_kernel,
        [
            ((TOK, 768), F32),
            ((4, 192, TOK), BF16),
            ((16, TOK), F32),
            ((384, 256), BF16),
            ((TOK, 768), F32),
            ((8, TOK), F32),
        ],
        limit=20,
        fetch=(0, 9, 10, 11, 12, 13),
        stacks=(1, 5),
        free=(1,),
        store=(0, 1, 2),
    )(inputs, *pieces, *packed, up_weight, mid_gain, mid_shift, inner_gain, inner_grad, st_all)
    sums = sums + lax.ppermute(sums, "c", FLIP)
    sums = sums + lax.ppermute(sums, "yl", FLIP)
    inner_low, pre_grad, keep, send, inner_vectors = call(
        inner_kernel,
        [((TOK, 768), BF16), ((TOK, 768), BF16), half, half, ((8, 768), F32)],
        fetch=(2, 3, 4, 5),
        store=(4,),
        limit=12,
    )(sums, pre, inner_grad, up_weight, inner_gain, inner_shift)
    mid_half = add(keep, lax.ppermute(send, "c", FLIP))

    slices, feed_keep, feed_send = call(
        slices_kernel, [((4, 1152, TOK), BF16), half, half], fetch=(3, 4), store=(0,), limit=16
    )(inner_low, pre_grad, mid_blocks, feed_blocks, down_weight, after=(mid_half,))
    slices = lax.all_to_all(slices, "x", 0, 0, tiled=True)
    mid_got = lax.ppermute(mid_half, "yl", FLIP)
    mid_sent, _ = lax.optimization_barrier((mid_got, feed_keep))
    mid_parts = (mid_half, mid_got, lax.ppermute(mid_half, "c", FLIP), lax.ppermute(mid_sent, "c", FLIP))
    hidden_grad, grad_mixed, st_near, pay_a, pay_b, pay_c, out_grad, vectors = call(
        outer_kernel,
        [((TOK, 768), F32), ((192, TOK), BF16), ((8, TOK), F32)]
        + [((208, SLOTS), BF16)] * 3
        + [((192, 768), BF16), ((8, 768), F32)],
        [pltpu.VMEM((4, 192, TOK), F32)],
        limit=20,
        scalars=1,
        fetch=(5, 6, 7, 8, 9, 14, 15),
        stacks=(10,),
        store=(0, 6, 7),
    )(valid_length, *mid_parts, hidden, cotangent, mid_gain, mid_shift, pieces, *packed, st_all, inner_vectors)
    grads = visit(pay_a, pay_b, pay_c)

    dq_near, dkv = call(
        backward_near_kernel,
        [((192, TOK), F32), ((PLANE, 384, TOK), BF16)],
        [
            pltpu.VMEM((n, 64, TOK), BF16),
            pltpu.VMEM((n, 64, TOK), BF16),
            pltpu.VMEM((n, TOK, 128), BF16),
            pltpu.VMEM((n, TOK, 80), BF16),
            pltpu.VMEM((n, HDIM, TOK), F32),
        ],
        scalars=1,
        limit=12,
        store=(0, 1),
    )(valid_length, q, grad_mixed, st_near, kvs)
    dq_a, dq_b, dq_c, dkv = call(
        backward_far_kernel,
        [((192, SLOTS), BF16)] * 3 + [((PLANE, 384, TOK), BF16)],
        [
            pltpu.VMEM((n, 128, KEYS), BF16),
            pltpu.VMEM((n, 128, KEYS), BF16),
            *[pltpu.VMEM((n, 128, KEYS), BF16)] * 2,
            *[pltpu.VMEM((n, 80, KEYS), BF16)] * 2,
        ],
        limit=20,
        fetch=(0, 1, 2, 3, 7),
        store=(3,),
    )(dkv, *visitors, *grads, loc, kvs)
    dkv = lax.all_to_all(dkv, ("yh", "x"), 0, 0, tiled=True)
    dqs = visit(dq_a, dq_b, dq_c, back)

    feed_half = add(feed_keep, lax.ppermute(feed_send, "c", FLIP), after=(dq_a,))
    slices, _ = lax.optimization_barrier((slices, feed_half))
    others = lax.ppermute(slices, "c", FLIP)
    keep, send = call(
        products_kernel,
        [((2, 2, CHUNK, 768), BF16)] * 2,
        [
            pltpu.VMEM((4, 2, CHUNK, 768), BF16),
            *[pltpu.VMEM((4 * TOK, 768), BF16)] * 2,
            *[pltpu.VMEM((192, 4 * TOK), BF16)] * 2,
        ],
        limit=16,
    )(slices, others, after=(dq_a, feed_half))
    keep, send = call(functools.partial(halve_kernel, "z"), [((2, CHUNK, 768), BF16)] * 2)(keep, travel(send, "zb"))
    keep, send = call(functools.partial(halve_kernel, "y"), [((CHUNK, 768), BF16)] * 2)(keep, travel(send, "za"))
    sum_keep, sum_send = keep, send
    sums, keep, send, in_sums = call(
        weights_kernel,
        [((PARTS, ROW, 896), BF16), half, half, ((8, 768), F32)],
        [pltpu.VMEM((576, TOK), BF16)],
        limit=20,
        fetch=(0, 1, 2, 3, 4, 5, 6, 7, 8, 9, 10),
        store=(0,),
    )(inputs, in_gain, in_shift, weights, dq_near, *dqs, dkv, out_grad, vectors, after=(sum_keep,))
    got = lax.all_to_all(sums, SEQ, 0, 0, tiled=True)
    in_sums = in_sums + lax.ppermute(in_sums, "c", FLIP)
    in_sums = in_sums + lax.ppermute(in_sums, "yl", FLIP)
    have = call(chunk_sum_kernel, [((24, 768), BF16)] * 2)(
        sum_keep, lax.ppermute(sum_send, "yh", FLIP)
    )
    (have,) = call(reduce_kernel, [((24, 2432), BF16)])(got, in_sums, *have)
    in_half = add(keep, lax.ppermute(send, "c", FLIP))
    have = call(join_y_kernel, [((2, 24, 1152), BF16), ((2, 24, 1280), BF16)])(
        have, lax.ppermute(have, "yh", FLIP), after=(in_half,)
    )
    in_half = add(in_half, lax.ppermute(in_half, "yl", FLIP))
    have = call(
        functools.partial(join_kernel, ("zb1", "xb1")), [((2, 2, 24, 1152), BF16), ((2, 2, 24, 1280), BF16)]
    )(*have, *[travel(v, name) for v, name in zip(have, ("zb", "xb"))], after=(in_half,))
    feed_half = add(feed_half, lax.ppermute(feed_half, "yl", FLIP), after=(in_half,))
    feed_other = lax.ppermute(feed_half, "c", FLIP)
    (inputs_grad,) = call(
        input_grad_kernel, [((TOK, 768), BF16)], fetch=(0, 1, 2, 3), store=(0,), limit=12
    )(
        inputs, hidden_grad, in_gain, in_shift, in_half, lax.ppermute(in_half, "c", FLIP)
    )
    have = call(
        functools.partial(join_kernel, ("za2", "xa2")), [((4, 2, 24, 1152), BF16), ((4, 2, 24, 1280), BF16)]
    )(*have, *[travel(v, name) for v, name in zip(have, ("za", "xa"))], after=(feed_half,))
    have = call(split_kernel, [((4, 2, 24, w), BF16) for w in WIDTHS])(*have)
    have = call(
        functools.partial(join_kernel, ("xb1", "xa1", "zb1", "za1")), [((2, 4, 2, 24, w), BF16) for w in WIDTHS]
    )(*have, *[travel(v, name) for v, name in zip(have, ("xb", "xa", "zb", "za"))], behind=(inputs_grad,))
    down_grad, up_grad, head_grad, out_grad, *vectors = call(
        unpack_kernel,
        [
            ((PARTS, ROW, 768), F32),
            ((768, 768), F32),
            ((24, ROW, 768), F32),
            ((8, ROW, 768), F32),
            *[((768,), F32)] * 4,
            *[((192,), F32)] * 2,
            *[((768,), F32)] * 2,
        ],
        [pltpu.VMEM((PARTS, ROW, 768), F32), pltpu.VMEM((PARTS, ROW, 896), F32)],
        limit=40,
        store=(0, 1, 2, 3),
    )(*have, *[travel(v, name) for v, name in zip(have, ("xa", "xb", "za", "zb"))])
    feed_out = jnp.where(
        core == 0, jnp.concatenate([feed_half, feed_other]), jnp.concatenate([feed_other, feed_half])
    ).astype(F32)
    result = jnp.where(row_valid, hidden + feed_out, 0.0).astype(BF16)
    return (
        result,
        inputs_grad,
        head_grad.reshape(3, 192, 768).transpose(0, 2, 1),
        out_grad.reshape(192, 768),
        up_grad,
        down_grad.reshape(768, 768),
        vectors[6],
        vectors[7],
        vectors[4],
        vectors[5],
        vectors[0],
        vectors[1],
        vectors[2],
        vectors[3],
    )


def solution(mesh):
    fine = Mesh(np.asarray(mesh.devices).reshape(4, 2, 4, 2, 2), SEQ + TENSOR)
    in_specs = (
        P(SEQ, None),
        P(None, None, TENSOR),
        P(TENSOR, None),
        P(None, TENSOR),
        P(TENSOR, None),
        P(),
        P(),
        P(TENSOR),
        P(TENSOR),
        P(),
        P(),
        P(TENSOR),
        P(TENSOR),
        P(),
        P(SEQ, None),
    )
    out_specs = (
        P(SEQ, None),
        P(SEQ, None),
        P(None, None, TENSOR),
        P(TENSOR, None),
        P(None, TENSOR),
        P(TENSOR, None),
        P(),
        P(),
        P(TENSOR),
        P(TENSOR),
        P(),
        P(),
        P(TENSOR),
        P(TENSOR),
    )
    return jax.shard_map(per_device, mesh=fine, in_specs=in_specs, out_specs=out_specs, check_vma=False)
```

```python
import functools
import itertools

import jax
import jax.numpy as jnp
import numpy as np
from jax import lax
from jax.experimental import pallas as pl
from jax.experimental.pallas import tpu as pltpu
from jax.sharding import Mesh
from jax.sharding import PartitionSpec as P


HDIM = 64
HEADS_HERE = 3
TOK = 256
PLANE = 8
SLOTS = 128
KEYS = PLANE * SLOTS
PARTS = 32
ROW = 24
EPSILON = 1e-05
NONE = -1e30
NEAR = (1, 2, 4, 6, 12)
MID = (2, 4, 6, 12)
FAR = (4, 6, 12)
F32 = jnp.float32
BF16 = jnp.bfloat16
SEQ = ("z", "yh", "x")
TENSOR = ("yl", "c")
FLIP = [(0, 1), (1, 0)]
NN = ((1,), (0,))
NT = ((1,), (1,))
TN = ((0,), (0,))


class Here:
    def __init__(self):
        self.plane, y, self.x = (lax.axis_index(a) for a in SEQ)
        low, self.core = (lax.axis_index(a) for a in TENSOR)
        self.y = y
        self.place = y * 4 + self.x
        self.tensor = low * 2 + self.core
        self.head0 = self.tensor * HEADS_HERE
        self.base = (self.plane * PLANE + self.place) * TOK


def dot(a, b, dims=NN):
    return lax.dot_general(a, b, (dims, ((), ())), preferred_element_type=F32)


def split3(v):
    hi = v.astype(BF16).astype(F32)
    mid = (v - hi).astype(BF16).astype(F32)
    return hi, mid, v - hi - mid


def mid_offsets(head):
    slot = lax.broadcasted_iota(jnp.int32, (1, SLOTS), 1)
    return 2 * slot + lax.rem(head, 2)


def far_offsets(head, base):
    slot = lax.broadcasted_iota(jnp.int32, (1, SLOTS), 1)
    which = lax.rem(slot, 4)
    kind = jnp.where(which == 0, 0, 2 * which + 2)
    first = lax.div(base + 12 - head, 12) - 1
    return 12 * (first + lax.div(slot, 4)) + kind + head - base, kind


def one_hot_rows(offsets):
    rows = lax.broadcasted_iota(jnp.int32, (TOK, SLOTS), 0)
    return (rows == offsets).astype(F32).astype(BF16)


def picks(head, base):
    return one_hot_rows(mid_offsets(head)), one_hot_rows(far_offsets(head, base)[0])


def count_table(kind, usable, dilations):
    row = lax.broadcasted_iota(jnp.int32, (16, kind.shape[1]), 0)
    count = jnp.zeros(row.shape, F32)
    for step in dilations:
        count += jnp.where((lax.rem(row, step) == 0) & (lax.rem(kind, step) == 0), 1.0, 0.0)
    live = (count > 0) & usable & (row < 12)
    log_count = jnp.log(jnp.maximum(count, 1.0))
    hi = log_count.astype(BF16).astype(F32)
    return jnp.where(live, hi, NONE), jnp.where(live, log_count - hi, 0.0)


def score_columns(ref, lo, kind, usable, dilations):
    hi, low = count_table(kind, usable, dilations)
    return jnp.concatenate([ref[lo : lo + HDIM, :].astype(F32) * 0.125, hi, low], 0)


def own_columns(head, base, q, lo):
    kind = lax.rem(base - head + 12 + lax.broadcasted_iota(jnp.int32, (1, TOK), 1), 12)
    return score_columns(q, lo, kind, kind >= 0, NEAR)


def query_columns(head, base, plane, visitors, lo):
    if len(visitors) == 1:
        at = mid_offsets(head)
        return score_columns(visitors[0], lo, lax.rem(base + 2048 + at - head + 12, 12), at >= 0, MID)
    parts = []
    for visitor, origin in zip(visitors, (plane + 2, 3 - plane)):
        at, kind = far_offsets(head, origin * 2048 + lax.rem(base, 2048))
        parts.append(score_columns(visitor, lo, kind, (at >= 0) & (at < TOK), FAR))
    return jnp.concatenate(parts, 1)


def one_hot_kind(kind):
    return (kind == lax.broadcasted_iota(jnp.int32, (16, kind.shape[1]), 0)).astype(F32).astype(BF16)


def ones(rows, columns):
    return jnp.ones((rows, columns), BF16)


def diagonal_mask(base, valid):
    rows = lax.broadcasted_iota(jnp.int32, (TOK, TOK), 0)
    cols = lax.broadcasted_iota(jnp.int32, (TOK, TOK), 1)
    return (cols <= rows) & (cols + base < valid)


def norm_rows(v, gain, shift):
    mean = jnp.sum(v, 1, keepdims=True) / v.shape[1]
    spread = jnp.sum(v * v, 1, keepdims=True) / v.shape[1] - mean * mean
    scale = lax.rsqrt(spread + EPSILON)
    unit = (v - mean) * scale
    return unit * gain + shift, unit, scale


def norm_rows_back(grad, unit, scale, gain):
    q = grad * gain
    n = grad.shape[1]
    return scale * (q - jnp.sum(q, 1, keepdims=True) / n - unit * (jnp.sum(q * unit, 1, keepdims=True) / n))


def project_kernel(inputs, weights, gain, shift, q, spread):
    v = norm_rows(inputs[...].astype(F32), gain[...], shift[...])[0].astype(BF16)
    spread[0, 0:192, :] = dot(weights[1], v, NT).astype(BF16)
    spread[0, 192:384, :] = dot(weights[2], v, NT).astype(BF16)
    for i in range(1, PLANE):
        spread[i] = spread[0]
    q[...] = dot(weights[0], v, NT).astype(BF16)


def select_kernel(q, out_weight, mix_gain, mix_shift, q_mid, q_far, packed):
    here = Here()
    head0, base = here.head0, here.base
    for h in range(HEADS_HERE):
        rows = slice(h * HDIM, (h + 1) * HDIM)
        pick_mid, pick_far = picks(head0 + h, base)
        q_mid[rows, :] = dot(q[rows, :], pick_mid).astype(BF16)
        q_far[rows, :] = dot(q[rows, :], pick_far).astype(BF16)
    packed[0:192, :] = out_weight[...]
    terms = list(split3(mix_gain[...])) + list(split3(mix_shift[...])) + [jnp.zeros((10, 192), F32)]
    packed[192:208, 0:192] = jnp.concatenate(terms, 0).astype(BF16)


def weigh(s):
    return jnp.exp(s).astype(BF16)


def widest(s):
    return functools.reduce(jnp.maximum, [s[:, i * 128 : (i + 1) * 128] for i in range(s.shape[1] // 128)])


def shifted(m, rows):
    top = jnp.max(m.T, 0, keepdims=True)
    minus = jnp.concatenate(list(split3(-top)) + [jnp.zeros((29, top.shape[1]), F32)], 0)
    return top, jnp.concatenate([rows, minus], 0).T.astype(BF16)


def near_keys(kvs, block, lo, head, base):
    kind = lax.rem(base - head + 12 + lax.broadcasted_iota(jnp.int32, (1, TOK), 1), 12)
    hot = one_hot_kind(kind)
    return jnp.concatenate([kvs[block, lo : lo + HDIM, :], hot, hot, ones(32, TOK)], 0)


def near_values(kvs, block, lo):
    return jnp.concatenate([kvs[block, 192 + lo : 192 + lo + HDIM, :], ones(16, TOK)], 0)


def gather_keys(kvs, head0, plane, far, rights, values):
    for h in range(HEADS_HERE):
        lo, head = h * HDIM, head0 + h
        for k in range(PLANE):
            start = plane * 2048 + k * TOK
            if far:
                offsets, kind = far_offsets(head, start)
                kind = jnp.where((offsets >= 0) & (offsets < TOK), kind, 12)
            else:
                offsets = mid_offsets(head)
                kind = lax.rem(start + offsets - head + 12, 12)
            both = jnp.concatenate([kvs[k, lo : lo + HDIM, :], kvs[k, 192 + lo : 192 + lo + HDIM, :]], 0)
            at = slice(k * SLOTS, (k + 1) * SLOTS)
            small = dot(both, one_hot_rows(offsets)).astype(BF16)
            hot = one_hot_kind(kind)
            rights[h, :, at] = jnp.concatenate([small[0:HDIM], hot, hot, ones(32, SLOTS)], 0)
            values[h, :, at] = jnp.concatenate([small[HDIM:], ones(16, SLOTS)], 0)


def forward_far_kernel(qa, qb, qc, kvs, pay_a, pay_b, pay_c, loc, right_a, right_f, value_a, value_f):
    here = Here()
    head0, base, plane = here.head0, here.base, here.plane
    heads = range(HEADS_HERE)
    row = lax.broadcasted_iota(jnp.int32, (16, SLOTS), 0)
    loc[...] = jnp.zeros(loc.shape, F32)

    def attend(queries, rights, values, first, pays):
        extra = [jnp.where(row == 9, 1.0, 0.0) for _ in pays]
        rows = [query_columns(head0 + h, base, plane, queries, h * HDIM) for h in heads]
        zeros = jnp.zeros((32, SLOTS * len(pays)), F32)
        marks = [widest(dot(jnp.concatenate([rows[h], zeros], 0).T.astype(BF16), rights[h])) for h in heads]
        lefts = [shifted(marks[h], rows[h]) for h in heads]
        accs = [dot(values[h], weigh(dot(lefts[h][1], rights[h])), NT) for h in heads]
        for h in heads:
            total = accs[h][64:65, :]
            log = jnp.maximum(lefts[h][0] + jnp.log(total), NONE)
            out = accs[h][0:64, :] / total
            for i, pay in enumerate(pays):
                at = slice(i * SLOTS, (i + 1) * SLOTS)
                loc[h : h + 1, first + i * SLOTS : first + (i + 1) * SLOTS] = log[:, at]
                pay[h * HDIM : (h + 1) * HDIM, :] = out[:, at].astype(BF16)
                for j, term in enumerate(split3(log[:, at])):
                    extra[i] = jnp.where(row == 3 * h + j, term, extra[i])
        for e, pay in zip(extra, pays):
            pay[192:208, :] = e.astype(BF16)

    @pl.when(lax.rem(plane, 2) == 0)
    def _():
        gather_keys(kvs, head0, plane, False, right_a, value_a)
        attend((qa,), right_a, value_a, 0, (pay_a,))

    @pl.when(plane < 2)
    def _():
        gather_keys(kvs, head0, plane, True, right_f, value_f)
        attend((qb, qc), right_f, value_f, SLOTS, (pay_b, pay_c))


def forward_near_kernel(length, q, kvs, o_near, st_near, right, rows, left, marks, acc):
    here, valid = Here(), length[0]
    head0, base, place = here.head0, here.base, here.place
    heads = range(HEADS_HERE)
    for h in heads:
        lo = h * HDIM
        head = head0 + h
        rows[h] = own_columns(head, base, q, lo)
        left[h] = jnp.concatenate([rows[h], jnp.zeros((32, TOK), F32)], 0).T.astype(BF16)
    marks[...] = jnp.full(marks.shape, 2 * NONE, F32)
    wait_for(kvs)
    for k in range(PLANE):

        @pl.when(k <= place)
        def _():
            for h in heads:
                right[h, k] = near_keys(kvs, place - k, h * HDIM, head0 + h, base - k * TOK)
                s = dot(left[h], right[h, k])
                if k == 0:
                    s = jnp.where(diagonal_mask(base, valid), s, NONE)
                marks[h] = jnp.maximum(marks[h], widest(s))

    tops = []
    for h in heads:
        top, turned = shifted(marks[h], rows[h])
        tops.append(top)
        left[h] = turned
    acc[...] = jnp.zeros(acc.shape, F32)
    for k in range(PLANE):

        @pl.when(k <= place)
        def _():
            for h in heads:
                lo = h * HDIM
                s = dot(left[h], right[h, k])
                if k == 0:
                    s = jnp.where(diagonal_mask(base, valid), s, NONE)
                acc[h] += dot(near_values(kvs, place - k, lo), weigh(s), NT)

    st_near[...] = jnp.zeros(st_near.shape, F32)
    for h in heads:
        total = acc[h, 64:65, :]
        o_near[h * HDIM : (h + 1) * HDIM, :] = acc[h, 0:64, :] / total
        st_near[h : h + 1, :] = tops[h] + jnp.log(total)


def combine_kernel(o_near, st_near, ra, rb, rc, mixed, st_all):
    here = Here()
    head0, base = here.head0, here.base
    st_all[...] = jnp.zeros(st_all.shape, F32)
    for h in range(HEADS_HERE):
        rows = slice(h * HDIM, (h + 1) * HDIM)
        pick_mid, pick_far = picks(head0 + h, base)
        outs, logs = [o_near[rows, :]], [st_near[h : h + 1, :]]
        for pay, pick in ((ra, pick_mid), (rb, pick_far), (rc, pick_far)):
            wide = dot(jnp.concatenate([pay[rows, :], pay[192:208, :]], 0), pick, NT)
            log = wide[64 + 3 * h : 65 + 3 * h] + wide[65 + 3 * h : 66 + 3 * h] + wide[66 + 3 * h : 67 + 3 * h]
            outs.append(wide[0:64])
            logs.append(jnp.where(wide[73:74] > 0.5, log, NONE))
        top = functools.reduce(jnp.maximum, logs)
        weights = [jnp.exp(v - top) for v in logs]
        total = sum(weights)
        mixed[rows, :] = sum((w / total) * o for w, o in zip(weights, outs)).astype(BF16)
        st_all[h : h + 1, :] = top + jnp.log(total)
        for i in range(3):
            st_all[3 + 3 * i + h : 4 + 3 * i + h, :] = weights[i + 1] / total


def mix_norm(pieces):
    first = sum(jnp.sum(pieces[i].astype(F32), 0, keepdims=True) for i in range(4)) / 768
    second = sum(jnp.sum(jnp.square(pieces[i].astype(F32)), 0, keepdims=True) for i in range(4)) / 768
    return first, lax.rsqrt(second - first * first + EPSILON)


def mix_parameters(packed, i):
    tail = jnp.concatenate([packed[i, 192:208, 0:256].astype(F32), jnp.zeros((112, 256), F32)], 0).T[0:192]
    return tail[:, 0:1] + tail[:, 1:2] + tail[:, 2:3], tail[:, 3:4] + tail[:, 4:5] + tail[:, 5:6]


def gelu_parts(v):
    a, b = 0.7978845608028654, 0.044715
    square = v * v
    t = jnp.tanh(a * v * (1.0 + b * square))
    active = 0.5 * v * (1.0 + t)
    slope = 0.5 * (1.0 + t) + 0.5 * v * (1.0 - t * t) * (a * (1.0 + 3.0 * b * square))
    return active, slope


def half_blocks(core, v):
    half = jnp.where(core == 0, v[0:128], v[128:256])
    return jnp.concatenate([half[:, i * 256 : (i + 1) * 256] for i in range(3)], 0).astype(BF16)


def feed_kernel(length, down, cotangent, feed_blocks, inner_grad):
    here = Here()
    row = here.base + lax.broadcasted_iota(jnp.int32, (TOK, 1), 0)
    feed = jnp.where(row < length[0], cotangent[...].astype(F32), 0.0)
    feed_blocks[...] = half_blocks(here.core, feed)
    grad = dot(feed.astype(BF16), down[...], NT)
    inner_grad[...] = grad


def middle_kernel(
    inputs, pieces, packed, up, gain, shift, inner_gain, inner_grad, st_all,
    hidden, pieces_kept, st_kept, mid_blocks, pre, sums,
):
    st_kept[...] = st_all[...]
    st_kept.flush()
    pieces.wait()
    pieces_kept[...] = pieces[...]
    pieces_kept.flush()
    mean, scale = mix_norm(pieces)
    total = inputs[...].astype(F32)
    branch = None
    for i in range(4):
        mix_gain, mix_shift = mix_parameters(packed, i)
        low = ((pieces[i].astype(F32) - mean) * scale * mix_gain + mix_shift).astype(BF16)
        term = dot(low, packed[i, 0:192, :], TN)
        branch = term if branch is None else branch + term
    total = total + branch
    hidden[...] = total
    hidden.flush()
    low = norm_rows(total, gain[...], shift[...])[0]
    mid_blocks[...] = half_blocks(Here().core, low)
    pre[...] = dot(low.astype(BF16), up[...])
    active = gelu_parts(pre[...])[0]
    lane = lax.broadcasted_iota(jnp.int32, (1, 128), 1)
    st = jnp.zeros((TOK, 128), F32)
    scaled = inner_grad[...] * inner_gain[...]
    for i, v in enumerate((active, active * active, scaled, scaled * active)):
        st = jnp.where(lane == i, jnp.sum(v, 1, keepdims=True), st)
    sums[...] = st.T[0:8]


def halves(core, v, keep, send):
    for c in range(2):

        @pl.when(core == c)
        def _():
            keep[...] = v[c * 128 : (c + 1) * 128].astype(BF16)
            send[...] = v[(1 - c) * 128 : (2 - c) * 128].astype(BF16)


def whole(core, own, other):
    return jnp.concatenate([jnp.where(core == 0, own, other), jnp.where(core == 0, other, own)], 0)


def inner_kernel(sums, pre, inner_grad, up, gain, shift, inner_low, pre_grad, keep, send, vectors):
    st = jnp.concatenate([sums[...], jnp.zeros((120, TOK), F32)], 0).T
    width = 3072
    mean = st[:, 0:1] / width
    scale = lax.rsqrt(st[:, 1:2] / width - mean * mean + EPSILON)
    first = st[:, 2:3]
    second = scale * (st[:, 3:4] - mean * first)
    active, slope = gelu_parts(pre[...])
    unit = (active - mean) * scale
    inner_low[...] = (unit * gain[...] + shift[...]).astype(BF16)
    grad = inner_grad[...]
    vectors[...] = jnp.zeros(vectors.shape, F32)
    vectors[0:1, :] = jnp.sum(grad * unit, 0, keepdims=True)
    vectors[1:2, :] = jnp.sum(grad, 0, keepdims=True)
    back = scale * (grad * gain[...] - first / width - unit * (second / width))
    low = (back * slope).astype(BF16)
    pre_grad[...] = low
    halves(Here().core, dot(low, up[...], NT), keep, send)


def outer_kernel(
    length, mid_own, mid_got, other_own, other_got, hidden, cotangent, gain, shift, pieces, packed, st_all,
    inner_vectors, hidden_grad, grad_mixed, st_near, pay_a, pay_b, pay_c, out_grad, all_vectors, scratch,
):
    here, valid = Here(), length[0]
    head0, base, tensor = here.head0, here.base, here.tensor
    row = base + lax.broadcasted_iota(jnp.int32, (TOK, 1), 0)
    upstream = jnp.where(row < valid, cotangent[...].astype(F32), 0.0)
    _, unit, scale = norm_rows(hidden[...], gain[...], shift[...])
    own = mid_own[...].astype(F32) + mid_got[...].astype(F32)
    grad = whole(here.core, own, other_own[...].astype(F32) + other_got[...].astype(F32))
    vectors = [jnp.sum(grad * unit, 0, keepdims=True), jnp.sum(grad, 0, keepdims=True)]
    total = upstream + norm_rows_back(grad, unit, scale, gain[...])
    hidden_grad[...] = total
    hidden_grad.flush()
    branch = total.astype(BF16)

    mean, scale = mix_norm(pieces)
    first, second = jnp.zeros((1, TOK), F32), jnp.zeros((1, TOK), F32)
    for i in range(4):
        grad = dot(packed[i, 0:192, :], branch, NT)
        scratch[i] = grad
        q = grad * mix_parameters(packed, i)[0]
        first += jnp.sum(q, 0, keepdims=True)
        second += jnp.sum(q * (pieces[i].astype(F32) - mean), 0, keepdims=True)
    second = second * scale
    output = pieces[tensor].astype(F32)
    unit = (output - mean) * scale
    grad = scratch[tensor]
    gain_own, shift_own = mix_parameters(packed, tensor)
    low = (unit * gain_own + shift_own).astype(BF16)
    lane = lax.broadcasted_iota(jnp.int32, (1, 128), 1)
    columns = jnp.where(
        lane == 0, jnp.sum(grad * unit, 1, keepdims=True), jnp.where(lane == 1, jnp.sum(grad, 1, keepdims=True), 0.0)
    )
    vectors += [inner_vectors[0:2], jnp.concatenate([columns.T[0:2], jnp.zeros((2, 576), F32)], 1)]
    all_vectors[...] = jnp.concatenate(vectors + [jnp.zeros((2, 768), F32)], 0)
    out_grad[...] = dot(low, branch).astype(BF16)
    out_grad.flush()
    all_vectors.flush()
    back = scale * (grad * gain_own - first / 768 - unit * (second / 768))
    back = back.astype(BF16).astype(F32)
    grad_mixed[...] = back.astype(BF16)
    st_near[...] = jnp.zeros(st_near.shape, F32)
    tails = [[], [], []]
    for h in range(HEADS_HERE):
        rows = slice(h * HDIM, (h + 1) * HDIM)
        mine = back[rows]
        centre = jnp.sum(mine * output[rows], 0, keepdims=True)
        st_near[h : h + 1, :] = st_all[h : h + 1, :]
        st_near[3 + h : 4 + h, :] = centre
        pick_mid, pick_far = picks(head0 + h, base)
        for i, (pay, pick) in enumerate(((pay_a, pick_mid), (pay_b, pick_far), (pay_c, pick_far))):
            share = st_all[3 + 3 * i + h : 4 + 3 * i + h, :]
            terms = list(split3(centre * share)) + [jnp.zeros((13, TOK), F32)]
            wide = jnp.concatenate([mine * share] + terms, 0).astype(BF16)
            small = dot(wide, pick)
            pay[rows, :] = small[0:64].astype(BF16)
            tails[i].append(small[64:67])
    for pay, tail in zip((pay_a, pay_b, pay_c), tails):
        pay[192:208, :] = jnp.concatenate(tail + [jnp.zeros((7, SLOTS), F32)], 0).astype(BF16)


def gradients(left, grad_left, rows_q, rows_g, rights, values, mask=None):
    s = dot(left, rights)
    if mask is not None:
        s = jnp.where(mask, s, NONE)
    w = jnp.exp(s)
    ds = (w * dot(grad_left, values)).astype(BF16)
    dq = dot(rights[0:64], ds, NT)
    return dq, jnp.concatenate([dot(rows_q, ds), dot(rows_g, w.astype(BF16))], 0)


def with_logs(rows, logs):
    minus = split3(jnp.where(logs > NONE * 0.1, -logs, 0.0))
    return jnp.concatenate([rows] + list(minus) + [jnp.zeros((29, logs.shape[1]), F32)], 0)


def with_centres(rows, centres):
    return jnp.concatenate([rows] + list(split3(-centres)) + [jnp.zeros((13, centres.shape[1]), F32)], 0)


def backward_near_kernel(length, q, grad, st, kvs, dq_near, dkv, rows_q, rows_g, left, grad_left, acc_q):
    here, valid = Here(), length[0]
    head0, base, place = here.head0, here.base, here.place
    heads = range(HEADS_HERE)
    for h in heads:
        lo = h * HDIM
        rows = with_logs(own_columns(head0 + h, base, q, lo), st[h : h + 1, :])
        rows_q[h] = rows[0:64].astype(BF16)
        left[h] = rows.T.astype(BF16)
        rows = with_centres(grad[lo : lo + HDIM, :].astype(F32), st[3 + h : 4 + h, :])
        rows_g[h] = rows[0:64].astype(BF16)
        grad_left[h] = rows.T.astype(BF16)
    acc_q[...] = jnp.zeros(acc_q.shape, F32)
    for k in range(PLANE):
        block = lax.rem(place - k + PLANE, PLANE)

        @pl.when(k > place)
        def _():
            dkv[block] = jnp.zeros((384, TOK), BF16)

        @pl.when(k <= place)
        def _():
            mask = diagonal_mask(base, valid) if k == 0 else None
            for h in heads:
                lo = h * HDIM
                keys = near_keys(kvs, place - k, lo, head0 + h, base - k * TOK)
                values = near_values(kvs, place - k, lo)
                dq, both = gradients(left[h], grad_left[h], rows_q[h], rows_g[h], keys, values, mask)
                acc_q[h] += dq
                dkv[block, lo : lo + HDIM, :] = both[0:64].astype(BF16)
                dkv[block, 192 + lo : 192 + lo + HDIM, :] = both[64:128].astype(BF16)

        dkv.flush_part(block)

    for h in heads:
        dq_near[h * HDIM : (h + 1) * HDIM, :] = acc_q[h] * 0.125


def backward_far_kernel(dkv_near, qa, qb, qc, ga, gb, gc, loc, kvs, *refs):
    dq_a, dq_b, dq_c, dkv, small_a, small_f, right_a, right_f, value_a, value_f = refs
    here = Here()
    head0, base, plane = here.head0, here.base, here.plane
    heads = range(HEADS_HERE)
    wait_for(qa, qb, qc, loc)

    def part(queries, pays, first, rights, values, dqs, small):
        n = SLOTS * len(pays)
        for h in heads:
            lo = h * HDIM
            rows = query_columns(head0 + h, base, plane, queries, lo)
            rows = with_logs(rows, loc[h : h + 1, first : first + n])
            columns, centres = [], []
            for pay in pays:
                columns.append(pay[lo : lo + HDIM, :].astype(F32))
                tail = pay[192:208, :].astype(F32)
                centres.append(tail[3 * h : 3 * h + 1] + tail[3 * h + 1 : 3 * h + 2] + tail[3 * h + 2 : 3 * h + 3])
            grads = with_centres(jnp.concatenate(columns, 1), jnp.concatenate(centres, 1))
            dq, both = gradients(
                rows.T.astype(BF16),
                grads.T.astype(BF16),
                rows[0:64].astype(BF16),
                grads[0:64].astype(BF16),
                rights[h],
                values[h],
            )
            dq = (dq * 0.125).astype(BF16)
            for i, out in enumerate(dqs):
                out[lo : lo + HDIM, :] = dq[:, i * SLOTS : (i + 1) * SLOTS]
            small[h] = both.astype(BF16)

    @pl.when((plane == 1) | (plane == 2))
    def _():
        small_a[...] = jnp.zeros(small_a.shape, BF16)
        small_f[...] = jnp.zeros(small_f.shape, BF16)

    @pl.when(lax.rem(plane, 2) == 0)
    def _():
        gather_keys(kvs, head0, plane, False, right_a, value_a)
        part((qa,), (ga,), 0, right_a, value_a, (dq_a,), small_a)

    @pl.when(plane < 2)
    def _():
        gather_keys(kvs, head0, plane, True, right_f, value_f)
        part((qb, qc), (gb, gc), SLOTS, right_f, value_f, (dq_b, dq_c), small_f)

    wait_for(dkv_near)

    @pl.when(plane == 3)
    def _():
        dkv[...] = dkv_near[...]
        for block in range(PLANE):
            dkv.flush_part(block)

    @pl.when(plane < 3)
    def _():
        for block in range(PLANE):
            at = slice(block * SLOTS, (block + 1) * SLOTS)
            for h in heads:
                lo = h * HDIM
                pick = jnp.concatenate(picks(head0 + h, plane * 2048 + block * TOK), 1)
                wide = dot(jnp.concatenate([small_a[h, :, at], small_f[h, :, at]], 1), pick, NT)
                for i, at_row in ((0, lo), (64, 192 + lo)):
                    near = dkv_near[block, at_row : at_row + HDIM, :].astype(F32)
                    dkv[block, at_row : at_row + HDIM, :] = (near + wide[i : i + 64]).astype(BF16)
            dkv.flush_part(block)


def weights_kernel(
    inputs, gain, shift, weights, dq_near, ra, rb, rc, dkv, out_grad, vectors, sums, keep, send, in_sums, grads
):
    here = Here()
    head0, base = here.head0, here.base
    normed, unit, _ = norm_rows(inputs[...].astype(F32), gain[...], shift[...])
    for h in range(HEADS_HERE):
        rows = slice(h * HDIM, (h + 1) * HDIM)
        pick_mid, pick_far = picks(head0 + h, base)
        dq = dq_near[rows, :] + dot(ra[rows, :], pick_mid, NT) + dot(rb[rows, :], pick_far, NT) + dot(rc[rows, :], pick_far, NT)
        grads[rows, :] = dq.astype(BF16)
    total = dkv[0].astype(F32)
    for k in range(1, PLANE):
        total += dkv[k].astype(F32)
    grads[192:576, :] = total.astype(BF16)
    sums[0:24, :, 0:768] = dot(grads[...], normed.astype(BF16)).reshape(24, ROW, 768).astype(BF16)
    sums[24:32, :, 0:768] = out_grad[...].astype(F32).reshape(8, ROW, 768).astype(BF16)
    sums[:, :, 768:896] = jnp.zeros((PARTS, ROW, 128), BF16)
    mixed = jnp.concatenate([vectors[4:5, 0:192], vectors[5:6, 0:192], jnp.zeros((1, 384), F32)], 1)
    for i, v in enumerate((vectors[0:1], vectors[1:2], vectors[2:3], vectors[3:4], mixed)):
        rows = [v[:, j * 128 : (j + 1) * 128] for j in range(6)] + [jnp.zeros((2, 128), F32)]
        sums[i, 0:8, 768:896] = jnp.concatenate(rows, 0).astype(BF16)
    sums.flush()
    back = dot(grads[0:192, :], weights[0], TN)
    back += dot(grads[192:384, :], weights[1], TN)
    back += dot(grads[384:576, :], weights[2], TN)
    halves(here.core, back, keep, send)
    rows = [jnp.sum(back * unit, 0, keepdims=True), jnp.sum(back, 0, keepdims=True), jnp.zeros((6, 768), F32)]
    in_sums[...] = jnp.concatenate(rows, 0)


def reduce_kernel(got, in_sums, down, up, out):
    total = got[0].astype(F32)
    for i in range(1, PARTS):
        total += got[i].astype(F32)
    rows = [[in_sums[j : j + 1, i * 128 : (i + 1) * 128] for i in range(6)] + [jnp.zeros((2, 128), F32)] for j in (0, 1)]
    out[:, 0:768] = down[...]
    out[:, 768:1152] = total[:, 0:384].astype(BF16)
    out[:, 1152:1920] = up[...]
    out[:, 1920:2304] = total[:, 384:768].astype(BF16)
    out[:, 2304:2432] = jnp.concatenate([total[0:8, 768:896], *rows[0], *rows[1]], 0).astype(BF16)


def input_grad_kernel(inputs, hidden_grad, gain, shift, own, other, inputs_grad):
    _, unit, scale = norm_rows(inputs[...].astype(F32), gain[...], shift[...])
    grad = whole(Here().core, own[...].astype(F32), other[...].astype(F32))
    inputs_grad[...] = (hidden_grad[...] + norm_rows_back(grad, unit, scale, gain[...])).astype(BF16)


CHUNK = 48
PAIR_A = [(0, 1), (1, 0), (2, 3), (3, 2)]
PAIR_B = [(0, 3), (3, 0), (1, 2), (2, 1)]
STEPS = {"xa": ("x", PAIR_A), "xb": ("x", PAIR_B), "za": ("z", PAIR_A), "zb": ("z", PAIR_B)}


def travel(v, name):
    axis, perm = STEPS[name]
    return lax.ppermute(v, axis, perm)


def slices_kernel(inner_low, pre_grad, mid_blocks, feed_blocks, down, slices, feed_keep, feed_send):
    for first, ref in ((0, inner_low), (192, pre_grad)):
        turned = ref[...].astype(F32).T.astype(BF16)
        for i in range(4):
            slices[i, first : first + 192, :] = turned[i * 192 : (i + 1) * 192]
    for i in range(4):
        slices[i, 384:768, :] = mid_blocks[...]
        slices[i, 768:1152, :] = feed_blocks[...]
    slices.flush()
    halves(Here().core, dot(inner_low[...], down[...]), feed_keep, feed_send)


def products_kernel(slices, others, keep, send, full, *operands):
    here = Here()
    products = []
    for (first, second), rows, columns in zip(((0, 768), (192, 384)), operands[0:2], operands[2:4]):
        for i in range(4):
            columns[:, i * TOK : (i + 1) * TOK] = slices[i, first : first + 192, :]
            for b in range(3):
                block = slice(b * 256, (b + 1) * 256)
                own = pl.multiple_of(i * TOK + here.core * 128, 128)
                other = pl.multiple_of(i * TOK + 128 - here.core * 128, 128)
                rows[pl.ds(own, 128), block] = slices[i, second + b * 128 : second + (b + 1) * 128, :]
                rows[pl.ds(other, 128), block] = others[i, second + b * 128 : second + (b + 1) * 128, :]
        products.append(dot(columns[...], rows[...]))
    down, up = products
    full[:, :, 0:24, :] = down.reshape(4, 2, 24, 768).astype(BF16)
    full[:, :, 24:48, :] = up.reshape(4, 2, 24, 768).astype(BF16)
    high = lax.div(here.plane, 2)
    keep[...] = full[pl.ds(2 * high, 2)]
    send[...] = full[pl.ds(2 - 2 * high, 2)]


def halve_kernel(axis, keep, got, new_keep, new_send):
    i = lax.rem(Here().plane, 2) if axis == "z" else Here().y
    new_keep[...] = (keep[i].astype(F32) + got[i].astype(F32)).astype(BF16)
    new_send[...] = (keep[1 - i].astype(F32) + got[1 - i].astype(F32)).astype(BF16)


def chunk_sum_kernel(keep, got, down, up):
    total = keep[...].astype(F32) + got[...].astype(F32)
    down[...] = total[0:24].astype(BF16)
    up[...] = total[24:48].astype(BF16)


def join_y_kernel(own, other, down, up):
    y = Here().y
    for at, part in ((y, own), (1 - y, other)):
        down[at] = part[:, 0:1152]
        up[at] = part[:, 1152:2432]


def join_pair(i, name, own, other, out):
    high = lax.div(i, 2)
    if name == "b1":
        out[high] = own[...]
        out[1 - high] = other[...]
    elif name == "a1":
        low = lax.rem(i, 2)
        out[low] = own[...]
        out[1 - low] = other[...]
    elif name == "a2":
        first = jnp.where(high == 0, i, 3 - i)
        out[first] = own[0]
        out[3 - first] = own[1]
        out[1 - first] = other[0]
        out[2 + first] = other[1]
    else:
        out[pl.ds(2 * high, 2)] = own[...]
        out[pl.ds(2 - 2 * high, 2)] = other[...]


def join_kernel(step, own, other, out):
    here = Here()
    join_pair(here.x if step[0] == "x" else here.plane, step[1:], own, other, out)


def join(v, step, after=(), behind=()):
    shape = (4, *v.shape[1:]) if step[2] == "2" else (2, *v.shape)
    (out,) = call(functools.partial(join_kernel, step), [(shape, v.dtype)])(
        v, travel(v, step[0:2]), after=after, behind=behind
    )
    return out


WIDTHS = (512, 640, 640, 640)


def split_kernel(tail_width, full, first, second):
    columns = ((0, 384), (384, 768))
    for out, (lo, hi) in zip((first, second), columns):
        out[:, :, :, 0:384] = full[:, :, :, lo:hi]
    first[:, :, :, 384:] = full[:, :, :, 768 : 768 + tail_width]
    second[:, :, :, 384:] = full[:, :, :, 768 + tail_width :]


def split(v, widths):
    return call(functools.partial(split_kernel, widths[0] - 384), [((4, 2, 24, w), BF16) for w in widths])(v)


def last_places(i, step):
    high = lax.div(i, 2)
    if step == "a":
        first = jnp.where(high == 0, i, 3 - i)
        return (first, 3 - first), (1 - first, 2 + first)
    return (2 * high, 2 * high + 1), (2 - 2 * high, 3 - 2 * high)


def unpack_down_kernel(own0, own1, other0, other1, down, tail):
    x_now = Here().x
    for d, z, y, e in itertools.product(range(2), range(4), range(2), range(2)):
        places = last_places(x_now, "ab"[d])
        for pair, side in ((0, (own0, own1)), (1, (other0, other1))):
            x = places[pair][e]
            value = side[d][e, z, y]
            down[x * 8 + z * 2 + y, :, d * 384 : (d + 1) * 384] = value[:, 0:384].astype(F32)
            tail[z * 8 + y * 4 + x, :, d * 128 : 128 + d * 256] = value[:, 384:]


def unpack_kernel(tail_d, own0, own1, other0, other1, up, head_grad, out_grad, *rest):
    *vectors, up_turned, tail = rest
    plane = Here().plane
    for d, x, y, e in itertools.product(range(2), range(4), range(2), range(2)):
        places = last_places(plane, "ab"[d])
        for pair, side in ((0, (own0, own1)), (1, (other0, other1))):
            z = places[pair][e]
            value = side[d][e, x, y].astype(F32)
            up_turned[x * 8 + z * 2 + y, :, d * 384 : (d + 1) * 384] = value[:, 0:384]
            tail[z * 8 + y * 4 + x, :, d * 256 : 256 + d * 256] = value[:, 384:]
    for ref, rows in ((head_grad, slice(0, 24)), (out_grad, slice(24, 32))):
        ref[:, :, 0:384] = tail_d[rows].astype(F32)
        ref[:, :, 384:768] = tail[rows, :, 0:384]
        ref.flush()
    up[...] = up_turned[...].reshape(768, 768).T
    up.flush()
    rows = [tail[i, 0:6, 384:512] for i in range(5)] + [jnp.sum(tail[:, i : i + 6, 384:512], 0) for i in (8, 16)]
    rows = [jnp.concatenate([v[i : i + 1] for i in range(6)], 1) for v in rows]
    rows[4:5] = [rows[4][:, 0:192], rows[4][:, 192:384]]
    for ref, row in zip(vectors, rows):
        ref[...] = row.reshape(ref.shape)


def add_kernel(a, b, out):
    out[...] = (a[...].astype(F32) + b[...].astype(F32)).astype(out.dtype)


TIMES = {
    "project_kernel": 1.2,
    "forward_far_kernel": 4.3,
    "forward_near_kernel": 7.0,
    "combine_kernel": 1.0,
    "feed_kernel": 1.5,
    "middle_kernel": 3.4,
    "inner_kernel": 2.0,
    "outer_kernel": 4.0,
    "slices_kernel": 3.0,
    "products_kernel": 3.0,
    "backward_near_kernel": 9.0,
    "backward_far_kernel": 7.0,
    "weights_kernel": 4.0,
    "reduce_kernel": 2.0,
    "unpack_kernel": 3.5,
    "unpack_down_kernel": 1.5,
    "join_kernel": 0.1,
}


class Fetched:
    def __init__(self, copies, ref):
        self.copies, self.ref, self.shape = copies, ref, ref.shape

    def wait(self):
        for copy in self.copies:
            copy.wait()
        self.copies = ()

    def __getitem__(self, index):
        self.wait()
        return self.ref[index]


class Stored:
    def __init__(self, copy, ref):
        self.copy, self.ref, self.shape, self.started = copy, ref, ref.shape, False
        self.parts = None

    def flush(self):
        if not self.started:
            self.copy.start()
        self.started = True

    def flush_part(self, i):
        self.started = True
        self.parts(i).start()

    def finish(self):
        self.flush()
        self.copy.wait()

    def __getitem__(self, index):
        return self.ref[index]

    def __setitem__(self, index, value):
        self.ref[index] = value


def part_copy(ref, target, semaphore, i):
    return pltpu.make_async_copy(ref.at[i], target.at[i], semaphore)


def wait_for(*operands):
    for operand in operands:
        if isinstance(operand, Fetched):
            operand.wait()


def call(kernel, out_shapes, scratch=(), scalars=0, limit=8, fetch=(), stacks=(), store=(), free=()):
    def run(*args, after=(), behind=()):
        after = (*after, *[pltpu.with_memory_space_constraint(v, pltpu.HBM) for v in behind])
        n, extra, outs = len(args), len(after), len(out_shapes)
        name = getattr(kernel, "func", kernel).__name__
        vmem, hbm = pl.BlockSpec(memory_space=pltpu.VMEM), pl.BlockSpec(memory_space=pltpu.HBM)
        specs = [vmem] * n + [pl.BlockSpec(memory_space=pl.ANY)] * (extra - len(behind)) + [hbm] * len(behind)
        out_specs = [hbm if i in store else vmem for i in range(outs)]
        for i in range(scalars):
            specs[i] = pl.BlockSpec(memory_space=pltpu.SMEM)
        buffers, sizes = [], {}
        for i in sorted((*fetch, *stacks)):
            sizes[i] = 4 if i in stacks else 1
            for j in range(sizes[i]):
                specs[i + j] = pl.BlockSpec(memory_space=pl.ANY) if i in free else hbm
            shape = args[i].shape
            shape = (4, *shape) if i in stacks else (1, *shape) if len(shape) == 1 else shape
            buffers.append(pltpu.VMEM(shape, args[i].dtype))
        for i in store:
            buffers.append(pltpu.VMEM(*out_shapes[i]))
        total = sum(sizes.values()) + len(store)
        if total:
            buffers.append(pltpu.SemaphoreType.DMA((total,)))

        def body(*refs):
            results = list(refs[n + extra : n + extra + outs])
            own = refs[n + extra + outs : n + extra + outs + len(scratch)]
            landing = refs[n + extra + outs + len(scratch) :]
            operands, pending, i, slot = [], [], 0, 0
            while i < n:
                if i not in sizes:
                    operands.append(refs[i])
                    i += 1
                    continue
                ref, copies = landing[len(pending)], []
                for j in range(sizes[i]):
                    place = ref
                    if i in stacks:
                        place = ref.at[jnp.bitwise_xor(Here().tensor, j)]
                    elif len(args[i].shape) == 1:
                        place = ref.at[0]
                    copies.append(pltpu.make_async_copy(refs[i + j], place, landing[-1].at[slot]))
                    copies[-1].start()
                    slot += 1
                pending.append(Fetched(copies, ref))
                operands.append(pending[-1])
                i += sizes[i]
            for k, i in enumerate(store):
                ref = landing[len(pending) + k]
                copy_target = results[i]
                copy = pltpu.make_async_copy(ref, copy_target, landing[-1].at[slot])
                results[i] = Stored(copy, ref)
                results[i].parts = functools.partial(part_copy, ref, copy_target, landing[-1].at[slot])
                slot += 1
            kernel(*operands, *results, *own)
            for operand in pending:
                operand.wait()
            for i in store:
                results[i].flush()
            for i in store:
                results[i].finish()

        args = list(args)
        for i, size in sizes.items():
            for j in range(i, i + size if i not in free else i):
                args[j] = pltpu.with_memory_space_constraint(args[j], pltpu.HBM)
        return pl.pallas_call(
            body,
            out_shape=[(pltpu.HBM if i in store else jax.ShapeDtypeStruct)(*shape) for i, shape in enumerate(out_shapes)],
            in_specs=specs,
            out_specs=out_specs,
            scratch_shapes=[*scratch, *buffers],
            compiler_params=pltpu.CompilerParams(vmem_limit_bytes=limit * 1024 * 1024),
            name=name,
            cost_estimate=pl.CostEstimate(
                flops=int(TIMES.get(name, 0.6) * 1e9), bytes_accessed=0, transcendentals=0
            ),
        )(*args, *after)

    return run


def add(a, b, after=()):
    (out,) = call(add_kernel, [(a.shape, a.dtype)])(a, b, after=after)
    return out


def others_over_tensor(v):
    across = lax.ppermute(v, "yl", FLIP)
    beside = lax.ppermute(v, "c", FLIP)
    return beside, across, lax.ppermute(across, "c", FLIP)


MID_GO = [(1, 0), (3, 2)]
B_GO = [(2, 0), (3, 1)]
C_GO = [(3, 0), (2, 1)]


def back(perm):
    return [(b, a) for a, b in perm]


def visit(a, b, c, turn=lambda perm: perm):
    return tuple(lax.ppermute(v, "z", turn(perm)) for v, perm in ((a, MID_GO), (b, B_GO), (c, C_GO)))


def per_device(
    inputs,
    head_weights,
    out_weight,
    up_weight,
    down_weight,
    in_gain,
    in_shift,
    mix_gain,
    mix_shift,
    mid_gain,
    mid_shift,
    inner_gain,
    inner_shift,
    valid_length,
    cotangent,
):
    here = Here()
    core = here.core
    row_valid = (here.base + jnp.arange(TOK, dtype=jnp.int32) < valid_length[0])[:, None]
    n = HEADS_HERE
    half = ((128, 768), BF16)

    weights = head_weights.transpose(0, 2, 1)
    q, spread = call(
        project_kernel, [((192, TOK), BF16), ((PLANE, 384, TOK), BF16)], fetch=(0, 1, 2, 3), limit=12
    )(inputs, weights, in_gain, in_shift)
    kvs = lax.all_to_all(spread, ("yh", "x"), 0, 0, tiled=True)
    q_mid, q_far, packed = call(
        select_kernel,
        [((192, SLOTS), BF16), ((192, SLOTS), BF16), ((208, 768), BF16)],
        fetch=(1, 2, 3),
        store=(2,),
    )(q, out_weight, mix_gain, mix_shift)
    visitors = visit(q_mid, q_far, q_far)
    feed_blocks, inner_grad = call(
        feed_kernel,
        [((384, 256), BF16), ((TOK, 768), F32)],
        scalars=1,
        fetch=(1, 2),
        store=(0, 1),
        limit=12,
    )(valid_length, down_weight, cotangent, after=(q_mid,))
    pay_a, pay_b, pay_c, loc = call(
        forward_far_kernel,
        [((208, SLOTS), BF16)] * 3 + [((8, 384), F32)],
        [
            *[pltpu.VMEM((n, 128, KEYS), BF16)] * 2,
            *[pltpu.VMEM((n, 80, KEYS), BF16)] * 2,
        ],
        limit=16,
        store=(3,),
    )(*visitors, kvs, behind=(inner_grad,))
    returned = visit(pay_a, pay_b, pay_c, back)
    packed, _ = lax.optimization_barrier((packed, pay_a))
    packed_beside, packed_across = lax.ppermute(packed, "c", FLIP), lax.ppermute(packed, "yl", FLIP)
    o_near, st_near = call(
        forward_near_kernel,
        [((192, TOK), F32), ((8, TOK), F32)],
        [
            pltpu.VMEM((n, PLANE, 128, TOK), BF16),
            pltpu.VMEM((n, 96, TOK), F32),
            pltpu.VMEM((n, TOK, 128), BF16),
            pltpu.VMEM((n, TOK, 128), F32),
            pltpu.VMEM((n, 80, TOK), F32),
        ],
        scalars=1,
    )(valid_length, q, kvs)
    mixed, st_all = call(combine_kernel, [((192, TOK), BF16), ((16, TOK), F32)])(o_near, st_near, *returned)
    pieces = (mixed, *others_over_tensor(mixed))
    relay, _ = lax.optimization_barrier((packed_across, o_near))
    packed = (packed, packed_beside, packed_across, lax.ppermute(relay, "c", FLIP))
    hidden, pieces, st_all, mid_blocks, pre, sums = call(
        middle_kernel,
        [
            ((TOK, 768), F32),
            ((4, 192, TOK), BF16),
            ((16, TOK), F32),
            ((384, 256), BF16),
            ((TOK, 768), F32),
            ((8, TOK), F32),
        ],
        limit=20,
        fetch=(0, 9, 10, 11, 12, 13),
        stacks=(1, 5),
        free=(1,),
        store=(0, 1, 2),
    )(inputs, *pieces, *packed, up_weight, mid_gain, mid_shift, inner_gain, inner_grad, st_all)
    sums = sums + lax.ppermute(sums, "c", FLIP)
    sums = sums + lax.ppermute(sums, "yl", FLIP)
    inner_low, pre_grad, keep, send, inner_vectors = call(
        inner_kernel,
        [((TOK, 768), BF16), ((TOK, 768), BF16), half, half, ((8, 768), F32)],
        fetch=(2, 3, 4, 5),
        store=(4,),
        limit=12,
    )(sums, pre, inner_grad, up_weight, inner_gain, inner_shift)
    mid_half = add(keep, lax.ppermute(send, "c", FLIP))

    slices, feed_keep, feed_send = call(
        slices_kernel, [((4, 1152, TOK), BF16), half, half], fetch=(3, 4), store=(0,), limit=16
    )(inner_low, pre_grad, mid_blocks, feed_blocks, down_weight, after=(mid_half,))
    slices = lax.all_to_all(slices, "x", 0, 0, tiled=True)
    mid_got = lax.ppermute(mid_half, "yl", FLIP)
    mid_sent, _ = lax.optimization_barrier((mid_got, feed_keep))
    mid_parts = (mid_half, mid_got, lax.ppermute(mid_half, "c", FLIP), lax.ppermute(mid_sent, "c", FLIP))
    hidden_grad, grad_mixed, st_near, pay_a, pay_b, pay_c, out_grad, vectors = call(
        outer_kernel,
        [((TOK, 768), F32), ((192, TOK), BF16), ((8, TOK), F32)]
        + [((208, SLOTS), BF16)] * 3
        + [((192, 768), BF16), ((8, 768), F32)],
        [pltpu.VMEM((4, 192, TOK), F32)],
        limit=20,
        scalars=1,
        fetch=(5, 6, 7, 8, 9, 14, 15),
        stacks=(10,),
        store=(0, 6, 7),
    )(valid_length, *mid_parts, hidden, cotangent, mid_gain, mid_shift, pieces, *packed, st_all, inner_vectors)
    grads = visit(pay_a, pay_b, pay_c)

    dq_near, dkv = call(
        backward_near_kernel,
        [((192, TOK), F32), ((PLANE, 384, TOK), BF16)],
        [
            pltpu.VMEM((n, 64, TOK), BF16),
            pltpu.VMEM((n, 64, TOK), BF16),
            pltpu.VMEM((n, TOK, 128), BF16),
            pltpu.VMEM((n, TOK, 80), BF16),
            pltpu.VMEM((n, HDIM, TOK), F32),
        ],
        scalars=1,
        limit=12,
        store=(0, 1),
    )(valid_length, q, grad_mixed, st_near, kvs)
    dq_a, dq_b, dq_c, dkv = call(
        backward_far_kernel,
        [((192, SLOTS), BF16)] * 3 + [((PLANE, 384, TOK), BF16)],
        [
            pltpu.VMEM((n, 128, KEYS), BF16),
            pltpu.VMEM((n, 128, KEYS), BF16),
            *[pltpu.VMEM((n, 128, KEYS), BF16)] * 2,
            *[pltpu.VMEM((n, 80, KEYS), BF16)] * 2,
        ],
        limit=20,
        fetch=(0, 1, 2, 3, 7),
        store=(3,),
    )(dkv, *visitors, *grads, loc, kvs)
    dkv = lax.all_to_all(dkv, ("yh", "x"), 0, 0, tiled=True)
    dqs = visit(dq_a, dq_b, dq_c, back)

    feed_half = add(feed_keep, lax.ppermute(feed_send, "c", FLIP), after=(dq_a,))
    slices, _ = lax.optimization_barrier((slices, feed_half))
    others = lax.ppermute(slices, "c", FLIP)
    keep, send = call(
        products_kernel,
        [((2, 2, CHUNK, 768), BF16)] * 2,
        [
            pltpu.VMEM((4, 2, CHUNK, 768), BF16),
            *[pltpu.VMEM((4 * TOK, 768), BF16)] * 2,
            *[pltpu.VMEM((192, 4 * TOK), BF16)] * 2,
        ],
        limit=16,
    )(slices, others, after=(dq_a, feed_half))
    keep, send = call(functools.partial(halve_kernel, "z"), [((2, CHUNK, 768), BF16)] * 2)(keep, travel(send, "zb"))
    keep, send = call(functools.partial(halve_kernel, "y"), [((CHUNK, 768), BF16)] * 2)(keep, travel(send, "za"))
    sum_keep, sum_send = keep, send
    sums, keep, send, in_sums = call(
        weights_kernel,
        [((PARTS, ROW, 896), BF16), half, half, ((8, 768), F32)],
        [pltpu.VMEM((576, TOK), BF16)],
        limit=20,
        fetch=(0, 1, 2, 3, 4, 5, 6, 7, 8, 9, 10),
        store=(0,),
    )(inputs, in_gain, in_shift, weights, dq_near, *dqs, dkv, out_grad, vectors, after=(sum_keep,))
    got = lax.all_to_all(sums, SEQ, 0, 0, tiled=True)
    in_sums = in_sums + lax.ppermute(in_sums, "c", FLIP)
    in_sums = in_sums + lax.ppermute(in_sums, "yl", FLIP)
    have = call(chunk_sum_kernel, [((24, 768), BF16)] * 2)(
        sum_keep, lax.ppermute(sum_send, "yh", FLIP)
    )
    (have,) = call(reduce_kernel, [((24, 2432), BF16)])(got, in_sums, *have)
    in_half = add(keep, lax.ppermute(send, "c", FLIP))
    down, up = call(join_y_kernel, [((2, 24, 1152), BF16), ((2, 24, 1280), BF16)])(
        have, lax.ppermute(have, "yh", FLIP), after=(in_half,)
    )
    in_half = add(in_half, lax.ppermute(in_half, "yl", FLIP))
    down, up = join(down, "zb1"), join(up, "xb1", after=(in_half,))
    feed_half = add(feed_half, lax.ppermute(feed_half, "yl", FLIP), after=(in_half,))
    feed_other = lax.ppermute(feed_half, "c", FLIP)
    (inputs_grad,) = call(
        input_grad_kernel, [((TOK, 768), BF16)], fetch=(0, 1, 2, 3), store=(0,), limit=12
    )(inputs, hidden_grad, in_gain, in_shift, in_half, lax.ppermute(in_half, "c", FLIP))
    down, up = join(down, "za2"), join(up, "xa2", after=(feed_half,))
    downs = [join(v, step) for v, step in zip(split(down, WIDTHS[0:2]), ("xb1", "xa1"))]
    ups = [join(v, step, behind=(inputs_grad,)) for v, step in zip(split(up, WIDTHS[2:4]), ("zb1", "za1"))]
    down_grad, tail = call(
        unpack_down_kernel,
        [((PARTS, ROW, 768), F32), ((PARTS, ROW, 384), BF16)],
        limit=16,
        store=(0,),
    )(*downs, *[travel(v, name) for v, name in zip(downs, ("xa", "xb"))])
    up_grad, head_grad, out_grad, *vectors = call(
        unpack_kernel,
        [
            ((768, 768), F32),
            ((24, ROW, 768), F32),
            ((8, ROW, 768), F32),
            *[((768,), F32)] * 4,
            *[((192,), F32)] * 2,
            *[((768,), F32)] * 2,
        ],
        [pltpu.VMEM((PARTS, ROW, 768), F32), pltpu.VMEM((PARTS, ROW, 512), F32)],
        limit=24,
        store=(0, 1, 2),
    )(tail, *ups, *[travel(v, name) for v, name in zip(ups, ("za", "zb"))])
    feed_out = jnp.where(
        core == 0, jnp.concatenate([feed_half, feed_other]), jnp.concatenate([feed_other, feed_half])
    ).astype(F32)
    result = jnp.where(row_valid, hidden + feed_out, 0.0).astype(BF16)
    return (
        result,
        inputs_grad,
        head_grad.reshape(3, 192, 768).transpose(0, 2, 1),
        out_grad.reshape(192, 768),
        up_grad,
        down_grad.reshape(768, 768),
        vectors[6],
        vectors[7],
        vectors[4],
        vectors[5],
        vectors[0],
        vectors[1],
        vectors[2],
        vectors[3],
    )


def solution(mesh):
    fine = Mesh(np.asarray(mesh.devices).reshape(4, 2, 4, 2, 2), SEQ + TENSOR)
    in_specs = (
        P(SEQ, None),
        P(None, None, TENSOR),
        P(TENSOR, None),
        P(None, TENSOR),
        P(TENSOR, None),
        P(),
        P(),
        P(TENSOR),
        P(TENSOR),
        P(),
        P(),
        P(TENSOR),
        P(TENSOR),
        P(),
        P(SEQ, None),
    )
    out_specs = (
        P(SEQ, None),
        P(SEQ, None),
        P(None, None, TENSOR),
        P(TENSOR, None),
        P(None, TENSOR),
        P(TENSOR, None),
        P(),
        P(),
        P(TENSOR),
        P(TENSOR),
        P(),
        P(),
        P(TENSOR),
        P(TENSOR),
    )
    return jax.shard_map(per_device, mesh=fine, in_specs=in_specs, out_specs=out_specs, check_vma=False)
```

```python
import functools
import itertools

import jax
import jax.numpy as jnp
import numpy as np
from jax import lax
from jax.experimental import pallas as pl
from jax.experimental.pallas import tpu as pltpu
from jax.sharding import Mesh
from jax.sharding import PartitionSpec as P


HDIM = 64
HEADS_HERE = 3
TOK = 256
PLANE = 8
SLOTS = 128
KEYS = PLANE * SLOTS
PARTS = 32
ROW = 24
EPSILON = 1e-05
NONE = -1e30
NEAR = (1, 2, 4, 6, 12)
MID = (2, 4, 6, 12)
FAR = (4, 6, 12)
F32 = jnp.float32
BF16 = jnp.bfloat16
SEQ = ("z", "yh", "x")
TENSOR = ("yl", "c")
FLIP = [(0, 1), (1, 0)]
NN = ((1,), (0,))
NT = ((1,), (1,))
TN = ((0,), (0,))


class Here:
    def __init__(self):
        self.plane, y, self.x = (lax.axis_index(a) for a in SEQ)
        low, self.core = (lax.axis_index(a) for a in TENSOR)
        self.y = y
        self.place = y * 4 + self.x
        self.tensor = low * 2 + self.core
        self.head0 = self.tensor * HEADS_HERE
        self.base = (self.plane * PLANE + self.place) * TOK


def dot(a, b, dims=NN):
    return lax.dot_general(a, b, (dims, ((), ())), preferred_element_type=F32)


def split3(v):
    hi = v.astype(BF16).astype(F32)
    mid = (v - hi).astype(BF16).astype(F32)
    return hi, mid, v - hi - mid


def mid_offsets(head):
    slot = lax.broadcasted_iota(jnp.int32, (1, SLOTS), 1)
    return 2 * slot + lax.rem(head, 2)


def far_offsets(head, base):
    slot = lax.broadcasted_iota(jnp.int32, (1, SLOTS), 1)
    which = lax.rem(slot, 4)
    kind = jnp.where(which == 0, 0, 2 * which + 2)
    first = lax.div(base + 12 - head, 12) - 1
    return 12 * (first + lax.div(slot, 4)) + kind + head - base, kind


def one_hot_rows(offsets):
    rows = lax.broadcasted_iota(jnp.int32, (TOK, SLOTS), 0)
    return (rows == offsets).astype(F32).astype(BF16)


def picks(head, base):
    return one_hot_rows(mid_offsets(head)), one_hot_rows(far_offsets(head, base)[0])


def count_table(kind, usable, dilations):
    row = lax.broadcasted_iota(jnp.int32, (16, kind.shape[1]), 0)
    count = jnp.zeros(row.shape, F32)
    for step in dilations:
        count += jnp.where((lax.rem(row, step) == 0) & (lax.rem(kind, step) == 0), 1.0, 0.0)
    live = (count > 0) & usable & (row < 12)
    log_count = jnp.log(jnp.maximum(count, 1.0))
    hi = log_count.astype(BF16).astype(F32)
    return jnp.where(live, hi, NONE), jnp.where(live, log_count - hi, 0.0)


def score_columns(ref, lo, kind, usable, dilations):
    hi, low = count_table(kind, usable, dilations)
    return jnp.concatenate([ref[lo : lo + HDIM, :].astype(F32) * 0.125, hi, low], 0)


def own_columns(head, base, q, lo):
    kind = lax.rem(base - head + 12 + lax.broadcasted_iota(jnp.int32, (1, TOK), 1), 12)
    return score_columns(q, lo, kind, kind >= 0, NEAR)


def query_columns(head, base, plane, visitors, lo):
    if len(visitors) == 1:
        at = mid_offsets(head)
        return score_columns(visitors[0], lo, lax.rem(base + 2048 + at - head + 12, 12), at >= 0, MID)
    parts = []
    for visitor, origin in zip(visitors, (plane + 2, 3 - plane)):
        at, kind = far_offsets(head, origin * 2048 + lax.rem(base, 2048))
        parts.append(score_columns(visitor, lo, kind, (at >= 0) & (at < TOK), FAR))
    return jnp.concatenate(parts, 1)


def one_hot_kind(kind):
    return (kind == lax.broadcasted_iota(jnp.int32, (16, kind.shape[1]), 0)).astype(F32).astype(BF16)


def ones(rows, columns):
    return jnp.ones((rows, columns), BF16)


def diagonal_mask(base, valid):
    rows = lax.broadcasted_iota(jnp.int32, (TOK, TOK), 0)
    cols = lax.broadcasted_iota(jnp.int32, (TOK, TOK), 1)
    return (cols <= rows) & (cols + base < valid)


def norm_rows(v, gain, shift):
    mean = jnp.sum(v, 1, keepdims=True) / v.shape[1]
    spread = jnp.sum(v * v, 1, keepdims=True) / v.shape[1] - mean * mean
    scale = lax.rsqrt(spread + EPSILON)
    unit = (v - mean) * scale
    return unit * gain + shift, unit, scale


def norm_rows_back(grad, unit, scale, gain):
    q = grad * gain
    n = grad.shape[1]
    return scale * (q - jnp.sum(q, 1, keepdims=True) / n - unit * (jnp.sum(q * unit, 1, keepdims=True) / n))


def project_kernel(inputs, weights, gain, shift, q, spread):
    v = norm_rows(inputs[...].astype(F32), gain[...], shift[...])[0].astype(BF16)
    spread[0, 0:192, :] = dot(weights[1], v, NT).astype(BF16)
    spread[0, 192:384, :] = dot(weights[2], v, NT).astype(BF16)
    for i in range(1, PLANE):
        spread[i] = spread[0]
    q[...] = dot(weights[0], v, NT).astype(BF16)


def select_kernel(q, out_weight, mix_gain, mix_shift, q_mid, q_far, packed):
    here = Here()
    head0, base = here.head0, here.base
    for h in range(HEADS_HERE):
        rows = slice(h * HDIM, (h + 1) * HDIM)
        pick_mid, pick_far = picks(head0 + h, base)
        q_mid[rows, :] = dot(q[rows, :], pick_mid).astype(BF16)
        q_far[rows, :] = dot(q[rows, :], pick_far).astype(BF16)
    packed[0:192, :] = out_weight[...]
    terms = list(split3(mix_gain[...])) + list(split3(mix_shift[...])) + [jnp.zeros((10, 192), F32)]
    packed[192:208, 0:192] = jnp.concatenate(terms, 0).astype(BF16)


def weigh(s):
    return jnp.exp(s).astype(BF16)


def widest(s):
    return functools.reduce(jnp.maximum, [s[:, i * 128 : (i + 1) * 128] for i in range(s.shape[1] // 128)])


def shifted(m, rows):
    top = jnp.max(m.T, 0, keepdims=True)
    minus = jnp.concatenate(list(split3(-top)) + [jnp.zeros((29, top.shape[1]), F32)], 0)
    return top, jnp.concatenate([rows, minus], 0).T.astype(BF16)


def near_keys(kvs, block, lo, head, base):
    kind = lax.rem(base - head + 12 + lax.broadcasted_iota(jnp.int32, (1, TOK), 1), 12)
    hot = one_hot_kind(kind)
    return jnp.concatenate([kvs[block, lo : lo + HDIM, :], hot, hot, ones(32, TOK)], 0)


def near_values(kvs, block, lo):
    return jnp.concatenate([kvs[block, 192 + lo : 192 + lo + HDIM, :], ones(16, TOK)], 0)


def gather_keys(kvs, head0, plane, far, rights, values):
    for h in range(HEADS_HERE):
        lo, head = h * HDIM, head0 + h
        for k in range(PLANE):
            start = plane * 2048 + k * TOK
            if far:
                offsets, kind = far_offsets(head, start)
                kind = jnp.where((offsets >= 0) & (offsets < TOK), kind, 12)
            else:
                offsets = mid_offsets(head)
                kind = lax.rem(start + offsets - head + 12, 12)
            both = jnp.concatenate([kvs[k, lo : lo + HDIM, :], kvs[k, 192 + lo : 192 + lo + HDIM, :]], 0)
            at = slice(k * SLOTS, (k + 1) * SLOTS)
            small = dot(both, one_hot_rows(offsets)).astype(BF16)
            hot = one_hot_kind(kind)
            rights[h, :, at] = jnp.concatenate([small[0:HDIM], hot, hot, ones(32, SLOTS)], 0)
            values[h, :, at] = jnp.concatenate([small[HDIM:], ones(16, SLOTS)], 0)


def forward_far_kernel(qa, qb, qc, kvs, pay_a, pay_b, pay_c, loc, right_a, right_f, value_a, value_f):
    here = Here()
    head0, base, plane = here.head0, here.base, here.plane
    heads = range(HEADS_HERE)
    row = lax.broadcasted_iota(jnp.int32, (16, SLOTS), 0)
    loc[...] = jnp.zeros(loc.shape, F32)

    def attend(queries, rights, values, first, pays):
        extra = [jnp.where(row == 9, 1.0, 0.0) for _ in pays]
        rows = [query_columns(head0 + h, base, plane, queries, h * HDIM) for h in heads]
        zeros = jnp.zeros((32, SLOTS * len(pays)), F32)
        marks = [widest(dot(jnp.concatenate([rows[h], zeros], 0).T.astype(BF16), rights[h])) for h in heads]
        lefts = [shifted(marks[h], rows[h]) for h in heads]
        accs = [dot(values[h], weigh(dot(lefts[h][1], rights[h])), NT) for h in heads]
        for h in heads:
            total = accs[h][64:65, :]
            log = jnp.maximum(lefts[h][0] + jnp.log(total), NONE)
            out = accs[h][0:64, :] / total
            for i, pay in enumerate(pays):
                at = slice(i * SLOTS, (i + 1) * SLOTS)
                loc[h : h + 1, first + i * SLOTS : first + (i + 1) * SLOTS] = log[:, at]
                pay[h * HDIM : (h + 1) * HDIM, :] = out[:, at].astype(BF16)
                for j, term in enumerate(split3(log[:, at])):
                    extra[i] = jnp.where(row == 3 * h + j, term, extra[i])
        for e, pay in zip(extra, pays):
            pay[192:208, :] = e.astype(BF16)

    @pl.when(lax.rem(plane, 2) == 0)
    def _():
        gather_keys(kvs, head0, plane, False, right_a, value_a)
        attend((qa,), right_a, value_a, 0, (pay_a,))

    @pl.when(plane < 2)
    def _():
        gather_keys(kvs, head0, plane, True, right_f, value_f)
        attend((qb, qc), right_f, value_f, SLOTS, (pay_b, pay_c))


def forward_near_kernel(length, q, kvs, o_near, st_near, right, rows, left, marks, acc):
    here, valid = Here(), length[0]
    head0, base, place = here.head0, here.base, here.place
    heads = range(HEADS_HERE)
    for h in heads:
        lo = h * HDIM
        head = head0 + h
        rows[h] = own_columns(head, base, q, lo)
        left[h] = jnp.concatenate([rows[h], jnp.zeros((32, TOK), F32)], 0).T.astype(BF16)
    marks[...] = jnp.full(marks.shape, 2 * NONE, F32)
    wait_for(kvs)
    for k in range(PLANE):

        @pl.when(k <= place)
        def _():
            for h in heads:
                right[h, k] = near_keys(kvs, place - k, h * HDIM, head0 + h, base - k * TOK)
                s = dot(left[h], right[h, k])
                if k == 0:
                    s = jnp.where(diagonal_mask(base, valid), s, NONE)
                marks[h] = jnp.maximum(marks[h], widest(s))

    tops = []
    for h in heads:
        top, turned = shifted(marks[h], rows[h])
        tops.append(top)
        left[h] = turned
    acc[...] = jnp.zeros(acc.shape, F32)
    for k in range(PLANE):

        @pl.when(k <= place)
        def _():
            for h in heads:
                lo = h * HDIM
                s = dot(left[h], right[h, k])
                if k == 0:
                    s = jnp.where(diagonal_mask(base, valid), s, NONE)
                acc[h] += dot(near_values(kvs, place - k, lo), weigh(s), NT)

    st_near[...] = jnp.zeros(st_near.shape, F32)
    for h in heads:
        total = acc[h, 64:65, :]
        o_near[h * HDIM : (h + 1) * HDIM, :] = acc[h, 0:64, :] / total
        st_near[h : h + 1, :] = tops[h] + jnp.log(total)


def combine_kernel(o_near, st_near, ra, rb, rc, mixed, st_all):
    here = Here()
    head0, base = here.head0, here.base
    st_all[...] = jnp.zeros(st_all.shape, F32)
    for h in range(HEADS_HERE):
        rows = slice(h * HDIM, (h + 1) * HDIM)
        pick_mid, pick_far = picks(head0 + h, base)
        outs, logs = [o_near[rows, :]], [st_near[h : h + 1, :]]
        for pay, pick in ((ra, pick_mid), (rb, pick_far), (rc, pick_far)):
            wide = dot(jnp.concatenate([pay[rows, :], pay[192:208, :]], 0), pick, NT)
            log = wide[64 + 3 * h : 65 + 3 * h] + wide[65 + 3 * h : 66 + 3 * h] + wide[66 + 3 * h : 67 + 3 * h]
            outs.append(wide[0:64])
            logs.append(jnp.where(wide[73:74] > 0.5, log, NONE))
        top = functools.reduce(jnp.maximum, logs)
        weights = [jnp.exp(v - top) for v in logs]
        total = sum(weights)
        mixed[rows, :] = sum((w / total) * o for w, o in zip(weights, outs)).astype(BF16)
        st_all[h : h + 1, :] = top + jnp.log(total)
        for i in range(3):
            st_all[3 + 3 * i + h : 4 + 3 * i + h, :] = weights[i + 1] / total


def mix_norm(pieces):
    first = sum(jnp.sum(pieces[i].astype(F32), 0, keepdims=True) for i in range(4)) / 768
    second = sum(jnp.sum(jnp.square(pieces[i].astype(F32)), 0, keepdims=True) for i in range(4)) / 768
    return first, lax.rsqrt(second - first * first + EPSILON)


def mix_parameters(packed, i):
    tail = jnp.concatenate([packed[i, 192:208, 0:256].astype(F32), jnp.zeros((112, 256), F32)], 0).T[0:192]
    return tail[:, 0:1] + tail[:, 1:2] + tail[:, 2:3], tail[:, 3:4] + tail[:, 4:5] + tail[:, 5:6]


def gelu_parts(v):
    a, b = 0.7978845608028654, 0.044715
    square = v * v
    t = jnp.tanh(a * v * (1.0 + b * square))
    active = 0.5 * v * (1.0 + t)
    slope = 0.5 * (1.0 + t) + 0.5 * v * (1.0 - t * t) * (a * (1.0 + 3.0 * b * square))
    return active, slope


def half_blocks(core, v):
    half = jnp.where(core == 0, v[0:128], v[128:256])
    return jnp.concatenate([half[:, i * 256 : (i + 1) * 256] for i in range(3)], 0).astype(BF16)


def feed_kernel(length, down, cotangent, feed_blocks, inner_grad):
    here = Here()
    row = here.base + lax.broadcasted_iota(jnp.int32, (TOK, 1), 0)
    feed = jnp.where(row < length[0], cotangent[...].astype(F32), 0.0)
    feed_blocks[...] = half_blocks(here.core, feed)
    grad = dot(feed.astype(BF16), down[...], NT)
    inner_grad[...] = grad


def middle_kernel(
    inputs, pieces, packed, up, gain, shift, inner_gain, inner_grad, st_all,
    hidden, pieces_kept, st_kept, mid_blocks, pre, sums,
):
    st_kept[...] = st_all[...]
    st_kept.flush()
    pieces.wait()
    pieces_kept[...] = pieces[...]
    pieces_kept.flush()
    mean, scale = mix_norm(pieces)
    total = inputs[...].astype(F32)
    branch = None
    for i in range(4):
        mix_gain, mix_shift = mix_parameters(packed, i)
        low = ((pieces[i].astype(F32) - mean) * scale * mix_gain + mix_shift).astype(BF16)
        term = dot(low, packed[i, 0:192, :], TN)
        branch = term if branch is None else branch + term
    total = total + branch
    hidden[...] = total
    hidden.flush()
    low = norm_rows(total, gain[...], shift[...])[0]
    mid_blocks[...] = half_blocks(Here().core, low)
    pre[...] = dot(low.astype(BF16), up[...])
    active = gelu_parts(pre[...])[0]
    lane = lax.broadcasted_iota(jnp.int32, (1, 128), 1)
    st = jnp.zeros((TOK, 128), F32)
    scaled = inner_grad[...] * inner_gain[...]
    for i, v in enumerate((active, active * active, scaled, scaled * active)):
        st = jnp.where(lane == i, jnp.sum(v, 1, keepdims=True), st)
    sums[...] = st.T[0:8]


def halves(core, v, keep, send):
    for c in range(2):

        @pl.when(core == c)
        def _():
            keep[...] = v[c * 128 : (c + 1) * 128].astype(BF16)
            send[...] = v[(1 - c) * 128 : (2 - c) * 128].astype(BF16)


def whole(core, own, other):
    return jnp.concatenate([jnp.where(core == 0, own, other), jnp.where(core == 0, other, own)], 0)


def inner_kernel(sums, pre, inner_grad, up, gain, shift, inner_low, pre_grad, keep, send, vectors):
    st = jnp.concatenate([sums[...], jnp.zeros((120, TOK), F32)], 0).T
    width = 3072
    mean = st[:, 0:1] / width
    scale = lax.rsqrt(st[:, 1:2] / width - mean * mean + EPSILON)
    first = st[:, 2:3]
    second = scale * (st[:, 3:4] - mean * first)
    active, slope = gelu_parts(pre[...])
    unit = (active - mean) * scale
    inner_low[...] = (unit * gain[...] + shift[...]).astype(BF16)
    grad = inner_grad[...]
    vectors[...] = jnp.zeros(vectors.shape, F32)
    vectors[0:1, :] = jnp.sum(grad * unit, 0, keepdims=True)
    vectors[1:2, :] = jnp.sum(grad, 0, keepdims=True)
    back = scale * (grad * gain[...] - first / width - unit * (second / width))
    low = (back * slope).astype(BF16)
    pre_grad[...] = low
    halves(Here().core, dot(low, up[...], NT), keep, send)


def outer_kernel(
    length, mid_own, mid_got, other_own, other_got, hidden, cotangent, gain, shift, pieces, packed, st_all,
    inner_vectors, hidden_grad, grad_mixed, st_near, pay_a, pay_b, pay_c, out_grad, all_vectors, scratch,
):
    here, valid = Here(), length[0]
    head0, base, tensor = here.head0, here.base, here.tensor
    row = base + lax.broadcasted_iota(jnp.int32, (TOK, 1), 0)
    upstream = jnp.where(row < valid, cotangent[...].astype(F32), 0.0)
    _, unit, scale = norm_rows(hidden[...], gain[...], shift[...])
    own = mid_own[...].astype(F32) + mid_got[...].astype(F32)
    grad = whole(here.core, own, other_own[...].astype(F32) + other_got[...].astype(F32))
    vectors = [jnp.sum(grad * unit, 0, keepdims=True), jnp.sum(grad, 0, keepdims=True)]
    total = upstream + norm_rows_back(grad, unit, scale, gain[...])
    hidden_grad[...] = total
    hidden_grad.flush()
    branch = total.astype(BF16)

    mean, scale = mix_norm(pieces)
    first, second = jnp.zeros((1, TOK), F32), jnp.zeros((1, TOK), F32)
    for i in range(4):
        grad = dot(packed[i, 0:192, :], branch, NT)
        scratch[i] = grad
        q = grad * mix_parameters(packed, i)[0]
        first += jnp.sum(q, 0, keepdims=True)
        second += jnp.sum(q * (pieces[i].astype(F32) - mean), 0, keepdims=True)
    second = second * scale
    output = pieces[tensor].astype(F32)
    unit = (output - mean) * scale
    grad = scratch[tensor]
    gain_own, shift_own = mix_parameters(packed, tensor)
    low = (unit * gain_own + shift_own).astype(BF16)
    lane = lax.broadcasted_iota(jnp.int32, (1, 128), 1)
    columns = jnp.where(
        lane == 0, jnp.sum(grad * unit, 1, keepdims=True), jnp.where(lane == 1, jnp.sum(grad, 1, keepdims=True), 0.0)
    )
    vectors += [inner_vectors[0:2], jnp.concatenate([columns.T[0:2], jnp.zeros((2, 576), F32)], 1)]
    all_vectors[...] = jnp.concatenate(vectors + [jnp.zeros((2, 768), F32)], 0)
    out_grad[...] = dot(low, branch).astype(BF16)
    out_grad.flush()
    all_vectors.flush()
    back = scale * (grad * gain_own - first / 768 - unit * (second / 768))
    back = back.astype(BF16).astype(F32)
    grad_mixed[...] = back.astype(BF16)
    st_near[...] = jnp.zeros(st_near.shape, F32)
    tails = [[], [], []]
    for h in range(HEADS_HERE):
        rows = slice(h * HDIM, (h + 1) * HDIM)
        mine = back[rows]
        centre = jnp.sum(mine * output[rows], 0, keepdims=True)
        st_near[h : h + 1, :] = st_all[h : h + 1, :]
        st_near[3 + h : 4 + h, :] = centre
        pick_mid, pick_far = picks(head0 + h, base)
        for i, (pay, pick) in enumerate(((pay_a, pick_mid), (pay_b, pick_far), (pay_c, pick_far))):
            share = st_all[3 + 3 * i + h : 4 + 3 * i + h, :]
            terms = list(split3(centre * share)) + [jnp.zeros((13, TOK), F32)]
            wide = jnp.concatenate([mine * share] + terms, 0).astype(BF16)
            small = dot(wide, pick)
            pay[rows, :] = small[0:64].astype(BF16)
            tails[i].append(small[64:67])
    for pay, tail in zip((pay_a, pay_b, pay_c), tails):
        pay[192:208, :] = jnp.concatenate(tail + [jnp.zeros((7, SLOTS), F32)], 0).astype(BF16)


def gradients(left, grad_left, rows_q, rows_g, rights, values, mask=None):
    s = dot(left, rights)
    if mask is not None:
        s = jnp.where(mask, s, NONE)
    w = jnp.exp(s)
    ds = (w * dot(grad_left, values)).astype(BF16)
    dq = dot(rights[0:64], ds, NT)
    return dq, jnp.concatenate([dot(rows_q, ds), dot(rows_g, w.astype(BF16))], 0)


def with_logs(rows, logs):
    minus = split3(jnp.where(logs > NONE * 0.1, -logs, 0.0))
    return jnp.concatenate([rows] + list(minus) + [jnp.zeros((29, logs.shape[1]), F32)], 0)


def with_centres(rows, centres):
    return jnp.concatenate([rows] + list(split3(-centres)) + [jnp.zeros((13, centres.shape[1]), F32)], 0)


def backward_near_kernel(length, q, grad, st, kvs, dq_near, dkv, rows_q, rows_g, left, grad_left, acc_q):
    here, valid = Here(), length[0]
    head0, base, place = here.head0, here.base, here.place
    heads = range(HEADS_HERE)
    for h in heads:
        lo = h * HDIM
        rows = with_logs(own_columns(head0 + h, base, q, lo), st[h : h + 1, :])
        rows_q[h] = rows[0:64].astype(BF16)
        left[h] = rows.T.astype(BF16)
        rows = with_centres(grad[lo : lo + HDIM, :].astype(F32), st[3 + h : 4 + h, :])
        rows_g[h] = rows[0:64].astype(BF16)
        grad_left[h] = rows.T.astype(BF16)
    acc_q[...] = jnp.zeros(acc_q.shape, F32)
    for k in range(PLANE):
        block = lax.rem(place - k + PLANE, PLANE)

        @pl.when(k > place)
        def _():
            dkv[block] = jnp.zeros((384, TOK), BF16)

        @pl.when(k <= place)
        def _():
            mask = diagonal_mask(base, valid) if k == 0 else None
            for h in heads:
                lo = h * HDIM
                keys = near_keys(kvs, place - k, lo, head0 + h, base - k * TOK)
                values = near_values(kvs, place - k, lo)
                dq, both = gradients(left[h], grad_left[h], rows_q[h], rows_g[h], keys, values, mask)
                acc_q[h] += dq
                dkv[block, lo : lo + HDIM, :] = both[0:64].astype(BF16)
                dkv[block, 192 + lo : 192 + lo + HDIM, :] = both[64:128].astype(BF16)

        dkv.flush_part(block)

    for h in heads:
        dq_near[h * HDIM : (h + 1) * HDIM, :] = acc_q[h] * 0.125


def backward_far_kernel(dkv_near, qa, qb, qc, ga, gb, gc, loc, kvs, *refs):
    dq_a, dq_b, dq_c, dkv, small_a, small_f, right_a, right_f, value_a, value_f = refs
    here = Here()
    head0, base, plane = here.head0, here.base, here.plane
    heads = range(HEADS_HERE)
    wait_for(qa, qb, qc, loc)

    def part(queries, pays, first, rights, values, dqs, small):
        n = SLOTS * len(pays)
        for h in heads:
            lo = h * HDIM
            rows = query_columns(head0 + h, base, plane, queries, lo)
            rows = with_logs(rows, loc[h : h + 1, first : first + n])
            columns, centres = [], []
            for pay in pays:
                columns.append(pay[lo : lo + HDIM, :].astype(F32))
                tail = pay[192:208, :].astype(F32)
                centres.append(tail[3 * h : 3 * h + 1] + tail[3 * h + 1 : 3 * h + 2] + tail[3 * h + 2 : 3 * h + 3])
            grads = with_centres(jnp.concatenate(columns, 1), jnp.concatenate(centres, 1))
            dq, both = gradients(
                rows.T.astype(BF16),
                grads.T.astype(BF16),
                rows[0:64].astype(BF16),
                grads[0:64].astype(BF16),
                rights[h],
                values[h],
            )
            dq = (dq * 0.125).astype(BF16)
            for i, out in enumerate(dqs):
                out[lo : lo + HDIM, :] = dq[:, i * SLOTS : (i + 1) * SLOTS]
            small[h] = both.astype(BF16)

    @pl.when((plane == 1) | (plane == 2))
    def _():
        small_a[...] = jnp.zeros(small_a.shape, BF16)
        small_f[...] = jnp.zeros(small_f.shape, BF16)

    @pl.when(lax.rem(plane, 2) == 0)
    def _():
        gather_keys(kvs, head0, plane, False, right_a, value_a)
        part((qa,), (ga,), 0, right_a, value_a, (dq_a,), small_a)

    @pl.when(plane < 2)
    def _():
        gather_keys(kvs, head0, plane, True, right_f, value_f)
        part((qb, qc), (gb, gc), SLOTS, right_f, value_f, (dq_b, dq_c), small_f)

    wait_for(dkv_near)

    @pl.when(plane == 3)
    def _():
        dkv[...] = dkv_near[...]
        for block in range(PLANE):
            dkv.flush_part(block)

    @pl.when(plane < 3)
    def _():
        for block in range(PLANE):
            at = slice(block * SLOTS, (block + 1) * SLOTS)
            for h in heads:
                lo = h * HDIM
                pick = jnp.concatenate(picks(head0 + h, plane * 2048 + block * TOK), 1)
                wide = dot(jnp.concatenate([small_a[h, :, at], small_f[h, :, at]], 1), pick, NT)
                for i, at_row in ((0, lo), (64, 192 + lo)):
                    near = dkv_near[block, at_row : at_row + HDIM, :].astype(F32)
                    dkv[block, at_row : at_row + HDIM, :] = (near + wide[i : i + 64]).astype(BF16)
            dkv.flush_part(block)


def weights_kernel(
    inputs, gain, shift, weights, dq_near, ra, rb, rc, dkv, out_grad, vectors, sums, keep, send, in_sums, grads
):
    here = Here()
    head0, base = here.head0, here.base
    normed, unit, _ = norm_rows(inputs[...].astype(F32), gain[...], shift[...])
    for h in range(HEADS_HERE):
        rows = slice(h * HDIM, (h + 1) * HDIM)
        pick_mid, pick_far = picks(head0 + h, base)
        dq = dq_near[rows, :] + dot(ra[rows, :], pick_mid, NT) + dot(rb[rows, :], pick_far, NT) + dot(rc[rows, :], pick_far, NT)
        grads[rows, :] = dq.astype(BF16)
    total = dkv[0].astype(F32)
    for k in range(1, PLANE):
        total += dkv[k].astype(F32)
    grads[192:576, :] = total.astype(BF16)
    sums[0:12, :, 0:768] = dot(grads[...], normed.astype(BF16)).reshape(12, 48, 768).astype(BF16)
    sums[12:16, :, 0:768] = out_grad[...].astype(F32).reshape(4, 48, 768).astype(BF16)
    sums[:, :, 768:896] = jnp.zeros((16, 48, 128), BF16)
    mixed = jnp.concatenate([vectors[4:5, 0:192], vectors[5:6, 0:192], jnp.zeros((1, 384), F32)], 1)
    for i, v in enumerate((vectors[0:1], vectors[1:2], vectors[2:3], vectors[3:4], mixed)):
        rows = [v[:, j * 128 : (j + 1) * 128] for j in range(6)] + [jnp.zeros((2, 128), F32)]
        sums[i, 0:8, 768:896] = jnp.concatenate(rows, 0).astype(BF16)
    sums.flush()
    back = dot(grads[0:192, :], weights[0], TN)
    back += dot(grads[192:384, :], weights[1], TN)
    back += dot(grads[384:576, :], weights[2], TN)
    halves(here.core, back, keep, send)
    rows = [jnp.sum(back * unit, 0, keepdims=True), jnp.sum(back, 0, keepdims=True), jnp.zeros((6, 768), F32)]
    in_sums[...] = jnp.concatenate(rows, 0)


def reduce_kernel(got, in_sums, weight_sums, out):
    total = got[0].astype(F32)
    for i in range(1, 16):
        total += got[i].astype(F32)
    y_now = Here().y
    rows = [[in_sums[j : j + 1, i * 128 : (i + 1) * 128] for i in range(6)] + [jnp.zeros((2, 128), F32)] for j in (0, 1)]
    rows = jnp.concatenate([*rows[0], *rows[1]], 0)
    for y in range(2):
        tail = total[y * 24 : (y + 1) * 24]
        out[y, :, 0:768] = weight_sums[y, 0:24, :]
        out[y, :, 768:1152] = tail[:, 0:384].astype(BF16)
        out[y, :, 1152:1920] = weight_sums[y, 24:48, :]
        out[y, :, 1920:2304] = tail[:, 384:768].astype(BF16)
        mine = jnp.where(y_now == y, rows, 0.0)
        out[y, :, 2304:2432] = jnp.concatenate([tail[0:8, 768:896], mine], 0).astype(BF16)


def input_grad_kernel(inputs, hidden_grad, gain, shift, own, other, inputs_grad):
    _, unit, scale = norm_rows(inputs[...].astype(F32), gain[...], shift[...])
    grad = whole(Here().core, own[...].astype(F32), other[...].astype(F32))
    inputs_grad[...] = (hidden_grad[...] + norm_rows_back(grad, unit, scale, gain[...])).astype(BF16)


CHUNK = 48
PAIR_A = [(0, 1), (1, 0), (2, 3), (3, 2)]
PAIR_B = [(0, 3), (3, 0), (1, 2), (2, 1)]
STEPS = {"xa": ("x", PAIR_A), "xb": ("x", PAIR_B), "za": ("z", PAIR_A), "zb": ("z", PAIR_B)}


def travel(v, name):
    axis, perm = STEPS[name]
    return lax.ppermute(v, axis, perm)


def slices_kernel(inner_low, pre_grad, mid_blocks, feed_blocks, down, slices, feed_keep, feed_send):
    for first, ref in ((0, inner_low), (192, pre_grad)):
        turned = ref[...].astype(F32).T.astype(BF16)
        for i in range(4):
            slices[i, first : first + 192, :] = turned[i * 192 : (i + 1) * 192]
    for i in range(4):
        slices[i, 384:768, :] = mid_blocks[...]
        slices[i, 768:1152, :] = feed_blocks[...]
    slices.flush()
    halves(Here().core, dot(inner_low[...], down[...]), feed_keep, feed_send)


def products_kernel(slices, others, keep, send, full, *operands):
    here = Here()
    products = []
    for (first, second), rows, columns in zip(((0, 768), (192, 384)), operands[0:2], operands[2:4]):
        for i in range(4):
            columns[:, i * TOK : (i + 1) * TOK] = slices[i, first : first + 192, :]
            for b in range(3):
                block = slice(b * 256, (b + 1) * 256)
                own = pl.multiple_of(i * TOK + here.core * 128, 128)
                other = pl.multiple_of(i * TOK + 128 - here.core * 128, 128)
                rows[pl.ds(own, 128), block] = slices[i, second + b * 128 : second + (b + 1) * 128, :]
                rows[pl.ds(other, 128), block] = others[i, second + b * 128 : second + (b + 1) * 128, :]
        products.append(dot(columns[...], rows[...]))
    down, up = products
    full[:, :, 0:24, :] = down.reshape(4, 2, 24, 768).astype(BF16)
    full[:, :, 24:48, :] = up.reshape(4, 2, 24, 768).astype(BF16)
    high = lax.div(here.plane, 2)
    keep[...] = full[pl.ds(2 * high, 2)]
    send[...] = full[pl.ds(2 - 2 * high, 2)]


def halve_kernel(keep, got, new_keep, new_send):
    i = lax.rem(Here().plane, 2)
    new_keep[...] = (keep[i].astype(F32) + got[i].astype(F32)).astype(BF16)
    new_send[...] = (keep[1 - i].astype(F32) + got[1 - i].astype(F32)).astype(BF16)


def sum_y_kernel(own, other, down, up):
    total = own[...].astype(F32) + other[...].astype(F32)
    down[...] = total[:, :, 0:1152].astype(BF16)
    up[...] = total[:, :, 1152:2432].astype(BF16)


def join_pair(i, name, own, other, out):
    high = lax.div(i, 2)
    if name == "b1":
        out[high] = own[...]
        out[1 - high] = other[...]
    elif name == "a1":
        low = lax.rem(i, 2)
        out[low] = own[...]
        out[1 - low] = other[...]
    elif name == "a2":
        first = jnp.where(high == 0, i, 3 - i)
        out[first] = own[0]
        out[3 - first] = own[1]
        out[1 - first] = other[0]
        out[2 + first] = other[1]
    else:
        out[pl.ds(2 * high, 2)] = own[...]
        out[pl.ds(2 - 2 * high, 2)] = other[...]


def join_kernel(step, own, other, out):
    here = Here()
    join_pair(here.x if step[0] == "x" else here.plane, step[1:], own, other, out)


def join(v, step, after=(), behind=()):
    shape = (4, *v.shape[1:]) if step[2] == "2" else (2, *v.shape)
    (out,) = call(functools.partial(join_kernel, step), [(shape, v.dtype)])(
        v, travel(v, step[0:2]), after=after, behind=behind
    )
    return out


WIDTHS = (512, 640, 640, 640)


def split_kernel(tail_width, full, first, second):
    columns = ((0, 384), (384, 768))
    for out, (lo, hi) in zip((first, second), columns):
        out[:, :, :, 0:384] = full[:, :, :, lo:hi]
    first[:, :, :, 384:] = full[:, :, :, 768 : 768 + tail_width]
    second[:, :, :, 384:] = full[:, :, :, 768 + tail_width :]


def split(v, widths):
    return call(functools.partial(split_kernel, widths[0] - 384), [((4, 2, 24, w), BF16) for w in widths])(v)


def last_places(i, step):
    high = lax.div(i, 2)
    if step == "a":
        first = jnp.where(high == 0, i, 3 - i)
        return (first, 3 - first), (1 - first, 2 + first)
    return (2 * high, 2 * high + 1), (2 - 2 * high, 3 - 2 * high)


def unpack_down_kernel(own0, own1, other0, other1, down, tail):
    x_now = Here().x
    for d, z, y, e in itertools.product(range(2), range(4), range(2), range(2)):
        places = last_places(x_now, "ab"[d])
        for pair, side in ((0, (own0, own1)), (1, (other0, other1))):
            x = places[pair][e]
            value = side[d][e, z, y]
            down[x * 8 + z * 2 + y, :, d * 384 : (d + 1) * 384] = value[:, 0:384].astype(F32)
            tail[z * 8 + x * 2 + y, :, d * 128 : 128 + d * 256] = value[:, 384:]


def unpack_kernel(tail_d, own0, own1, other0, other1, up, head_grad, out_grad, *rest):
    *vectors, up_turned, tail = rest
    plane = Here().plane
    for d, x, y, e in itertools.product(range(2), range(4), range(2), range(2)):
        places = last_places(plane, "ab"[d])
        for pair, side in ((0, (own0, own1)), (1, (other0, other1))):
            z = places[pair][e]
            value = side[d][e, x, y].astype(F32)
            up_turned[x * 8 + z * 2 + y, :, d * 384 : (d + 1) * 384] = value[:, 0:384]
            tail[z * 8 + x * 2 + y, :, d * 256 : 256 + d * 256] = value[:, 384:]
    for ref, rows in ((head_grad, slice(0, 24)), (out_grad, slice(24, 32))):
        ref[:, :, 0:384] = tail_d[rows].astype(F32)
        ref[:, :, 384:768] = tail[rows, :, 0:384]
        ref.flush()
    up[...] = up_turned[...].reshape(768, 768).T
    up.flush()
    rows = [tail[2 * i, 0:6, 384:512] for i in range(5)] + [jnp.sum(tail[:, i : i + 6, 384:512], 0) for i in (8, 16)]
    rows = [jnp.concatenate([v[i : i + 1] for i in range(6)], 1) for v in rows]
    rows[4:5] = [rows[4][:, 0:192], rows[4][:, 192:384]]
    for ref, row in zip(vectors, rows):
        ref[...] = row.reshape(ref.shape)


def add_kernel(a, b, out):
    out[...] = (a[...].astype(F32) + b[...].astype(F32)).astype(out.dtype)


TIMES = {
    "project_kernel": 1.2,
    "forward_far_kernel": 4.3,
    "forward_near_kernel": 7.0,
    "combine_kernel": 1.0,
    "feed_kernel": 1.5,
    "middle_kernel": 3.4,
    "inner_kernel": 2.0,
    "outer_kernel": 4.0,
    "slices_kernel": 3.0,
    "products_kernel": 3.0,
    "backward_near_kernel": 9.0,
    "backward_far_kernel": 7.0,
    "weights_kernel": 4.0,
    "reduce_kernel": 2.0,
    "unpack_kernel": 3.5,
    "unpack_down_kernel": 1.5,
    "join_kernel": 0.1,
}


class Fetched:
    def __init__(self, copies, ref):
        self.copies, self.ref, self.shape = copies, ref, ref.shape

    def wait(self):
        for copy in self.copies:
            copy.wait()
        self.copies = ()

    def __getitem__(self, index):
        self.wait()
        return self.ref[index]


class Stored:
    def __init__(self, copy, ref):
        self.copy, self.ref, self.shape, self.started = copy, ref, ref.shape, False
        self.parts = None

    def flush(self):
        if not self.started:
            self.copy.start()
        self.started = True

    def flush_part(self, i):
        self.started = True
        self.parts(i).start()

    def finish(self):
        self.flush()
        self.copy.wait()

    def __getitem__(self, index):
        return self.ref[index]

    def __setitem__(self, index, value):
        self.ref[index] = value


def part_copy(ref, target, semaphore, i):
    return pltpu.make_async_copy(ref.at[i], target.at[i], semaphore)


def wait_for(*operands):
    for operand in operands:
        if isinstance(operand, Fetched):
            operand.wait()


def call(kernel, out_shapes, scratch=(), scalars=0, limit=8, fetch=(), stacks=(), store=(), free=()):
    def run(*args, after=(), behind=()):
        after = (*after, *[pltpu.with_memory_space_constraint(v, pltpu.HBM) for v in behind])
        n, extra, outs = len(args), len(after), len(out_shapes)
        name = getattr(kernel, "func", kernel).__name__
        vmem, hbm = pl.BlockSpec(memory_space=pltpu.VMEM), pl.BlockSpec(memory_space=pltpu.HBM)
        specs = [vmem] * n + [pl.BlockSpec(memory_space=pl.ANY)] * (extra - len(behind)) + [hbm] * len(behind)
        out_specs = [hbm if i in store else vmem for i in range(outs)]
        for i in range(scalars):
            specs[i] = pl.BlockSpec(memory_space=pltpu.SMEM)
        buffers, sizes = [], {}
        for i in sorted((*fetch, *stacks)):
            sizes[i] = 4 if i in stacks else 1
            for j in range(sizes[i]):
                specs[i + j] = pl.BlockSpec(memory_space=pl.ANY) if i in free else hbm
            shape = args[i].shape
            shape = (4, *shape) if i in stacks else (1, *shape) if len(shape) == 1 else shape
            buffers.append(pltpu.VMEM(shape, args[i].dtype))
        for i in store:
            buffers.append(pltpu.VMEM(*out_shapes[i]))
        total = sum(sizes.values()) + len(store)
        if total:
            buffers.append(pltpu.SemaphoreType.DMA((total,)))

        def body(*refs):
            results = list(refs[n + extra : n + extra + outs])
            own = refs[n + extra + outs : n + extra + outs + len(scratch)]
            landing = refs[n + extra + outs + len(scratch) :]
            operands, pending, i, slot = [], [], 0, 0
            while i < n:
                if i not in sizes:
                    operands.append(refs[i])
                    i += 1
                    continue
                ref, copies = landing[len(pending)], []
                for j in range(sizes[i]):
                    place = ref
                    if i in stacks:
                        place = ref.at[jnp.bitwise_xor(Here().tensor, j)]
                    elif len(args[i].shape) == 1:
                        place = ref.at[0]
                    copies.append(pltpu.make_async_copy(refs[i + j], place, landing[-1].at[slot]))
                    copies[-1].start()
                    slot += 1
                pending.append(Fetched(copies, ref))
                operands.append(pending[-1])
                i += sizes[i]
            for k, i in enumerate(store):
                ref = landing[len(pending) + k]
                copy_target = results[i]
                copy = pltpu.make_async_copy(ref, copy_target, landing[-1].at[slot])
                results[i] = Stored(copy, ref)
                results[i].parts = functools.partial(part_copy, ref, copy_target, landing[-1].at[slot])
                slot += 1
            kernel(*operands, *results, *own)
            for operand in pending:
                operand.wait()
            for i in store:
                results[i].flush()
            for i in store:
                results[i].finish()

        args = list(args)
        for i, size in sizes.items():
            for j in range(i, i + size if i not in free else i):
                args[j] = pltpu.with_memory_space_constraint(args[j], pltpu.HBM)
        return pl.pallas_call(
            body,
            out_shape=[(pltpu.HBM if i in store else jax.ShapeDtypeStruct)(*shape) for i, shape in enumerate(out_shapes)],
            in_specs=specs,
            out_specs=out_specs,
            scratch_shapes=[*scratch, *buffers],
            compiler_params=pltpu.CompilerParams(vmem_limit_bytes=limit * 1024 * 1024),
            name=name,
            cost_estimate=pl.CostEstimate(
                flops=int(TIMES.get(name, 0.6) * 1e9), bytes_accessed=0, transcendentals=0
            ),
        )(*args, *after)

    return run


def add(a, b, after=()):
    (out,) = call(add_kernel, [(a.shape, a.dtype)])(a, b, after=after)
    return out


def others_over_tensor(v):
    across = lax.ppermute(v, "yl", FLIP)
    beside = lax.ppermute(v, "c", FLIP)
    return beside, across, lax.ppermute(across, "c", FLIP)


MID_GO = [(1, 0), (3, 2)]
B_GO = [(2, 0), (3, 1)]
C_GO = [(3, 0), (2, 1)]


def back(perm):
    return [(b, a) for a, b in perm]


def visit(a, b, c, turn=lambda perm: perm):
    return tuple(lax.ppermute(v, "z", turn(perm)) for v, perm in ((a, MID_GO), (b, B_GO), (c, C_GO)))


def per_device(
    inputs,
    head_weights,
    out_weight,
    up_weight,
    down_weight,
    in_gain,
    in_shift,
    mix_gain,
    mix_shift,
    mid_gain,
    mid_shift,
    inner_gain,
    inner_shift,
    valid_length,
    cotangent,
):
    here = Here()
    core = here.core
    row_valid = (here.base + jnp.arange(TOK, dtype=jnp.int32) < valid_length[0])[:, None]
    n = HEADS_HERE
    half = ((128, 768), BF16)

    weights = head_weights.transpose(0, 2, 1)
    q, spread = call(
        project_kernel, [((192, TOK), BF16), ((PLANE, 384, TOK), BF16)], fetch=(0, 1, 2, 3), limit=12
    )(inputs, weights, in_gain, in_shift)
    kvs = lax.all_to_all(spread, ("yh", "x"), 0, 0, tiled=True)
    q_mid, q_far, packed = call(
        select_kernel,
        [((192, SLOTS), BF16), ((192, SLOTS), BF16), ((208, 768), BF16)],
        fetch=(1, 2, 3),
        store=(2,),
    )(q, out_weight, mix_gain, mix_shift)
    visitors = visit(q_mid, q_far, q_far)
    feed_blocks, inner_grad = call(
        feed_kernel,
        [((384, 256), BF16), ((TOK, 768), F32)],
        scalars=1,
        fetch=(1, 2),
        store=(0, 1),
        limit=12,
    )(valid_length, down_weight, cotangent, after=(q_mid,))
    pay_a, pay_b, pay_c, loc = call(
        forward_far_kernel,
        [((208, SLOTS), BF16)] * 3 + [((8, 384), F32)],
        [
            *[pltpu.VMEM((n, 128, KEYS), BF16)] * 2,
            *[pltpu.VMEM((n, 80, KEYS), BF16)] * 2,
        ],
        limit=16,
        store=(3,),
    )(*visitors, kvs, behind=(inner_grad,))
    returned = visit(pay_a, pay_b, pay_c, back)
    packed, _ = lax.optimization_barrier((packed, pay_a))
    packed_beside, packed_across = lax.ppermute(packed, "c", FLIP), lax.ppermute(packed, "yl", FLIP)
    o_near, st_near = call(
        forward_near_kernel,
        [((192, TOK), F32), ((8, TOK), F32)],
        [
            pltpu.VMEM((n, PLANE, 128, TOK), BF16),
            pltpu.VMEM((n, 96, TOK), F32),
            pltpu.VMEM((n, TOK, 128), BF16),
            pltpu.VMEM((n, TOK, 128), F32),
            pltpu.VMEM((n, 80, TOK), F32),
        ],
        scalars=1,
    )(valid_length, q, kvs)
    mixed, st_all = call(combine_kernel, [((192, TOK), BF16), ((16, TOK), F32)])(o_near, st_near, *returned)
    pieces = (mixed, *others_over_tensor(mixed))
    relay, _ = lax.optimization_barrier((packed_across, o_near))
    packed = (packed, packed_beside, packed_across, lax.ppermute(relay, "c", FLIP))
    hidden, pieces, st_all, mid_blocks, pre, sums = call(
        middle_kernel,
        [
            ((TOK, 768), F32),
            ((4, 192, TOK), BF16),
            ((16, TOK), F32),
            ((384, 256), BF16),
            ((TOK, 768), F32),
            ((8, TOK), F32),
        ],
        limit=20,
        fetch=(0, 9, 10, 11, 12, 13),
        stacks=(1, 5),
        free=(1,),
        store=(0, 1, 2),
    )(inputs, *pieces, *packed, up_weight, mid_gain, mid_shift, inner_gain, inner_grad, st_all)
    sums = sums + lax.ppermute(sums, "c", FLIP)
    sums = sums + lax.ppermute(sums, "yl", FLIP)
    inner_low, pre_grad, keep, send, inner_vectors = call(
        inner_kernel,
        [((TOK, 768), BF16), ((TOK, 768), BF16), half, half, ((8, 768), F32)],
        fetch=(2, 3, 4, 5),
        store=(4,),
        limit=12,
    )(sums, pre, inner_grad, up_weight, inner_gain, inner_shift)
    mid_half = add(keep, lax.ppermute(send, "c", FLIP))

    slices, feed_keep, feed_send = call(
        slices_kernel, [((4, 1152, TOK), BF16), half, half], fetch=(3, 4), store=(0,), limit=16
    )(inner_low, pre_grad, mid_blocks, feed_blocks, down_weight, after=(mid_half,))
    slices = lax.all_to_all(slices, "x", 0, 0, tiled=True)
    mid_got = lax.ppermute(mid_half, "yl", FLIP)
    mid_sent, _ = lax.optimization_barrier((mid_got, feed_keep))
    mid_parts = (mid_half, mid_got, lax.ppermute(mid_half, "c", FLIP), lax.ppermute(mid_sent, "c", FLIP))
    hidden_grad, grad_mixed, st_near, pay_a, pay_b, pay_c, out_grad, vectors = call(
        outer_kernel,
        [((TOK, 768), F32), ((192, TOK), BF16), ((8, TOK), F32)]
        + [((208, SLOTS), BF16)] * 3
        + [((192, 768), BF16), ((8, 768), F32)],
        [pltpu.VMEM((4, 192, TOK), F32)],
        limit=20,
        scalars=1,
        fetch=(5, 6, 7, 8, 9, 14, 15),
        stacks=(10,),
        store=(0, 6, 7),
    )(valid_length, *mid_parts, hidden, cotangent, mid_gain, mid_shift, pieces, *packed, st_all, inner_vectors)
    grads = visit(pay_a, pay_b, pay_c)

    dq_near, dkv = call(
        backward_near_kernel,
        [((192, TOK), F32), ((PLANE, 384, TOK), BF16)],
        [
            pltpu.VMEM((n, 64, TOK), BF16),
            pltpu.VMEM((n, 64, TOK), BF16),
            pltpu.VMEM((n, TOK, 128), BF16),
            pltpu.VMEM((n, TOK, 80), BF16),
            pltpu.VMEM((n, HDIM, TOK), F32),
        ],
        scalars=1,
        limit=12,
        store=(0, 1),
    )(valid_length, q, grad_mixed, st_near, kvs)
    dq_a, dq_b, dq_c, dkv = call(
        backward_far_kernel,
        [((192, SLOTS), BF16)] * 3 + [((PLANE, 384, TOK), BF16)],
        [
            pltpu.VMEM((n, 128, KEYS), BF16),
            pltpu.VMEM((n, 128, KEYS), BF16),
            *[pltpu.VMEM((n, 128, KEYS), BF16)] * 2,
            *[pltpu.VMEM((n, 80, KEYS), BF16)] * 2,
        ],
        limit=20,
        fetch=(0, 1, 2, 3, 7),
        store=(3,),
    )(dkv, *visitors, *grads, loc, kvs)
    dkv = lax.all_to_all(dkv, ("yh", "x"), 0, 0, tiled=True)
    dqs = visit(dq_a, dq_b, dq_c, back)

    feed_half = add(feed_keep, lax.ppermute(feed_send, "c", FLIP), after=(dq_a,))
    slices, _ = lax.optimization_barrier((slices, feed_half))
    others = lax.ppermute(slices, "c", FLIP)
    keep, send = call(
        products_kernel,
        [((2, 2, CHUNK, 768), BF16)] * 2,
        [
            pltpu.VMEM((4, 2, CHUNK, 768), BF16),
            *[pltpu.VMEM((4 * TOK, 768), BF16)] * 2,
            *[pltpu.VMEM((192, 4 * TOK), BF16)] * 2,
        ],
        limit=16,
    )(slices, others, after=(dq_a, feed_half))
    keep, send = call(halve_kernel, [((2, CHUNK, 768), BF16)] * 2)(keep, travel(send, "zb"))
    weight_sums = add(keep, travel(send, "za"))
    sums, keep, send, in_sums = call(
        weights_kernel,
        [((16, 48, 896), BF16), half, half, ((8, 768), F32)],
        [pltpu.VMEM((576, TOK), BF16)],
        limit=20,
        fetch=(0, 1, 2, 3, 4, 5, 6, 7, 8, 9, 10),
        store=(0,),
    )(inputs, in_gain, in_shift, weights, dq_near, *dqs, dkv, out_grad, vectors, after=(weight_sums,))
    got = lax.all_to_all(sums, ("z", "x"), 0, 0, tiled=True)
    in_sums = in_sums + lax.ppermute(in_sums, "c", FLIP)
    in_sums = in_sums + lax.ppermute(in_sums, "yl", FLIP)
    (have,) = call(reduce_kernel, [((2, 24, 2432), BF16)])(got, in_sums, weight_sums)
    in_half = add(keep, lax.ppermute(send, "c", FLIP))
    down, up = call(sum_y_kernel, [((2, 24, 1152), BF16), ((2, 24, 1280), BF16)])(
        have, lax.ppermute(have, "yh", FLIP), after=(in_half,)
    )
    in_half = add(in_half, lax.ppermute(in_half, "yl", FLIP))
    down, up = join(down, "zb1"), join(up, "xb1", after=(in_half,))
    feed_half = add(feed_half, lax.ppermute(feed_half, "yl", FLIP), after=(in_half,))
    feed_other = lax.ppermute(feed_half, "c", FLIP)
    (inputs_grad,) = call(
        input_grad_kernel, [((TOK, 768), BF16)], fetch=(0, 1, 2, 3), store=(0,), limit=12
    )(inputs, hidden_grad, in_gain, in_shift, in_half, lax.ppermute(in_half, "c", FLIP))
    down, up = join(down, "za2"), join(up, "xa2", after=(feed_half,))
    downs = [join(v, step) for v, step in zip(split(down, WIDTHS[0:2]), ("xb1", "xa1"))]
    ups = [join(v, step, behind=(inputs_grad,)) for v, step in zip(split(up, WIDTHS[2:4]), ("zb1", "za1"))]
    down_grad, tail = call(
        unpack_down_kernel,
        [((PARTS, ROW, 768), F32), ((PARTS, ROW, 384), BF16)],
        limit=16,
        store=(0,),
    )(*downs, *[travel(v, name) for v, name in zip(downs, ("xa", "xb"))])
    up_grad, head_grad, out_grad, *vectors = call(
        unpack_kernel,
        [
            ((768, 768), F32),
            ((24, ROW, 768), F32),
            ((8, ROW, 768), F32),
            *[((768,), F32)] * 4,
            *[((192,), F32)] * 2,
            *[((768,), F32)] * 2,
        ],
        [pltpu.VMEM((PARTS, ROW, 768), F32), pltpu.VMEM((PARTS, ROW, 512), F32)],
        limit=24,
        store=(0, 1, 2),
    )(tail, *ups, *[travel(v, name) for v, name in zip(ups, ("za", "zb"))])
    feed_out = jnp.where(
        core == 0, jnp.concatenate([feed_half, feed_other]), jnp.concatenate([feed_other, feed_half])
    ).astype(F32)
    result = jnp.where(row_valid, hidden + feed_out, 0.0).astype(BF16)
    return (
        result,
        inputs_grad,
        head_grad.reshape(3, 192, 768).transpose(0, 2, 1),
        out_grad.reshape(192, 768),
        up_grad,
        down_grad.reshape(768, 768),
        vectors[6],
        vectors[7],
        vectors[4],
        vectors[5],
        vectors[0],
        vectors[1],
        vectors[2],
        vectors[3],
    )


def solution(mesh):
    fine = Mesh(np.asarray(mesh.devices).reshape(4, 2, 4, 2, 2), SEQ + TENSOR)
    in_specs = (
        P(SEQ, None),
        P(None, None, TENSOR),
        P(TENSOR, None),
        P(None, TENSOR),
        P(TENSOR, None),
        P(),
        P(),
        P(TENSOR),
        P(TENSOR),
        P(),
        P(),
        P(TENSOR),
        P(TENSOR),
        P(),
        P(SEQ, None),
    )
    out_specs = (
        P(SEQ, None),
        P(SEQ, None),
        P(None, None, TENSOR),
        P(TENSOR, None),
        P(None, TENSOR),
        P(TENSOR, None),
        P(),
        P(),
        P(TENSOR),
        P(TENSOR),
        P(),
        P(),
        P(TENSOR),
        P(TENSOR),
    )
    return jax.shard_map(per_device, mesh=fine, in_specs=in_specs, out_specs=out_specs, check_vma=False)
```

```python
import functools
import itertools

import jax
import jax.numpy as jnp
import numpy as np
from jax import lax
from jax.experimental import pallas as pl
from jax.experimental.pallas import tpu as pltpu
from jax.sharding import Mesh
from jax.sharding import PartitionSpec as P


HDIM = 64
HEADS_HERE = 3
TOK = 256
PLANE = 8
SLOTS = 128
KEYS = PLANE * SLOTS
PARTS = 32
ROW = 24
EPSILON = 1e-05
NONE = -1e30
NEAR = (1, 2, 4, 6, 12)
MID = (2, 4, 6, 12)
FAR = (4, 6, 12)
F32 = jnp.float32
BF16 = jnp.bfloat16
SEQ = ("z", "yh", "x")
TENSOR = ("yl", "c")
FLIP = [(0, 1), (1, 0)]
NN = ((1,), (0,))
NT = ((1,), (1,))
TN = ((0,), (0,))


class Here:
    def __init__(self):
        self.plane, y, self.x = (lax.axis_index(a) for a in SEQ)
        low, self.core = (lax.axis_index(a) for a in TENSOR)
        self.y = y
        self.place = y * 4 + self.x
        self.tensor = low * 2 + self.core
        self.head0 = self.tensor * HEADS_HERE
        self.base = (self.plane * PLANE + self.place) * TOK


def dot(a, b, dims=NN):
    return lax.dot_general(a, b, (dims, ((), ())), preferred_element_type=F32)


def split3(v):
    hi = v.astype(BF16).astype(F32)
    mid = (v - hi).astype(BF16).astype(F32)
    return hi, mid, v - hi - mid


def mid_offsets(head):
    slot = lax.broadcasted_iota(jnp.int32, (1, SLOTS), 1)
    return 2 * slot + lax.rem(head, 2)


def far_offsets(head, base):
    slot = lax.broadcasted_iota(jnp.int32, (1, SLOTS), 1)
    which = lax.rem(slot, 4)
    kind = jnp.where(which == 0, 0, 2 * which + 2)
    first = lax.div(base + 12 - head, 12) - 1
    return 12 * (first + lax.div(slot, 4)) + kind + head - base, kind


def one_hot_rows(offsets):
    rows = lax.broadcasted_iota(jnp.int32, (TOK, SLOTS), 0)
    return (rows == offsets).astype(F32).astype(BF16)


def picks(head, base):
    return one_hot_rows(mid_offsets(head)), one_hot_rows(far_offsets(head, base)[0])


def count_table(kind, usable, dilations):
    row = lax.broadcasted_iota(jnp.int32, (16, kind.shape[1]), 0)
    count = jnp.zeros(row.shape, F32)
    for step in dilations:
        count += jnp.where((lax.rem(row, step) == 0) & (lax.rem(kind, step) == 0), 1.0, 0.0)
    live = (count > 0) & usable & (row < 12)
    log_count = jnp.log(jnp.maximum(count, 1.0))
    hi = log_count.astype(BF16).astype(F32)
    return jnp.where(live, hi, NONE), jnp.where(live, log_count - hi, 0.0)


def score_columns(ref, lo, kind, usable, dilations):
    hi, low = count_table(kind, usable, dilations)
    return jnp.concatenate([ref[lo : lo + HDIM, :].astype(F32) * 0.125, hi, low], 0)


def own_columns(head, base, q, lo):
    kind = lax.rem(base - head + 12 + lax.broadcasted_iota(jnp.int32, (1, TOK), 1), 12)
    return score_columns(q, lo, kind, kind >= 0, NEAR)


def query_columns(head, base, plane, visitors, lo):
    if len(visitors) == 1:
        at = mid_offsets(head)
        return score_columns(visitors[0], lo, lax.rem(base + 2048 + at - head + 12, 12), at >= 0, MID)
    parts = []
    for visitor, origin in zip(visitors, (plane + 2, 3 - plane)):
        at, kind = far_offsets(head, origin * 2048 + lax.rem(base, 2048))
        parts.append(score_columns(visitor, lo, kind, (at >= 0) & (at < TOK), FAR))
    return jnp.concatenate(parts, 1)


def one_hot_kind(kind):
    return (kind == lax.broadcasted_iota(jnp.int32, (16, kind.shape[1]), 0)).astype(F32).astype(BF16)


def ones(rows, columns):
    return jnp.ones((rows, columns), BF16)


def diagonal_mask(base, valid):
    rows = lax.broadcasted_iota(jnp.int32, (TOK, TOK), 0)
    cols = lax.broadcasted_iota(jnp.int32, (TOK, TOK), 1)
    return (cols <= rows) & (cols + base < valid)


def norm_rows(v, gain, shift):
    mean = jnp.sum(v, 1, keepdims=True) / v.shape[1]
    spread = jnp.sum(v * v, 1, keepdims=True) / v.shape[1] - mean * mean
    scale = lax.rsqrt(spread + EPSILON)
    unit = (v - mean) * scale
    return unit * gain + shift, unit, scale


def norm_rows_back(grad, unit, scale, gain):
    q = grad * gain
    n = grad.shape[1]
    return scale * (q - jnp.sum(q, 1, keepdims=True) / n - unit * (jnp.sum(q * unit, 1, keepdims=True) / n))


def project_kernel(inputs, weights, gain, shift, q, spread):
    v = norm_rows(inputs[...].astype(F32), gain[...], shift[...])[0].astype(BF16)
    spread[0, 0:192, :] = dot(weights[1], v, NT).astype(BF16)
    spread[0, 192:384, :] = dot(weights[2], v, NT).astype(BF16)
    for i in range(1, PLANE):
        spread[i] = spread[0]
    q[...] = dot(weights[0], v, NT).astype(BF16)


def select_kernel(q, out_weight, mix_gain, mix_shift, q_mid, q_far, packed):
    here = Here()
    head0, base = here.head0, here.base
    for h in range(HEADS_HERE):
        rows = slice(h * HDIM, (h + 1) * HDIM)
        pick_mid, pick_far = picks(head0 + h, base)
        q_mid[rows, :] = dot(q[rows, :], pick_mid).astype(BF16)
        q_far[rows, :] = dot(q[rows, :], pick_far).astype(BF16)
    packed[0:192, :] = out_weight[...]
    terms = list(split3(mix_gain[...])) + list(split3(mix_shift[...])) + [jnp.zeros((10, 192), F32)]
    packed[192:208, 0:192] = jnp.concatenate(terms, 0).astype(BF16)


def weigh(s):
    return jnp.exp(s).astype(BF16)


def widest(s):
    return functools.reduce(jnp.maximum, [s[:, i * 128 : (i + 1) * 128] for i in range(s.shape[1] // 128)])


def shifted(m, rows):
    top = jnp.max(m.T, 0, keepdims=True)
    minus = jnp.concatenate(list(split3(-top)) + [jnp.zeros((29, top.shape[1]), F32)], 0)
    return top, jnp.concatenate([rows, minus], 0).T.astype(BF16)


def near_keys(kvs, block, lo, head, base):
    kind = lax.rem(base - head + 12 + lax.broadcasted_iota(jnp.int32, (1, TOK), 1), 12)
    hot = one_hot_kind(kind)
    return jnp.concatenate([kvs[block, lo : lo + HDIM, :], hot, hot, ones(32, TOK)], 0)


def near_values(kvs, block, lo):
    return jnp.concatenate([kvs[block, 192 + lo : 192 + lo + HDIM, :], ones(16, TOK)], 0)


def gather_keys(kvs, head0, plane, far, rights, values):
    for h in range(HEADS_HERE):
        lo, head = h * HDIM, head0 + h
        for k in range(PLANE):
            start = plane * 2048 + k * TOK
            if far:
                offsets, kind = far_offsets(head, start)
                kind = jnp.where((offsets >= 0) & (offsets < TOK), kind, 12)
            else:
                offsets = mid_offsets(head)
                kind = lax.rem(start + offsets - head + 12, 12)
            both = jnp.concatenate([kvs[k, lo : lo + HDIM, :], kvs[k, 192 + lo : 192 + lo + HDIM, :]], 0)
            at = slice(k * SLOTS, (k + 1) * SLOTS)
            small = dot(both, one_hot_rows(offsets)).astype(BF16)
            hot = one_hot_kind(kind)
            rights[h, :, at] = jnp.concatenate([small[0:HDIM], hot, hot, ones(32, SLOTS)], 0)
            values[h, :, at] = jnp.concatenate([small[HDIM:], ones(16, SLOTS)], 0)


def forward_far_kernel(qa, qb, qc, kvs, pay_a, pay_b, pay_c, loc, right_a, right_f, value_a, value_f):
    here = Here()
    head0, base, plane = here.head0, here.base, here.plane
    heads = range(HEADS_HERE)
    row = lax.broadcasted_iota(jnp.int32, (16, SLOTS), 0)
    loc[...] = jnp.zeros(loc.shape, F32)

    def attend(queries, rights, values, first, pays):
        extra = [jnp.where(row == 9, 1.0, 0.0) for _ in pays]
        rows = [query_columns(head0 + h, base, plane, queries, h * HDIM) for h in heads]
        zeros = jnp.zeros((32, SLOTS * len(pays)), F32)
        marks = [widest(dot(jnp.concatenate([rows[h], zeros], 0).T.astype(BF16), rights[h])) for h in heads]
        lefts = [shifted(marks[h], rows[h]) for h in heads]
        accs = [dot(values[h], weigh(dot(lefts[h][1], rights[h])), NT) for h in heads]
        for h in heads:
            total = accs[h][64:65, :]
            log = jnp.maximum(lefts[h][0] + jnp.log(total), NONE)
            out = accs[h][0:64, :] / total
            for i, pay in enumerate(pays):
                at = slice(i * SLOTS, (i + 1) * SLOTS)
                loc[h : h + 1, first + i * SLOTS : first + (i + 1) * SLOTS] = log[:, at]
                pay[h * HDIM : (h + 1) * HDIM, :] = out[:, at].astype(BF16)
                for j, term in enumerate(split3(log[:, at])):
                    extra[i] = jnp.where(row == 3 * h + j, term, extra[i])
        for e, pay in zip(extra, pays):
            pay[192:208, :] = e.astype(BF16)

    @pl.when(lax.rem(plane, 2) == 0)
    def _():
        gather_keys(kvs, head0, plane, False, right_a, value_a)
        attend((qa,), right_a, value_a, 0, (pay_a,))

    @pl.when(plane < 2)
    def _():
        gather_keys(kvs, head0, plane, True, right_f, value_f)
        attend((qb, qc), right_f, value_f, SLOTS, (pay_b, pay_c))


def forward_near_kernel(length, q, kvs, o_near, st_near, right, rows, left, marks, acc):
    here, valid = Here(), length[0]
    head0, base, place = here.head0, here.base, here.place
    heads = range(HEADS_HERE)
    for h in heads:
        lo = h * HDIM
        head = head0 + h
        rows[h] = own_columns(head, base, q, lo)
        left[h] = jnp.concatenate([rows[h], jnp.zeros((32, TOK), F32)], 0).T.astype(BF16)
    marks[...] = jnp.full(marks.shape, 2 * NONE, F32)
    wait_for(kvs)
    for k in range(PLANE):

        @pl.when(k <= place)
        def _():
            for h in heads:
                right[h, k] = near_keys(kvs, place - k, h * HDIM, head0 + h, base - k * TOK)
                s = dot(left[h], right[h, k])
                if k == 0:
                    s = jnp.where(diagonal_mask(base, valid), s, NONE)
                marks[h] = jnp.maximum(marks[h], widest(s))

    tops = []
    for h in heads:
        top, turned = shifted(marks[h], rows[h])
        tops.append(top)
        left[h] = turned
    acc[...] = jnp.zeros(acc.shape, F32)
    for k in range(PLANE):

        @pl.when(k <= place)
        def _():
            for h in heads:
                lo = h * HDIM
                s = dot(left[h], right[h, k])
                if k == 0:
                    s = jnp.where(diagonal_mask(base, valid), s, NONE)
                acc[h] += dot(near_values(kvs, place - k, lo), weigh(s), NT)

    st_near[...] = jnp.zeros(st_near.shape, F32)
    for h in heads:
        total = acc[h, 64:65, :]
        o_near[h * HDIM : (h + 1) * HDIM, :] = acc[h, 0:64, :] / total
        st_near[h : h + 1, :] = tops[h] + jnp.log(total)


def combine_kernel(o_near, st_near, ra, rb, rc, mixed, st_all):
    here = Here()
    head0, base = here.head0, here.base
    st_all[...] = jnp.zeros(st_all.shape, F32)
    for h in range(HEADS_HERE):
        rows = slice(h * HDIM, (h + 1) * HDIM)
        pick_mid, pick_far = picks(head0 + h, base)
        outs, logs = [o_near[rows, :]], [st_near[h : h + 1, :]]
        for pay, pick in ((ra, pick_mid), (rb, pick_far), (rc, pick_far)):
            wide = dot(jnp.concatenate([pay[rows, :], pay[192:208, :]], 0), pick, NT)
            log = wide[64 + 3 * h : 65 + 3 * h] + wide[65 + 3 * h : 66 + 3 * h] + wide[66 + 3 * h : 67 + 3 * h]
            outs.append(wide[0:64])
            logs.append(jnp.where(wide[73:74] > 0.5, log, NONE))
        top = functools.reduce(jnp.maximum, logs)
        weights = [jnp.exp(v - top) for v in logs]
        total = sum(weights)
        mixed[rows, :] = sum((w / total) * o for w, o in zip(weights, outs)).astype(BF16)
        st_all[h : h + 1, :] = top + jnp.log(total)
        for i in range(3):
            st_all[3 + 3 * i + h : 4 + 3 * i + h, :] = weights[i + 1] / total


def mix_norm(pieces):
    first = sum(jnp.sum(pieces[i].astype(F32), 0, keepdims=True) for i in range(4)) / 768
    second = sum(jnp.sum(jnp.square(pieces[i].astype(F32)), 0, keepdims=True) for i in range(4)) / 768
    return first, lax.rsqrt(second - first * first + EPSILON)


def mix_parameters(packed, i):
    tail = jnp.concatenate([packed[i, 192:208, 0:256].astype(F32), jnp.zeros((112, 256), F32)], 0).T[0:192]
    return tail[:, 0:1] + tail[:, 1:2] + tail[:, 2:3], tail[:, 3:4] + tail[:, 4:5] + tail[:, 5:6]


def gelu_parts(v):
    a, b = 0.7978845608028654, 0.044715
    square = v * v
    t = jnp.tanh(a * v * (1.0 + b * square))
    active = 0.5 * v * (1.0 + t)
    slope = 0.5 * (1.0 + t) + 0.5 * v * (1.0 - t * t) * (a * (1.0 + 3.0 * b * square))
    return active, slope


def half_blocks(core, v):
    half = jnp.where(core == 0, v[0:128], v[128:256])
    return jnp.concatenate([half[:, i * 256 : (i + 1) * 256] for i in range(3)], 0).astype(BF16)


def feed_kernel(length, down, cotangent, feed_blocks, inner_grad):
    here = Here()
    row = here.base + lax.broadcasted_iota(jnp.int32, (TOK, 1), 0)
    feed = jnp.where(row < length[0], cotangent[...].astype(F32), 0.0)
    feed_blocks[...] = half_blocks(here.core, feed)
    grad = dot(feed.astype(BF16), down[...], NT)
    inner_grad[...] = grad


def middle_kernel(
    inputs, pieces, packed, up, gain, shift, inner_gain, inner_grad, st_all,
    hidden, pieces_kept, st_kept, mid_blocks, pre, sums,
):
    st_kept[...] = st_all[...]
    st_kept.flush()
    pieces.wait()
    pieces_kept[...] = pieces[...]
    pieces_kept.flush()
    mean, scale = mix_norm(pieces)
    total = inputs[...].astype(F32)
    branch = None
    for i in range(4):
        mix_gain, mix_shift = mix_parameters(packed, i)
        low = ((pieces[i].astype(F32) - mean) * scale * mix_gain + mix_shift).astype(BF16)
        term = dot(low, packed[i, 0:192, :], TN)
        branch = term if branch is None else branch + term
    total = total + branch
    hidden[...] = total
    hidden.flush()
    low = norm_rows(total, gain[...], shift[...])[0]
    mid_blocks[...] = half_blocks(Here().core, low)
    pre[...] = dot(low.astype(BF16), up[...])
    active = gelu_parts(pre[...])[0]
    lane = lax.broadcasted_iota(jnp.int32, (1, 128), 1)
    st = jnp.zeros((TOK, 128), F32)
    scaled = inner_grad[...] * inner_gain[...]
    for i, v in enumerate((active, active * active, scaled, scaled * active)):
        st = jnp.where(lane == i, jnp.sum(v, 1, keepdims=True), st)
    sums[...] = st.T[0:8]


def halves(core, v, keep, send):
    for c in range(2):

        @pl.when(core == c)
        def _():
            keep[...] = v[c * 128 : (c + 1) * 128].astype(BF16)
            send[...] = v[(1 - c) * 128 : (2 - c) * 128].astype(BF16)


def whole(core, own, other):
    return jnp.concatenate([jnp.where(core == 0, own, other), jnp.where(core == 0, other, own)], 0)


def inner_kernel(sums, pre, inner_grad, up, gain, shift, inner_low, pre_grad, keep, send, vectors):
    st = jnp.concatenate([sums[...], jnp.zeros((120, TOK), F32)], 0).T
    width = 3072
    mean = st[:, 0:1] / width
    scale = lax.rsqrt(st[:, 1:2] / width - mean * mean + EPSILON)
    first = st[:, 2:3]
    second = scale * (st[:, 3:4] - mean * first)
    active, slope = gelu_parts(pre[...])
    unit = (active - mean) * scale
    inner_low[...] = (unit * gain[...] + shift[...]).astype(BF16)
    grad = inner_grad[...]
    vectors[...] = jnp.zeros(vectors.shape, F32)
    vectors[0:1, :] = jnp.sum(grad * unit, 0, keepdims=True)
    vectors[1:2, :] = jnp.sum(grad, 0, keepdims=True)
    back = scale * (grad * gain[...] - first / width - unit * (second / width))
    low = (back * slope).astype(BF16)
    pre_grad[...] = low
    halves(Here().core, dot(low, up[...], NT), keep, send)


def outer_kernel(
    length, mid_own, mid_got, other_own, other_got, hidden, cotangent, gain, shift, pieces, packed, st_all,
    inner_vectors, hidden_grad, grad_mixed, st_near, pay_a, pay_b, pay_c, out_grad, all_vectors, scratch,
):
    here, valid = Here(), length[0]
    head0, base, tensor = here.head0, here.base, here.tensor
    row = base + lax.broadcasted_iota(jnp.int32, (TOK, 1), 0)
    upstream = jnp.where(row < valid, cotangent[...].astype(F32), 0.0)
    _, unit, scale = norm_rows(hidden[...], gain[...], shift[...])
    own = mid_own[...].astype(F32) + mid_got[...].astype(F32)
    grad = whole(here.core, own, other_own[...].astype(F32) + other_got[...].astype(F32))
    vectors = [jnp.sum(grad * unit, 0, keepdims=True), jnp.sum(grad, 0, keepdims=True)]
    total = upstream + norm_rows_back(grad, unit, scale, gain[...])
    hidden_grad[...] = total
    hidden_grad.flush()
    branch = total.astype(BF16)

    mean, scale = mix_norm(pieces)
    first, second = jnp.zeros((1, TOK), F32), jnp.zeros((1, TOK), F32)
    for i in range(4):
        grad = dot(packed[i, 0:192, :], branch, NT)
        scratch[i] = grad
        q = grad * mix_parameters(packed, i)[0]
        first += jnp.sum(q, 0, keepdims=True)
        second += jnp.sum(q * (pieces[i].astype(F32) - mean), 0, keepdims=True)
    second = second * scale
    output = pieces[tensor].astype(F32)
    unit = (output - mean) * scale
    grad = scratch[tensor]
    gain_own, shift_own = mix_parameters(packed, tensor)
    low = (unit * gain_own + shift_own).astype(BF16)
    lane = lax.broadcasted_iota(jnp.int32, (1, 128), 1)
    columns = jnp.where(
        lane == 0, jnp.sum(grad * unit, 1, keepdims=True), jnp.where(lane == 1, jnp.sum(grad, 1, keepdims=True), 0.0)
    )
    vectors += [inner_vectors[0:2], jnp.concatenate([columns.T[0:2], jnp.zeros((2, 576), F32)], 1)]
    all_vectors[...] = jnp.concatenate(vectors + [jnp.zeros((2, 768), F32)], 0)
    out_grad[...] = dot(low, branch).astype(BF16)
    out_grad.flush()
    all_vectors.flush()
    back = scale * (grad * gain_own - first / 768 - unit * (second / 768))
    back = back.astype(BF16).astype(F32)
    grad_mixed[...] = back.astype(BF16)
    st_near[...] = jnp.zeros(st_near.shape, F32)
    tails = [[], [], []]
    for h in range(HEADS_HERE):
        rows = slice(h * HDIM, (h + 1) * HDIM)
        mine = back[rows]
        centre = jnp.sum(mine * output[rows], 0, keepdims=True)
        st_near[h : h + 1, :] = st_all[h : h + 1, :]
        st_near[3 + h : 4 + h, :] = centre
        pick_mid, pick_far = picks(head0 + h, base)
        for i, (pay, pick) in enumerate(((pay_a, pick_mid), (pay_b, pick_far), (pay_c, pick_far))):
            share = st_all[3 + 3 * i + h : 4 + 3 * i + h, :]
            terms = list(split3(centre * share)) + [jnp.zeros((13, TOK), F32)]
            wide = jnp.concatenate([mine * share] + terms, 0).astype(BF16)
            small = dot(wide, pick)
            pay[rows, :] = small[0:64].astype(BF16)
            tails[i].append(small[64:67])
    for pay, tail in zip((pay_a, pay_b, pay_c), tails):
        pay[192:208, :] = jnp.concatenate(tail + [jnp.zeros((7, SLOTS), F32)], 0).astype(BF16)


def gradients(left, grad_left, rows_q, rows_g, rights, values, mask=None):
    s = dot(left, rights)
    if mask is not None:
        s = jnp.where(mask, s, NONE)
    w = jnp.exp(s)
    ds = (w * dot(grad_left, values)).astype(BF16)
    dq = dot(rights[0:64], ds, NT)
    return dq, jnp.concatenate([dot(rows_q, ds), dot(rows_g, w.astype(BF16))], 0)


def with_logs(rows, logs):
    minus = split3(jnp.where(logs > NONE * 0.1, -logs, 0.0))
    return jnp.concatenate([rows] + list(minus) + [jnp.zeros((29, logs.shape[1]), F32)], 0)


def with_centres(rows, centres):
    return jnp.concatenate([rows] + list(split3(-centres)) + [jnp.zeros((13, centres.shape[1]), F32)], 0)


def backward_near_kernel(length, q, grad, st, kvs, dq_near, dkv, rows_q, rows_g, left, grad_left, acc_q):
    here, valid = Here(), length[0]
    head0, base, place = here.head0, here.base, here.place
    heads = range(HEADS_HERE)
    for h in heads:
        lo = h * HDIM
        rows = with_logs(own_columns(head0 + h, base, q, lo), st[h : h + 1, :])
        rows_q[h] = rows[0:64].astype(BF16)
        left[h] = rows.T.astype(BF16)
        rows = with_centres(grad[lo : lo + HDIM, :].astype(F32), st[3 + h : 4 + h, :])
        rows_g[h] = rows[0:64].astype(BF16)
        grad_left[h] = rows.T.astype(BF16)
    acc_q[...] = jnp.zeros(acc_q.shape, F32)
    for k in range(PLANE):
        block = lax.rem(place - k + PLANE, PLANE)

        @pl.when(k > place)
        def _():
            dkv[block] = jnp.zeros((384, TOK), BF16)

        @pl.when(k <= place)
        def _():
            mask = diagonal_mask(base, valid) if k == 0 else None
            for h in heads:
                lo = h * HDIM
                keys = near_keys(kvs, place - k, lo, head0 + h, base - k * TOK)
                values = near_values(kvs, place - k, lo)
                dq, both = gradients(left[h], grad_left[h], rows_q[h], rows_g[h], keys, values, mask)
                acc_q[h] += dq
                dkv[block, lo : lo + HDIM, :] = both[0:64].astype(BF16)
                dkv[block, 192 + lo : 192 + lo + HDIM, :] = both[64:128].astype(BF16)

        dkv.flush_part(block)

    for h in heads:
        dq_near[h * HDIM : (h + 1) * HDIM, :] = acc_q[h] * 0.125


def backward_far_kernel(dkv_near, qa, qb, qc, ga, gb, gc, loc, kvs, *refs):
    dq_a, dq_b, dq_c, dkv, small_a, small_f, right_a, right_f, value_a, value_f = refs
    here = Here()
    head0, base, plane = here.head0, here.base, here.plane
    heads = range(HEADS_HERE)
    wait_for(qa, qb, qc, loc)

    def part(queries, pays, first, rights, values, dqs, small):
        n = SLOTS * len(pays)
        for h in heads:
            lo = h * HDIM
            rows = query_columns(head0 + h, base, plane, queries, lo)
            rows = with_logs(rows, loc[h : h + 1, first : first + n])
            columns, centres = [], []
            for pay in pays:
                columns.append(pay[lo : lo + HDIM, :].astype(F32))
                tail = pay[192:208, :].astype(F32)
                centres.append(tail[3 * h : 3 * h + 1] + tail[3 * h + 1 : 3 * h + 2] + tail[3 * h + 2 : 3 * h + 3])
            grads = with_centres(jnp.concatenate(columns, 1), jnp.concatenate(centres, 1))
            dq, both = gradients(
                rows.T.astype(BF16),
                grads.T.astype(BF16),
                rows[0:64].astype(BF16),
                grads[0:64].astype(BF16),
                rights[h],
                values[h],
            )
            dq = (dq * 0.125).astype(BF16)
            for i, out in enumerate(dqs):
                out[lo : lo + HDIM, :] = dq[:, i * SLOTS : (i + 1) * SLOTS]
            small[h] = both.astype(BF16)

    @pl.when((plane == 1) | (plane == 2))
    def _():
        small_a[...] = jnp.zeros(small_a.shape, BF16)
        small_f[...] = jnp.zeros(small_f.shape, BF16)

    @pl.when(lax.rem(plane, 2) == 0)
    def _():
        gather_keys(kvs, head0, plane, False, right_a, value_a)
        part((qa,), (ga,), 0, right_a, value_a, (dq_a,), small_a)

    @pl.when(plane < 2)
    def _():
        gather_keys(kvs, head0, plane, True, right_f, value_f)
        part((qb, qc), (gb, gc), SLOTS, right_f, value_f, (dq_b, dq_c), small_f)

    wait_for(dkv_near)

    @pl.when(plane == 3)
    def _():
        dkv[...] = dkv_near[...]
        for block in range(PLANE):
            dkv.flush_part(block)

    @pl.when(plane < 3)
    def _():
        for block in range(PLANE):
            at = slice(block * SLOTS, (block + 1) * SLOTS)
            for h in heads:
                lo = h * HDIM
                pick = jnp.concatenate(picks(head0 + h, plane * 2048 + block * TOK), 1)
                wide = dot(jnp.concatenate([small_a[h, :, at], small_f[h, :, at]], 1), pick, NT)
                for i, at_row in ((0, lo), (64, 192 + lo)):
                    near = dkv_near[block, at_row : at_row + HDIM, :].astype(F32)
                    dkv[block, at_row : at_row + HDIM, :] = (near + wide[i : i + 64]).astype(BF16)
            dkv.flush_part(block)


def weights_kernel(
    inputs, gain, shift, weights, dq_near, ra, rb, rc, dkv, out_grad, vectors, sums, keep, send, in_sums, grads
):
    here = Here()
    head0, base = here.head0, here.base
    normed, unit, _ = norm_rows(inputs[...].astype(F32), gain[...], shift[...])
    for h in range(HEADS_HERE):
        rows = slice(h * HDIM, (h + 1) * HDIM)
        pick_mid, pick_far = picks(head0 + h, base)
        dq = dq_near[rows, :] + dot(ra[rows, :], pick_mid, NT) + dot(rb[rows, :], pick_far, NT) + dot(rc[rows, :], pick_far, NT)
        grads[rows, :] = dq.astype(BF16)
    total = dkv[0].astype(F32)
    for k in range(1, PLANE):
        total += dkv[k].astype(F32)
    grads[192:576, :] = total.astype(BF16)
    sums[0:12, :, 0:768] = dot(grads[...], normed.astype(BF16)).reshape(12, 48, 768).astype(BF16)
    sums[12:16, :, 0:768] = out_grad[...].astype(F32).reshape(4, 48, 768).astype(BF16)
    sums[:, :, 768:896] = jnp.zeros((16, 48, 128), BF16)
    mixed = jnp.concatenate([vectors[4:5, 0:192], vectors[5:6, 0:192], jnp.zeros((1, 384), F32)], 1)
    for i, v in enumerate((vectors[0:1], vectors[1:2], vectors[2:3], vectors[3:4], mixed)):
        rows = [v[:, j * 128 : (j + 1) * 128] for j in range(6)] + [jnp.zeros((2, 128), F32)]
        sums[i, 0:8, 768:896] = jnp.concatenate(rows, 0).astype(BF16)
    sums.flush()
    back = dot(grads[0:192, :], weights[0], TN)
    back += dot(grads[192:384, :], weights[1], TN)
    back += dot(grads[384:576, :], weights[2], TN)
    halves(here.core, back, keep, send)
    rows = [jnp.sum(back * unit, 0, keepdims=True), jnp.sum(back, 0, keepdims=True), jnp.zeros((6, 768), F32)]
    in_sums[...] = jnp.concatenate(rows, 0)


def reduce_kernel(got, in_sums, weight_sums, out):
    total = got[0].astype(F32)
    for i in range(1, 16):
        total += got[i].astype(F32)
    y_now = Here().y
    rows = [[in_sums[j : j + 1, i * 128 : (i + 1) * 128] for i in range(6)] + [jnp.zeros((2, 128), F32)] for j in (0, 1)]
    rows = jnp.concatenate([*rows[0], *rows[1]], 0)
    for y in range(2):
        tail = total[y * 24 : (y + 1) * 24]
        out[y, :, 0:768] = weight_sums[y, 0:24, :]
        out[y, :, 768:1152] = tail[:, 0:384].astype(BF16)
        out[y, :, 1152:1920] = weight_sums[y, 24:48, :]
        out[y, :, 1920:2304] = tail[:, 384:768].astype(BF16)
        mine = jnp.where(y_now == y, rows, 0.0)
        out[y, :, 2304:2432] = jnp.concatenate([tail[0:8, 768:896], mine], 0).astype(BF16)


def input_grad_kernel(inputs, hidden_grad, gain, shift, own, other, inputs_grad):
    _, unit, scale = norm_rows(inputs[...].astype(F32), gain[...], shift[...])
    grad = whole(Here().core, own[...].astype(F32), other[...].astype(F32))
    inputs_grad[...] = (hidden_grad[...] + norm_rows_back(grad, unit, scale, gain[...])).astype(BF16)


CHUNK = 48
PAIR_A = [(0, 1), (1, 0), (2, 3), (3, 2)]
PAIR_B = [(0, 3), (3, 0), (1, 2), (2, 1)]
STEPS = {"xa": ("x", PAIR_A), "xb": ("x", PAIR_B), "za": ("z", PAIR_A), "zb": ("z", PAIR_B)}


def travel(v, name):
    axis, perm = STEPS[name]
    return lax.ppermute(v, axis, perm)


def slices_kernel(inner_low, pre_grad, mid_blocks, feed_blocks, down, slices, feed_keep, feed_send):
    for first, ref in ((0, inner_low), (192, pre_grad)):
        turned = ref[...].astype(F32).T.astype(BF16)
        for i in range(4):
            slices[i, first : first + 192, :] = turned[i * 192 : (i + 1) * 192]
    for i in range(4):
        slices[i, 384:768, :] = mid_blocks[...]
        slices[i, 768:1152, :] = feed_blocks[...]
    slices.flush()
    halves(Here().core, dot(inner_low[...], down[...]), feed_keep, feed_send)


def products_kernel(slices, others, keep, send, full, *operands):
    here = Here()
    products = []
    for (first, second), rows, columns in zip(((0, 768), (192, 384)), operands[0:2], operands[2:4]):
        for i in range(4):
            columns[:, i * TOK : (i + 1) * TOK] = slices[i, first : first + 192, :]
            for b in range(3):
                block = slice(b * 256, (b + 1) * 256)
                own = pl.multiple_of(i * TOK + here.core * 128, 128)
                other = pl.multiple_of(i * TOK + 128 - here.core * 128, 128)
                rows[pl.ds(own, 128), block] = slices[i, second + b * 128 : second + (b + 1) * 128, :]
                rows[pl.ds(other, 128), block] = others[i, second + b * 128 : second + (b + 1) * 128, :]
        products.append(dot(columns[...], rows[...]))
    down, up = products
    full[:, :, 0:24, :] = down.reshape(4, 2, 24, 768).astype(BF16)
    full[:, :, 24:48, :] = up.reshape(4, 2, 24, 768).astype(BF16)
    high = lax.div(here.plane, 2)
    keep[...] = full[pl.ds(2 * high, 2)]
    send[...] = full[pl.ds(2 - 2 * high, 2)]


def halve_kernel(keep, got, new_keep, new_send):
    i = lax.rem(Here().plane, 2)
    new_keep[...] = (keep[i].astype(F32) + got[i].astype(F32)).astype(BF16)
    new_send[...] = (keep[1 - i].astype(F32) + got[1 - i].astype(F32)).astype(BF16)


def sum_y_kernel(own, other, down, up):
    total = own[...].astype(F32) + other[...].astype(F32)
    down[...] = total[:, :, 0:1152].astype(BF16)
    up[...] = total[:, :, 1152:2432].astype(BF16)


def join_pair(i, name, own, other, out):
    high = lax.div(i, 2)
    if name == "b1":
        out[high] = own[...]
        out[1 - high] = other[...]
    elif name == "a1":
        low = lax.rem(i, 2)
        out[low] = own[...]
        out[1 - low] = other[...]
    elif name == "a2":
        first = jnp.where(high == 0, i, 3 - i)
        out[first] = own[0]
        out[3 - first] = own[1]
        out[1 - first] = other[0]
        out[2 + first] = other[1]
    else:
        out[pl.ds(2 * high, 2)] = own[...]
        out[pl.ds(2 - 2 * high, 2)] = other[...]


def join_kernel(step, own, other, out):
    here = Here()
    join_pair(here.x if step[0] == "x" else here.plane, step[1:], own, other, out)


def join(v, step, after=(), behind=()):
    shape = (4, *v.shape[1:]) if step[2] == "2" else (2, *v.shape)
    (out,) = call(functools.partial(join_kernel, step), [(shape, v.dtype)])(
        v, travel(v, step[0:2]), after=after, behind=behind
    )
    return out


WIDTHS = (512, 640, 640, 640)


def split_kernel(tail_width, full, first, second):
    columns = ((0, 384), (384, 768))
    for out, (lo, hi) in zip((first, second), columns):
        out[:, :, :, 0:384] = full[:, :, :, lo:hi]
    first[:, :, :, 384:] = full[:, :, :, 768 : 768 + tail_width]
    second[:, :, :, 384:] = full[:, :, :, 768 + tail_width :]


def split(v, widths):
    return call(functools.partial(split_kernel, widths[0] - 384), [((4, 2, 24, w), BF16) for w in widths])(v)


def last_places(i, step):
    high = lax.div(i, 2)
    if step == "a":
        first = jnp.where(high == 0, i, 3 - i)
        return (first, 3 - first), (1 - first, 2 + first)
    return (2 * high, 2 * high + 1), (2 - 2 * high, 3 - 2 * high)


def unpack_down_kernel(own0, own1, other0, other1, down, tail):
    x_now = Here().x
    for d, z, y, e in itertools.product(range(2), range(4), range(2), range(2)):
        places = last_places(x_now, "ab"[d])
        for pair, side in ((0, (own0, own1)), (1, (other0, other1))):
            x = places[pair][e]
            value = side[d][e, z, y]
            down[x * 8 + z * 2 + y, :, d * 384 : (d + 1) * 384] = value[:, 0:384].astype(F32)
            tail[z * 8 + x * 2 + y, :, d * 128 : 128 + d * 256] = value[:, 384:]


def unpack_kernel(tail_d, own0, own1, other0, other1, up, head_grad, out_grad, *rest):
    *vectors, up_turned, tail = rest
    plane = Here().plane
    for d, x, y, e in itertools.product(range(2), range(4), range(2), range(2)):
        places = last_places(plane, "ab"[d])
        for pair, side in ((0, (own0, own1)), (1, (other0, other1))):
            z = places[pair][e]
            value = side[d][e, x, y].astype(F32)
            up_turned[x * 8 + z * 2 + y, :, d * 384 : (d + 1) * 384] = value[:, 0:384]
            tail[z * 8 + x * 2 + y, :, d * 256 : 256 + d * 256] = value[:, 384:]
    for ref, rows in ((head_grad, slice(0, 24)), (out_grad, slice(24, 32))):
        ref[:, :, 0:384] = tail_d[rows].astype(F32)
        ref[:, :, 384:768] = tail[rows, :, 0:384]
        ref.flush()
    up[...] = up_turned[...].reshape(768, 768).T
    up.flush()
    rows = [tail[2 * i, 0:6, 384:512] for i in range(5)] + [jnp.sum(tail[:, i : i + 6, 384:512], 0) for i in (8, 16)]
    rows = [jnp.concatenate([v[i : i + 1] for i in range(6)], 1) for v in rows]
    rows[4:5] = [rows[4][:, 0:192], rows[4][:, 192:384]]
    for ref, row in zip(vectors, rows):
        ref[...] = row.reshape(ref.shape)


def add_kernel(a, b, out):
    out[...] = (a[...].astype(F32) + b[...].astype(F32)).astype(out.dtype)


TIMES = {
    "project_kernel": 1.2,
    "forward_far_kernel": 4.3,
    "forward_near_kernel": 7.0,
    "combine_kernel": 1.0,
    "feed_kernel": 1.5,
    "middle_kernel": 3.4,
    "inner_kernel": 2.0,
    "outer_kernel": 4.0,
    "slices_kernel": 3.0,
    "products_kernel": 3.0,
    "backward_near_kernel": 9.0,
    "backward_far_kernel": 7.0,
    "weights_kernel": 4.0,
    "reduce_kernel": 2.0,
    "unpack_kernel": 3.5,
    "unpack_down_kernel": 1.5,
    "join_kernel": 0.1,
}


class Fetched:
    def __init__(self, copies, ref):
        self.copies, self.ref, self.shape = copies, ref, ref.shape

    def wait(self):
        for copy in self.copies:
            copy.wait()
        self.copies = ()

    def __getitem__(self, index):
        self.wait()
        return self.ref[index]


class Stored:
    def __init__(self, copy, ref):
        self.copy, self.ref, self.shape, self.started = copy, ref, ref.shape, False
        self.parts = None

    def flush(self):
        if not self.started:
            self.copy.start()
        self.started = True

    def flush_part(self, i):
        self.started = True
        self.parts(i).start()

    def finish(self):
        self.flush()
        self.copy.wait()

    def __getitem__(self, index):
        return self.ref[index]

    def __setitem__(self, index, value):
        self.ref[index] = value


def part_copy(ref, target, semaphore, i):
    return pltpu.make_async_copy(ref.at[i], target.at[i], semaphore)


def wait_for(*operands):
    for operand in operands:
        if isinstance(operand, Fetched):
            operand.wait()


def call(kernel, out_shapes, scratch=(), scalars=0, limit=8, fetch=(), stacks=(), store=(), free=()):
    def run(*args, after=(), behind=()):
        after = (*after, *[pltpu.with_memory_space_constraint(v, pltpu.HBM) for v in behind])
        n, extra, outs = len(args), len(after), len(out_shapes)
        name = getattr(kernel, "func", kernel).__name__
        vmem, hbm = pl.BlockSpec(memory_space=pltpu.VMEM), pl.BlockSpec(memory_space=pltpu.HBM)
        specs = [vmem] * n + [pl.BlockSpec(memory_space=pl.ANY)] * (extra - len(behind)) + [hbm] * len(behind)
        out_specs = [hbm if i in store else vmem for i in range(outs)]
        for i in range(scalars):
            specs[i] = pl.BlockSpec(memory_space=pltpu.SMEM)
        buffers, sizes = [], {}
        for i in sorted((*fetch, *stacks)):
            sizes[i] = 4 if i in stacks else 1
            for j in range(sizes[i]):
                specs[i + j] = pl.BlockSpec(memory_space=pl.ANY) if i in free else hbm
            shape = args[i].shape
            shape = (4, *shape) if i in stacks else (1, *shape) if len(shape) == 1 else shape
            buffers.append(pltpu.VMEM(shape, args[i].dtype))
        for i in store:
            buffers.append(pltpu.VMEM(*out_shapes[i]))
        total = sum(sizes.values()) + len(store)
        if total:
            buffers.append(pltpu.SemaphoreType.DMA((total,)))

        def body(*refs):
            results = list(refs[n + extra : n + extra + outs])
            own = refs[n + extra + outs : n + extra + outs + len(scratch)]
            landing = refs[n + extra + outs + len(scratch) :]
            operands, pending, i, slot = [], [], 0, 0
            while i < n:
                if i not in sizes:
                    operands.append(refs[i])
                    i += 1
                    continue
                ref, copies = landing[len(pending)], []
                for j in range(sizes[i]):
                    place = ref
                    if i in stacks:
                        place = ref.at[jnp.bitwise_xor(Here().tensor, j)]
                    elif len(args[i].shape) == 1:
                        place = ref.at[0]
                    copies.append(pltpu.make_async_copy(refs[i + j], place, landing[-1].at[slot]))
                    copies[-1].start()
                    slot += 1
                pending.append(Fetched(copies, ref))
                operands.append(pending[-1])
                i += sizes[i]
            for k, i in enumerate(store):
                ref = landing[len(pending) + k]
                copy_target = results[i]
                copy = pltpu.make_async_copy(ref, copy_target, landing[-1].at[slot])
                results[i] = Stored(copy, ref)
                results[i].parts = functools.partial(part_copy, ref, copy_target, landing[-1].at[slot])
                slot += 1
            kernel(*operands, *results, *own)
            for operand in pending:
                operand.wait()
            for i in store:
                results[i].flush()
            for i in store:
                results[i].finish()

        args = list(args)
        for i, size in sizes.items():
            for j in range(i, i + size if i not in free else i):
                args[j] = pltpu.with_memory_space_constraint(args[j], pltpu.HBM)
        return pl.pallas_call(
            body,
            out_shape=[(pltpu.HBM if i in store else jax.ShapeDtypeStruct)(*shape) for i, shape in enumerate(out_shapes)],
            in_specs=specs,
            out_specs=out_specs,
            scratch_shapes=[*scratch, *buffers],
            compiler_params=pltpu.CompilerParams(vmem_limit_bytes=limit * 1024 * 1024),
            name=name,
            cost_estimate=pl.CostEstimate(
                flops=int(TIMES.get(name, 0.6) * 1e9), bytes_accessed=0, transcendentals=0
            ),
        )(*args, *after)

    return run


def add(a, b, after=()):
    (out,) = call(add_kernel, [(a.shape, a.dtype)])(a, b, after=after)
    return out


def others_over_tensor(v):
    across = lax.ppermute(v, "yl", FLIP)
    beside = lax.ppermute(v, "c", FLIP)
    return beside, across, lax.ppermute(across, "c", FLIP)


MID_GO = [(1, 0), (3, 2)]
B_GO = [(2, 0), (3, 1)]
C_GO = [(3, 0), (2, 1)]


def back(perm):
    return [(b, a) for a, b in perm]


def visit(a, b, c, turn=lambda perm: perm):
    return tuple(lax.ppermute(v, "z", turn(perm)) for v, perm in ((a, MID_GO), (b, B_GO), (c, C_GO)))


def per_device(
    inputs,
    head_weights,
    out_weight,
    up_weight,
    down_weight,
    in_gain,
    in_shift,
    mix_gain,
    mix_shift,
    mid_gain,
    mid_shift,
    inner_gain,
    inner_shift,
    valid_length,
    cotangent,
):
    here = Here()
    core = here.core
    row_valid = (here.base + jnp.arange(TOK, dtype=jnp.int32) < valid_length[0])[:, None]
    n = HEADS_HERE
    half = ((128, 768), BF16)

    weights = head_weights.transpose(0, 2, 1)
    q, spread = call(
        project_kernel, [((192, TOK), BF16), ((PLANE, 384, TOK), BF16)], fetch=(0, 1, 2, 3), limit=12
    )(inputs, weights, in_gain, in_shift)
    kvs = lax.all_to_all(spread, ("yh", "x"), 0, 0, tiled=True)
    q_mid, q_far, packed = call(
        select_kernel,
        [((192, SLOTS), BF16), ((192, SLOTS), BF16), ((208, 768), BF16)],
        fetch=(1, 2, 3),
        store=(2,),
    )(q, out_weight, mix_gain, mix_shift)
    visitors = visit(q_mid, q_far, q_far)
    feed_blocks, inner_grad = call(
        feed_kernel,
        [((384, 256), BF16), ((TOK, 768), F32)],
        scalars=1,
        fetch=(1, 2),
        store=(0, 1),
        limit=12,
    )(valid_length, down_weight, cotangent, after=(q_mid,))
    pay_a, pay_b, pay_c, loc = call(
        forward_far_kernel,
        [((208, SLOTS), BF16)] * 3 + [((8, 384), F32)],
        [
            *[pltpu.VMEM((n, 128, KEYS), BF16)] * 2,
            *[pltpu.VMEM((n, 80, KEYS), BF16)] * 2,
        ],
        limit=16,
        store=(3,),
    )(*visitors, kvs, behind=(inner_grad,))
    returned = visit(pay_a, pay_b, pay_c, back)
    packed, _ = lax.optimization_barrier((packed, pay_a))
    packed_beside, packed_across = lax.ppermute(packed, "c", FLIP), lax.ppermute(packed, "yl", FLIP)
    o_near, st_near = call(
        forward_near_kernel,
        [((192, TOK), F32), ((8, TOK), F32)],
        [
            pltpu.VMEM((n, PLANE, 128, TOK), BF16),
            pltpu.VMEM((n, 96, TOK), F32),
            pltpu.VMEM((n, TOK, 128), BF16),
            pltpu.VMEM((n, TOK, 128), F32),
            pltpu.VMEM((n, 80, TOK), F32),
        ],
        scalars=1,
    )(valid_length, q, kvs)
    mixed, st_all = call(combine_kernel, [((192, TOK), BF16), ((16, TOK), F32)])(o_near, st_near, *returned)
    pieces = (mixed, *others_over_tensor(mixed))
    relay, _ = lax.optimization_barrier((packed_across, o_near))
    packed = (packed, packed_beside, packed_across, lax.ppermute(relay, "c", FLIP))
    hidden, pieces, st_all, mid_blocks, pre, sums = call(
        middle_kernel,
        [
            ((TOK, 768), F32),
            ((4, 192, TOK), BF16),
            ((16, TOK), F32),
            ((384, 256), BF16),
            ((TOK, 768), F32),
            ((8, TOK), F32),
        ],
        limit=20,
        fetch=(0, 9, 10, 11, 12, 13),
        stacks=(1, 5),
        free=(1,),
        store=(0, 1, 2),
    )(inputs, *pieces, *packed, up_weight, mid_gain, mid_shift, inner_gain, inner_grad, st_all)
    sums = sums + lax.ppermute(sums, "c", FLIP)
    sums = sums + lax.ppermute(sums, "yl", FLIP)
    inner_low, pre_grad, keep, send, inner_vectors = call(
        inner_kernel,
        [((TOK, 768), BF16), ((TOK, 768), BF16), half, half, ((8, 768), F32)],
        fetch=(2, 3, 4, 5),
        store=(4,),
        limit=12,
    )(sums, pre, inner_grad, up_weight, inner_gain, inner_shift)
    mid_half = add(keep, lax.ppermute(send, "c", FLIP))

    slices, feed_keep, feed_send = call(
        slices_kernel, [((4, 1152, TOK), BF16), half, half], fetch=(3, 4), store=(0,), limit=16
    )(inner_low, pre_grad, mid_blocks, feed_blocks, down_weight, after=(mid_half,))
    slices = lax.all_to_all(slices, "x", 0, 0, tiled=True)
    mid_got = lax.ppermute(mid_half, "yl", FLIP)
    mid_sent, _ = lax.optimization_barrier((mid_got, feed_keep))
    mid_parts = (mid_half, mid_got, lax.ppermute(mid_half, "c", FLIP), lax.ppermute(mid_sent, "c", FLIP))
    hidden_grad, grad_mixed, st_near, pay_a, pay_b, pay_c, out_grad, vectors = call(
        outer_kernel,
        [((TOK, 768), F32), ((192, TOK), BF16), ((8, TOK), F32)]
        + [((208, SLOTS), BF16)] * 3
        + [((192, 768), BF16), ((8, 768), F32)],
        [pltpu.VMEM((4, 192, TOK), F32)],
        limit=20,
        scalars=1,
        fetch=(5, 6, 7, 8, 9, 14, 15),
        stacks=(10,),
        store=(0, 6, 7),
    )(valid_length, *mid_parts, hidden, cotangent, mid_gain, mid_shift, pieces, *packed, st_all, inner_vectors)
    grads = visit(pay_a, pay_b, pay_c)

    dq_near, dkv = call(
        backward_near_kernel,
        [((192, TOK), F32), ((PLANE, 384, TOK), BF16)],
        [
            pltpu.VMEM((n, 64, TOK), BF16),
            pltpu.VMEM((n, 64, TOK), BF16),
            pltpu.VMEM((n, TOK, 128), BF16),
            pltpu.VMEM((n, TOK, 80), BF16),
            pltpu.VMEM((n, HDIM, TOK), F32),
        ],
        scalars=1,
        limit=12,
        store=(0, 1),
    )(valid_length, q, grad_mixed, st_near, kvs)
    dq_a, dq_b, dq_c, dkv = call(
        backward_far_kernel,
        [((192, SLOTS), BF16)] * 3 + [((PLANE, 384, TOK), BF16)],
        [
            pltpu.VMEM((n, 128, KEYS), BF16),
            pltpu.VMEM((n, 128, KEYS), BF16),
            *[pltpu.VMEM((n, 128, KEYS), BF16)] * 2,
            *[pltpu.VMEM((n, 80, KEYS), BF16)] * 2,
        ],
        limit=20,
        fetch=(0, 1, 2, 3, 7),
        store=(3,),
    )(dkv, *visitors, *grads, loc, kvs)
    dkv = lax.all_to_all(dkv, ("yh", "x"), 0, 0, tiled=True)
    dqs = visit(dq_a, dq_b, dq_c, back)

    feed_half = add(feed_keep, lax.ppermute(feed_send, "c", FLIP), after=(dq_a,))
    slices, _ = lax.optimization_barrier((slices, feed_half))
    others = lax.ppermute(slices, "c", FLIP)
    keep, send = call(
        products_kernel,
        [((2, 2, CHUNK, 768), BF16)] * 2,
        [
            pltpu.VMEM((4, 2, CHUNK, 768), BF16),
            *[pltpu.VMEM((4 * TOK, 768), BF16)] * 2,
            *[pltpu.VMEM((192, 4 * TOK), BF16)] * 2,
        ],
        limit=16,
    )(slices, others, after=(dq_a, feed_half))
    keep, send = call(halve_kernel, [((2, CHUNK, 768), BF16)] * 2)(keep, travel(send, "zb"))
    weight_sums = add(keep, travel(send, "za"))
    sums, keep, send, in_sums = call(
        weights_kernel,
        [((16, 48, 896), BF16), half, half, ((8, 768), F32)],
        [pltpu.VMEM((576, TOK), BF16)],
        limit=20,
        fetch=(0, 1, 2, 3, 4, 5, 6, 7, 8, 9, 10),
        store=(0,),
    )(inputs, in_gain, in_shift, weights, dq_near, *dqs, dkv, out_grad, vectors, after=(weight_sums,))
    got = lax.all_to_all(sums, ("z", "x"), 0, 0, tiled=True)
    in_sums = in_sums + lax.ppermute(in_sums, "c", FLIP)
    in_sums = in_sums + lax.ppermute(in_sums, "yl", FLIP)
    (have,) = call(reduce_kernel, [((2, 24, 2432), BF16)])(got, in_sums, weight_sums)
    down, up = call(sum_y_kernel, [((2, 24, 1152), BF16), ((2, 24, 1280), BF16)])(
        have, lax.ppermute(have, "yh", FLIP)
    )
    in_half = add(keep, lax.ppermute(send, "c", FLIP), after=(down,))
    in_half = add(in_half, lax.ppermute(in_half, "yl", FLIP))
    down, up = join(down, "zb1"), join(up, "xb1", after=(in_half,))
    feed_half = add(feed_half, lax.ppermute(feed_half, "yl", FLIP), after=(in_half,))
    feed_other = lax.ppermute(feed_half, "c", FLIP)
    (inputs_grad,) = call(
        input_grad_kernel, [((TOK, 768), BF16)], fetch=(0, 1, 2, 3), store=(0,), limit=12
    )(inputs, hidden_grad, in_gain, in_shift, in_half, lax.ppermute(in_half, "c", FLIP))
    down, up = join(down, "za2"), join(up, "xa2", after=(feed_half,))
    downs = [join(v, step) for v, step in zip(split(down, WIDTHS[0:2]), ("xb1", "xa1"))]
    ups = [join(v, step, behind=(inputs_grad,)) for v, step in zip(split(up, WIDTHS[2:4]), ("zb1", "za1"))]
    down_grad, tail = call(
        unpack_down_kernel,
        [((PARTS, ROW, 768), F32), ((PARTS, ROW, 384), BF16)],
        limit=16,
        store=(0,),
    )(*downs, *[travel(v, name) for v, name in zip(downs, ("xa", "xb"))])
    up_grad, head_grad, out_grad, *vectors = call(
        unpack_kernel,
        [
            ((768, 768), F32),
            ((24, ROW, 768), F32),
            ((8, ROW, 768), F32),
            *[((768,), F32)] * 4,
            *[((192,), F32)] * 2,
            *[((768,), F32)] * 2,
        ],
        [pltpu.VMEM((PARTS, ROW, 768), F32), pltpu.VMEM((PARTS, ROW, 512), F32)],
        limit=24,
        store=(0, 1, 2),
    )(tail, *ups, *[travel(v, name) for v, name in zip(ups, ("za", "zb"))])
    feed_out = jnp.where(
        core == 0, jnp.concatenate([feed_half, feed_other]), jnp.concatenate([feed_other, feed_half])
    ).astype(F32)
    result = jnp.where(row_valid, hidden + feed_out, 0.0).astype(BF16)
    return (
        result,
        inputs_grad,
        head_grad.reshape(3, 192, 768).transpose(0, 2, 1),
        out_grad.reshape(192, 768),
        up_grad,
        down_grad.reshape(768, 768),
        vectors[6],
        vectors[7],
        vectors[4],
        vectors[5],
        vectors[0],
        vectors[1],
        vectors[2],
        vectors[3],
    )


def solution(mesh):
    fine = Mesh(np.asarray(mesh.devices).reshape(4, 2, 4, 2, 2), SEQ + TENSOR)
    in_specs = (
        P(SEQ, None),
        P(None, None, TENSOR),
        P(TENSOR, None),
        P(None, TENSOR),
        P(TENSOR, None),
        P(),
        P(),
        P(TENSOR),
        P(TENSOR),
        P(),
        P(),
        P(TENSOR),
        P(TENSOR),
        P(),
        P(SEQ, None),
    )
    out_specs = (
        P(SEQ, None),
        P(SEQ, None),
        P(None, None, TENSOR),
        P(TENSOR, None),
        P(None, TENSOR),
        P(TENSOR, None),
        P(),
        P(),
        P(TENSOR),
        P(TENSOR),
        P(),
        P(),
        P(TENSOR),
        P(TENSOR),
    )
    return jax.shard_map(per_device, mesh=fine, in_specs=in_specs, out_specs=out_specs, check_vma=False)
```
